32 devices in a mesh: comp: 4 (over x, core), tx: 4 (over z), ty: 2 (over y).
Axes of the slice: x: 2, y: 2, z: 4, core: 2. Of those that a mesh axis runs over, the one named last changes fastest.
Arguments:
- model_state: float32 [4, 4, 8, 512, 512], P('comp', None, None, 'tx', 'ty'), may hold values from -6 to 6
- sea_mask: int32 [4, 512, 512], P('comp', 'tx', 'ty'), may hold values 0 or 1
- wave_speed: float32 [4, 8], P('comp'), may hold values from 0.1 to 0.4
- diffusivity: float32 [4, 8], P('comp'), may hold values from 0.02 to 0.2
- surface_gains: float32 [4, 3], P('comp'), may hold values from 0.1 to 0.5
- area_table: float32 [256], replicated, may hold values from 0.2 to 1
- own_cells: int32 [4, 8, 4, 2048], P('comp', ('tx', 'ty')), may hold values from 0 to 32767
- target_cells: int32 [4, 8, 4, 2048], P('comp', ('tx', 'ty')), may hold values from 0 to 32767
- weight_ids: int32 [4, 8, 4, 2048], P('comp', ('tx', 'ty')), may hold values from 0 to 255
- pair_counts: int32 [4, 8, 4], P('comp', ('tx', 'ty')), may hold values from 512 to 2048, as said below
- fold_map: int32 [512], replicated, may hold values from 0 to 511, as said below
Outputs:
- new_state: float32 [4, 4, 8, 512, 512], P('comp', None, None, 'tx', 'ty')
The draws below stay inside these ranges and needn't reach their ends.
Inputs may be any that keep to these rules, and one draw needn't show every extreme that they name: pair_counts[g, s, n] counts the live slots that position s of component g sends to its partner n; in every component one receiving position gets 2048 from each of the positions that have it as a partner. fold_map[fold_map[x]] == x.
All inputs are finite; a program needn't handle non-finite values. No bound on the sum of `sea_mask` on one device may be relied on, other than what follows from the above.
Results may differ from the reference program's by a relative error of at most 0.0001.
Values sent between devices are 32-bit elements; how exact they have to be, the bound alone decides.
No kernel may reach another device: no remote copies, remote signals or barrier semaphores. Data moves between devices by JAX's collectives and lax.ppermute only.
A program may use at most 192 MiB of HBM per device.

```python
import math
import jax
import jax.numpy as jnp

LEV = 8
CX = 128
CY = 256
NEAR = 4
SLOTS = 2048
AREAS = 256
NPOS = 8
ROWSTEP = 2
NX = 512
NY = 512
N_COMP = 4
N_TX = 4
N_TY = 2


def cell_pairs(key):
    shape = (N_COMP, NPOS, NEAR, SLOTS)
    own = jax.random.randint(jax.random.fold_in(key, 101), shape, 0, CX * CY)
    row_shift = jax.random.randint(jax.random.fold_in(key, 102), shape, -2, 3)
    col_shift = jax.random.randint(jax.random.fold_in(key, 103), shape, -4, 5)
    row = jnp.clip(own // CY + row_shift, 0, CX - 1)
    col = jnp.clip(own % CY + col_shift, 0, CY - 1)
    return (own.astype(jnp.int32), (row * CY + col).astype(jnp.int32))


def draw_own_cells(key, part):
    pairs = cell_pairs(key)
    return pairs[0]


def draw_target_cells(key, part):
    pairs = cell_pairs(key)
    return pairs[1]


def draw_pair_counts(key, part):
    key = jax.random.fold_in(key, 12)
    base_counts = jax.random.randint(jax.random.fold_in(key, 1), (N_COMP, NPOS, NEAR), SLOTS // 4, SLOTS + 1)
    busiest = jax.random.randint(jax.random.fold_in(key, 2), (N_COMP, 1, 1), 0, NPOS)
    sources = jnp.arange(NPOS, dtype=jnp.int32)[None, :, None]
    partners = jnp.arange(NEAR, dtype=jnp.int32)[None, None, :]
    targets = (sources + partners % 2 + partners // 2 * ROWSTEP) % NPOS
    return jnp.where(targets == busiest, SLOTS, base_counts).astype(jnp.int32)


def draw_fold_map(key, part):
    key = jax.random.fold_in(key, 13)
    offset = jax.random.randint(key, (), 0, NX)
    return ((offset - jnp.arange(NX, dtype=jnp.int32)) % NX).astype(jnp.int32)


def set_ends(values, own_key, smallest, top_value):
    shape = values.shape
    index_at = [jax.random.randint(jax.random.fold_in(own_key, axis), (), 0, shape[axis]) for axis in range(len(shape))]
    values = values.at[tuple(index_at)].set(smallest)
    longest = shape.index(max(shape))
    index_at[longest] = (index_at[longest] + 1) % shape[longest]
    return values.at[tuple(index_at)].set(top_value)


def block_scale(rng, extent, cuts, low, top_value):
    def one(axis_at, blocks):
        steps = jax.random.uniform(jax.random.fold_in(jax.random.fold_in(rng, 6), axis_at), (blocks,), jnp.float32, low / len(cuts), top_value / len(cuts))
        return jnp.repeat(jnp.exp(steps), extent[axis_at] // blocks).reshape((-1,) + (1,) * (len(extent) - axis_at - 1))

    gain = one(*cuts[0])
    for cut in cuts[1:]:
        gain = gain * one(*cut)
    return gain


def noise(key, shape, scale, bound, pieces=(), kind=jnp.bfloat16):
    result = scale * jax.random.normal(key, shape, jnp.float32)
    if pieces:
        result = result * block_scale(key, shape, pieces, -0.22, 0.18)
    return jnp.clip(result, -bound, bound).astype(kind)


def setup_inputs(seed: int = 0) -> dict:
    key_of = jax.random.split(jax.random.key(seed), 12)
    model_state = noise(key_of[0], (N_COMP, 4, LEV, NX, NY), 1.0, 6.0, ((0, 4), (3, 4), (4, 2)), jnp.float32)
    sea_mask = set_ends((jax.random.randint(key_of[1], (N_COMP, NX, NY), 0, 10) < 7).astype(jnp.int32), jax.random.fold_in(key_of[1], 1), 0, 1)
    wave_speed = jnp.clip(jnp.exp(math.log(0.4) - 1.3862944 * jax.random.uniform(key_of[2], (N_COMP, LEV), jnp.float32) ** block_scale(key_of[2], (N_COMP, LEV), ((0, 4),), -0.2, 0.2)), 0.1, 0.4)
    diffusivity = jnp.clip(jnp.exp(math.log(0.2) - 2.3025851 * jax.random.uniform(key_of[3], (N_COMP, LEV), jnp.float32) ** block_scale(key_of[3], (N_COMP, LEV), ((0, 4),), -0.2, 0.2)), 0.02, 0.2)
    surface_gains = jnp.clip(jnp.exp(math.log(0.5) - 1.609438 * jax.random.uniform(key_of[4], (N_COMP, 3), jnp.float32) ** block_scale(key_of[4], (N_COMP, 3), ((0, 4),), -0.2, 0.2)), 0.1, 0.5)
    area_table = jnp.clip(jnp.exp(jax.random.uniform(key_of[5], (AREAS,), jnp.float32, math.log(0.2), math.log(1.0))), 0.2, 1.0)
    own_cells = draw_own_cells(jax.random.fold_in(key_of[11], 71), 0)
    target_cells = draw_target_cells(jax.random.fold_in(key_of[11], 71), 0)
    weight_ids = set_ends(jax.random.randint(key_of[8], (N_COMP, NPOS, NEAR, SLOTS), 0, AREAS), jax.random.fold_in(key_of[8], 1), 0, AREAS - 1).astype(jnp.int32)
    pair_counts = draw_pair_counts(jax.random.fold_in(key_of[11], 71), 0)
    fold_map = draw_fold_map(jax.random.fold_in(key_of[11], 71), 0)
    return {"model_state": model_state, "sea_mask": sea_mask, "wave_speed": wave_speed, "diffusivity": diffusivity, "surface_gains": surface_gains, "area_table": area_table, "own_cells": own_cells, "target_cells": target_cells, "weight_ids": weight_ids, "pair_counts": pair_counts, "fold_map": fold_map}


def to_tiles(grid):
    leading = grid.shape[:-2]
    blocks = grid.reshape(leading + (N_TX, CX, N_TY, CY))
    blocks = jnp.moveaxis(blocks, -3, -2)
    return blocks.reshape(leading + (N_TX * N_TY, CX * CY))


def from_tiles(tiled):
    leading = tiled.shape[:-2]
    blocks = tiled.reshape(leading + (N_TX, N_TY, CX, CY))
    blocks = jnp.moveaxis(blocks, -2, -3)
    return blocks.reshape(leading + (N_TX * CX, N_TY * CY))


def surface_sums(model_state, area_table, own_cells, target_cells, weight_ids, pair_counts):
    positions = N_TX * N_TY
    tile_size = CX * CY
    slot_ids = jnp.arange(SLOTS, dtype=jnp.int32)[None, None, None, :]
    living = slot_ids < pair_counts[..., None]
    weight = jnp.where(living, area_table[weight_ids], 0.0).astype(jnp.float32)
    surface = to_tiles(model_state[:, :, 0])
    groups = jnp.arange(N_COMP, dtype=jnp.int32)[:, None, None, None]
    sources = jnp.arange(positions, dtype=jnp.int32)[None, :, None, None]
    partners = jnp.arange(NEAR, dtype=jnp.int32)[None, None, :, None]
    offsets = partners % 2 + (partners // 2) * ROWSTEP
    targets = ((sources + offsets) % positions).astype(jnp.int32)
    receiver = jnp.where(groups == N_COMP - 1, slot_ids % (N_COMP - 1), N_COMP - 1).astype(jnp.int32)
    anchor = ((groups * positions + sources) * tile_size + own_cells).reshape(-1)
    placed = ((receiver * positions + targets) * tile_size + target_cells).reshape(-1)
    weight_flat = weight.reshape(-1)
    segments = N_COMP * positions * tile_size
    totals = []
    for column in (3, 1, 2):
        picked = surface[:, column].reshape(-1)[anchor]
        totals.append(jax.ops.segment_sum(weight_flat * picked, placed, segments))
    totals.append(jax.ops.segment_sum(weight_flat, placed, segments))
    stacked = jnp.stack([summed.reshape(N_COMP, positions, tile_size) for summed in totals], axis=1)
    return from_tiles(stacked)


def extend_component(fields, parity, fold_map, is_ocean):
    zero_column = jnp.zeros(fields.shape[:-2] + (1, fields.shape[-1]), jnp.float32)
    zero_row = jnp.zeros(fields.shape[:-1] + (1,), jnp.float32)
    if is_ocean:
        west_edge = fields[..., -1:, :]
        east_edge = fields[..., :1, :]
        north_edge = parity * fields[:, :, fold_map, -1][..., None]
    else:
        west_edge = zero_column
        east_edge = zero_column
        north_edge = zero_row
    middle = jnp.concatenate([zero_row, fields, north_edge], axis=-1)
    corner = jnp.zeros(fields.shape[:-2] + (1, 1), jnp.float32)
    west_edge = jnp.concatenate([corner, west_edge, corner], axis=-1)
    east_edge = jnp.concatenate([corner, east_edge, corner], axis=-1)
    return jnp.concatenate([west_edge, middle, east_edge], axis=-2)


def reference(model_state, sea_mask, wave_speed, diffusivity, surface_gains, area_table, own_cells, target_cells, weight_ids, pair_counts, fold_map):
    fluxes = surface_sums(model_state, area_table, own_cells, target_cells, weight_ids, pair_counts)
    results = []
    for component in range(N_COMP):
        is_ocean = component == N_COMP - 1
        fields = model_state[component]
        sea_cells = sea_mask[component].astype(jnp.float32)
        pressure, zonal, meridional, tracer = fields[0], fields[1], fields[2], fields[3]
        first_level = (jnp.arange(LEV, dtype=jnp.int32) == 0)[:, None, None]
        if is_ocean:
            keeping = jnp.broadcast_to(sea_cells, pressure.shape)
            tendency_mask = sea_cells
        else:
            keeping = jnp.where(first_level, 1.0 - surface_gains[component, 2] * (1.0 - sea_cells), 1.0)
            tendency_mask = jnp.ones_like(sea_cells)
        wave_factor = wave_speed[component][:, None, None]
        spread = diffusivity[component][:, None, None]
        scalars = extend_component(jnp.stack([pressure, tracer]), 1.0, fold_map, is_ocean)
        pressure_pad, tracer_pad = scalars[0], scalars[1]
        new_zonal = keeping * (zonal - 0.5 * wave_factor * (pressure_pad[:, 2:, 1:-1] - pressure_pad[:, :-2, 1:-1]))
        new_meridional = keeping * (meridional - 0.5 * wave_factor * (pressure_pad[:, 1:-1, 2:] - pressure_pad[:, 1:-1, :-2]))
        laplace = tracer_pad[:, 2:, 1:-1] + tracer_pad[:, :-2, 1:-1] + tracer_pad[:, 1:-1, 2:] + tracer_pad[:, 1:-1, :-2] - 4.0 * tracer
        new_tracer = tracer + spread * tendency_mask * laplace
        velocity = extend_component(jnp.stack([new_zonal, new_meridional]), -1.0, fold_map, is_ocean)
        divergence = velocity[0][:, 2:, 1:-1] - velocity[0][:, :-2, 1:-1] + velocity[1][:, 1:-1, 2:] - velocity[1][:, 1:-1, :-2]
        new_pressure = pressure - 0.5 * wave_factor * divergence
        heat_sum, east_sum, north_sum, area_sum = fluxes[component][0], fluxes[component][1], fluxes[component][2], fluxes[component][3]
        new_tracer = new_tracer.at[0].add(tendency_mask * surface_gains[component, 0] * (heat_sum - area_sum * tracer[0]))
        new_zonal = new_zonal.at[0].add(tendency_mask * surface_gains[component, 1] * (east_sum - area_sum * zonal[0]))
        new_meridional = new_meridional.at[0].add(tendency_mask * surface_gains[component, 1] * (north_sum - area_sum * meridional[0]))
        results.append(jnp.stack([new_pressure, new_zonal, new_meridional, new_tracer]))
    return jnp.stack(results)
```

```python
import functools

import jax
import jax.numpy as jnp
from jax import lax
from jax.experimental import pallas as pl
from jax.experimental.pallas import tpu as pltpu
from jax.sharding import PartitionSpec as P

LANES = 128
VMEM_BYTES = 56 * 1024 * 1024
F32 = jnp.float32
BF16 = jnp.bfloat16
I32 = jnp.int32

EDGE_P, SECOND_P, EDGE_VELOCITY, EDGE_T = range(4)
CHANNELS = 5


def split_two(values):
    high = values.astype(BF16)
    low = (values - high.astype(F32)).astype(BF16)
    return high, low


def iota(shape, dim):
    return lax.broadcasted_iota(I32, shape, dim)


def halo_rows(levels):
    return (4 * levels + 1 + 7) // 8 * 8


def pack_body(levels, rows, cols, y_pair, state_ref, mask_ref, up_ref, down_ref, *y_refs):
    level = pl.program_id(0)
    height = halo_rows(levels)
    pressure, zonal, meridional, tracer = (state_ref[0, v, 0] for v in range(4))
    lane = iota((rows, LANES), 1)

    def put_rows(ref, row, values):
        for part in range(cols // LANES):
            ref[pl.ds(part * height + row, 1), :] = values[:, part * LANES : (part + 1) * LANES]

    def row_of(field, at):
        return field[at : at + 1, :]

    for ref, edge, second in ((up_ref, rows - 1, rows - 2), (down_ref, 0, 1)):
        put_rows(ref, EDGE_P * levels + level, row_of(pressure, edge))
        put_rows(ref, SECOND_P * levels + level, row_of(pressure, second))
        put_rows(ref, EDGE_VELOCITY * levels + level, row_of(zonal, edge))
        put_rows(ref, EDGE_T * levels + level, row_of(tracer, edge))

    def columns(field_list):
        picked = []
        for field, at in field_list:
            picked.append(jnp.broadcast_to(field[:, at : at + 1], (rows, LANES)))
        return picked

    high = columns(((pressure, cols - 1), (pressure, cols - 2), (meridional, cols - 1), (tracer, cols - 1)))
    low = columns(((pressure, 0), (pressure, 1), (meridional, 0), (tracer, 0)))

    def put_columns(ref, start, values):
        block = ref[pl.ds(start, rows), :]
        for q in range(4):
            block = jnp.where(lane == q * levels + level, values[q], block)
        ref[pl.ds(start, rows), :] = block

    fold_start = height * (cols // LANES)

    @pl.when(level == 0)
    def _():
        sea = mask_ref[0].astype(F32)
        at = 4 * levels
        for ref, edge in ((up_ref, rows - 1), (down_ref, 0)):
            for part in range(cols // LANES):
                ref[part * height + at : (part + 1) * height, :] = jnp.zeros((height - at, LANES), F32)
            put_rows(ref, at, row_of(sea, edge))
        sea_high = jnp.where(lane == at, jnp.broadcast_to(sea[:, cols - 1 : cols], (rows, LANES)), 0.0)
        sea_low = jnp.where(lane == at, jnp.broadcast_to(sea[:, 0:1], (rows, LANES)), 0.0)
        up_ref[fold_start : fold_start + rows, :] = sea_high
        if y_pair:
            first = lax.axis_index("ty") == 0
            y_refs[0][...] = jnp.where(first, sea_high, sea_low)
        else:
            y_refs[0][...] = sea_low

    put_columns(up_ref, fold_start, high)
    if y_pair:
        first = lax.axis_index("ty") == 0
        put_columns(y_refs[0], 0, [jnp.where(first, h, lo) for h, lo in zip(high, low)])
    else:
        put_columns(y_refs[0], 0, low)

    @pl.when(level == levels - 1)
    def _():
        down_ref[fold_start : fold_start + rows, :] = up_ref[fold_start : fold_start + rows, :]


def pack_halos(model_state, sea_mask, y_pair):
    levels, rows, cols = model_state.shape[2:]
    height = halo_rows(levels) * (cols // LANES)
    tall = jax.ShapeDtypeStruct((height + rows, LANES), F32)
    whole = lambda shape: pl.BlockSpec(shape, lambda l: (0,) * len(shape))
    return pl.pallas_call(
        functools.partial(pack_body, levels, rows, cols, y_pair),
        grid=(levels,),
        in_specs=[
            pl.BlockSpec((1, 4, 1, rows, cols), lambda l: (0, 0, l, 0, 0)),
            whole((1, rows, cols)),
        ],
        out_specs=[whole((height + rows, LANES))] * 2 + [whole((rows, LANES))],
        out_shape=[tall, tall, jax.ShapeDtypeStruct((rows, LANES), F32)],
        compiler_params=pltpu.CompilerParams(vmem_limit_bytes=VMEM_BYTES),
    )(model_state, sea_mask)


def gather_body(rows, cols, slots, state_ref, own_ref, target_ref, ids_ref, table_ref, counts_ref, *rest):
    out_refs, fields_ref = rest[:-1], rest[-1]
    near = own_ref.shape[2]
    for v in range(3):
        high, low = split_two(state_ref[0, v + 1, 0])
        fields_ref[v * rows : (v + 1) * rows, :] = high
        fields_ref[(v + 3) * rows : (v + 4) * rows, :] = low
    step = 512
    tables = [
        jnp.broadcast_to(table_ref[t : t + 1, :], (8, LANES)) for t in range(table_ref.shape[0])
    ]
    col_ids = iota((cols, step), 0)
    row_ids = iota((rows, step), 0)
    lane = iota((1, LANES), 1)
    for n in range(near):
        count = counts_ref[0, 0, n]

        def one(c, carry, n=n, count=count):
            start = pl.multiple_of(c * step, step)
            cells = own_ref[0, 0, n : n + 1, pl.ds(start, step)]
            picks = (col_ids == cells % cols).astype(F32).astype(BF16)
            found = jnp.dot(fields_ref[...], picks, preferred_element_type=F32)
            in_row = row_ids == cells // cols
            values = []
            for v in range(3):
                both = found[v * rows : (v + 1) * rows] + found[(v + 3) * rows : (v + 4) * rows]
                values.append(jnp.sum(jnp.where(in_row, both, 0.0), axis=0, keepdims=True))
            for part in range(step // LANES):
                at = c * (step // LANES) + part
                here = pl.multiple_of(start + part * LANES, LANES)
                ids = jnp.broadcast_to(ids_ref[0, 0, n : n + 1, pl.ds(here, LANES)], (8, LANES))
                weight = jnp.zeros((8, LANES), F32)
                for t, table in enumerate(tables):
                    looked = jnp.take_along_axis(table, ids % LANES, axis=1)
                    weight = jnp.where(ids // LANES == t, looked, weight)
                weight = jnp.where(here + lane < count, weight[:1], 0.0)
                cut = slice(part * LANES, (part + 1) * LANES)
                out = out_refs[n]
                out[0, pl.ds(at, 1), :] = weight * values[2][:, cut]
                out[1, pl.ds(at, 1), :] = weight * values[0][:, cut]
                out[2, pl.ds(at, 1), :] = weight * values[1][:, cut]
                out[3, pl.ds(at, 1), :] = weight
                out[4, pl.ds(at, 1), :] = target_ref[0, 0, n : n + 1, pl.ds(here, LANES)].astype(F32)
            return carry

        lax.fori_loop(0, slots // step, one, 0)


def gather_slots(model_state, own_cells, target_cells, weight_ids, area_table, pair_counts):
    rows, cols = model_state.shape[3:]
    near, slots = own_cells.shape[2:]
    table = area_table.reshape(-1, LANES)
    whole = lambda shape: pl.BlockSpec(shape, lambda i: (0,) * len(shape))
    slab = (CHANNELS, slots // LANES, LANES)
    return pl.pallas_call(
        functools.partial(gather_body, rows, cols, slots),
        grid=(1,),
        in_specs=[
            whole((1, 4, 1, rows, cols)),
            whole(own_cells.shape),
            whole(target_cells.shape),
            whole(weight_ids.shape),
            whole(table.shape),
            pl.BlockSpec(memory_space=pltpu.SMEM),
        ],
        out_specs=[whole(slab)] * near,
        out_shape=[jax.ShapeDtypeStruct(slab, F32)] * near,
        scratch_shapes=[pltpu.VMEM((6 * rows, cols), BF16)],
        compiler_params=pltpu.CompilerParams(vmem_limit_bytes=VMEM_BYTES),
    )(model_state, own_cells, target_cells, weight_ids, table, pair_counts)


def stencil_body(
    levels, rows, cols, comps, count_x, count_y,
    state_ref, mask_ref, west_ref, east_ref, south_ref, north_ref, own_ref, fold_ref,
    wave_ref, spread_ref, gains_ref, *rest,
):
    far_refs, out_ref, turned_ref = rest[:-2], rest[-2], rest[-1]
    level = pl.program_id(0)
    height = halo_rows(levels)
    fold_start = height * (cols // LANES)
    index_x = lax.axis_index("tx")
    index_y = lax.axis_index("ty")
    is_ocean = lax.axis_index("comp") == comps - 1
    last_y = index_y == count_y - 1
    mask_at = 4 * levels

    @pl.when(level == 0)
    def _():
        fold = fold_ref[pl.ds(index_x, 1), :]
        total = jnp.zeros((rows, LANES), F32)
        sources = [(0, own_ref), (-1, west_ref), (1, east_ref)]
        sources += [(shift, ref) for shift, ref in zip(range(2, count_x - 1), far_refs)]
        for shift, ref in sources:
            at = lax.rem(index_x + shift + count_x, count_x)
            block = ref[...] if ref.shape[0] == rows else ref[fold_start : fold_start + rows, :]
            chosen = (iota((rows, rows), 0) + at * rows == fold).astype(F32)
            total += lax.dot_general(
                chosen, block, (((0,), (0,)), ((), ())),
                precision=lax.Precision.HIGHEST, preferred_element_type=F32,
            )
        lane = iota((rows, LANES), 1)
        flipped = jnp.logical_and(lane >= EDGE_VELOCITY * levels, lane < (EDGE_VELOCITY + 1) * levels)
        total = jnp.where(flipped, -total, total)
        turned_ref[...] = jnp.where(
            last_y, jnp.where(is_ocean, total, 0.0), north_ref[...]
        )

    pressure, zonal, meridional, tracer = (state_ref[0, v, 0] for v in range(4))
    sea = mask_ref[0].astype(F32)
    half = 0.5 * wave_ref[0, level]
    spread = spread_ref[0, level]
    drag = gains_ref[0, 2]

    def keeping(sea_values):
        first = jnp.where(level == 0, drag, 0.0)
        return jnp.where(is_ocean, sea_values, 1.0 - first * (1.0 - sea_values))

    has_west = jnp.where(jnp.logical_or(is_ocean, index_x > 0), 1.0, 0.0)
    has_east = jnp.where(jnp.logical_or(is_ocean, index_x < count_x - 1), 1.0, 0.0)
    has_south = jnp.where(index_y > 0, 1.0, 0.0)
    has_north = jnp.where(jnp.logical_or(is_ocean, jnp.logical_not(last_y)), 1.0, 0.0)

    def row_at(ref, row):
        parts = [ref[pl.ds(p * height + row, 1), :] for p in range(cols // LANES)]
        return jnp.concatenate(parts, axis=1)

    def west_row(q):
        return row_at(west_ref, q * levels + level)

    def east_row(q):
        return row_at(east_ref, q * levels + level)

    def south_col(at):
        return pltpu.roll(south_ref[...], lax.rem(LANES - at, LANES), 1)

    def north_col(at):
        return pltpu.roll(turned_ref[...], LANES - 1 - at, 1)

    row_ids = iota((rows, cols), 0)
    col_ids = iota((rows, cols), 1)

    def from_west(field, edge):
        return jnp.where(row_ids == 0, edge, pltpu.roll(field, 1, 0))

    def from_east(field, edge):
        return jnp.where(row_ids == rows - 1, edge, pltpu.roll(field, rows - 1, 0))

    def from_south(field, edge):
        wide = jnp.concatenate([edge, jnp.zeros((rows, cols - LANES), F32)], axis=1)
        return jnp.where(col_ids == 0, wide, pltpu.roll(field, 1, 1))

    def from_north(field, edge):
        wide = jnp.concatenate([jnp.zeros((rows, cols - LANES), F32), edge], axis=1)
        return jnp.where(col_ids == cols - 1, wide, pltpu.roll(field, cols - 1, 1))

    keep = keeping(sea)
    tendency = jnp.where(is_ocean, sea, 1.0)
    new_zonal = keep * (
        zonal
        - half * (
            from_east(pressure, has_east * east_row(EDGE_P))
            - from_west(pressure, has_west * west_row(EDGE_P))
        )
    )
    south_p = south_col(EDGE_P * levels + level)
    north_p = north_col(EDGE_P * levels + level)
    new_meridional = keep * (
        meridional
        - half * (from_north(pressure, has_north * north_p) - from_south(pressure, has_south * south_p))
    )
    laplace = (
        from_east(tracer, has_east * east_row(EDGE_T))
        + from_west(tracer, has_west * west_row(EDGE_T))
        + from_north(tracer, has_north * north_col(EDGE_T * levels + level))
        + from_south(tracer, has_south * south_col(EDGE_T * levels + level))
        - 4.0 * tracer
    )
    new_tracer = tracer + spread * tendency * laplace
    west_zonal = keeping(row_at(west_ref, mask_at)) * (
        west_row(EDGE_VELOCITY) - half * (pressure[0:1, :] - west_row(SECOND_P))
    )
    east_zonal = keeping(row_at(east_ref, mask_at)) * (
        east_row(EDGE_VELOCITY) - half * (east_row(SECOND_P) - pressure[rows - 1 : rows, :])
    )
    south_meridional = keeping(south_col(mask_at)) * (
        south_col(EDGE_VELOCITY * levels + level)
        - half * (pressure[:, :LANES] - south_col(SECOND_P * levels + level))
    )
    north_meridional = keeping(north_col(mask_at)) * (
        north_col(EDGE_VELOCITY * levels + level)
        - half * (north_col(SECOND_P * levels + level) - pressure[:, cols - LANES :])
    )
    divergence = (
        from_east(new_zonal, has_east * east_zonal)
        - from_west(new_zonal, has_west * west_zonal)
        + from_north(new_meridional, has_north * north_meridional)
        - from_south(new_meridional, has_south * south_meridional)
    )
    out_ref[0, 0, 0] = pressure - half * divergence
    out_ref[0, 1, 0] = new_zonal
    out_ref[0, 2, 0] = new_meridional
    out_ref[0, 3, 0] = new_tracer


def stencil(model_state, sea_mask, west, east, south, north, own, fars, fold_map, wave_speed, diffusivity, gains, sizes):
    comps, count_x, count_y = sizes
    levels, rows, cols = model_state.shape[2:]
    fold = fold_map.reshape(count_x, rows)
    whole = lambda array: pl.BlockSpec(array.shape, lambda l: (0,) * array.ndim)
    scalar = pl.BlockSpec(memory_space=pltpu.SMEM)
    own_rows = pl.BlockSpec(own.shape, lambda l: (0, 0))
    field = pl.BlockSpec((1, 4, 1, rows, cols), lambda l: (0, 0, l, 0, 0))
    return pl.pallas_call(
        functools.partial(stencil_body, levels, rows, cols, comps, count_x, count_y),
        grid=(levels,),
        in_specs=[
            field, whole(sea_mask), whole(west), whole(east), whole(south), whole(north),
            own_rows, whole(fold), scalar, scalar, scalar,
        ] + [whole(far) for far in fars],
        out_specs=field,
        out_shape=jax.ShapeDtypeStruct(model_state.shape, F32),
        scratch_shapes=[pltpu.VMEM((rows, LANES), F32)],
        compiler_params=pltpu.CompilerParams(vmem_limit_bytes=VMEM_BYTES),
    )(model_state, sea_mask, west, east, south, north, own, fold, wave_speed, diffusivity, gains, *fars)


def scatter_body(rows, cols, comps, block_count, new_ref, state_ref, mask_ref, gains_ref, *rest):
    slab_refs, out_ref = rest[:block_count], rest[block_count]
    spread_ref, column_ref, total_ref = rest[block_count + 1 :]
    here = lax.axis_index("comp")
    is_ocean = here == comps - 1
    near, channels, groups, lanes = slab_refs[0].shape
    total_ref[...] = jnp.zeros_like(total_ref)
    row_ids = iota((rows, lanes), 0)
    col_ids = iota((cols, lanes), 0)
    lane = iota((1, lanes), 1)
    for slab_ref in slab_refs:

        def one(n, carry, slab_ref=slab_ref):
            for g in range(groups):
                cells = slab_ref[n, 4, g : g + 1, :].astype(I32)
                slot = lane + g * lanes
                mine = jnp.logical_or(is_ocean, slot % (comps - 1) == here)
                row = jnp.where(mine, cells // cols, -1)
                cut = slice(g * lanes, (g + 1) * lanes)
                column_ref[:, cut] = (col_ids == cells % cols).astype(F32).astype(BF16)
                in_row = row_ids == row
                for v in range(4):
                    high, low = split_two(slab_ref[n, v, g : g + 1, :])
                    spread_ref[v * rows : (v + 1) * rows, cut] = jnp.where(
                        in_row, high.astype(F32), 0.0
                    ).astype(BF16)
                    spread_ref[(v + 4) * rows : (v + 5) * rows, cut] = jnp.where(
                        in_row, low.astype(F32), 0.0
                    ).astype(BF16)
            total_ref[...] += lax.dot_general(
                spread_ref[...], column_ref[...], (((1,), (1,)), ((), ())),
                preferred_element_type=F32,
            )
            return carry

        lax.fori_loop(0, near, one, 0)

    sea = mask_ref[0].astype(F32)
    tendency = jnp.where(is_ocean, sea, 1.0)
    sums = [
        total_ref[v * rows : (v + 1) * rows, :] + total_ref[(v + 4) * rows : (v + 5) * rows, :]
        for v in range(4)
    ]
    out_ref[0, 0, 0] = new_ref[0, 0, 0]
    for v, total, gain in ((3, sums[0], 0), (1, sums[1], 1), (2, sums[2], 1)):
        change = tendency * gains_ref[0, gain] * (total - sums[3] * state_ref[0, v, 0])
        out_ref[0, v, 0] = new_ref[0, v, 0] + change


def scatter_slots(new_state, model_state, sea_mask, gains, slabs, comps):
    rows, cols = model_state.shape[3:]
    near, channels, groups, lanes = slabs[0].shape
    whole = lambda array: pl.BlockSpec(array.shape, lambda i: (0,) * array.ndim)
    surface = pl.BlockSpec((1, 4, 1, rows, cols), lambda i: (0, 0, 0, 0, 0))
    return pl.pallas_call(
        functools.partial(scatter_body, rows, cols, comps, len(slabs)),
        grid=(1,),
        in_specs=[surface, surface, whole(sea_mask), pl.BlockSpec(memory_space=pltpu.SMEM)]
        + [whole(slab) for slab in slabs],
        out_specs=surface,
        out_shape=jax.ShapeDtypeStruct(new_state.shape, F32),
        scratch_shapes=[
            pltpu.VMEM((8 * rows, groups * lanes), BF16),
            pltpu.VMEM((cols, groups * lanes), BF16),
            pltpu.VMEM((8 * rows, cols), F32),
        ],
        input_output_aliases={0: 0},
        compiler_params=pltpu.CompilerParams(vmem_limit_bytes=VMEM_BYTES),
    )(new_state, model_state, sea_mask, gains, *slabs)


def shards(
    model_state, sea_mask, wave_speed, diffusivity, surface_gains, area_table,
    own_cells, target_cells, weight_ids, pair_counts, fold_map,
):
    comps, count_x, count_y = (lax.axis_size(a) for a in ("comp", "tx", "ty"))
    positions = count_x * count_y

    def around(block, shift):
        return lax.ppermute(block, "tx", [(i, (i + shift) % count_x) for i in range(count_x)])

    y_pair = count_y == 2
    up, down, y_block = pack_halos(model_state, sea_mask, y_pair)
    rows = model_state.shape[3]
    own_high = up[up.shape[0] - rows :]
    west = around(up, 1)
    east = around(down, -1)
    if y_pair:
        south = north = lax.ppermute(y_block, "ty", [(0, 1), (1, 0)])
    else:
        south = lax.ppermute(own_high, "ty", [(j, j + 1) for j in range(count_y - 1)])
        north = lax.ppermute(y_block, "ty", [(j + 1, j) for j in range(count_y - 1)])
    fars = []
    for shift in range(2, count_x - 1):
        pairs = []
        for i in range(count_x):
            ends = [((comps - 1) * count_x + k) * count_y + count_y - 1 for k in ((i + shift) % count_x, i)]
            pairs.append(tuple(ends))
        fars.append(lax.ppermute(own_high, ("comp", "tx", "ty"), pairs))

    slabs = gather_slots(model_state, own_cells, target_cells, weight_ids, area_table, pair_counts)
    arrived = [slabs[0]]
    for n in range(1, len(slabs)):
        offset = n % 2 + n // 2 * count_y
        arrived.append(
            lax.ppermute(slabs[n], ("tx", "ty"), [(s, (s + offset) % positions) for s in range(positions)])
        )
    arrived = jnp.stack(arrived)
    received = [
        lax.ppermute(arrived, "comp", [(g, comps - 1), (comps - 1, g)]) for g in range(comps - 1)
    ]
    new_state = stencil(
        model_state, sea_mask, west, east, south, north, own_high, fars, fold_map,
        wave_speed, diffusivity, surface_gains, (comps, count_x, count_y),
    )
    return scatter_slots(new_state, model_state, sea_mask, surface_gains, received, comps)


def solution(mesh):
    in_specs = (
        P("comp", None, None, "tx", "ty"),
        P("comp", "tx", "ty"),
        P("comp", None),
        P("comp", None),
        P("comp", None),
        P(),
        P("comp", ("tx", "ty"), None, None),
        P("comp", ("tx", "ty"), None, None),
        P("comp", ("tx", "ty"), None, None),
        P("comp", ("tx", "ty"), None),
        P(),
    )
    out_specs = P("comp", None, None, "tx", "ty")
    return jax.shard_map(shards, mesh=mesh, in_specs=in_specs, out_specs=out_specs, check_vma=False)
```

```python
import functools

import jax
import jax.numpy as jnp
from jax import lax
from jax.experimental import pallas as pl
from jax.experimental.pallas import tpu as pltpu
from jax.sharding import PartitionSpec as P

LANES = 128
PACKED = 16
VMEM_BYTES = 28 * 1024 * 1024
F32 = jnp.float32
BF16 = jnp.bfloat16
I32 = jnp.int32
CHANNELS = 5

EDGE_P, SECOND_P, EDGE_VELOCITY, EDGE_T, MASK = range(5)


def iota(shape, dim):
    return lax.broadcasted_iota(I32, shape, dim)


def halo_rows(levels):
    return (4 * levels + 1 + 7) // 8 * 8


def split_two(values):
    high = values.astype(BF16)
    low = (values - high.astype(F32)).astype(BF16)
    return high, low


def packed_ids(count):
    ids = iota((count, LANES), 0).astype(F32).astype(BF16)
    return ids.reshape(count // PACKED, PACKED, LANES)


def spread_row(row):
    return jnp.broadcast_to(row, (PACKED, LANES))


def send_body(
    levels, rows, cols, slots,
    state_ref, mask_ref, own_ref, target_ref, ids_ref, table_ref, counts_ref,
    slab0_ref, one_ref, up_ref, slab3_ref, down_ref, low_ref, high_ref,
    fields_ref, halves_ref, copies,
):
    near = own_ref.shape[2]
    height = halo_rows(levels)
    parts = cols // LANES
    groups = slots // LANES
    slab_rows = CHANNELS * groups
    fetches = [
        pltpu.make_async_copy(state_ref.at[0, :, l], fields_ref.at[l], copies.at[l])
        for l in range(levels)
    ]
    for fetch in fetches:
        fetch.start()

    fetches[0].wait()
    for v in range(3):
        high, low = split_two(fields_ref[0, v + 1])
        halves_ref[v * rows : (v + 1) * rows, :cols] = high
        halves_ref[v * rows : (v + 1) * rows, cols:] = low
    tables = [
        jnp.broadcast_to(table_ref[t : t + 1, :], (8, LANES)) for t in range(table_ref.shape[0])
    ]
    lane = iota((1, LANES), 1)
    col_ids = packed_ids(cols)
    row_ids = iota((rows, LANES), 0)
    one = jnp.ones((), BF16)
    zero = jnp.zeros((), BF16)
    wide = 2
    slab_refs = (slab0_ref, one_ref, up_ref, slab3_ref)
    for n in range(near):
        count = counts_ref[0, 0, n]
        out = slab_refs[n]

        def some(c, carry, n=n, count=count, out=out):
            for sub in range(2):
                first = (c * 2 + sub) * wide
                picks = []
                cells = []
                for g in range(wide):
                    here = pl.multiple_of((first + g) * LANES, LANES)
                    cell = own_ref[0, 0, n : n + 1, pl.ds(here, LANES)]
                    cells.append(cell)
                    col = spread_row(cell % cols).astype(F32).astype(BF16)
                    picks.append(jnp.where(col_ids == col[None], one, zero).reshape(cols, LANES))
                picks = jnp.concatenate(picks, axis=1)
                picks = jnp.concatenate([picks, picks], axis=0)
                found = jnp.dot(halves_ref[...], picks, preferred_element_type=F32)
                for g in range(wide):
                    at = first + g
                    here = pl.multiple_of(at * LANES, LANES)
                    in_row = row_ids == cells[g] // cols
                    ids = jnp.broadcast_to(ids_ref[0, 0, n : n + 1, pl.ds(here, LANES)], (8, LANES))
                    weight = jnp.zeros((8, LANES), F32)
                    for t, table in enumerate(tables):
                        looked = jnp.take_along_axis(table, ids % LANES, axis=1)
                        weight = jnp.where(ids // LANES == t, looked, weight)
                    weight = jnp.where(here + lane < count, weight[:1], 0.0)
                    for place, v in enumerate((2, 0, 1)):
                        block = found[v * rows : (v + 1) * rows, g * LANES : (g + 1) * LANES]
                        value = jnp.sum(jnp.where(in_row, block, 0.0), axis=0, keepdims=True)
                        out[pl.ds(place * groups + at, 1), :] = weight * value
                    out[pl.ds(3 * groups + at, 1), :] = weight
                    target = target_ref[0, 0, n : n + 1, pl.ds(here, LANES)]
                    out[pl.ds(4 * groups + at, 1), :] = target.astype(F32)
            return carry

        lax.fori_loop(0, groups // (2 * wide), some, 0)

    for fetch in fetches[1:]:
        fetch.wait()

    sea = mask_ref[0].astype(F32)

    def put_row(ref, start, q, level, field, at):
        row = start + q * levels + level
        for part in range(parts):
            cut = slice(part * LANES, (part + 1) * LANES)
            ref[part * height + row : part * height + row + 1, :] = field[at : at + 1, cut]

    for ref, start, edge, second in ((up_ref, slab_rows, rows - 1, rows - 2), (down_ref, 0, 0, 1)):
        for part in range(parts):
            ref[start + part * height + 4 * levels : start + (part + 1) * height, :] = jnp.zeros(
                (height - 4 * levels, LANES), F32
            )
        put_row(ref, start, 4, 0, sea, edge)
        for l in range(levels):
            put_row(ref, start, EDGE_P, l, fields_ref.at[l, 0], edge)
            put_row(ref, start, SECOND_P, l, fields_ref.at[l, 0], second)
            put_row(ref, start, EDGE_VELOCITY, l, fields_ref.at[l, 1], edge)
            put_row(ref, start, EDGE_T, l, fields_ref.at[l, 3], edge)

    lanes = iota((rows, LANES), 1)

    def columns(start, begin):
        edge = 1 if begin else 0
        total = pltpu.roll(sea[:, start : start + LANES], (4 * levels - begin - edge) % LANES, 1)
        for l in range(levels):
            pair = pltpu.roll(fields_ref[l, 0, :, start : start + LANES], (2 * l - begin) % LANES, 1)
            total = jnp.where(lanes // 2 == l, pair, total)
            for q, v in ((EDGE_VELOCITY, 2), (EDGE_T, 3)):
                at = q * levels + l
                moved = pltpu.roll(fields_ref[l, v, :, start : start + LANES], (at - begin - edge) % LANES, 1)
                total = jnp.where(lanes == at, moved, total)
        return total

    highest = columns(cols - LANES, LANES - 2)
    high_ref[...] = highest
    one_ref[slab_rows:, :] = highest
    up_ref[slab_rows + height * parts :, :] = highest
    down_ref[height * parts :, :] = highest
    low_ref[...] = columns(0, 0)


def send_side(model_state, sea_mask, own_cells, target_cells, weight_ids, area_table, pair_counts):
    levels, rows, cols = model_state.shape[2:]
    slots = own_cells.shape[3]
    table = area_table.reshape(-1, LANES)
    tall = halo_rows(levels) * (cols // LANES)
    slab = CHANNELS * slots // LANES
    heights = (slab, slab + rows, slab + tall + rows, slab, tall + rows, rows, rows)
    vmem = pl.BlockSpec(memory_space=pltpu.VMEM)
    return pl.pallas_call(
        functools.partial(send_body, levels, rows, cols, slots),
        in_specs=[pl.BlockSpec(memory_space=pl.ANY)] + [vmem] * 5 + [pl.BlockSpec(memory_space=pltpu.SMEM)],
        out_specs=[vmem] * len(heights),
        out_shape=[jax.ShapeDtypeStruct((h, LANES), F32) for h in heights],
        scratch_shapes=[
            pltpu.VMEM((levels, 4, rows, cols), F32),
            pltpu.VMEM((3 * rows, 2 * cols), BF16),
            pltpu.SemaphoreType.DMA((levels,)),
        ],
        compiler_params=pltpu.CompilerParams(vmem_limit_bytes=VMEM_BYTES),
    )(model_state, sea_mask, own_cells, target_cells, weight_ids, table, pair_counts)


def stencil_body(
    levels, rows, cols, comps, count_x, count_y, slab_rows,
    state_ref, mask_ref, up_ref, down_ref, one_ref, low_ref, own_ref, fold_ref,
    wave_ref, spread_ref, gains_ref, *rest,
):
    far_refs, (out_ref, turned_ref, fields_ref, news_ref, loads, stores) = rest[:-6], rest[-6:]
    height = halo_rows(levels)
    parts = cols // LANES
    index_x = lax.axis_index("tx")
    index_y = lax.axis_index("ty")
    is_ocean = lax.axis_index("comp") == comps - 1
    last_y = index_y == count_y - 1
    mask_at = 4 * levels

    def fetch(l):
        return pltpu.make_async_copy(state_ref.at[0, :, l], fields_ref.at[l], loads.at[l])

    def store(l):
        return pltpu.make_async_copy(news_ref.at[l], out_ref.at[0, :, l], stores.at[l])

    for l in range(levels):
        fetch(l).start()

    fold = fold_ref[pl.ds(index_x, 1), :]
    total = jnp.zeros((rows, LANES), F32)
    sources = [(0, own_ref, 0), (-1, up_ref, slab_rows + height * parts), (1, down_ref, height * parts)]
    sources += [(shift, ref, 0) for shift, ref in zip(range(2, count_x - 1), far_refs)]
    for shift, ref, start in sources:
        at = lax.rem(index_x + shift + count_x, count_x)
        chosen = (iota((rows, rows), 0) + at * rows == fold).astype(F32)
        total += lax.dot_general(
            chosen, ref[start : start + rows, :], (((0,), (0,)), ((), ())),
            precision=lax.Precision.HIGHEST, preferred_element_type=F32,
        )
    lane = iota((rows, LANES), 1)
    swapped = jnp.where(lane % 2 == 0, pltpu.roll(total, LANES - 1, 1), pltpu.roll(total, 1, 1))
    total = jnp.where(lane < 2 * levels, swapped, total)
    flipped = jnp.logical_and(lane >= EDGE_VELOCITY * levels, lane < (EDGE_VELOCITY + 1) * levels)
    total = jnp.where(flipped, -total, total)
    turned_ref[...] = jnp.where(last_y, jnp.where(is_ocean, total, 0.0), low_ref[...])

    sea = mask_ref[0].astype(F32)
    tendency = jnp.where(is_ocean, sea, 1.0)
    drag = gains_ref[0, 2]
    has_west = jnp.where(jnp.logical_or(is_ocean, index_x > 0), 1.0, 0.0)
    has_east = jnp.where(jnp.logical_or(is_ocean, index_x < count_x - 1), 1.0, 0.0)
    has_south = jnp.where(index_y > 0, 1.0, 0.0)
    has_north = jnp.where(jnp.logical_or(is_ocean, jnp.logical_not(last_y)), 1.0, 0.0)
    row_ids = iota((rows, cols), 0)
    col_ids = iota((rows, cols), 1)
    blank = jnp.zeros((rows, cols - LANES), F32)

    def from_west(field, edge):
        return jnp.where(row_ids == 0, edge, pltpu.roll(field, 1, 0))

    def from_east(field, edge):
        return jnp.where(row_ids == rows - 1, edge, pltpu.roll(field, rows - 1, 0))

    def from_south(field, edge):
        wide = jnp.concatenate([edge, blank], axis=1)
        return jnp.where(col_ids == 0, wide, pltpu.roll(field, 1, 1))

    def from_north(field, edge):
        wide = jnp.concatenate([blank, edge], axis=1)
        return jnp.where(col_ids == cols - 1, wide, pltpu.roll(field, cols - 1, 1))

    def row_at(ref, start, row):
        halves = [ref[pl.ds(start + p * height + row, 1), :] for p in range(parts)]
        return jnp.concatenate(halves, axis=1)

    def one_level(level, carry):
        fetch(level).wait()
        pressure, zonal, meridional, tracer = (fields_ref[level, v] for v in range(4))
        half = 0.5 * wave_ref[0, level]
        spread = spread_ref[0, level]
        first = jnp.where(level == 0, drag, 0.0)

        def keeping(sea_values):
            return jnp.where(is_ocean, sea_values, 1.0 - first * (1.0 - sea_values))

        def west_row(q):
            return row_at(up_ref, slab_rows, q * levels + level)

        def east_row(q):
            return row_at(down_ref, 0, q * levels + level)

        def south_col(at):
            return pltpu.roll(one_ref[slab_rows:, :], lax.rem(LANES - at, LANES), 1)

        def north_col(at):
            return pltpu.roll(turned_ref[...], LANES - 1 - at, 1)

        keep = keeping(sea)
        south_p = south_col(2 * level + 1)
        north_p = north_col(2 * level)
        new_zonal = keep * (
            zonal
            - half * (
                from_east(pressure, has_east * east_row(EDGE_P))
                - from_west(pressure, has_west * west_row(EDGE_P))
            )
        )
        new_meridional = keep * (
            meridional
            - half * (from_north(pressure, has_north * north_p) - from_south(pressure, has_south * south_p))
        )
        laplace = (
            from_east(tracer, has_east * east_row(EDGE_T))
            + from_west(tracer, has_west * west_row(EDGE_T))
            + from_north(tracer, has_north * north_col(EDGE_T * levels + level))
            + from_south(tracer, has_south * south_col(EDGE_T * levels + level))
            - 4.0 * tracer
        )
        new_tracer = tracer + spread * tendency * laplace
        west_zonal = keeping(row_at(up_ref, slab_rows, mask_at)) * (
            west_row(EDGE_VELOCITY) - half * (pressure[0:1, :] - west_row(SECOND_P))
        )
        east_zonal = keeping(row_at(down_ref, 0, mask_at)) * (
            east_row(EDGE_VELOCITY) - half * (east_row(SECOND_P) - pressure[rows - 1 : rows, :])
        )
        south_meridional = keeping(south_col(mask_at)) * (
            south_col(EDGE_VELOCITY * levels + level)
            - half * (pressure[:, :LANES] - south_col(2 * level))
        )
        north_meridional = keeping(north_col(mask_at)) * (
            north_col(EDGE_VELOCITY * levels + level)
            - half * (north_col(2 * level + 1) - pressure[:, cols - LANES :])
        )
        divergence = (
            from_east(new_zonal, has_east * east_zonal)
            - from_west(new_zonal, has_west * west_zonal)
            + from_north(new_meridional, has_north * north_meridional)
            - from_south(new_meridional, has_south * south_meridional)
        )
        news_ref[level, 0] = pressure - half * divergence
        news_ref[level, 1] = new_zonal
        news_ref[level, 2] = new_meridional
        news_ref[level, 3] = new_tracer
        store(level).start()
        return carry

    lax.fori_loop(0, levels, one_level, 0)
    for l in range(levels):
        store(l).wait()


def stencil(model_state, sea_mask, up, down, one, low, own, fars, fold_map, wave_speed, diffusivity, gains, sizes, slab_rows):
    comps, count_x, count_y = sizes
    levels, rows, cols = model_state.shape[2:]
    fold = fold_map.reshape(count_x, rows)
    vmem = pl.BlockSpec(memory_space=pltpu.VMEM)
    scalar = pl.BlockSpec(memory_space=pltpu.SMEM)
    anywhere = pl.BlockSpec(memory_space=pl.ANY)
    return pl.pallas_call(
        functools.partial(stencil_body, levels, rows, cols, comps, count_x, count_y, slab_rows),
        in_specs=[anywhere] + [vmem] * 7 + [scalar] * 3 + [vmem] * len(fars),
        out_specs=anywhere,
        out_shape=jax.ShapeDtypeStruct(model_state.shape, F32),
        scratch_shapes=[
            pltpu.VMEM((rows, LANES), F32),
            pltpu.VMEM((levels, 4, rows, cols), F32),
            pltpu.VMEM((levels, 4, rows, cols), F32),
            pltpu.SemaphoreType.DMA((levels,)),
            pltpu.SemaphoreType.DMA((levels,)),
        ],
        compiler_params=pltpu.CompilerParams(vmem_limit_bytes=VMEM_BYTES),
    )(model_state, sea_mask, up, down, one, low, own, fold, wave_speed, diffusivity, gains, *fars)


def scatter_body(
    rows, cols, comps, chunks, groups,
    new_ref, state_ref, mask_ref, gains_ref, slabs_ref, out_ref,
    spread_refs, column_refs, total_ref, news_ref, olds_ref, copies,
):
    here = lax.axis_index("comp")
    is_ocean = here == comps - 1
    surface = lambda ref: ref.at[0, pl.ds(1, 3), 0]
    load_new = pltpu.make_async_copy(surface(new_ref), news_ref, copies.at[0])
    load_old = pltpu.make_async_copy(surface(state_ref), olds_ref, copies.at[1])
    load_new.start()
    load_old.start()
    total_ref[...] = jnp.zeros_like(total_ref)
    row_ids = packed_ids(rows)
    col_ids = packed_ids(cols)
    lane = iota((1, LANES), 1)
    one = jnp.ones((), BF16)
    zero = jnp.zeros((), BF16)

    def build(chunk, buffer):
        start = chunk * (CHANNELS * groups)
        for g in range(groups):
            cells = slabs_ref[pl.ds(start + 4 * groups + g, 1), :].astype(I32)
            slot = lane + g * LANES
            mine = jnp.logical_or(is_ocean, slot % (comps - 1) == here)
            row = spread_row(jnp.where(mine, cells // cols, -1)).astype(F32).astype(BF16)
            col = spread_row(cells % cols).astype(F32).astype(BF16)
            cut = slice(g * LANES, (g + 1) * LANES)
            column_refs[buffer, :, cut] = jnp.where(col_ids == col[None], one, zero).reshape(cols, LANES)
            in_row = row_ids == row[None]
            for v in range(4):
                value = spread_row(slabs_ref[pl.ds(start + v * groups + g, 1), :])
                high, low = split_two(value)
                spread_refs[buffer, v * rows : (v + 1) * rows, cut] = jnp.where(
                    in_row, high[None], zero
                ).reshape(rows, LANES)
                spread_refs[buffer, (v + 4) * rows : (v + 5) * rows, cut] = jnp.where(
                    in_row, low[None], zero
                ).reshape(rows, LANES)

    def multiply(buffer):
        total_ref[...] += lax.dot_general(
            spread_refs[buffer], column_refs[buffer], (((1,), (1,)), ((), ())),
            preferred_element_type=F32,
        )

    build(0, 0)

    def pair(c, carry):
        multiply(0)
        build(2 * c + 1, 1)
        multiply(1)
        build(jnp.minimum(2 * c + 2, chunks - 1), 0)
        return carry

    lax.fori_loop(0, chunks // 2, pair, 0)
    load_new.wait()
    load_old.wait()
    sea = mask_ref[0].astype(F32)
    tendency = jnp.where(is_ocean, sea, 1.0)
    sums = [
        total_ref[v * rows : (v + 1) * rows, :] + total_ref[(v + 4) * rows : (v + 5) * rows, :]
        for v in range(4)
    ]
    for v, total, gain in ((2, sums[0], 0), (0, sums[1], 1), (1, sums[2], 1)):
        change = tendency * gains_ref[0, gain] * (total - sums[3] * olds_ref[v])
        news_ref[v] = news_ref[v] + change
    save = pltpu.make_async_copy(news_ref, surface(out_ref), copies.at[2])
    save.start()
    save.wait()


def scatter_slots(new_state, model_state, sea_mask, gains, slabs, comps, slots):
    rows, cols = model_state.shape[3:]
    groups = slots // LANES
    chunks = slabs.shape[0] // (CHANNELS * groups)
    vmem = pl.BlockSpec(memory_space=pltpu.VMEM)
    anywhere = pl.BlockSpec(memory_space=pl.ANY)
    return pl.pallas_call(
        functools.partial(scatter_body, rows, cols, comps, chunks, groups),
        in_specs=[anywhere, anywhere, vmem, pl.BlockSpec(memory_space=pltpu.SMEM), vmem],
        out_specs=anywhere,
        out_shape=jax.ShapeDtypeStruct(new_state.shape, F32),
        scratch_shapes=[
            pltpu.VMEM((2, 8 * rows, slots), BF16),
            pltpu.VMEM((2, cols, slots), BF16),
            pltpu.VMEM((8 * rows, cols), F32),
            pltpu.VMEM((3, rows, cols), F32),
            pltpu.VMEM((3, rows, cols), F32),
            pltpu.SemaphoreType.DMA((3,)),
        ],
        input_output_aliases={0: 0},
        compiler_params=pltpu.CompilerParams(vmem_limit_bytes=VMEM_BYTES),
    )(new_state, model_state, sea_mask, gains, slabs)


def shards(
    model_state, sea_mask, wave_speed, diffusivity, surface_gains, area_table,
    own_cells, target_cells, weight_ids, pair_counts, fold_map,
):
    comps, count_x, count_y = (lax.axis_size(a) for a in ("comp", "tx", "ty"))
    positions = count_x * count_y
    slots = own_cells.shape[3]
    slab_rows = CHANNELS * slots // LANES

    slab0, one, up, slab3, down, low, high = send_side(
        model_state, sea_mask, own_cells, target_cells, weight_ids, area_table, pair_counts
    )

    def along(block, shift):
        return lax.ppermute(block, ("tx", "ty"), [(s, (s + shift) % positions) for s in range(positions)])

    slab3 = along(slab3, 1 + count_y)
    one = along(one, 1)
    up = along(up, count_y)
    down = along(down, -count_y)
    fars = []
    for shift in range(2, count_x - 1):
        pairs = []
        for i in range(count_x):
            ends = [((comps - 1) * count_x + k) * count_y + count_y - 1 for k in ((i + shift) % count_x, i)]
            pairs.append(tuple(ends))
        fars.append(lax.ppermute(high, ("comp", "tx", "ty"), pairs))
    low = lax.ppermute(low, "ty", [(j + 1, j) for j in range(count_y - 1)])

    arrived = jnp.concatenate([slab0, one[:slab_rows], up[:slab_rows], slab3])
    received = jnp.concatenate(
        [lax.ppermute(arrived, "comp", [(g, comps - 1), (comps - 1, g)]) for g in range(comps - 1)]
    )
    new_state = stencil(
        model_state, sea_mask, up, down, one, low, high, fars, fold_map,
        wave_speed, diffusivity, surface_gains, (comps, count_x, count_y), slab_rows,
    )
    return scatter_slots(new_state, model_state, sea_mask, surface_gains, received, comps, slots)


def solution(mesh):
    in_specs = (
        P("comp", None, None, "tx", "ty"),
        P("comp", "tx", "ty"),
        P("comp", None),
        P("comp", None),
        P("comp", None),
        P(),
        P("comp", ("tx", "ty"), None, None),
        P("comp", ("tx", "ty"), None, None),
        P("comp", ("tx", "ty"), None, None),
        P("comp", ("tx", "ty"), None),
        P(),
    )
    out_specs = P("comp", None, None, "tx", "ty")
    return jax.shard_map(shards, mesh=mesh, in_specs=in_specs, out_specs=out_specs, check_vma=False)
```

```python
import functools

import jax
import jax.numpy as jnp
from jax import lax
from jax.experimental import pallas as pl
from jax.experimental.pallas import tpu as pltpu
from jax.sharding import PartitionSpec as P

LANES = 128
PACKED = 16
VMEM_BYTES = 28 * 1024 * 1024
F32 = jnp.float32
BF16 = jnp.bfloat16
I32 = jnp.int32
CHANNELS = 5

EDGE_P, SECOND_P, EDGE_VELOCITY, EDGE_T, MASK = range(5)


def iota(shape, dim):
    return lax.broadcasted_iota(I32, shape, dim)


def halo_rows(levels):
    return (4 * levels + 1 + 7) // 8 * 8


def split_two(values):
    high = values.astype(BF16)
    low = (values - high.astype(F32)).astype(BF16)
    return high, low


def packed_ids(count):
    ids = iota((count, LANES), 0).astype(F32).astype(BF16)
    return ids.reshape(count // PACKED, PACKED, LANES)


def spread_row(row):
    return jnp.broadcast_to(row, (PACKED, LANES))


def share_bounds(slots, shares):
    bounds = [0]
    for m in range(shares):
        bounds.append(bounds[-1] + (slots - m + shares - 1) // shares)
    return bounds


def slot_order(slots, shares, sort, half):
    place = iota((8, LANES), 0) * LANES + iota((8, LANES), 1) + half * 8 * LANES
    source = jnp.zeros((8, LANES), I32)
    bounds = share_bounds(slots, shares)
    for m in range(shares):
        inside = jnp.logical_and(place >= bounds[m], place < bounds[m + 1])
        source = jnp.where(inside, (place - bounds[m]) * shares + m, source)
    return jnp.where(sort, source, place)


def pick_rows(ref, n, source):
    total = jnp.zeros((8, LANES), I32)
    for t in range(ref.shape[3] // LANES):
        row = jnp.broadcast_to(ref[0, 0, n : n + 1, t * LANES : (t + 1) * LANES], (8, LANES))
        picked = jnp.take_along_axis(row, source % LANES, axis=1)
        total = jnp.where(source // LANES == t, picked, total)
    return total


def gather_partner(n, rows, cols, comps, own_ref, target_ref, ids_ref, table_ref, counts_ref, halves_ref, cells_ref, out):
    slots = own_ref.shape[3]
    groups = slots // LANES
    is_ocean = lax.axis_index("comp") == comps - 1
    weights = []
    count = jnp.broadcast_to(counts_ref[0, :, n : n + 1], (8, LANES))
    for half in range(groups // 8):
        source = slot_order(slots, comps - 1, is_ocean, half)
        cells_ref[half * 8 : (half + 1) * 8, :] = pick_rows(own_ref, n, source)
        targets = pick_rows(target_ref, n, source)
        ids = pick_rows(ids_ref, n, source)
        weight = jnp.zeros((8, LANES), F32)
        for t in range(table_ref.shape[0]):
            table = jnp.broadcast_to(table_ref[t : t + 1, :], (8, LANES))
            looked = jnp.take_along_axis(table, ids % LANES, axis=1)
            weight = jnp.where(ids // LANES == t, looked, weight)
        weights.append(jnp.where(source < count, weight, 0.0))
        out[3 * groups + half * 8 : 3 * groups + (half + 1) * 8, :] = weights[-1]
        out[4 * groups + half * 8 : 4 * groups + (half + 1) * 8, :] = targets.astype(F32)
    col_ids = packed_ids(cols)
    row_ids = iota((rows, LANES), 0)
    one = jnp.ones((), BF16)
    zero = jnp.zeros((), BF16)
    wide, subs = 2, 4

    def some(c, carry):
        for sub in range(subs):
            first = (c * subs + sub) * wide
            cells = [cells_ref[pl.ds(first + g, 1), :] for g in range(wide)]
            picks = []
            for cell in cells:
                col = spread_row(cell % cols).astype(F32).astype(BF16)
                picks.append(jnp.where(col_ids == col[None], one, zero).reshape(cols, LANES))
            picks = jnp.concatenate(picks, axis=1)
            picks = jnp.concatenate([picks, picks], axis=0)
            found = jnp.dot(halves_ref[...], picks, preferred_element_type=F32)
            for g in range(wide):
                in_row = row_ids == cells[g] // cols
                for place, v in enumerate((2, 0, 1)):
                    block = found[v * rows : (v + 1) * rows, g * LANES : (g + 1) * LANES]
                    value = jnp.sum(jnp.where(in_row, block, 0.0), axis=0, keepdims=True)
                    out[pl.ds(place * groups + first + g, 1), :] = value
        return carry

    lax.fori_loop(0, groups // (subs * wide), some, 0)
    for half, weight in enumerate(weights):
        for place in range(3):
            at = slice(place * groups + half * 8, place * groups + (half + 1) * 8)
            out[at, :] = out[at, :] * weight


def split_surface(surface_ref, halves_ref, rows, cols):
    for v in range(3):
        high, low = split_two(surface_ref[v])
        halves_ref[v * rows : (v + 1) * rows, :cols] = high
        halves_ref[v * rows : (v + 1) * rows, cols:] = low


def first_body(
    rows, cols, comps,
    state_hbm, own_hbm, target_hbm, ids_hbm, table_hbm, counts_hbm,
    slab1_ref, slab2_ref, slab3_ref,
    surface_ref, own_ref, target_ref, ids_ref, table_ref, counts_ref, halves_ref, cells_ref, copies,
):
    sources = (state_hbm.at[0, pl.ds(1, 3), 0], own_hbm, target_hbm, ids_hbm, table_hbm, counts_hbm)
    places = (surface_ref, own_ref, target_ref, ids_ref, table_ref, counts_ref)
    fetches = [
        pltpu.make_async_copy(source, place, copies.at[i])
        for i, (source, place) in enumerate(zip(sources, places))
    ]
    for fetch in fetches:
        fetch.start()
    for fetch in fetches:
        fetch.wait()
    split_surface(surface_ref, halves_ref, rows, cols)
    for n, out in ((3, slab3_ref), (1, slab1_ref), (2, slab2_ref)):
        gather_partner(
            n, rows, cols, comps, own_ref, target_ref, ids_ref, table_ref, counts_ref, halves_ref, cells_ref, out
        )


def slot_scratch(rows, cols, slots, near, table_shape):
    return [
        pltpu.VMEM((1, 1, near, slots), I32),
        pltpu.VMEM((1, 1, near, slots), I32),
        pltpu.VMEM((1, 1, near, slots), I32),
        pltpu.VMEM(table_shape, F32),
        pltpu.VMEM((1, 1, near), I32),
        pltpu.VMEM((3 * rows, 2 * cols), BF16),
        pltpu.VMEM((slots // LANES, LANES), I32),
    ]


def first_side(model_state, slot_arrays, comps):
    rows, cols = model_state.shape[3:]
    near, slots = slot_arrays[0].shape[2:]
    table_shape = slot_arrays[3].shape
    slab = jax.ShapeDtypeStruct((CHANNELS * slots // LANES, LANES), F32)
    vmem = pl.BlockSpec(memory_space=pltpu.VMEM)
    return pl.pallas_call(
        functools.partial(first_body, rows, cols, comps),
        in_specs=[pl.BlockSpec(memory_space=pl.ANY)] * 6,
        out_specs=[vmem] * 3,
        out_shape=[slab] * 3,
        scratch_shapes=[pltpu.VMEM((3, rows, cols), F32)]
        + slot_scratch(rows, cols, slots, near, table_shape)
        + [pltpu.SemaphoreType.DMA((6,))],
        compiler_params=pltpu.CompilerParams(vmem_limit_bytes=VMEM_BYTES),
    )(model_state, *slot_arrays)


def second_body(
    levels, rows, cols, comps,
    state_hbm, own_hbm, target_hbm, ids_hbm, table_hbm, counts_hbm, mask_hbm,
    slab0_ref, up_ref, down_ref, high_ref, low_ref, pair_ref,
    own_ref, target_ref, ids_ref, table_ref, counts_ref, halves_ref, cells_ref,
    fields_ref, mask_ref, copies, loads,
):
    height = halo_rows(levels)
    parts = cols // LANES
    sources = (own_hbm, target_hbm, ids_hbm, table_hbm, counts_hbm, mask_hbm)
    places = (own_ref, target_ref, ids_ref, table_ref, counts_ref, mask_ref)
    fetches = [
        pltpu.make_async_copy(source, place, copies.at[i])
        for i, (source, place) in enumerate(zip(sources, places))
    ]
    fields = [
        pltpu.make_async_copy(state_hbm.at[0, :, l], fields_ref.at[l], loads.at[l])
        for l in range(levels)
    ]
    fields[0].start()
    for fetch in fetches + fields[1:]:
        fetch.start()
    for fetch in fetches + fields[:1]:
        fetch.wait()
    split_surface(fields_ref.at[0, pl.ds(1, 3)], halves_ref, rows, cols)
    gather_partner(
        0, rows, cols, comps, own_ref, target_ref, ids_ref, table_ref, counts_ref, halves_ref, cells_ref, slab0_ref
    )
    for fetch in fields[1:]:
        fetch.wait()

    sea = mask_ref[0].astype(F32)

    def put_row(ref, q, level, field, at):
        row = q * levels + level
        for part in range(parts):
            cut = slice(part * LANES, (part + 1) * LANES)
            ref[part * height + row : part * height + row + 1, :] = field[at : at + 1, cut]

    for ref, edge, second in ((up_ref, rows - 1, rows - 2), (down_ref, 0, 1)):
        for part in range(parts):
            ref[part * height + 4 * levels : (part + 1) * height, :] = jnp.zeros(
                (height - 4 * levels, LANES), F32
            )
        put_row(ref, 4, 0, sea, edge)
        for l in range(levels):
            put_row(ref, EDGE_P, l, fields_ref.at[l, 0], edge)
            put_row(ref, SECOND_P, l, fields_ref.at[l, 0], second)
            put_row(ref, EDGE_VELOCITY, l, fields_ref.at[l, 1], edge)
            put_row(ref, EDGE_T, l, fields_ref.at[l, 3], edge)

    lanes = iota((rows, LANES), 1)

    def columns(start, begin):
        edge = 1 if begin else 0
        total = pltpu.roll(sea[:, start : start + LANES], (4 * levels - begin - edge) % LANES, 1)
        for l in range(levels):
            pair = pltpu.roll(fields_ref[l, 0, :, start : start + LANES], (2 * l - begin) % LANES, 1)
            total = jnp.where(lanes // 2 == l, pair, total)
            for q, v in ((EDGE_VELOCITY, 2), (EDGE_T, 3)):
                at = q * levels + l
                moved = pltpu.roll(fields_ref[l, v, :, start : start + LANES], (at - begin - edge) % LANES, 1)
                total = jnp.where(lanes == at, moved, total)
        return total.T[:height]

    highest = columns(cols - LANES, LANES - 2)
    lowest = columns(0, 0)
    high_ref[...] = highest
    low_ref[...] = lowest
    up_ref[height * parts :, :] = highest
    down_ref[height * parts :, :] = highest
    pair_ref[...] = jnp.where(lax.axis_index("ty") == 0, highest, lowest)


def second_side(model_state, slot_arrays, sea_mask, comps):
    levels, rows, cols = model_state.shape[2:]
    near, slots = slot_arrays[0].shape[2:]
    table_shape = slot_arrays[3].shape
    height = halo_rows(levels)
    tall = height * (cols // LANES) + height
    heights = (CHANNELS * slots // LANES, tall, tall, height, height, height)
    vmem = pl.BlockSpec(memory_space=pltpu.VMEM)
    return pl.pallas_call(
        functools.partial(second_body, levels, rows, cols, comps),
        in_specs=[pl.BlockSpec(memory_space=pl.ANY)] * 7,
        out_specs=[vmem] * len(heights),
        out_shape=[jax.ShapeDtypeStruct((h, LANES), F32) for h in heights],
        scratch_shapes=slot_scratch(rows, cols, slots, near, table_shape)
        + [
            pltpu.VMEM((levels, 4, rows, cols), F32),
            pltpu.VMEM((1, rows, cols), I32),
            pltpu.SemaphoreType.DMA((6,)),
            pltpu.SemaphoreType.DMA((levels,)),
        ],
        compiler_params=pltpu.CompilerParams(vmem_limit_bytes=VMEM_BYTES),
    )(model_state, *slot_arrays, sea_mask)


def stencil_body(
    levels, rows, cols, comps, count_x, count_y,
    state_ref, mask_ref, up_ref, down_ref, south_ref, north_ref, own_ref, fold_ref,
    wave_ref, spread_ref, gains_ref, *rest,
):
    far_refs = rest[: max(count_x - 3, 0)]
    out_ref, new_surface_ref, old_surface_ref = rest[len(far_refs) : len(far_refs) + 3]
    south_turned_ref, turned_ref, fields_ref, news_ref, loads, stores = rest[len(far_refs) + 3 :]
    height = halo_rows(levels)
    parts = cols // LANES
    index_x = lax.axis_index("tx")
    index_y = lax.axis_index("ty")
    is_ocean = lax.axis_index("comp") == comps - 1
    last_y = index_y == count_y - 1
    mask_at = 4 * levels

    def fetch(l):
        return pltpu.make_async_copy(state_ref.at[0, :, l], fields_ref.at[l], loads.at[l])

    def store(l):
        return pltpu.make_async_copy(news_ref.at[l], out_ref.at[0, :, l], stores.at[l])

    for l in range(levels):
        fetch(l).start()

    fold = fold_ref[pl.ds(index_x, 1), :]
    total = jnp.zeros((height, LANES), F32)
    sources = [(0, own_ref, 0), (-1, up_ref, height * parts), (1, down_ref, height * parts)]
    sources += [(shift, ref, 0) for shift, ref in zip(range(2, count_x - 1), far_refs)]
    for shift, ref, start in sources:
        at = lax.rem(index_x + shift + count_x, count_x)
        chosen = (iota((rows, rows), 0) + at * rows == fold).astype(F32)
        total += jnp.dot(
            ref[start : start + height, :], chosen,
            precision=lax.Precision.HIGHEST, preferred_element_type=F32,
        )
    line = iota((height, LANES), 0)
    swapped = jnp.where(line % 2 == 0, pltpu.roll(total, height - 1, 0), pltpu.roll(total, 1, 0))
    total = jnp.where(line < 2 * levels, swapped, total)
    flipped = jnp.logical_and(line >= EDGE_VELOCITY * levels, line < (EDGE_VELOCITY + 1) * levels)
    total = jnp.where(flipped, -total, total)
    total = jnp.where(last_y, jnp.where(is_ocean, total, 0.0), north_ref[...])
    fill = jnp.zeros((LANES - height, LANES), F32)
    turned_ref[...] = jnp.concatenate([total, fill], axis=0).T
    south_turned_ref[...] = jnp.concatenate([south_ref[...], fill], axis=0).T

    sea = mask_ref[0].astype(F32)
    tendency = jnp.where(is_ocean, sea, 1.0)
    drag = gains_ref[0, 2]
    has_west = jnp.where(jnp.logical_or(is_ocean, index_x > 0), 1.0, 0.0)
    has_east = jnp.where(jnp.logical_or(is_ocean, index_x < count_x - 1), 1.0, 0.0)
    has_south = jnp.where(index_y > 0, 1.0, 0.0)
    has_north = jnp.where(jnp.logical_or(is_ocean, jnp.logical_not(last_y)), 1.0, 0.0)
    row_ids = iota((rows, cols), 0)
    col_ids = iota((rows, cols), 1)
    blank = jnp.zeros((rows, cols - LANES), F32)

    def from_west(field, edge):
        return jnp.where(row_ids == 0, edge, pltpu.roll(field, 1, 0))

    def from_east(field, edge):
        return jnp.where(row_ids == rows - 1, edge, pltpu.roll(field, rows - 1, 0))

    def from_south(field, edge):
        wide = jnp.concatenate([edge, blank], axis=1)
        return jnp.where(col_ids == 0, wide, pltpu.roll(field, 1, 1))

    def from_north(field, edge):
        wide = jnp.concatenate([blank, edge], axis=1)
        return jnp.where(col_ids == cols - 1, wide, pltpu.roll(field, cols - 1, 1))

    def row_at(ref, start, row):
        halves = [ref[pl.ds(start + p * height + row, 1), :] for p in range(parts)]
        return jnp.concatenate(halves, axis=1)

    def one_level(level, carry):
        fetch(level).wait()
        pressure, zonal, meridional, tracer = (fields_ref[level, v] for v in range(4))
        half = 0.5 * wave_ref[0, level]
        spread = spread_ref[0, level]
        first = jnp.where(level == 0, drag, 0.0)

        def keeping(sea_values):
            return jnp.where(is_ocean, sea_values, 1.0 - first * (1.0 - sea_values))

        def west_row(q):
            return row_at(up_ref, 0, q * levels + level)

        def east_row(q):
            return row_at(down_ref, 0, q * levels + level)

        def south_col(at):
            return pltpu.roll(south_turned_ref[...], lax.rem(LANES - at, LANES), 1)

        def north_col(at):
            return pltpu.roll(turned_ref[...], LANES - 1 - at, 1)

        keep = keeping(sea)
        south_p = south_col(2 * level + 1)
        north_p = north_col(2 * level)
        new_zonal = keep * (
            zonal
            - half * (
                from_east(pressure, has_east * east_row(EDGE_P))
                - from_west(pressure, has_west * west_row(EDGE_P))
            )
        )
        new_meridional = keep * (
            meridional
            - half * (from_north(pressure, has_north * north_p) - from_south(pressure, has_south * south_p))
        )
        laplace = (
            from_east(tracer, has_east * east_row(EDGE_T))
            + from_west(tracer, has_west * west_row(EDGE_T))
            + from_north(tracer, has_north * north_col(EDGE_T * levels + level))
            + from_south(tracer, has_south * south_col(EDGE_T * levels + level))
            - 4.0 * tracer
        )
        new_tracer = tracer + spread * tendency * laplace
        west_zonal = keeping(row_at(up_ref, 0, mask_at)) * (
            west_row(EDGE_VELOCITY) - half * (pressure[0:1, :] - west_row(SECOND_P))
        )
        east_zonal = keeping(row_at(down_ref, 0, mask_at)) * (
            east_row(EDGE_VELOCITY) - half * (east_row(SECOND_P) - pressure[rows - 1 : rows, :])
        )
        south_meridional = keeping(south_col(mask_at)) * (
            south_col(EDGE_VELOCITY * levels + level)
            - half * (pressure[:, :LANES] - south_col(2 * level))
        )
        north_meridional = keeping(north_col(mask_at)) * (
            north_col(EDGE_VELOCITY * levels + level)
            - half * (north_col(2 * level + 1) - pressure[:, cols - LANES :])
        )
        divergence = (
            from_east(new_zonal, has_east * east_zonal)
            - from_west(new_zonal, has_west * west_zonal)
            + from_north(new_meridional, has_north * north_meridional)
            - from_south(new_meridional, has_south * south_meridional)
        )
        news_ref[level, 0] = pressure - half * divergence
        news_ref[level, 1] = new_zonal
        news_ref[level, 2] = new_meridional
        news_ref[level, 3] = new_tracer
        store(level).start()

        @pl.when(level == 0)
        def _():
            new_surface_ref[0] = new_zonal
            new_surface_ref[1] = new_meridional
            new_surface_ref[2] = new_tracer
            old_surface_ref[0] = zonal
            old_surface_ref[1] = meridional
            old_surface_ref[2] = tracer

        return carry

    lax.fori_loop(0, levels, one_level, 0)
    for l in range(levels):
        store(l).wait()


def stencil(model_state, sea_mask, up, down, south, north, own, fars, fold_map, wave_speed, diffusivity, gains, sizes):
    comps, count_x, count_y = sizes
    levels, rows, cols = model_state.shape[2:]
    fold = fold_map.reshape(count_x, rows)
    vmem = pl.BlockSpec(memory_space=pltpu.VMEM)
    scalar = pl.BlockSpec(memory_space=pltpu.SMEM)
    anywhere = pl.BlockSpec(memory_space=pl.ANY)
    surface = jax.ShapeDtypeStruct((3, rows, cols), F32)
    return pl.pallas_call(
        functools.partial(stencil_body, levels, rows, cols, comps, count_x, count_y),
        in_specs=[anywhere] + [vmem] * 7 + [scalar] * 3 + [vmem] * len(fars),
        out_specs=[anywhere, vmem, vmem],
        out_shape=[jax.ShapeDtypeStruct(model_state.shape, F32), surface, surface],
        scratch_shapes=[
            pltpu.VMEM((rows, LANES), F32),
            pltpu.VMEM((rows, LANES), F32),
            pltpu.VMEM((levels, 4, rows, cols), F32),
            pltpu.VMEM((levels, 4, rows, cols), F32),
            pltpu.SemaphoreType.DMA((levels,)),
            pltpu.SemaphoreType.DMA((levels,)),
        ],
        compiler_params=pltpu.CompilerParams(vmem_limit_bytes=VMEM_BYTES),
    )(model_state, sea_mask, up, down, south, north, own, fold, wave_speed, diffusivity, gains, *fars)


def add_slots(rows, cols, groups, slab_ref, total_ref, spread_refs, column_refs, chunks, plan):
    row_ids = packed_ids(rows)
    col_ids = packed_ids(cols)
    lane = iota((1, LANES), 1)
    one = jnp.ones((), BF16)
    zero = jnp.zeros((), BF16)
    depth = spread_refs.shape[2] // LANES

    def build(chunk, buffer):
        n, first, low_slot, high_slot, _ = plan(chunk)
        start = n * (CHANNELS * groups) + first
        for g in range(depth):
            cells = slab_ref[pl.ds(start + 4 * groups + g, 1), :].astype(I32)
            slot = lane + (first + g) * LANES
            mine = jnp.logical_and(slot >= low_slot, slot < high_slot)
            row = spread_row(jnp.where(mine, cells // cols, -1)).astype(F32).astype(BF16)
            col = spread_row(cells % cols).astype(F32).astype(BF16)
            cut = slice(g * LANES, (g + 1) * LANES)
            column_refs[buffer, :, cut] = jnp.where(col_ids == col[None], one, zero).reshape(cols, LANES)
            in_row = row_ids == row[None]
            for v in range(4):
                value = spread_row(slab_ref[pl.ds(start + v * groups + g, 1), :])
                high, low = split_two(value)
                spread_refs[buffer, v * rows : (v + 1) * rows, cut] = jnp.where(
                    in_row, high[None], zero
                ).reshape(rows, LANES)
                spread_refs[buffer, (v + 4) * rows : (v + 5) * rows, cut] = jnp.where(
                    in_row, low[None], zero
                ).reshape(rows, LANES)

    def multiply(chunk, buffer):
        which = plan(chunk)[4]
        total_ref[which] += lax.dot_general(
            spread_refs[buffer], column_refs[buffer], (((1,), (1,)), ((), ())),
            preferred_element_type=F32,
        )

    @pl.when(chunks > 0)
    def _():
        build(0, 0)

    def pair(c, carry):
        multiply(2 * c, 0)
        build(2 * c + 1, 1)
        multiply(2 * c + 1, 1)
        build(jnp.minimum(2 * c + 2, chunks - 1), 0)
        return carry

    lax.fori_loop(0, chunks // 2, pair, 0)


def halves_added(total, rows):
    return total[: 4 * rows] + total[4 * rows :]


KEPT, SENT = 0, 1


def own_body(rows, cols, comps, groups, slab_ref, sent_ref, spread_refs, column_refs, total_ref):
    here = lax.axis_index("comp")
    depth = spread_refs.shape[2] // LANES
    pieces = groups // depth
    near = slab_ref.shape[0] // (CHANNELS * groups)
    bounds = share_bounds(groups * LANES, comps - 1)
    is_ocean = here == comps - 1
    beside = here == comps - 2
    total_ref[...] = jnp.zeros_like(total_ref)

    def plan(chunk):
        n = jnp.where(is_ocean, chunk, chunk // pieces)
        first = jnp.where(is_ocean, groups - depth, chunk % pieces * depth)
        return n, first, jnp.where(is_ocean, bounds[comps - 2], 0), groups * LANES, 0

    chunks = jnp.where(is_ocean, near, jnp.where(beside, near * pieces, 0))
    add_slots(rows, cols, groups, slab_ref, total_ref, spread_refs, column_refs, chunks, plan)
    sent_ref[...] = halves_added(total_ref[0], rows)


def other_body(
    rows, cols, comps, groups, slab_ref, before_ref, kept_ref, sent_ref, spread_refs, column_refs, total_ref
):
    here = lax.axis_index("comp")
    depth = spread_refs.shape[2] // LANES
    pieces = groups // depth
    near = slab_ref.shape[0] // (CHANNELS * groups)
    bounds = share_bounds(groups * LANES, comps - 1)
    is_ocean = here == comps - 1
    for_two = here == comps - 3
    total_ref[...] = jnp.zeros_like(total_ref)
    middle = bounds[1] // LANES // 4 * 4

    def plan(chunk):
        mine = chunk >= near
        n = jnp.where(for_two, chunk % near, chunk // pieces)
        first = jnp.where(for_two, jnp.where(mine, middle, 0), chunk % pieces * depth)
        low_slot = jnp.where(jnp.logical_and(for_two, mine), bounds[1], 0)
        high_slot = jnp.where(for_two, jnp.where(mine, bounds[2], bounds[1]), groups * LANES)
        kept = jnp.logical_or(is_ocean, jnp.logical_and(for_two, mine))
        return n, first, low_slot, high_slot, jnp.where(kept, KEPT, SENT)

    chunks = jnp.where(here == 0, 0, near * pieces)
    add_slots(rows, cols, groups, slab_ref, total_ref, spread_refs, column_refs, chunks, plan)
    kept_ref[...] = halves_added(total_ref[KEPT], rows)
    sent_ref[...] = halves_added(total_ref[SENT], rows) + before_ref[...]


def scatter_call(body, totals, outs, rows, cols, comps, slots, *operands):
    vmem = pl.BlockSpec(memory_space=pltpu.VMEM)
    depth = 8 * LANES
    return pl.pallas_call(
        functools.partial(body, rows, cols, comps, slots // LANES),
        in_specs=[vmem] * len(operands),
        out_specs=[vmem] * outs,
        out_shape=[jax.ShapeDtypeStruct((4 * rows, cols), F32)] * outs,
        scratch_shapes=[
            pltpu.VMEM((2, 8 * rows, depth), BF16),
            pltpu.VMEM((2, cols, depth), BF16),
            pltpu.VMEM((totals, 8 * rows, cols), F32),
        ],
        compiler_params=pltpu.CompilerParams(vmem_limit_bytes=VMEM_BYTES),
    )(*operands)


def finish_body(rows, comps, state_ref, new_ref, old_ref, kept_ref, came_ref, mask_ref, gains_ref, out_ref, news_ref, copies):
    is_ocean = lax.axis_index("comp") == comps - 1
    tendency = jnp.where(is_ocean, mask_ref[0].astype(F32), 1.0)
    sums = [kept_ref[v * rows : (v + 1) * rows, :] + came_ref[v * rows : (v + 1) * rows, :] for v in range(4)]
    saves = []
    for v, total, gain in ((0, sums[1], 1), (1, sums[2], 1), (2, sums[0], 0)):
        news_ref[v] = new_ref[v] + tendency * gains_ref[0, gain] * (total - sums[3] * old_ref[v])
        saves.append(pltpu.make_async_copy(news_ref.at[v], out_ref.at[0, v + 1, 0], copies.at[v]))
        saves[-1].start()
    for save in saves:
        save.wait()


def finish(state, new_surface, old_surface, kept, came, sea_mask, gains, comps):
    rows, cols = state.shape[3:]
    vmem = pl.BlockSpec(memory_space=pltpu.VMEM)
    anywhere = pl.BlockSpec(memory_space=pl.ANY)
    return pl.pallas_call(
        functools.partial(finish_body, rows, comps),
        in_specs=[anywhere] + [vmem] * 5 + [pl.BlockSpec(memory_space=pltpu.SMEM)],
        out_specs=anywhere,
        out_shape=jax.ShapeDtypeStruct(state.shape, F32),
        scratch_shapes=[pltpu.VMEM((3, rows, cols), F32), pltpu.SemaphoreType.DMA((3,))],
        input_output_aliases={0: 0},
        compiler_params=pltpu.CompilerParams(vmem_limit_bytes=VMEM_BYTES),
    )(state, new_surface, old_surface, kept, came, sea_mask, gains)


def shards(
    model_state, sea_mask, wave_speed, diffusivity, surface_gains, area_table,
    own_cells, target_cells, weight_ids, pair_counts, fold_map,
):
    comps, count_x, count_y = (lax.axis_size(a) for a in ("comp", "tx", "ty"))
    positions = count_x * count_y
    rows, cols = model_state.shape[3:]
    slots = own_cells.shape[3]
    slot_arrays = (own_cells, target_cells, weight_ids, area_table.reshape(-1, LANES), pair_counts)

    def along(block, shift):
        return lax.ppermute(block, ("tx", "ty"), [(s, (s + shift) % positions) for s in range(positions)])

    slab1, slab2, slab3 = first_side(model_state, slot_arrays, comps)
    slab3 = along(slab3, 1 + count_y)
    slab1 = along(slab1, 1)
    slab2 = along(slab2, count_y)
    slab0, up, down, high, low, pair = second_side(model_state, slot_arrays, sea_mask, comps)
    arrived = jnp.concatenate([slab0, slab1, slab2, slab3])
    other = lax.ppermute(arrived, "comp", [(g, g ^ 2) for g in range(comps)])

    up = along(up, count_y)
    down = along(down, -count_y)
    if count_y == 2:
        south = north = lax.ppermute(pair, "ty", [(0, 1), (1, 0)])
    else:
        south = lax.ppermute(high, "ty", [(j, j + 1) for j in range(count_y - 1)])
        north = lax.ppermute(low, "ty", [(j + 1, j) for j in range(count_y - 1)])
    fars = []
    for shift in range(2, count_x - 1):
        pairs = []
        for i in range(count_x):
            ends = [((comps - 1) * count_x + k) * count_y + count_y - 1 for k in ((i + shift) % count_x, i)]
            pairs.append(tuple(ends))
        fars.append(lax.ppermute(high, ("comp", "tx", "ty"), pairs))

    (before,) = scatter_call(own_body, 1, 1, rows, cols, comps, slots, arrived)
    kept, sent = scatter_call(other_body, 2, 2, rows, cols, comps, slots, other, before)
    came = lax.ppermute(sent, "comp", [(g, g ^ 1) for g in range(comps)])
    up, down, south, north, high, _ = lax.optimization_barrier((up, down, south, north, high, kept))
    new_state, new_surface, old_surface = stencil(
        model_state, sea_mask, up, down, south, north, high, fars, fold_map,
        wave_speed, diffusivity, surface_gains, (comps, count_x, count_y),
    )
    return finish(new_state, new_surface, old_surface, kept, came, sea_mask, surface_gains, comps)


def solution(mesh):
    in_specs = (
        P("comp", None, None, "tx", "ty"),
        P("comp", "tx", "ty"),
        P("comp", None),
        P("comp", None),
        P("comp", None),
        P(),
        P("comp", ("tx", "ty"), None, None),
        P("comp", ("tx", "ty"), None, None),
        P("comp", ("tx", "ty"), None, None),
        P("comp", ("tx", "ty"), None),
        P(),
    )
    out_specs = P("comp", None, None, "tx", "ty")
    return jax.shard_map(shards, mesh=mesh, in_specs=in_specs, out_specs=out_specs, check_vma=False)
```

```python
import functools

import jax
import jax.numpy as jnp
from jax import lax
from jax.experimental import pallas as pl
from jax.experimental.pallas import tpu as pltpu
from jax.sharding import PartitionSpec as P

LANES = 128
PACKED = 16
VMEM_BYTES = 28 * 1024 * 1024
F32 = jnp.float32
BF16 = jnp.bfloat16
I32 = jnp.int32
CHANNELS = 5

EDGE_P, SECOND_P, EDGE_VELOCITY, EDGE_T, MASK = range(5)


def iota(shape, dim):
    return lax.broadcasted_iota(I32, shape, dim)


def halo_rows(levels):
    return (4 * levels + 1 + 7) // 8 * 8


def split_two(values):
    high = values.astype(BF16)
    low = (values - high.astype(F32)).astype(BF16)
    return high, low


def packed_ids(count):
    ids = iota((count, LANES), 0).astype(F32).astype(BF16)
    return ids.reshape(count // PACKED, PACKED, LANES)


def spread_row(row):
    return jnp.broadcast_to(row, (PACKED, LANES))


def share_bounds(slots, shares):
    bounds = [0]
    for m in range(shares):
        bounds.append(bounds[-1] + (slots - m + shares - 1) // shares)
    return bounds


def slot_order(slots, shares, sort, half):
    place = iota((8, LANES), 0) * LANES + iota((8, LANES), 1) + half * 8 * LANES
    source = jnp.zeros((8, LANES), I32)
    bounds = share_bounds(slots, shares)
    for m in range(shares):
        inside = jnp.logical_and(place >= bounds[m], place < bounds[m + 1])
        source = jnp.where(inside, (place - bounds[m]) * shares + m, source)
    return jnp.where(sort, source, place)


def pick_rows(ref, n, source):
    total = jnp.zeros((8, LANES), I32)
    for t in range(ref.shape[3] // LANES):
        row = jnp.broadcast_to(ref[0, 0, n : n + 1, t * LANES : (t + 1) * LANES], (8, LANES))
        picked = jnp.take_along_axis(row, source % LANES, axis=1)
        total = jnp.where(source // LANES == t, picked, total)
    return total


def gather_partner(n, rows, cols, comps, own_ref, target_ref, ids_ref, table_ref, counts_ref, halves_ref, cells_ref, out):
    slots = own_ref.shape[3]
    groups = slots // LANES
    is_ocean = lax.axis_index("comp") == comps - 1
    weights = []
    count = jnp.broadcast_to(counts_ref[0, :, n : n + 1], (8, LANES))
    for half in range(groups // 8):
        source = slot_order(slots, comps - 1, is_ocean, half)
        cells_ref[half * 8 : (half + 1) * 8, :] = pick_rows(own_ref, n, source)
        targets = pick_rows(target_ref, n, source)
        ids = pick_rows(ids_ref, n, source)
        weight = jnp.zeros((8, LANES), F32)
        for t in range(table_ref.shape[0]):
            table = jnp.broadcast_to(table_ref[t : t + 1, :], (8, LANES))
            looked = jnp.take_along_axis(table, ids % LANES, axis=1)
            weight = jnp.where(ids // LANES == t, looked, weight)
        weights.append(jnp.where(source < count, weight, 0.0))
        out[3 * groups + half * 8 : 3 * groups + (half + 1) * 8, :] = weights[-1]
        out[4 * groups + half * 8 : 4 * groups + (half + 1) * 8, :] = targets.astype(F32)
    col_ids = packed_ids(cols)
    row_ids = iota((rows, LANES), 0)
    one = jnp.ones((), BF16)
    zero = jnp.zeros((), BF16)
    wide, subs = 2, 4

    def some(c, carry):
        for sub in range(subs):
            first = (c * subs + sub) * wide
            cells = [cells_ref[pl.ds(first + g, 1), :] for g in range(wide)]
            picks = []
            for cell in cells:
                col = spread_row(cell % cols).astype(F32).astype(BF16)
                picks.append(jnp.where(col_ids == col[None], one, zero).reshape(cols, LANES))
            picks = jnp.concatenate(picks, axis=1)
            picks = jnp.concatenate([picks, picks], axis=0)
            found = jnp.dot(halves_ref[...], picks, preferred_element_type=F32)
            for g in range(wide):
                in_row = row_ids == cells[g] // cols
                for place, v in enumerate((2, 0, 1)):
                    block = found[v * rows : (v + 1) * rows, g * LANES : (g + 1) * LANES]
                    value = jnp.sum(jnp.where(in_row, block, 0.0), axis=0, keepdims=True)
                    out[pl.ds(place * groups + first + g, 1), :] = value
        return carry

    lax.fori_loop(0, groups // (subs * wide), some, 0)
    for half, weight in enumerate(weights):
        for place in range(3):
            at = slice(place * groups + half * 8, place * groups + (half + 1) * 8)
            out[at, :] = out[at, :] * weight


def split_surface(surface_ref, halves_ref, rows, cols):
    for v in range(3):
        high, low = split_two(surface_ref[v])
        halves_ref[v * rows : (v + 1) * rows, :cols] = high
        halves_ref[v * rows : (v + 1) * rows, cols:] = low


def first_body(
    rows, cols, comps,
    state_hbm, own_hbm, target_hbm, ids_hbm, table_hbm, counts_hbm,
    slab1_ref, slab2_ref, slab3_ref,
    surface_ref, own_ref, target_ref, ids_ref, table_ref, counts_ref, halves_ref, cells_ref, copies,
):
    sources = (state_hbm.at[0, pl.ds(1, 3), 0], own_hbm, target_hbm, ids_hbm, table_hbm, counts_hbm)
    places = (surface_ref, own_ref, target_ref, ids_ref, table_ref, counts_ref)
    fetches = [
        pltpu.make_async_copy(source, place, copies.at[i])
        for i, (source, place) in enumerate(zip(sources, places))
    ]
    for fetch in fetches:
        fetch.start()
    for fetch in fetches:
        fetch.wait()
    split_surface(surface_ref, halves_ref, rows, cols)
    for n, out in ((3, slab3_ref), (1, slab1_ref), (2, slab2_ref)):
        gather_partner(
            n, rows, cols, comps, own_ref, target_ref, ids_ref, table_ref, counts_ref, halves_ref, cells_ref, out
        )


def slot_scratch(rows, cols, slots, near, table_shape):
    return [
        pltpu.VMEM((1, 1, near, slots), I32),
        pltpu.VMEM((1, 1, near, slots), I32),
        pltpu.VMEM((1, 1, near, slots), I32),
        pltpu.VMEM(table_shape, F32),
        pltpu.VMEM((1, 1, near), I32),
        pltpu.VMEM((3 * rows, 2 * cols), BF16),
        pltpu.VMEM((slots // LANES, LANES), I32),
    ]


def first_side(model_state, slot_arrays, comps):
    rows, cols = model_state.shape[3:]
    near, slots = slot_arrays[0].shape[2:]
    table_shape = slot_arrays[3].shape
    slab = jax.ShapeDtypeStruct((CHANNELS * slots // LANES, LANES), F32)
    vmem = pl.BlockSpec(memory_space=pltpu.VMEM)
    return pl.pallas_call(
        functools.partial(first_body, rows, cols, comps),
        in_specs=[pl.BlockSpec(memory_space=pltpu.HBM)] * 6,
        out_specs=[vmem] * 3,
        out_shape=[slab] * 3,
        scratch_shapes=[pltpu.VMEM((3, rows, cols), F32)]
        + slot_scratch(rows, cols, slots, near, table_shape)
        + [pltpu.SemaphoreType.DMA((6,))],
        compiler_params=pltpu.CompilerParams(vmem_limit_bytes=VMEM_BYTES),
    )(*(pltpu.with_memory_space_constraint(array, pltpu.HBM) for array in (model_state, *slot_arrays)))


def second_body(
    levels, rows, cols, comps,
    state_ref, own_ref, target_ref, ids_ref, table_ref, counts_ref, mask_hbm,
    slab0_ref, up_ref, down_ref, high_ref, low_ref, pair_ref, halves_ref, cells_ref, mask_ref, copied,
):
    height = halo_rows(levels)
    parts = cols // LANES
    fetch = pltpu.make_async_copy(mask_hbm, mask_ref, copied)
    fetch.start()
    split_surface(state_ref.at[0, pl.ds(1, 3), 0], halves_ref, rows, cols)
    gather_partner(
        0, rows, cols, comps, own_ref, target_ref, ids_ref, table_ref, counts_ref, halves_ref, cells_ref, slab0_ref
    )
    fetch.wait()
    sea = mask_ref[0].astype(F32)

    def put_row(ref, q, level, field, at):
        row = q * levels + level
        for part in range(parts):
            cut = slice(part * LANES, (part + 1) * LANES)
            ref[part * height + row : part * height + row + 1, :] = field[at : at + 1, cut]

    for ref, edge, second in ((up_ref, rows - 1, rows - 2), (down_ref, 0, 1)):
        for part in range(parts):
            ref[part * height + 4 * levels : (part + 1) * height, :] = jnp.zeros(
                (height - 4 * levels, LANES), F32
            )
        put_row(ref, 4, 0, sea, edge)
        for l in range(levels):
            put_row(ref, EDGE_P, l, state_ref.at[0, 0, l], edge)
            put_row(ref, SECOND_P, l, state_ref.at[0, 0, l], second)
            put_row(ref, EDGE_VELOCITY, l, state_ref.at[0, 1, l], edge)
            put_row(ref, EDGE_T, l, state_ref.at[0, 3, l], edge)

    lanes = iota((rows, LANES), 1)

    def columns(start, begin):
        edge = 1 if begin else 0
        total = pltpu.roll(sea[:, start : start + LANES], (4 * levels - begin - edge) % LANES, 1)
        for l in range(levels):
            pair = pltpu.roll(state_ref[0, 0, l, :, start : start + LANES], (2 * l - begin) % LANES, 1)
            total = jnp.where(lanes // 2 == l, pair, total)
            for q, v in ((EDGE_VELOCITY, 2), (EDGE_T, 3)):
                at = q * levels + l
                moved = pltpu.roll(state_ref[0, v, l, :, start : start + LANES], (at - begin - edge) % LANES, 1)
                total = jnp.where(lanes == at, moved, total)
        return total.T[:height]

    highest = columns(cols - LANES, LANES - 2)
    lowest = columns(0, 0)
    high_ref[...] = highest
    low_ref[...] = lowest
    up_ref[height * parts :, :] = highest
    down_ref[height * parts :, :] = highest
    pair_ref[...] = jnp.where(lax.axis_index("ty") == 0, highest, lowest)


def second_side(model_state, slot_arrays, sea_mask, comps):
    levels, rows, cols = model_state.shape[2:]
    slots = slot_arrays[0].shape[3]
    height = halo_rows(levels)
    tall = height * (cols // LANES) + height
    heights = (CHANNELS * slots // LANES, tall, tall, height, height, height)
    vmem = pl.BlockSpec(memory_space=pltpu.VMEM)
    return pl.pallas_call(
        functools.partial(second_body, levels, rows, cols, comps),
        in_specs=[vmem] * 6 + [pl.BlockSpec(memory_space=pltpu.HBM)],
        out_specs=[vmem] * len(heights),
        out_shape=[jax.ShapeDtypeStruct((h, LANES), F32) for h in heights],
        scratch_shapes=[
            pltpu.VMEM((3 * rows, 2 * cols), BF16),
            pltpu.VMEM((slots // LANES, LANES), I32),
            pltpu.VMEM((1, rows, cols), I32),
            pltpu.SemaphoreType.DMA,
        ],
        compiler_params=pltpu.CompilerParams(vmem_limit_bytes=VMEM_BYTES),
    )(model_state, *slot_arrays, pltpu.with_memory_space_constraint(sea_mask, pltpu.HBM))


def stencil_body(
    levels, rows, cols, comps, count_x, count_y,
    state_ref, mask_ref, up_ref, down_ref, south_ref, north_ref, own_ref, fold_ref,
    wave_ref, spread_ref, gains_ref, *rest,
):
    far_refs = rest[: max(count_x - 3, 0)]
    out_ref, new_surface_ref, old_surface_ref = rest[len(far_refs) : len(far_refs) + 3]
    south_turned_ref, turned_ref, news_ref, stores = rest[len(far_refs) + 3 :]
    height = halo_rows(levels)
    parts = cols // LANES
    index_x = lax.axis_index("tx")
    index_y = lax.axis_index("ty")
    is_ocean = lax.axis_index("comp") == comps - 1
    last_y = index_y == count_y - 1
    mask_at = 4 * levels

    def store(l):
        return pltpu.make_async_copy(news_ref.at[l], out_ref.at[0, :, l], stores.at[l])

    fold = fold_ref[pl.ds(index_x, 1), :]
    total = jnp.zeros((height, LANES), F32)
    sources = [(0, own_ref, 0), (-1, up_ref, height * parts), (1, down_ref, height * parts)]
    sources += [(shift, ref, 0) for shift, ref in zip(range(2, count_x - 1), far_refs)]
    for shift, ref, start in sources:
        at = lax.rem(index_x + shift + count_x, count_x)
        chosen = (iota((rows, rows), 0) + at * rows == fold).astype(F32)
        total += jnp.dot(
            ref[start : start + height, :], chosen,
            precision=lax.Precision.HIGHEST, preferred_element_type=F32,
        )
    line = iota((height, LANES), 0)
    swapped = jnp.where(line % 2 == 0, pltpu.roll(total, height - 1, 0), pltpu.roll(total, 1, 0))
    total = jnp.where(line < 2 * levels, swapped, total)
    flipped = jnp.logical_and(line >= EDGE_VELOCITY * levels, line < (EDGE_VELOCITY + 1) * levels)
    total = jnp.where(flipped, -total, total)
    total = jnp.where(last_y, jnp.where(is_ocean, total, 0.0), north_ref[...])
    fill = jnp.zeros((LANES - height, LANES), F32)
    turned_ref[...] = jnp.concatenate([total, fill], axis=0).T
    south_turned_ref[...] = jnp.concatenate([south_ref[...], fill], axis=0).T

    sea = mask_ref[0].astype(F32)
    tendency = jnp.where(is_ocean, sea, 1.0)
    drag = gains_ref[0, 2]
    has_west = jnp.where(jnp.logical_or(is_ocean, index_x > 0), 1.0, 0.0)
    has_east = jnp.where(jnp.logical_or(is_ocean, index_x < count_x - 1), 1.0, 0.0)
    has_south = jnp.where(index_y > 0, 1.0, 0.0)
    has_north = jnp.where(jnp.logical_or(is_ocean, jnp.logical_not(last_y)), 1.0, 0.0)
    row_ids = iota((rows, cols), 0)
    col_ids = iota((rows, cols), 1)
    blank = jnp.zeros((rows, cols - LANES), F32)

    def from_west(field, edge):
        return jnp.where(row_ids == 0, edge, pltpu.roll(field, 1, 0))

    def from_east(field, edge):
        return jnp.where(row_ids == rows - 1, edge, pltpu.roll(field, rows - 1, 0))

    def from_south(field, edge):
        wide = jnp.concatenate([edge, blank], axis=1)
        return jnp.where(col_ids == 0, wide, pltpu.roll(field, 1, 1))

    def from_north(field, edge):
        wide = jnp.concatenate([blank, edge], axis=1)
        return jnp.where(col_ids == cols - 1, wide, pltpu.roll(field, cols - 1, 1))

    def row_at(ref, start, row):
        halves = [ref[pl.ds(start + p * height + row, 1), :] for p in range(parts)]
        return jnp.concatenate(halves, axis=1)

    def one_level(level, carry):
        pressure, zonal, meridional, tracer = (state_ref[0, v, level] for v in range(4))
        half = 0.5 * wave_ref[0, level]
        spread = spread_ref[0, level]
        first = jnp.where(level == 0, drag, 0.0)

        def keeping(sea_values):
            return jnp.where(is_ocean, sea_values, 1.0 - first * (1.0 - sea_values))

        def west_row(q):
            return row_at(up_ref, 0, q * levels + level)

        def east_row(q):
            return row_at(down_ref, 0, q * levels + level)

        def south_col(at):
            return pltpu.roll(south_turned_ref[...], lax.rem(LANES - at, LANES), 1)

        def north_col(at):
            return pltpu.roll(turned_ref[...], LANES - 1 - at, 1)

        keep = keeping(sea)
        south_p = south_col(2 * level + 1)
        north_p = north_col(2 * level)
        new_zonal = keep * (
            zonal
            - half * (
                from_east(pressure, has_east * east_row(EDGE_P))
                - from_west(pressure, has_west * west_row(EDGE_P))
            )
        )
        new_meridional = keep * (
            meridional
            - half * (from_north(pressure, has_north * north_p) - from_south(pressure, has_south * south_p))
        )
        laplace = (
            from_east(tracer, has_east * east_row(EDGE_T))
            + from_west(tracer, has_west * west_row(EDGE_T))
            + from_north(tracer, has_north * north_col(EDGE_T * levels + level))
            + from_south(tracer, has_south * south_col(EDGE_T * levels + level))
            - 4.0 * tracer
        )
        new_tracer = tracer + spread * tendency * laplace
        west_zonal = keeping(row_at(up_ref, 0, mask_at)) * (
            west_row(EDGE_VELOCITY) - half * (pressure[0:1, :] - west_row(SECOND_P))
        )
        east_zonal = keeping(row_at(down_ref, 0, mask_at)) * (
            east_row(EDGE_VELOCITY) - half * (east_row(SECOND_P) - pressure[rows - 1 : rows, :])
        )
        south_meridional = keeping(south_col(mask_at)) * (
            south_col(EDGE_VELOCITY * levels + level)
            - half * (pressure[:, :LANES] - south_col(2 * level))
        )
        north_meridional = keeping(north_col(mask_at)) * (
            north_col(EDGE_VELOCITY * levels + level)
            - half * (north_col(2 * level + 1) - pressure[:, cols - LANES :])
        )
        divergence = (
            from_east(new_zonal, has_east * east_zonal)
            - from_west(new_zonal, has_west * west_zonal)
            + from_north(new_meridional, has_north * north_meridional)
            - from_south(new_meridional, has_south * south_meridional)
        )
        news_ref[level, 0] = pressure - half * divergence
        news_ref[level, 1] = new_zonal
        news_ref[level, 2] = new_meridional
        news_ref[level, 3] = new_tracer
        store(level).start()

        @pl.when(level == 0)
        def _():
            new_surface_ref[0] = new_zonal
            new_surface_ref[1] = new_meridional
            new_surface_ref[2] = new_tracer
            old_surface_ref[0] = zonal
            old_surface_ref[1] = meridional
            old_surface_ref[2] = tracer

        return carry

    lax.fori_loop(0, levels, one_level, 0)
    for l in range(levels):
        store(l).wait()


def stencil(model_state, sea_mask, up, down, south, north, own, fars, fold_map, wave_speed, diffusivity, gains, sizes):
    comps, count_x, count_y = sizes
    levels, rows, cols = model_state.shape[2:]
    fold = fold_map.reshape(count_x, rows)
    vmem = pl.BlockSpec(memory_space=pltpu.VMEM)
    scalar = pl.BlockSpec(memory_space=pltpu.SMEM)
    anywhere = pl.BlockSpec(memory_space=pl.ANY)
    surface = jax.ShapeDtypeStruct((3, rows, cols), F32)
    return pl.pallas_call(
        functools.partial(stencil_body, levels, rows, cols, comps, count_x, count_y),
        in_specs=[vmem] * 8 + [scalar] * 3 + [vmem] * len(fars),
        out_specs=[anywhere, vmem, vmem],
        out_shape=[jax.ShapeDtypeStruct(model_state.shape, F32), surface, surface],
        scratch_shapes=[
            pltpu.VMEM((rows, LANES), F32),
            pltpu.VMEM((rows, LANES), F32),
            pltpu.VMEM((levels, 4, rows, cols), F32),
            pltpu.SemaphoreType.DMA((levels,)),
        ],
        compiler_params=pltpu.CompilerParams(vmem_limit_bytes=VMEM_BYTES),
    )(model_state, sea_mask, up, down, south, north, own, fold, wave_speed, diffusivity, gains, *fars)


def add_slots(rows, cols, groups, slab_ref, total_refs, spread_refs, column_refs, chunks, plan):
    row_ids = packed_ids(rows)
    col_ids = packed_ids(cols)
    lane = iota((1, LANES), 1)
    one = jnp.ones((), BF16)
    zero = jnp.zeros((), BF16)
    depth = spread_refs.shape[2] // LANES

    def build(chunk, buffer, part):
        n, first, low_slot, high_slot = plan(chunk)
        start = n * (CHANNELS * groups) + first
        for g in part:
            cells = slab_ref[pl.ds(start + 4 * groups + g, 1), :].astype(I32)
            slot = lane + (first + g) * LANES
            mine = jnp.logical_and(slot >= low_slot, slot < high_slot)
            row = spread_row(jnp.where(mine, cells // cols, -1)).astype(F32).astype(BF16)
            col = spread_row(cells % cols).astype(F32).astype(BF16)
            cut = slice(g * LANES, (g + 1) * LANES)
            column_refs[buffer, :, cut] = jnp.where(col_ids == col[None], one, zero).reshape(cols, LANES)
            in_row = row_ids == row[None]
            for v in range(4):
                value = spread_row(slab_ref[pl.ds(start + v * groups + g, 1), :])
                high, low = split_two(value)
                spread_refs[buffer, v * rows : (v + 1) * rows, cut] = jnp.where(
                    in_row, high[None], zero
                ).reshape(rows, LANES)
                spread_refs[buffer, (v + 4) * rows : (v + 5) * rows, cut] = jnp.where(
                    in_row, low[None], zero
                ).reshape(rows, LANES)

    def multiply(total_ref, buffer, part):
        total_ref[part, :] += lax.dot_general(
            spread_refs[buffer, part, :], column_refs[buffer], (((1,), (1,)), ((), ())),
            preferred_element_type=F32,
        )

    def both(total_ref, used, chunk, buffer):
        pieces = 2
        height = 8 * rows // pieces
        for p in range(pieces):
            multiply(total_ref, used, slice(p * height, (p + 1) * height))
            build(chunk, buffer, range(p * depth // pieces, (p + 1) * depth // pieces))

    @pl.when(chunks > 0)
    def _():
        build(0, 0, range(depth))

    done = 0
    for total_ref in total_refs:
        total_ref[...] = jnp.zeros_like(total_ref)

        def pair(c, carry, total_ref=total_ref):
            both(total_ref, 0, 2 * c + 1, 1)
            both(total_ref, 1, jnp.minimum(2 * c + 2, chunks - 1), 0)
            return carry

        step = chunks // 2 // len(total_refs)
        lax.fori_loop(done, done + step, pair, 0)
        done = done + step


def halves_added(total_ref, rows):
    return total_ref[: 4 * rows] + total_ref[4 * rows :]


def own_body(rows, cols, comps, groups, slab_ref, sent_ref, spread_refs, column_refs, total_ref):
    here = lax.axis_index("comp")
    depth = spread_refs.shape[2] // LANES
    pieces = groups // depth
    near = slab_ref.shape[0] // (CHANNELS * groups)
    bounds = share_bounds(groups * LANES, comps - 1)
    is_ocean = here == comps - 1
    beside = here == comps - 2

    def plan(chunk):
        n = jnp.where(is_ocean, chunk, chunk // pieces)
        first = jnp.where(is_ocean, groups - depth, chunk % pieces * depth)
        return n, first, jnp.where(is_ocean, bounds[comps - 2], 0), groups * LANES

    chunks = jnp.where(is_ocean, near, jnp.where(beside, near * pieces, 0))
    add_slots(rows, cols, groups, slab_ref, [total_ref], spread_refs, column_refs, chunks, plan)
    sent_ref[...] = halves_added(total_ref, rows)


def other_body(
    rows, cols, comps, groups, slab_ref, before_ref, kept_ref, sent_ref,
    spread_refs, column_refs, first_ref, second_ref,
):
    here = lax.axis_index("comp")
    depth = spread_refs.shape[2] // LANES
    pieces = groups // depth
    near = slab_ref.shape[0] // (CHANNELS * groups)
    bounds = share_bounds(groups * LANES, comps - 1)
    is_ocean = here == comps - 1
    beside = here == comps - 2
    for_two = here == comps - 3
    middle = bounds[1] // LANES // 4 * 4

    def plan(chunk):
        mine = chunk >= near
        n = jnp.where(for_two, chunk % near, chunk // pieces)
        first = jnp.where(for_two, jnp.where(mine, middle, 0), chunk % pieces * depth)
        low_slot = jnp.where(jnp.logical_and(for_two, mine), bounds[1], 0)
        high_slot = jnp.where(for_two, jnp.where(mine, bounds[2], bounds[1]), groups * LANES)
        return n, first, low_slot, high_slot

    chunks = jnp.where(here == 0, 0, near * pieces)
    totals = [first_ref, second_ref]
    add_slots(rows, cols, groups, slab_ref, totals, spread_refs, column_refs, chunks, plan)
    for start in range(0, 4 * rows, rows):
        first = first_ref[start : start + rows] + first_ref[start + 4 * rows : start + 5 * rows]
        second = second_ref[start : start + rows] + second_ref[start + 4 * rows : start + 5 * rows]
        kept_ref[start : start + rows] = jnp.where(beside, 0.0, second) + jnp.where(is_ocean, first, 0.0)
        sent = jnp.where(is_ocean, 0.0, first) + jnp.where(beside, second, 0.0)
        sent_ref[start : start + rows] = sent + before_ref[start : start + rows]


def scatter_call(body, totals, outs, rows, cols, comps, slots, *operands):
    vmem = pl.BlockSpec(memory_space=pltpu.VMEM)
    depth = 8 * LANES
    return pl.pallas_call(
        functools.partial(body, rows, cols, comps, slots // LANES),
        in_specs=[vmem] * len(operands),
        out_specs=[vmem] * outs,
        out_shape=[jax.ShapeDtypeStruct((4 * rows, cols), F32)] * outs,
        scratch_shapes=[
            pltpu.VMEM((2, 8 * rows, depth), BF16),
            pltpu.VMEM((2, cols, depth), BF16),
        ]
        + [pltpu.VMEM((8 * rows, cols), F32)] * totals,
        compiler_params=pltpu.CompilerParams(vmem_limit_bytes=VMEM_BYTES),
    )(*operands)


def finish_body(rows, comps, state_ref, new_ref, old_ref, kept_ref, came_ref, mask_ref, gains_ref, out_ref, news_ref, copies):
    is_ocean = lax.axis_index("comp") == comps - 1
    tendency = jnp.where(is_ocean, mask_ref[0].astype(F32), 1.0)
    sums = [kept_ref[v * rows : (v + 1) * rows, :] + came_ref[v * rows : (v + 1) * rows, :] for v in range(4)]
    saves = []
    for v, total, gain in ((0, sums[1], 1), (1, sums[2], 1), (2, sums[0], 0)):
        news_ref[v] = new_ref[v] + tendency * gains_ref[0, gain] * (total - sums[3] * old_ref[v])
        saves.append(pltpu.make_async_copy(news_ref.at[v], out_ref.at[0, v + 1, 0], copies.at[v]))
        saves[-1].start()
    for save in saves:
        save.wait()


def finish(state, new_surface, old_surface, kept, came, sea_mask, gains, comps):
    rows, cols = state.shape[3:]
    vmem = pl.BlockSpec(memory_space=pltpu.VMEM)
    anywhere = pl.BlockSpec(memory_space=pl.ANY)
    return pl.pallas_call(
        functools.partial(finish_body, rows, comps),
        in_specs=[anywhere] + [vmem] * 5 + [pl.BlockSpec(memory_space=pltpu.SMEM)],
        out_specs=anywhere,
        out_shape=jax.ShapeDtypeStruct(state.shape, F32),
        scratch_shapes=[pltpu.VMEM((3, rows, cols), F32), pltpu.SemaphoreType.DMA((3,))],
        input_output_aliases={0: 0},
        compiler_params=pltpu.CompilerParams(vmem_limit_bytes=VMEM_BYTES),
    )(state, new_surface, old_surface, kept, came, sea_mask, gains)


def shards(
    model_state, sea_mask, wave_speed, diffusivity, surface_gains, area_table,
    own_cells, target_cells, weight_ids, pair_counts, fold_map,
):
    comps, count_x, count_y = (lax.axis_size(a) for a in ("comp", "tx", "ty"))
    positions = count_x * count_y
    rows, cols = model_state.shape[3:]
    slots = own_cells.shape[3]
    slot_arrays = (own_cells, target_cells, weight_ids, area_table.reshape(-1, LANES), pair_counts)

    def along(block, shift):
        return lax.ppermute(block, ("tx", "ty"), [(s, (s + shift) % positions) for s in range(positions)])

    slab1, slab2, slab3 = first_side(model_state, slot_arrays, comps)
    slab3 = along(slab3, 1 + count_y)
    slab1 = along(slab1, 1)
    slab2 = along(slab2, count_y)
    slab0, up, down, high, low, pair = second_side(model_state, slot_arrays, sea_mask, comps)
    arrived = jnp.concatenate([slab0, slab1, slab2, slab3])
    other = lax.ppermute(arrived, "comp", [(g, g ^ 2) for g in range(comps)])

    up = along(up, count_y)
    down = along(down, -count_y)
    if count_y == 2:
        south = north = lax.ppermute(pair, "ty", [(0, 1), (1, 0)])
    else:
        south = lax.ppermute(high, "ty", [(j, j + 1) for j in range(count_y - 1)])
        north = lax.ppermute(low, "ty", [(j + 1, j) for j in range(count_y - 1)])
    fars = []
    for shift in range(2, count_x - 1):
        pairs = []
        for i in range(count_x):
            ends = [((comps - 1) * count_x + k) * count_y + count_y - 1 for k in ((i + shift) % count_x, i)]
            pairs.append(tuple(ends))
        fars.append(lax.ppermute(high, ("comp", "tx", "ty"), pairs))

    (before,) = scatter_call(own_body, 1, 1, rows, cols, comps, slots, arrived)
    other, before, up, down, south, north, *fars = lax.optimization_barrier(
        (other, before, up, down, south, north, *fars)
    )
    kept, sent = scatter_call(other_body, 2, 2, rows, cols, comps, slots, other, before)
    came = lax.ppermute(sent, "comp", [(g, g ^ 1) for g in range(comps)])
    up, down, south, north, high, kept = lax.optimization_barrier((up, down, south, north, high, kept))
    new_state, new_surface, old_surface = stencil(
        model_state, sea_mask, up, down, south, north, high, fars, fold_map,
        wave_speed, diffusivity, surface_gains, (comps, count_x, count_y),
    )
    return finish(new_state, new_surface, old_surface, kept, came, sea_mask, surface_gains, comps)


def solution(mesh):
    in_specs = (
        P("comp", None, None, "tx", "ty"),
        P("comp", "tx", "ty"),
        P("comp", None),
        P("comp", None),
        P("comp", None),
        P(),
        P("comp", ("tx", "ty"), None, None),
        P("comp", ("tx", "ty"), None, None),
        P("comp", ("tx", "ty"), None, None),
        P("comp", ("tx", "ty"), None),
        P(),
    )
    out_specs = P("comp", None, None, "tx", "ty")
    return jax.shard_map(shards, mesh=mesh, in_specs=in_specs, out_specs=out_specs, check_vma=False)
```

```python
import functools

import jax
import jax.numpy as jnp
from jax import lax
from jax.experimental import pallas as pl
from jax.experimental.pallas import tpu as pltpu
from jax.sharding import PartitionSpec as P

LANES = 128
PACKED = 16
VMEM_BYTES = 28 * 1024 * 1024
F32 = jnp.float32
BF16 = jnp.bfloat16
I32 = jnp.int32
CHANNELS = 5

EDGE_P, SECOND_P, EDGE_VELOCITY, EDGE_T, MASK = range(5)


def iota(shape, dim):
    return lax.broadcasted_iota(I32, shape, dim)


def halo_rows(levels):
    return (4 * levels + 1 + 7) // 8 * 8


def split_two(values):
    high = values.astype(BF16)
    low = (values - high.astype(F32)).astype(BF16)
    return high, low


def packed_ids(count):
    ids = iota((count, LANES), 0).astype(F32).astype(BF16)
    return ids.reshape(count // PACKED, PACKED, LANES)


def one_hot(ids, at):
    apart = ids - at[None]
    return jnp.maximum(jnp.ones((), BF16) - apart * apart, jnp.zeros((), BF16))


def spread_row(row):
    return jnp.broadcast_to(row, (PACKED, LANES))


def share_bounds(slots, shares):
    bounds = [0]
    for m in range(shares):
        bounds.append(bounds[-1] + (slots - m + shares - 1) // shares)
    return bounds


def slot_order(slots, shares, sort, half):
    place = iota((8, LANES), 0) * LANES + iota((8, LANES), 1) + half * 8 * LANES
    source = jnp.zeros((8, LANES), I32)
    bounds = share_bounds(slots, shares)
    for m in range(shares):
        inside = jnp.logical_and(place >= bounds[m], place < bounds[m + 1])
        source = jnp.where(inside, (place - bounds[m]) * shares + m, source)
    return jnp.where(sort, source, place)


def pick_rows(ref, n, source):
    total = jnp.zeros((8, LANES), I32)
    for t in range(ref.shape[3] // LANES):
        row = jnp.broadcast_to(ref[0, 0, n : n + 1, t * LANES : (t + 1) * LANES], (8, LANES))
        picked = jnp.take_along_axis(row, source % LANES, axis=1)
        total = jnp.where(source // LANES == t, picked, total)
    return total


def gather_partner(n, rows, cols, comps, own_ref, target_ref, ids_ref, table_ref, counts_ref, halves_ref, cells_ref, out):
    slots = own_ref.shape[3]
    groups = slots // LANES
    is_ocean = lax.axis_index("comp") == comps - 1
    weights = []
    count = jnp.broadcast_to(counts_ref[0, :, n : n + 1], (8, LANES))
    for half in range(groups // 8):
        source = slot_order(slots, comps - 1, is_ocean, half)
        cells_ref[half * 8 : (half + 1) * 8, :] = pick_rows(own_ref, n, source)
        targets = pick_rows(target_ref, n, source)
        ids = pick_rows(ids_ref, n, source)
        weight = jnp.zeros((8, LANES), F32)
        for t in range(table_ref.shape[0]):
            table = jnp.broadcast_to(table_ref[t : t + 1, :], (8, LANES))
            looked = jnp.take_along_axis(table, ids % LANES, axis=1)
            weight = jnp.where(ids // LANES == t, looked, weight)
        weights.append(jnp.where(source < count, weight, 0.0))
        out[3 * groups + half * 8 : 3 * groups + (half + 1) * 8, :] = weights[-1]
        out[4 * groups + half * 8 : 4 * groups + (half + 1) * 8, :] = targets.astype(F32)
    col_ids = packed_ids(cols)
    row_ids = iota((rows, LANES), 0)
    one = jnp.ones((), BF16)
    zero = jnp.zeros((), BF16)
    wide, subs = 2, 4

    def some(c, carry):
        for sub in range(subs):
            first = (c * subs + sub) * wide
            cells = [cells_ref[pl.ds(first + g, 1), :] for g in range(wide)]
            picks = []
            for cell in cells:
                col = spread_row(cell % cols).astype(F32).astype(BF16)
                picks.append(jnp.where(col_ids == col[None], one, zero).reshape(cols, LANES))
            picks = jnp.concatenate(picks, axis=1)
            picks = jnp.concatenate([picks, picks], axis=0)
            found = jnp.dot(halves_ref[...], picks, preferred_element_type=F32)
            for g in range(wide):
                in_row = row_ids == cells[g] // cols
                for place, v in enumerate((2, 0, 1)):
                    block = found[v * rows : (v + 1) * rows, g * LANES : (g + 1) * LANES]
                    value = jnp.sum(jnp.where(in_row, block, 0.0), axis=0, keepdims=True)
                    out[pl.ds(place * groups + first + g, 1), :] = value
        return carry

    lax.fori_loop(0, groups // (subs * wide), some, 0)
    for half, weight in enumerate(weights):
        for place in range(3):
            at = slice(place * groups + half * 8, place * groups + (half + 1) * 8)
            out[at, :] = out[at, :] * weight


def split_surface(surface_ref, halves_ref, rows, cols):
    for v in range(3):
        high, low = split_two(surface_ref[v])
        halves_ref[v * rows : (v + 1) * rows, :cols] = high
        halves_ref[v * rows : (v + 1) * rows, cols:] = low


def first_body(
    rows, cols, comps,
    state_hbm, own_hbm, target_hbm, ids_hbm, table_hbm, counts_hbm,
    both_ref,
    surface_ref, own_ref, target_ref, ids_ref, table_ref, counts_ref, halves_ref, cells_ref, copies,
):
    sources = (state_hbm.at[0, pl.ds(1, 3), 0], own_hbm, target_hbm, ids_hbm, table_hbm, counts_hbm)
    places = (surface_ref, own_ref, target_ref, ids_ref, table_ref, counts_ref)
    fetches = [
        pltpu.make_async_copy(source, place, copies.at[i])
        for i, (source, place) in enumerate(zip(sources, places))
    ]
    for fetch in fetches:
        fetch.start()
    for fetch in fetches:
        fetch.wait()
    split_surface(surface_ref, halves_ref, rows, cols)
    slab_rows = both_ref.shape[0] // 2
    for n, out in ((1, both_ref.at[pl.ds(0, slab_rows)]), (3, both_ref.at[pl.ds(slab_rows, slab_rows)])):
        gather_partner(
            n, rows, cols, comps, own_ref, target_ref, ids_ref, table_ref, counts_ref, halves_ref, cells_ref, out
        )


def slot_scratch(rows, cols, slots, near, table_shape):
    return [
        pltpu.VMEM((1, 1, near, slots), I32),
        pltpu.VMEM((1, 1, near, slots), I32),
        pltpu.VMEM((1, 1, near, slots), I32),
        pltpu.VMEM(table_shape, F32),
        pltpu.VMEM((1, 1, near), I32),
        pltpu.VMEM((3 * rows, 2 * cols), BF16),
        pltpu.VMEM((slots // LANES, LANES), I32),
    ]


def first_side(model_state, slot_arrays, comps):
    rows, cols = model_state.shape[3:]
    near, slots = slot_arrays[0].shape[2:]
    table_shape = slot_arrays[3].shape
    slabs = jax.ShapeDtypeStruct((2 * CHANNELS * slots // LANES, LANES), F32)
    vmem = pl.BlockSpec(memory_space=pltpu.VMEM)
    return pl.pallas_call(
        functools.partial(first_body, rows, cols, comps),
        in_specs=[pl.BlockSpec(memory_space=pltpu.HBM)] * 6,
        out_specs=vmem,
        out_shape=slabs,
        scratch_shapes=[pltpu.VMEM((3, rows, cols), F32)]
        + slot_scratch(rows, cols, slots, near, table_shape)
        + [pltpu.SemaphoreType.DMA((6,))],
        compiler_params=pltpu.CompilerParams(vmem_limit_bytes=VMEM_BYTES),
    )(*(pltpu.with_memory_space_constraint(array, pltpu.HBM) for array in (model_state, *slot_arrays)))


def second_body(
    rows, cols, comps, state_ref, own_ref, target_ref, ids_ref, table_ref, counts_ref,
    slab0_ref, slab2_ref, halves_ref, cells_ref,
):
    split_surface(state_ref.at[0, pl.ds(1, 3), 0], halves_ref, rows, cols)
    for n, out in ((2, slab2_ref), (0, slab0_ref)):
        gather_partner(
            n, rows, cols, comps, own_ref, target_ref, ids_ref, table_ref, counts_ref, halves_ref, cells_ref, out
        )


def second_side(model_state, slot_arrays, comps):
    rows, cols = model_state.shape[3:]
    slots = slot_arrays[0].shape[3]
    slab = jax.ShapeDtypeStruct((CHANNELS * slots // LANES, LANES), F32)
    vmem = pl.BlockSpec(memory_space=pltpu.VMEM)
    return pl.pallas_call(
        functools.partial(second_body, rows, cols, comps),
        in_specs=[vmem] * 6,
        out_specs=[vmem] * 2,
        out_shape=[slab] * 2,
        scratch_shapes=[
            pltpu.VMEM((3 * rows, 2 * cols), BF16),
            pltpu.VMEM((slots // LANES, LANES), I32),
        ],
        compiler_params=pltpu.CompilerParams(vmem_limit_bytes=VMEM_BYTES),
    )(model_state, *slot_arrays)


def pack_body(
    levels, rows, cols, state_ref, mask_hbm, up_ref, down_ref, high_ref, low_ref, pair_ref, mask_ref, copied,
):
    height = halo_rows(levels)
    parts = cols // LANES
    fetch = pltpu.make_async_copy(mask_hbm, mask_ref, copied)
    fetch.start()

    def put_row(ref, q, level, field, at):
        row = q * levels + level
        for part in range(parts):
            cut = slice(part * LANES, (part + 1) * LANES)
            ref[part * height + row : part * height + row + 1, :] = field[at : at + 1, cut]

    edges = ((up_ref, rows - 1, rows - 2), (down_ref, 0, 1))
    for ref, edge, second in edges:
        for l in range(levels):
            put_row(ref, EDGE_P, l, state_ref.at[0, 0, l], edge)
            put_row(ref, SECOND_P, l, state_ref.at[0, 0, l], second)
            put_row(ref, EDGE_VELOCITY, l, state_ref.at[0, 1, l], edge)
            put_row(ref, EDGE_T, l, state_ref.at[0, 3, l], edge)

    lanes = iota((rows, LANES), 1)

    def columns(start, begin):
        edge = 1 if begin else 0
        total = jnp.zeros((rows, LANES), F32)
        for l in range(levels):
            pair = pltpu.roll(state_ref[0, 0, l, :, start : start + LANES], (2 * l - begin) % LANES, 1)
            total = jnp.where(lanes // 2 == l, pair, total)
            for q, v in ((EDGE_VELOCITY, 2), (EDGE_T, 3)):
                at = q * levels + l
                moved = pltpu.roll(state_ref[0, v, l, :, start : start + LANES], (at - begin - edge) % LANES, 1)
                total = jnp.where(lanes == at, moved, total)
        return total

    highest = columns(cols - LANES, LANES - 2)
    lowest = columns(0, 0)
    fetch.wait()
    sea = mask_ref[0].astype(F32)
    at = 4 * levels
    for ref, edge, second in edges:
        for part in range(parts):
            ref[part * height + at : (part + 1) * height, :] = jnp.zeros((height - at, LANES), F32)
        put_row(ref, 4, 0, sea, edge)
    sea_high = pltpu.roll(sea[:, cols - LANES :], (at - (LANES - 1)) % LANES, 1)
    sea_low = pltpu.roll(sea[:, :LANES], at, 1)
    highest = jnp.where(lanes == at, sea_high, highest).T[:height]
    lowest = jnp.where(lanes == at, sea_low, lowest).T[:height]
    high_ref[...] = highest
    low_ref[...] = lowest
    up_ref[height * parts :, :] = highest
    down_ref[height * parts :, :] = highest
    pair_ref[...] = jnp.where(lax.axis_index("ty") == 0, highest, lowest)


def pack_halos(model_state, sea_mask):
    levels, rows, cols = model_state.shape[2:]
    height = halo_rows(levels)
    tall = height * (cols // LANES) + height
    heights = (tall, tall, height, height, height)
    vmem = pl.BlockSpec(memory_space=pltpu.VMEM)
    return pl.pallas_call(
        functools.partial(pack_body, levels, rows, cols),
        in_specs=[vmem, pl.BlockSpec(memory_space=pltpu.HBM)],
        out_specs=[vmem] * len(heights),
        out_shape=[jax.ShapeDtypeStruct((h, LANES), F32) for h in heights],
        scratch_shapes=[pltpu.VMEM((1, rows, cols), I32), pltpu.SemaphoreType.DMA],
        compiler_params=pltpu.CompilerParams(vmem_limit_bytes=VMEM_BYTES),
    )(model_state, pltpu.with_memory_space_constraint(sea_mask, pltpu.HBM))


def stencil_body(
    levels, rows, cols, comps, count_x, count_y,
    state_ref, mask_ref, up_ref, down_ref, south_ref, north_ref, own_ref, fold_ref,
    wave_ref, spread_ref, gains_ref, *rest,
):
    far_refs = rest[: max(count_x - 3, 0)]
    out_ref, new_surface_ref, old_surface_ref = rest[len(far_refs) : len(far_refs) + 3]
    south_turned_ref, turned_ref, news_ref, stores = rest[len(far_refs) + 3 :]
    height = halo_rows(levels)
    parts = cols // LANES
    index_x = lax.axis_index("tx")
    index_y = lax.axis_index("ty")
    is_ocean = lax.axis_index("comp") == comps - 1
    last_y = index_y == count_y - 1
    mask_at = 4 * levels

    def store(l):
        return pltpu.make_async_copy(news_ref.at[l], out_ref.at[0, :, l], stores.at[l])

    fold = fold_ref[pl.ds(index_x, 1), :]
    total = jnp.zeros((height, LANES), F32)
    sources = [(0, own_ref, 0), (-1, up_ref, height * parts), (1, down_ref, height * parts)]
    sources += [(shift, ref, 0) for shift, ref in zip(range(2, count_x - 1), far_refs)]
    for shift, ref, start in sources:
        at = lax.rem(index_x + shift + count_x, count_x)
        chosen = (iota((rows, rows), 0) + at * rows == fold).astype(F32)
        total += jnp.dot(
            ref[start : start + height, :], chosen,
            precision=lax.Precision.HIGHEST, preferred_element_type=F32,
        )
    line = iota((height, LANES), 0)
    swapped = jnp.where(line % 2 == 0, pltpu.roll(total, height - 1, 0), pltpu.roll(total, 1, 0))
    total = jnp.where(line < 2 * levels, swapped, total)
    flipped = jnp.logical_and(line >= EDGE_VELOCITY * levels, line < (EDGE_VELOCITY + 1) * levels)
    total = jnp.where(flipped, -total, total)
    total = jnp.where(last_y, jnp.where(is_ocean, total, 0.0), north_ref[...])
    fill = jnp.zeros((LANES - height, LANES), F32)
    turned_ref[...] = jnp.concatenate([total, fill], axis=0).T
    has_west = jnp.where(jnp.logical_or(is_ocean, index_x > 0), 1.0, 0.0)
    has_east = jnp.where(jnp.logical_or(is_ocean, index_x < count_x - 1), 1.0, 0.0)
    has_south = jnp.where(index_y > 0, 1.0, 0.0)
    has_north = jnp.where(jnp.logical_or(is_ocean, jnp.logical_not(last_y)), 1.0, 0.0)
    south_turned_ref[...] = jnp.concatenate([south_ref[...] * has_south, fill], axis=0).T
    drag = gains_ref[0, 2]
    deep = 16
    strips = rows // deep
    row_ids = iota((deep, LANES), 0)
    lane = iota((deep, LANES), 1)

    def tiles(ref, at, count=deep):
        return [ref[at : at + count, p * LANES : (p + 1) * LANES] for p in range(parts)]

    def halo_row(ref, row):
        return [ref[pl.ds(p * height + row, 1), :] for p in range(parts)]

    def from_west(strip, before):
        return [jnp.where(row_ids == 0, b, pltpu.roll(t, 1, 0)) for t, b in zip(strip, before)]

    def from_east(strip, after):
        return [jnp.where(row_ids == deep - 1, a, pltpu.roll(t, deep - 1, 0)) for t, a in zip(strip, after)]

    def from_south(strip, edge):
        moved = [pltpu.roll(t, 1, 1) for t in strip]
        return [jnp.where(lane == 0, low, t) for low, t in zip([edge] + moved[:-1], moved)]

    def from_north(strip, edge):
        moved = [pltpu.roll(t, LANES - 1, 1) for t in strip]
        return [jnp.where(lane == LANES - 1, high, t) for high, t in zip(moved[1:] + [edge], moved)]

    def one_level(level, carry):
        half = 0.5 * wave_ref[0, level]
        spread = spread_ref[0, level]
        first = jnp.where(level == 0, drag, 0.0)
        pressure_ref, zonal_ref, meridional_ref, tracer_ref = (state_ref.at[0, v, level] for v in range(4))

        def keeping(sea_values):
            return jnp.where(is_ocean, sea_values, 1.0 - first * (1.0 - sea_values))

        def sea_tiles(at, count=deep):
            return [t.astype(F32) for t in tiles(mask_ref.at[0], at, count)]

        def west_row(q):
            return halo_row(up_ref, q * levels + level)

        def east_row(q):
            return halo_row(down_ref, q * levels + level)

        west_p = [has_west * t for t in west_row(EDGE_P)]
        east_p = [has_east * t for t in east_row(EDGE_P)]
        west_t = [has_west * t for t in west_row(EDGE_T)]
        east_t = [has_east * t for t in east_row(EDGE_T)]
        west_zonal = [
            has_west * keeping(sea) * (u - half * (p - second))
            for sea, u, p, second in zip(
                halo_row(up_ref, mask_at), west_row(EDGE_VELOCITY), tiles(pressure_ref, 0, 1), west_row(SECOND_P)
            )
        ]
        east_zonal = [
            has_east * keeping(sea) * (u - half * (second - p))
            for sea, u, p, second in zip(
                halo_row(down_ref, mask_at), east_row(EDGE_VELOCITY),
                tiles(pressure_ref, rows - 1, 1), east_row(SECOND_P),
            )
        ]

        for k in range(strips):
            at = k * deep
            def south_col(place, at=at):
                return pltpu.roll(south_turned_ref[at : at + deep, :], lax.rem(LANES - place, LANES), 1)

            def north_col(place, at=at):
                return pltpu.roll(turned_ref[at : at + deep, :], LANES - 1 - place, 1)

            pressure, zonal, meridional, tracer = (
                tiles(ref, at) for ref in (pressure_ref, zonal_ref, meridional_ref, tracer_ref)
            )
            sea = sea_tiles(at)
            keep = [keeping(t) for t in sea]
            before_p = west_p if k == 0 else tiles(pressure_ref, at - 1, 1)
            after_p = east_p if k == strips - 1 else tiles(pressure_ref, at + deep, 1)
            new_zonal = [
                m * (u - half * (e - w))
                for m, u, e, w in zip(keep, zonal, from_east(pressure, after_p), from_west(pressure, before_p))
            ]
            south_p = south_col(2 * level + 1)
            north_p = north_col(2 * level)
            new_meridional = [
                m * (v - half * (n - s))
                for m, v, n, s in zip(
                    keep, meridional, from_north(pressure, north_p), from_south(pressure, south_p)
                )
            ]
            south_v = has_south * keeping(south_col(mask_at)) * (
                south_col(EDGE_VELOCITY * levels + level) - half * (pressure[0] - south_col(2 * level))
            )
            north_v = has_north * keeping(north_col(mask_at)) * (
                north_col(EDGE_VELOCITY * levels + level) - half * (north_col(2 * level + 1) - pressure[-1])
            )
            across = [
                n - s for n, s in zip(from_north(new_meridional, north_v), from_south(new_meridional, south_v))
            ]
            before_t = west_t if k == 0 else tiles(tracer_ref, at - 1, 1)
            after_t = east_t if k == strips - 1 else tiles(tracer_ref, at + deep, 1)
            new_tracer = [
                t + spread * jnp.where(is_ocean, m, 1.0) * (e + w + n + s - 4.0 * t)
                for t, m, e, w, n, s in zip(
                    tracer, sea, from_east(tracer, after_t), from_west(tracer, before_t),
                    from_north(tracer, north_col(EDGE_T * levels + level)),
                    from_south(tracer, south_col(EDGE_T * levels + level)),
                )
            ]
            for p in range(parts):
                cut = slice(p * LANES, (p + 1) * LANES)
                news_ref[level, 0, at : at + deep, cut] = pressure[p] - half * across[p]
                news_ref[level, 1, at : at + deep, cut] = new_zonal[p]
                news_ref[level, 2, at : at + deep, cut] = new_meridional[p]
                news_ref[level, 3, at : at + deep, cut] = new_tracer[p]

        for k in range(strips):
            at = k * deep
            new_zonal_ref = news_ref.at[level, 1]
            new_zonal = tiles(new_zonal_ref, at)
            before = west_zonal if k == 0 else tiles(new_zonal_ref, at - 1, 1)
            after = east_zonal if k == strips - 1 else tiles(new_zonal_ref, at + deep, 1)
            along = [e - w for e, w in zip(from_east(new_zonal, after), from_west(new_zonal, before))]
            for p in range(parts):
                cut = slice(p * LANES, (p + 1) * LANES)
                news_ref[level, 0, at : at + deep, cut] = news_ref[level, 0, at : at + deep, cut] - half * along[p]
        store(level).start()

        @pl.when(level == 0)
        def _():
            for v in range(3):
                new_surface_ref[v] = news_ref[0, v + 1]
                old_surface_ref[v] = state_ref[0, v + 1, 0]

        return carry

    lax.fori_loop(0, levels, one_level, 0)
    for l in range(levels):
        store(l).wait()


def stencil(model_state, sea_mask, up, down, south, north, own, fars, fold_map, wave_speed, diffusivity, gains, sizes):
    comps, count_x, count_y = sizes
    levels, rows, cols = model_state.shape[2:]
    fold = fold_map.reshape(count_x, rows)
    vmem = pl.BlockSpec(memory_space=pltpu.VMEM)
    scalar = pl.BlockSpec(memory_space=pltpu.SMEM)
    anywhere = pl.BlockSpec(memory_space=pl.ANY)
    surface = jax.ShapeDtypeStruct((3, rows, cols), F32)
    return pl.pallas_call(
        functools.partial(stencil_body, levels, rows, cols, comps, count_x, count_y),
        in_specs=[vmem] * 8 + [scalar] * 3 + [vmem] * len(fars),
        out_specs=[anywhere, vmem, vmem],
        out_shape=[jax.ShapeDtypeStruct(model_state.shape, F32), surface, surface],
        scratch_shapes=[
            pltpu.VMEM((rows, LANES), F32),
            pltpu.VMEM((rows, LANES), F32),
            pltpu.VMEM((levels, 4, rows, cols), F32),
            pltpu.SemaphoreType.DMA((levels,)),
        ],
        compiler_params=pltpu.CompilerParams(vmem_limit_bytes=VMEM_BYTES),
    )(model_state, sea_mask, up, down, south, north, own, fold, wave_speed, diffusivity, gains, *fars)


def add_slots(rows, cols, groups, slab_ref, total_refs, spread_refs, column_refs, chunks, plan):
    row_ids = packed_ids(rows)
    col_ids = packed_ids(cols)
    lane = iota((1, LANES), 1)
    depth = spread_refs.shape[2] // LANES

    def build(chunk, buffer, part):
        n, first, low_slot, high_slot = plan(chunk)
        start = n * (CHANNELS * groups) + first
        for g in part:
            cells = slab_ref[pl.ds(start + 4 * groups + g, 1), :].astype(I32)
            slot = lane + (first + g) * LANES
            mine = jnp.logical_and(slot >= low_slot, slot < high_slot)
            row = spread_row(jnp.where(mine, cells // cols, -1)).astype(F32).astype(BF16)
            col = spread_row(cells % cols).astype(F32).astype(BF16)
            cut = slice(g * LANES, (g + 1) * LANES)
            column_refs[buffer, :, cut] = one_hot(col_ids, col).reshape(cols, LANES)
            in_row = one_hot(row_ids, row)
            for v in range(4):
                value = spread_row(slab_ref[pl.ds(start + v * groups + g, 1), :])
                high, low = split_two(value)
                spread_refs[buffer, v * rows : (v + 1) * rows, cut] = (in_row * high[None]).reshape(rows, LANES)
                spread_refs[buffer, (v + 4) * rows : (v + 5) * rows, cut] = (in_row * low[None]).reshape(rows, LANES)

    def multiply(total_ref, buffer, part):
        total_ref[part, :] += lax.dot_general(
            spread_refs[buffer, part, :], column_refs[buffer], (((1,), (1,)), ((), ())),
            preferred_element_type=F32,
        )

    def both(total_ref, used, chunk, buffer):
        pieces = 2
        height = 8 * rows // pieces
        for p in range(pieces):
            multiply(total_ref, used, slice(p * height, (p + 1) * height))
            build(chunk, buffer, range(p * depth // pieces, (p + 1) * depth // pieces))

    @pl.when(chunks > 0)
    def _():
        build(0, 0, range(depth))

    done = 0
    for total_ref in total_refs:
        total_ref[...] = jnp.zeros_like(total_ref)

        def pair(c, carry, total_ref=total_ref):
            both(total_ref, 0, 2 * c + 1, 1)
            both(total_ref, 1, jnp.minimum(2 * c + 2, chunks - 1), 0)
            return carry

        step = chunks // 2 // len(total_refs)
        lax.fori_loop(done, done + step, pair, 0)
        done = done + step


def halves_added(total_ref, rows):
    return total_ref[: 4 * rows] + total_ref[4 * rows :]


def own_body(rows, cols, comps, groups, slab_ref, sent_ref, spread_refs, column_refs, total_ref):
    here = lax.axis_index("comp")
    depth = spread_refs.shape[2] // LANES
    pieces = groups // depth
    near = slab_ref.shape[0] // (CHANNELS * groups)
    bounds = share_bounds(groups * LANES, comps - 1)
    is_ocean = here == comps - 1
    beside = here == comps - 2

    def plan(chunk):
        n = jnp.where(is_ocean, chunk, chunk // pieces)
        first = jnp.where(is_ocean, groups - depth, chunk % pieces * depth)
        return n, first, jnp.where(is_ocean, bounds[comps - 2], 0), groups * LANES

    chunks = jnp.where(is_ocean, near, jnp.where(beside, near * pieces, 0))
    add_slots(rows, cols, groups, slab_ref, [total_ref], spread_refs, column_refs, chunks, plan)
    sent_ref[...] = halves_added(total_ref, rows)


def other_body(
    rows, cols, comps, groups, slab_ref, before_ref, kept_ref, sent_ref,
    spread_refs, column_refs, first_ref, second_ref,
):
    here = lax.axis_index("comp")
    depth = spread_refs.shape[2] // LANES
    pieces = groups // depth
    near = slab_ref.shape[0] // (CHANNELS * groups)
    bounds = share_bounds(groups * LANES, comps - 1)
    is_ocean = here == comps - 1
    beside = here == comps - 2
    for_two = here == comps - 3
    middle = bounds[1] // LANES // 4 * 4

    def plan(chunk):
        mine = chunk >= near
        n = jnp.where(for_two, chunk % near, chunk // pieces)
        first = jnp.where(for_two, jnp.where(mine, middle, 0), chunk % pieces * depth)
        low_slot = jnp.where(jnp.logical_and(for_two, mine), bounds[1], 0)
        high_slot = jnp.where(for_two, jnp.where(mine, bounds[2], bounds[1]), groups * LANES)
        return n, first, low_slot, high_slot

    chunks = jnp.where(here == 0, 0, near * pieces)
    totals = [first_ref, second_ref]
    add_slots(rows, cols, groups, slab_ref, totals, spread_refs, column_refs, chunks, plan)
    for start in range(0, 4 * rows, rows):
        first = first_ref[start : start + rows] + first_ref[start + 4 * rows : start + 5 * rows]
        second = second_ref[start : start + rows] + second_ref[start + 4 * rows : start + 5 * rows]
        kept_ref[start : start + rows] = jnp.where(beside, 0.0, second) + jnp.where(is_ocean, first, 0.0)
        sent = jnp.where(is_ocean, 0.0, first) + jnp.where(beside, second, 0.0)
        sent_ref[start : start + rows] = sent + before_ref[start : start + rows]


def scatter_call(body, totals, outs, rows, cols, comps, slots, *operands):
    vmem = pl.BlockSpec(memory_space=pltpu.VMEM)
    depth = 8 * LANES
    return pl.pallas_call(
        functools.partial(body, rows, cols, comps, slots // LANES),
        in_specs=[vmem] * len(operands),
        out_specs=[vmem] * outs,
        out_shape=[jax.ShapeDtypeStruct((4 * rows, cols), F32)] * outs,
        scratch_shapes=[
            pltpu.VMEM((2, 8 * rows, depth), BF16),
            pltpu.VMEM((2, cols, depth), BF16),
        ]
        + [pltpu.VMEM((8 * rows, cols), F32)] * totals,
        compiler_params=pltpu.CompilerParams(vmem_limit_bytes=VMEM_BYTES),
    )(*operands)


def finish_body(rows, comps, state_ref, new_ref, old_ref, kept_ref, came_ref, mask_ref, gains_ref, out_ref, news_ref, copies):
    is_ocean = lax.axis_index("comp") == comps - 1
    tendency = jnp.where(is_ocean, mask_ref[0].astype(F32), 1.0)
    sums = [kept_ref[v * rows : (v + 1) * rows, :] + came_ref[v * rows : (v + 1) * rows, :] for v in range(4)]
    saves = []
    for v, total, gain in ((0, sums[1], 1), (1, sums[2], 1), (2, sums[0], 0)):
        news_ref[v] = new_ref[v] + tendency * gains_ref[0, gain] * (total - sums[3] * old_ref[v])
        saves.append(pltpu.make_async_copy(news_ref.at[v], out_ref.at[0, v + 1, 0], copies.at[v]))
        saves[-1].start()
    for save in saves:
        save.wait()


def finish(state, new_surface, old_surface, kept, came, sea_mask, gains, comps):
    rows, cols = state.shape[3:]
    vmem = pl.BlockSpec(memory_space=pltpu.VMEM)
    anywhere = pl.BlockSpec(memory_space=pl.ANY)
    return pl.pallas_call(
        functools.partial(finish_body, rows, comps),
        in_specs=[anywhere] + [vmem] * 5 + [pl.BlockSpec(memory_space=pltpu.SMEM)],
        out_specs=anywhere,
        out_shape=jax.ShapeDtypeStruct(state.shape, F32),
        scratch_shapes=[pltpu.VMEM((3, rows, cols), F32), pltpu.SemaphoreType.DMA((3,))],
        input_output_aliases={0: 0},
        compiler_params=pltpu.CompilerParams(vmem_limit_bytes=VMEM_BYTES),
    )(state, new_surface, old_surface, kept, came, sea_mask, gains)


def shards(
    model_state, sea_mask, wave_speed, diffusivity, surface_gains, area_table,
    own_cells, target_cells, weight_ids, pair_counts, fold_map,
):
    comps, count_x, count_y = (lax.axis_size(a) for a in ("comp", "tx", "ty"))
    positions = count_x * count_y
    rows, cols = model_state.shape[3:]
    slots = own_cells.shape[3]
    slot_arrays = (own_cells, target_cells, weight_ids, area_table.reshape(-1, LANES), pair_counts)

    def along(block, shift):
        return lax.ppermute(block, ("tx", "ty"), [(s, (s + shift) % positions) for s in range(positions)])

    def beside(block, shift):
        pairs = []
        for g in range(comps):
            for i in range(count_x):
                if g == comps - 1 or 0 <= i + shift < count_x:
                    for j in range(count_y):
                        ends = [(g * count_x + k) * count_y + j for k in (i, (i + shift) % count_x)]
                        pairs.append(tuple(ends))
        return lax.ppermute(block, ("comp", "tx", "ty"), pairs)

    slab_rows = CHANNELS * slots // LANES
    odd = along(first_side(model_state, slot_arrays, comps), 1)
    slab0, slab2 = second_side(model_state, slot_arrays, comps)
    later = along(jnp.concatenate([slab2, odd[slab_rows:]]), count_y)
    later, *packed = lax.optimization_barrier((later, *pack_halos(model_state, sea_mask)))
    up, down, high, low, pair = packed
    arrived = jnp.concatenate([slab0, odd[:slab_rows], later])
    other = lax.ppermute(arrived, "comp", [(g, g ^ 2) for g in range(comps)])

    up = beside(up, 1)
    down = beside(down, -1)
    if count_y == 2:
        south = north = lax.ppermute(pair, "ty", [(0, 1), (1, 0)])
    else:
        south = lax.ppermute(high, "ty", [(j, j + 1) for j in range(count_y - 1)])
        north = lax.ppermute(low, "ty", [(j + 1, j) for j in range(count_y - 1)])
    fars = []
    for shift in range(2, count_x - 1):
        pairs = []
        for i in range(count_x):
            ends = [((comps - 1) * count_x + k) * count_y + count_y - 1 for k in ((i + shift) % count_x, i)]
            pairs.append(tuple(ends))
        fars.append(lax.ppermute(high, ("comp", "tx", "ty"), pairs))

    (before,) = scatter_call(own_body, 1, 1, rows, cols, comps, slots, arrived)
    other, before, up, down, south, north, *fars = lax.optimization_barrier(
        (other, before, up, down, south, north, *fars)
    )
    kept, sent = scatter_call(other_body, 2, 2, rows, cols, comps, slots, other, before)
    came = lax.ppermute(sent, "comp", [(g, g ^ 1) for g in range(comps)])
    up, down, south, north, high, kept = lax.optimization_barrier((up, down, south, north, high, kept))
    new_state, new_surface, old_surface = stencil(
        model_state, sea_mask, up, down, south, north, high, fars, fold_map,
        wave_speed, diffusivity, surface_gains, (comps, count_x, count_y),
    )
    return finish(new_state, new_surface, old_surface, kept, came, sea_mask, surface_gains, comps)


def solution(mesh):
    in_specs = (
        P("comp", None, None, "tx", "ty"),
        P("comp", "tx", "ty"),
        P("comp", None),
        P("comp", None),
        P("comp", None),
        P(),
        P("comp", ("tx", "ty"), None, None),
        P("comp", ("tx", "ty"), None, None),
        P("comp", ("tx", "ty"), None, None),
        P("comp", ("tx", "ty"), None),
        P(),
    )
    out_specs = P("comp", None, None, "tx", "ty")
    return jax.shard_map(shards, mesh=mesh, in_specs=in_specs, out_specs=out_specs, check_vma=False)
```

```python
import functools

import jax
import jax.numpy as jnp
from jax import lax
from jax.experimental import pallas as pl
from jax.experimental.pallas import tpu as pltpu
from jax.sharding import PartitionSpec as P

LANES = 128
PACKED = 16
VMEM_BYTES = 28 * 1024 * 1024
F32 = jnp.float32
BF16 = jnp.bfloat16
I32 = jnp.int32
CHANNELS = 5

EDGE_P, SECOND_P, EDGE_VELOCITY, EDGE_T, MASK = range(5)


def iota(shape, dim):
    return lax.broadcasted_iota(I32, shape, dim)


def halo_rows(levels):
    return (4 * levels + 1 + 7) // 8 * 8


def split_two(values):
    high = values.astype(BF16)
    low = (values - high.astype(F32)).astype(BF16)
    return high, low


def packed_ids(count):
    ids = iota((count, LANES), 0).astype(F32).astype(BF16)
    return ids.reshape(count // PACKED, PACKED, LANES)


def spread_row(row):
    return jnp.broadcast_to(row, (PACKED, LANES))


def share_bounds(slots, shares):
    bounds = [0]
    for m in range(shares):
        bounds.append(bounds[-1] + (slots - m + shares - 1) // shares)
    return bounds


def slot_order(slots, shares, sort, half):
    place = iota((8, LANES), 0) * LANES + iota((8, LANES), 1) + half * 8 * LANES
    source = jnp.zeros((8, LANES), I32)
    bounds = share_bounds(slots, shares)
    for m in range(shares):
        inside = jnp.logical_and(place >= bounds[m], place < bounds[m + 1])
        source = jnp.where(inside, (place - bounds[m]) * shares + m, source)
    return jnp.where(sort, source, place)


def pick_rows(ref, n, source):
    total = jnp.zeros((8, LANES), I32)
    for t in range(ref.shape[3] // LANES):
        row = jnp.broadcast_to(ref[0, 0, n : n + 1, t * LANES : (t + 1) * LANES], (8, LANES))
        picked = jnp.take_along_axis(row, source % LANES, axis=1)
        total = jnp.where(source // LANES == t, picked, total)
    return total


def gather_partner(n, rows, cols, comps, refs, out):
    own_ref, target_ref, ids_ref, table_ref, counts_ref, halves_ref, cells_ref, picked_ref, parts_ref = refs
    slots = own_ref.shape[3]
    groups = slots // LANES
    is_ocean = lax.axis_index("comp") == comps - 1

    @pl.when(is_ocean)
    def _():
        for half in range(groups // 8):
            source = slot_order(slots, comps - 1, True, half)
            at = slice(half * 8, (half + 1) * 8)
            cells_ref[at, :] = pick_rows(own_ref, n, source)
            picked_ref[at, :] = pick_rows(ids_ref, n, source)
            out[4 * groups + half * 8 : 4 * groups + (half + 1) * 8, :] = pick_rows(target_ref, n, source).astype(F32)

    @pl.when(jnp.logical_not(is_ocean))
    def _():
        for g in range(groups):
            cut = slice(g * LANES, (g + 1) * LANES)
            cells_ref[g : g + 1, :] = own_ref[0, 0, n : n + 1, cut]
            picked_ref[g : g + 1, :] = ids_ref[0, 0, n : n + 1, cut]
            out[4 * groups + g : 4 * groups + g + 1, :] = target_ref[0, 0, n : n + 1, cut].astype(F32)

    count = jnp.broadcast_to(counts_ref[0, :, n : n + 1], (8, LANES))
    for half in range(groups // 8):
        source = slot_order(slots, comps - 1, is_ocean, half)
        ids = picked_ref[half * 8 : (half + 1) * 8, :]
        weight = jnp.zeros((8, LANES), F32)
        for t in range(table_ref.shape[0]):
            table = jnp.broadcast_to(table_ref[t : t + 1, :], (8, LANES))
            looked = jnp.take_along_axis(table, ids % LANES, axis=1)
            weight = jnp.where(ids // LANES == t, looked, weight)
        out[3 * groups + half * 8 : 3 * groups + (half + 1) * 8, :] = jnp.where(source < count, weight, 0.0)
    col_ids = packed_ids(cols)
    row_ids = iota((rows, LANES), 0)
    one = jnp.ones((), BF16)
    zero = jnp.zeros((), BF16)
    wide, subs = 2, 4

    def some(c, carry):
        for sub in range(subs):
            first = (c * subs + sub) * wide
            cells = [cells_ref[pl.ds(first + g, 1), :] for g in range(wide)]
            picks = []
            for cell in cells:
                col = spread_row(cell % cols).astype(F32).astype(BF16)
                picks.append(jnp.where(col_ids == col[None], one, zero).reshape(cols, LANES))
            picks = jnp.concatenate(picks, axis=1)
            picks = jnp.concatenate([picks, picks], axis=0)
            found = jnp.dot(halves_ref[...], picks, preferred_element_type=F32)
            for g in range(wide):
                in_row = row_ids == cells[g] // cols
                for place, v in enumerate((2, 0, 1)):
                    block = found[v * rows : (v + 1) * rows, g * LANES : (g + 1) * LANES]
                    block = jnp.where(in_row, block, 0.0).reshape(rows // 8, 8, LANES)
                    start = pl.multiple_of((place * groups + first + g) * 8, 8)
                    parts_ref[pl.ds(start, 8), :] = jnp.sum(block, axis=0)
        return carry

    lax.fori_loop(0, groups // (subs * wide), some, 0)
    weight = out[3 * groups : 4 * groups, :]
    for place in range(3):
        total = jnp.zeros((groups, LANES), F32)
        for i in range(8):
            total += parts_ref[pl.ds(place * groups * 8 + i, groups, stride=8), :]
        out[place * groups : (place + 1) * groups, :] = total * weight


def split_surface(surface_ref, halves_ref, rows, cols):
    for v in range(3):
        high, low = split_two(surface_ref[v])
        halves_ref[v * rows : (v + 1) * rows, :cols] = high
        halves_ref[v * rows : (v + 1) * rows, cols:] = low


def first_body(
    rows, cols, comps,
    state_hbm, own_hbm, target_hbm, ids_hbm, table_hbm, counts_hbm,
    slab1_ref, slab2_ref, slab3_ref,
    surface_ref, own_ref, target_ref, ids_ref, table_ref, counts_ref,
    halves_ref, cells_ref, picked_ref, parts_ref, copies,
):
    sources = (state_hbm.at[0, pl.ds(1, 3), 0], own_hbm, target_hbm, ids_hbm, table_hbm, counts_hbm)
    places = (surface_ref, own_ref, target_ref, ids_ref, table_ref, counts_ref)
    fetches = [
        pltpu.make_async_copy(source, place, copies.at[i])
        for i, (source, place) in enumerate(zip(sources, places))
    ]
    for fetch in fetches:
        fetch.start()
    for fetch in fetches:
        fetch.wait()
    split_surface(surface_ref, halves_ref, rows, cols)
    for n, out in ((3, slab3_ref), (1, slab1_ref), (2, slab2_ref)):
        refs = (own_ref, target_ref, ids_ref, table_ref, counts_ref, halves_ref, cells_ref, picked_ref, parts_ref)
        gather_partner(n, rows, cols, comps, refs, out)


def gather_scratch(rows, cols, slots):
    return [
        pltpu.VMEM((3 * rows, 2 * cols), BF16),
        pltpu.VMEM((slots // LANES, LANES), I32),
        pltpu.VMEM((slots // LANES, LANES), I32),
        pltpu.VMEM((3 * slots // LANES * 8, LANES), F32),
    ]


def first_side(model_state, slot_arrays, comps):
    rows, cols = model_state.shape[3:]
    near, slots = slot_arrays[0].shape[2:]
    table_shape = slot_arrays[3].shape
    slab = jax.ShapeDtypeStruct((CHANNELS * slots // LANES, LANES), F32)
    vmem = pl.BlockSpec(memory_space=pltpu.VMEM)
    return pl.pallas_call(
        functools.partial(first_body, rows, cols, comps),
        in_specs=[pl.BlockSpec(memory_space=pltpu.HBM)] * 6,
        out_specs=[vmem] * 3,
        out_shape=[slab] * 3,
        scratch_shapes=[pltpu.VMEM((3, rows, cols), F32)]
        + [pltpu.VMEM((1, 1, near, slots), I32)] * 3
        + [pltpu.VMEM(table_shape, F32), pltpu.VMEM((1, 1, near), I32)]
        + gather_scratch(rows, cols, slots)
        + [pltpu.SemaphoreType.DMA((6,))],
        compiler_params=pltpu.CompilerParams(vmem_limit_bytes=VMEM_BYTES),
    )(*(pltpu.with_memory_space_constraint(array, pltpu.HBM) for array in (model_state, *slot_arrays)))


def second_body(
    levels, rows, cols, comps, y_pair,
    state_ref, own_ref, target_ref, ids_ref, table_ref, counts_ref, mask_hbm,
    slab0_ref, up_ref, down_ref, high_ref, low_ref, pair_ref,
    halves_ref, cells_ref, picked_ref, parts_ref, mask_ref, copied,
):
    height = halo_rows(levels)
    parts = cols // LANES
    fetch = pltpu.make_async_copy(mask_hbm, mask_ref, copied)
    fetch.start()
    split_surface(state_ref.at[0, pl.ds(1, 3), 0], halves_ref, rows, cols)
    refs = (own_ref, target_ref, ids_ref, table_ref, counts_ref, halves_ref, cells_ref, picked_ref, parts_ref)
    gather_partner(0, rows, cols, comps, refs, slab0_ref)
    fetch.wait()
    sea = mask_ref[0].astype(F32)

    def put_row(ref, q, level, field, at):
        row = q * levels + level
        for part in range(parts):
            cut = slice(part * LANES, (part + 1) * LANES)
            ref[part * height + row : part * height + row + 1, :] = field[at : at + 1, cut]

    for ref, edge, second in ((up_ref, rows - 1, rows - 2), (down_ref, 0, 1)):
        for part in range(parts):
            ref[part * height + 4 * levels : (part + 1) * height, :] = jnp.zeros(
                (height - 4 * levels, LANES), F32
            )
        put_row(ref, 4, 0, sea, edge)
        for l in range(levels):
            put_row(ref, EDGE_P, l, state_ref.at[0, 0, l], edge)
            put_row(ref, SECOND_P, l, state_ref.at[0, 0, l], second)
            put_row(ref, EDGE_VELOCITY, l, state_ref.at[0, 1, l], edge)
            put_row(ref, EDGE_T, l, state_ref.at[0, 3, l], edge)

    lanes = iota((rows, LANES), 1)

    def columns(start, begin):
        edge = 1 if begin else 0
        total = pltpu.roll(sea[:, start : start + LANES], (4 * levels - begin - edge) % LANES, 1)
        for l in range(levels):
            pair = pltpu.roll(state_ref[0, 0, l, :, start : start + LANES], (2 * l - begin) % LANES, 1)
            total = jnp.where(lanes // 2 == l, pair, total)
            for q, v in ((EDGE_VELOCITY, 2), (EDGE_T, 3)):
                at = q * levels + l
                moved = pltpu.roll(state_ref[0, v, l, :, start : start + LANES], (at - begin - edge) % LANES, 1)
                total = jnp.where(lanes == at, moved, total)
        return total.T[:height]

    index_y = lax.axis_index("ty")
    is_ocean = lax.axis_index("comp") == comps - 1
    fold = slice(height * parts, height * (parts + 1))
    if y_pair:
        high_used = jnp.logical_or(index_y == 0, is_ocean)
        low_used = index_y > 0
    else:
        high_used = low_used = index_y >= 0

    @pl.when(high_used)
    def _():
        highest = columns(cols - LANES, LANES - 2)
        for ref in (high_ref, pair_ref, up_ref.at[fold], down_ref.at[fold]):
            ref[...] = highest

    @pl.when(jnp.logical_not(high_used))
    def _():
        for ref in (high_ref, up_ref.at[fold], down_ref.at[fold]):
            ref[...] = jnp.zeros_like(ref)

    @pl.when(low_used)
    def _():
        lowest = columns(0, 0)
        for ref in (low_ref, pair_ref):
            ref[...] = lowest

    @pl.when(jnp.logical_not(low_used))
    def _():
        low_ref[...] = jnp.zeros_like(low_ref)


def second_side(model_state, slot_arrays, sea_mask, comps, y_pair):
    levels, rows, cols = model_state.shape[2:]
    slots = slot_arrays[0].shape[3]
    height = halo_rows(levels)
    tall = height * (cols // LANES) + height
    heights = (CHANNELS * slots // LANES, tall, tall, height, height, height)
    vmem = pl.BlockSpec(memory_space=pltpu.VMEM)
    return pl.pallas_call(
        functools.partial(second_body, levels, rows, cols, comps, y_pair),
        in_specs=[vmem] * 6 + [pl.BlockSpec(memory_space=pltpu.HBM)],
        out_specs=[vmem] * len(heights),
        out_shape=[jax.ShapeDtypeStruct((h, LANES), F32) for h in heights],
        scratch_shapes=gather_scratch(rows, cols, slots)
        + [pltpu.VMEM((1, rows, cols), I32), pltpu.SemaphoreType.DMA],
        compiler_params=pltpu.CompilerParams(vmem_limit_bytes=VMEM_BYTES),
    )(model_state, *slot_arrays, pltpu.with_memory_space_constraint(sea_mask, pltpu.HBM))


def stencil_body(
    levels, rows, cols, comps, count_x, count_y,
    state_ref, mask_ref, up_ref, down_ref, south_ref, north_ref, own_ref, fold_ref,
    wave_ref, spread_ref, gains_ref, *rest,
):
    far_refs = rest[: max(count_x - 3, 0)]
    out_ref, new_surface_ref, old_surface_ref = rest[len(far_refs) : len(far_refs) + 3]
    folded_ref, rows_ref, turned_ref, pad_ref, news_ref, stores = rest[len(far_refs) + 3 :]
    height = halo_rows(levels)
    parts = cols // LANES
    index_x = lax.axis_index("tx")
    index_y = lax.axis_index("ty")
    is_ocean = lax.axis_index("comp") == comps - 1
    last_y = index_y == count_y - 1
    has_west = jnp.where(jnp.logical_or(is_ocean, index_x > 0), 1.0, 0.0)
    has_east = jnp.where(jnp.logical_or(is_ocean, index_x < count_x - 1), 1.0, 0.0)
    has_south = jnp.where(index_y > 0, 1.0, 0.0)
    has_north = jnp.where(jnp.logical_or(is_ocean, jnp.logical_not(last_y)), 1.0, 0.0)
    drag = gains_ref[0, 2]
    mask_at = 4 * levels

    def store(l):
        return pltpu.make_async_copy(news_ref.at[l], out_ref.at[0, :, l], stores.at[l])

    fold = fold_ref[pl.ds(index_x, 1), :]
    total = jnp.zeros((height, LANES), F32)
    sources = [(0, own_ref, 0), (-1, up_ref, height * parts), (1, down_ref, height * parts)]
    sources += [(shift, ref, 0) for shift, ref in zip(range(2, count_x - 1), far_refs)]
    for shift, ref, start in sources:
        at = lax.rem(index_x + shift + count_x, count_x)
        chosen = (iota((rows, rows), 0) + at * rows == fold).astype(F32)
        total += jnp.dot(
            ref[start : start + height, :], chosen,
            precision=lax.Precision.HIGHEST, preferred_element_type=F32,
        )
    folded_ref[...] = total

    line = iota((levels, LANES), 0)
    halves = jnp.zeros((levels, LANES), F32)
    for l in range(levels):
        halves = jnp.where(line == l, 0.5 * wave_ref[0, l], halves)

    def keeping(sea_values, drags):
        return jnp.where(is_ocean, sea_values, 1.0 - drags * (1.0 - sea_values))

    drags = jnp.where(line == 0, drag, 0.0)

    def by_level(ref, start, q):
        return ref[start + q * levels : start + (q + 1) * levels, :]

    for side, (ref, sign, has) in enumerate(((up_ref, 1.0, has_west), (down_ref, -1.0, has_east))):
        for p in range(parts):
            start = p * height
            kept = keeping(ref[start + mask_at : start + mask_at + 1, :], drags)
            fixed = kept * (by_level(ref, start, EDGE_VELOCITY) + sign * halves * by_level(ref, start, SECOND_P))
            inner = rows - 1 if side else 0
            own = jnp.concatenate(
                [state_ref[0, 0, l, inner : inner + 1, p * LANES : (p + 1) * LANES] for l in range(levels)], axis=0
            )
            rows_ref[side, p, 0] = has * by_level(ref, start, EDGE_P)
            rows_ref[side, p, 1] = has * by_level(ref, start, EDGE_T)
            rows_ref[side, p, 2] = has * (fixed - sign * kept * halves * own)

    even = lambda ref: ref[pl.ds(0, levels, stride=2), :]
    odd = lambda ref: ref[pl.ds(1, levels, stride=2), :]
    north = [
        jnp.where(last_y, jnp.where(is_ocean, folded, 0.0), low)
        for folded, low in (
            (odd(folded_ref), even(north_ref)),
            (even(folded_ref), odd(north_ref)),
            (-by_level(folded_ref, 0, EDGE_VELOCITY), by_level(north_ref, 0, EDGE_VELOCITY)),
            (by_level(folded_ref, 0, EDGE_T), by_level(north_ref, 0, EDGE_T)),
            (folded_ref[mask_at : mask_at + 1, :], north_ref[mask_at : mask_at + 1, :]),
        )
    ]
    south = [
        odd(south_ref), even(south_ref), by_level(south_ref, 0, EDGE_VELOCITY), by_level(south_ref, 0, EDGE_T),
        south_ref[mask_at : mask_at + 1, :],
    ]
    fill = jnp.zeros((LANES - 4 * levels, LANES), F32)
    for side, ((edge, second, velocity, tracer, sea), sign, has) in enumerate(
        ((south, 1.0, has_south), (north, -1.0, has_north))
    ):
        kept = keeping(sea, drags)
        fixed = has * kept * (velocity + sign * halves * second)
        turned_ref[side] = jnp.concatenate(
            [has * edge, has * tracer, fixed, has * kept * halves, fill], axis=0
        ).T

    sea = mask_ref[0].astype(F32)
    lane = iota((rows, LANES), 1)

    def cut(p):
        return slice(p * LANES, (p + 1) * LANES)

    def south_col(q, level):
        return pltpu.roll(turned_ref[0], lax.rem(LANES - q * levels - level, LANES), 1)

    def north_col(q, level):
        return pltpu.roll(turned_ref[1], LANES - 1 - q * levels - level, 1)

    def from_south(field, edge):
        moved = [pltpu.roll(t, 1, 1) for t in field]
        return [jnp.where(lane == 0, low, t) for low, t in zip([edge] + moved[:-1], moved)]

    def from_north(field, edge):
        moved = [pltpu.roll(t, LANES - 1, 1) for t in field]
        return [jnp.where(lane == LANES - 1, high, t) for high, t in zip(moved[1:] + [edge], moved)]

    def one_level(level, carry):
        half = 0.5 * wave_ref[0, level]
        spread = spread_ref[0, level]
        level_drag = jnp.where(level == 0, drag, 0.0)
        shift = jnp.minimum(level, 0)

        def padded(which, q, field):
            both = []
            for p in range(parts):
                pad_ref[which, p, 8 : 8 + rows, :] = field[p]
                pad_ref[which, p, 7:8, :] = rows_ref[0, p, q, pl.ds(level, 1), :]
                pad_ref[which, p, 8 + rows : 9 + rows, :] = rows_ref[1, p, q, pl.ds(level, 1), :]
                both.append((pad_ref[which, p, pl.ds(7 + shift, rows), :], pad_ref[which, p, pl.ds(9 + shift, rows), :]))
            return both

        pressure, zonal, meridional, tracer = (
            [state_ref[0, v, level, :, cut(p)] for p in range(parts)] for v in range(4)
        )
        keep = [keeping(sea[:, cut(p)], level_drag) for p in range(parts)]
        new_zonal = [
            m * (u - half * (e - w)) for m, u, (w, e) in zip(keep, zonal, padded(0, 0, pressure))
        ]
        new_meridional = [
            m * (v - half * (n - s))
            for m, v, n, s in zip(
                keep, meridional,
                from_north(pressure, north_col(0, level)), from_south(pressure, south_col(0, level)),
            )
        ]
        new_tracer = [
            t + spread * jnp.where(is_ocean, sea[:, cut(p)], 1.0) * (e + w + n + s - 4.0 * t)
            for p, t, (w, e), n, s in zip(
                range(parts), tracer, padded(1, 1, tracer),
                from_north(tracer, north_col(1, level)), from_south(tracer, south_col(1, level)),
            )
        ]
        south_v = south_col(2, level) - south_col(3, level) * pressure[0]
        north_v = north_col(2, level) + north_col(3, level) * pressure[-1]
        new_pressure = [
            q - half * (e - w + n - s)
            for q, (w, e), n, s in zip(
                pressure, padded(2, 2, new_zonal),
                from_north(new_meridional, north_v), from_south(new_meridional, south_v),
            )
        ]
        for p in range(parts):
            for v, field in enumerate((new_pressure, new_zonal, new_meridional, new_tracer)):
                news_ref[level, v, :, cut(p)] = field[p]
        store(level).start()

        @pl.when(level == 0)
        def _():
            for v in range(3):
                new_surface_ref[v] = news_ref[0, v + 1]
                old_surface_ref[v] = state_ref[0, v + 1, 0]

        return carry

    lax.fori_loop(0, levels, one_level, 0)
    for l in range(levels):
        store(l).wait()


def stencil(model_state, sea_mask, up, down, south, north, own, fars, fold_map, wave_speed, diffusivity, gains, sizes):
    comps, count_x, count_y = sizes
    levels, rows, cols = model_state.shape[2:]
    fold = fold_map.reshape(count_x, rows)
    vmem = pl.BlockSpec(memory_space=pltpu.VMEM)
    scalar = pl.BlockSpec(memory_space=pltpu.SMEM)
    anywhere = pl.BlockSpec(memory_space=pl.ANY)
    surface = jax.ShapeDtypeStruct((3, rows, cols), F32)
    return pl.pallas_call(
        functools.partial(stencil_body, levels, rows, cols, comps, count_x, count_y),
        in_specs=[vmem] * 8 + [scalar] * 3 + [vmem] * len(fars),
        out_specs=[anywhere, vmem, vmem],
        out_shape=[jax.ShapeDtypeStruct(model_state.shape, F32), surface, surface],
        scratch_shapes=[
            pltpu.VMEM(own.shape, F32),
            pltpu.VMEM((2, cols // LANES, 3, levels, LANES), F32),
            pltpu.VMEM((2, rows, LANES), F32),
            pltpu.VMEM((3, cols // LANES, rows + 16, LANES), F32),
            pltpu.VMEM((levels, 4, rows, cols), F32),
            pltpu.SemaphoreType.DMA((levels,)),
        ],
        compiler_params=pltpu.CompilerParams(vmem_limit_bytes=VMEM_BYTES),
    )(model_state, sea_mask, up, down, south, north, own, fold, wave_speed, diffusivity, gains, *fars)


def add_slots(rows, cols, groups, slab_ref, total_refs, spread_refs, column_refs, chunks, plan):
    half_rows = rows // 2
    row_ids = packed_ids(half_rows)
    col_ids = packed_ids(cols)
    lane = iota((1, LANES), 1)
    one = jnp.ones((), BF16)
    zero = jnp.zeros((), BF16)
    depth = spread_refs.shape[2] // LANES

    def build(chunk, buffer, part):
        n, first, low_slot, high_slot = plan(chunk)
        start = n * (CHANNELS * groups) + first
        for g in part:
            cells = slab_ref[pl.ds(start + 4 * groups + g, 1), :].astype(I32)
            slot = lane + (first + g) * LANES
            mine = jnp.logical_and(slot >= low_slot, slot < high_slot)
            row = cells // cols
            near_row = spread_row(jnp.where(mine, row % half_rows, -1)).astype(F32).astype(BF16)
            cut = slice(g * LANES, (g + 1) * LANES)
            for upper in range(2):
                col = jnp.where(row // half_rows == upper, cells % cols, -1)
                col = spread_row(col).astype(F32).astype(BF16)
                column_refs[buffer, upper * cols : (upper + 1) * cols, cut] = jnp.where(
                    col_ids == col[None], one, zero
                ).reshape(cols, LANES)
            in_row = row_ids == near_row[None]
            for v in range(4):
                value = spread_row(slab_ref[pl.ds(start + v * groups + g, 1), :])
                for low, part_value in enumerate(split_two(value)):
                    at = (v + 4 * low) * half_rows
                    spread_refs[buffer, at : at + half_rows, cut] = jnp.where(
                        in_row, part_value[None], zero
                    ).reshape(half_rows, LANES)

    def multiply(total_ref, buffer, part):
        total_ref[part, :] += lax.dot_general(
            spread_refs[buffer, part, :], column_refs[buffer], (((1,), (1,)), ((), ())),
            preferred_element_type=F32,
        )

    def both(total_ref, used, chunk, buffer):
        pieces = 2
        height = 8 * half_rows // pieces
        for p in range(pieces):
            multiply(total_ref, used, slice(p * height, (p + 1) * height))
            build(chunk, buffer, range(p * depth // pieces, (p + 1) * depth // pieces))

    @pl.when(chunks > 0)
    def _():
        build(0, 0, range(depth))

    done = 0
    for total_ref in total_refs:
        total_ref[...] = jnp.zeros_like(total_ref)

        def pair(c, carry, total_ref=total_ref):
            both(total_ref, 0, 2 * c + 1, 1)
            both(total_ref, 1, jnp.minimum(2 * c + 2, chunks - 1), 0)
            return carry

        step = chunks // 2 // len(total_refs)
        lax.fori_loop(done, done + step, pair, 0)
        done = done + step


def halves_added(total_ref, rows):
    return total_ref[: 2 * rows] + total_ref[2 * rows :]


def own_body(rows, cols, comps, groups, slab_ref, sent_ref, spread_refs, column_refs, total_ref):
    here = lax.axis_index("comp")
    depth = spread_refs.shape[2] // LANES
    pieces = groups // depth
    near = slab_ref.shape[0] // (CHANNELS * groups)
    bounds = share_bounds(groups * LANES, comps - 1)
    is_ocean = here == comps - 1
    beside = here == comps - 2

    def plan(chunk):
        n = jnp.where(is_ocean, chunk, chunk // pieces)
        first = jnp.where(is_ocean, groups - depth, chunk % pieces * depth)
        return n, first, jnp.where(is_ocean, bounds[comps - 2], 0), groups * LANES

    chunks = jnp.where(is_ocean, near, jnp.where(beside, near * pieces, 0))
    add_slots(rows, cols, groups, slab_ref, [total_ref], spread_refs, column_refs, chunks, plan)
    sent_ref[...] = halves_added(total_ref, rows)


def other_body(
    rows, cols, comps, groups, slab_ref, before_ref, kept_ref, sent_ref,
    spread_refs, column_refs, first_ref, second_ref,
):
    here = lax.axis_index("comp")
    depth = spread_refs.shape[2] // LANES
    pieces = groups // depth
    near = slab_ref.shape[0] // (CHANNELS * groups)
    bounds = share_bounds(groups * LANES, comps - 1)
    is_ocean = here == comps - 1
    beside = here == comps - 2
    for_two = here == comps - 3
    middle = bounds[1] // LANES // 4 * 4

    def plan(chunk):
        mine = chunk >= near
        n = jnp.where(for_two, chunk % near, chunk // pieces)
        first = jnp.where(for_two, jnp.where(mine, middle, 0), chunk % pieces * depth)
        low_slot = jnp.where(jnp.logical_and(for_two, mine), bounds[1], 0)
        high_slot = jnp.where(for_two, jnp.where(mine, bounds[2], bounds[1]), groups * LANES)
        return n, first, low_slot, high_slot

    chunks = jnp.where(here == 0, 0, near * pieces)
    totals = [first_ref, second_ref]
    add_slots(rows, cols, groups, slab_ref, totals, spread_refs, column_refs, chunks, plan)
    for start in range(0, 2 * rows, rows):
        first = first_ref[start : start + rows] + first_ref[start + 2 * rows : start + 3 * rows]
        second = second_ref[start : start + rows] + second_ref[start + 2 * rows : start + 3 * rows]
        kept_ref[start : start + rows] = jnp.where(beside, 0.0, second) + jnp.where(is_ocean, first, 0.0)
        sent = jnp.where(is_ocean, 0.0, first) + jnp.where(beside, second, 0.0)
        sent_ref[start : start + rows] = sent + before_ref[start : start + rows]


def scatter_call(body, totals, outs, rows, cols, comps, slots, *operands):
    vmem = pl.BlockSpec(memory_space=pltpu.VMEM)
    depth = 8 * LANES
    return pl.pallas_call(
        functools.partial(body, rows, cols, comps, slots // LANES),
        in_specs=[vmem] * len(operands),
        out_specs=[vmem] * outs,
        out_shape=[jax.ShapeDtypeStruct((2 * rows, 2 * cols), F32)] * outs,
        scratch_shapes=[
            pltpu.VMEM((2, 4 * rows, depth), BF16),
            pltpu.VMEM((2, 2 * cols, depth), BF16),
        ]
        + [pltpu.VMEM((4 * rows, 2 * cols), F32)] * totals,
        compiler_params=pltpu.CompilerParams(vmem_limit_bytes=VMEM_BYTES),
    )(*operands)


def finish_body(rows, cols, comps, state_ref, new_ref, old_ref, kept_ref, came_ref, mask_ref, gains_ref, out_ref, news_ref, copies):
    is_ocean = lax.axis_index("comp") == comps - 1
    half_rows = rows // 2
    saves = []
    for place, v, gain in ((0, 1, 1), (1, 2, 1), (2, 0, 0)):
        for upper in range(2):
            at = slice(upper * half_rows, (upper + 1) * half_rows)
            side = slice(upper * cols, (upper + 1) * cols)
            total, area = (
                kept_ref[k * half_rows : (k + 1) * half_rows, side] + came_ref[k * half_rows : (k + 1) * half_rows, side]
                for k in (v, 3)
            )
            tendency = jnp.where(is_ocean, mask_ref[0, at].astype(F32), 1.0)
            news_ref[place, at] = new_ref[place, at] + tendency * gains_ref[0, gain] * (total - area * old_ref[place, at])
        saves.append(pltpu.make_async_copy(news_ref.at[place], out_ref.at[0, place + 1, 0], copies.at[place]))
        saves[-1].start()
    for save in saves:
        save.wait()


def finish(state, new_surface, old_surface, kept, came, sea_mask, gains, comps):
    rows, cols = state.shape[3:]
    vmem = pl.BlockSpec(memory_space=pltpu.VMEM)
    anywhere = pl.BlockSpec(memory_space=pl.ANY)
    return pl.pallas_call(
        functools.partial(finish_body, rows, cols, comps),
        in_specs=[anywhere] + [vmem] * 5 + [pl.BlockSpec(memory_space=pltpu.SMEM)],
        out_specs=anywhere,
        out_shape=jax.ShapeDtypeStruct(state.shape, F32),
        scratch_shapes=[pltpu.VMEM((3, rows, cols), F32), pltpu.SemaphoreType.DMA((3,))],
        input_output_aliases={0: 0},
        compiler_params=pltpu.CompilerParams(vmem_limit_bytes=VMEM_BYTES),
    )(state, new_surface, old_surface, kept, came, sea_mask, gains)


def shards(
    model_state, sea_mask, wave_speed, diffusivity, surface_gains, area_table,
    own_cells, target_cells, weight_ids, pair_counts, fold_map,
):
    comps, count_x, count_y = (lax.axis_size(a) for a in ("comp", "tx", "ty"))
    positions = count_x * count_y
    rows, cols = model_state.shape[3:]
    slots = own_cells.shape[3]
    slot_arrays = (own_cells, target_cells, weight_ids, area_table.reshape(-1, LANES), pair_counts)

    def along(block, shift):
        return lax.ppermute(block, ("tx", "ty"), [(s, (s + shift) % positions) for s in range(positions)])

    slab1, slab2, slab3 = first_side(model_state, slot_arrays, comps)
    slab3 = along(slab3, 1 + count_y)
    slab1 = along(slab1, 1)
    slab2 = along(slab2, count_y)
    slab0, up, down, high, low, pair = second_side(model_state, slot_arrays, sea_mask, comps, count_y == 2)
    arrived = jnp.concatenate([slab0, slab1, slab2, slab3])
    other = lax.ppermute(arrived, "comp", [(g, g ^ 2) for g in range(comps)])

    up = along(up, count_y)
    down = along(down, -count_y)
    if count_y == 2:
        south = north = lax.ppermute(pair, "ty", [(0, 1), (1, 0)])
    else:
        south = lax.ppermute(high, "ty", [(j, j + 1) for j in range(count_y - 1)])
        north = lax.ppermute(low, "ty", [(j + 1, j) for j in range(count_y - 1)])
    fars = []
    for shift in range(2, count_x - 1):
        pairs = []
        for i in range(count_x):
            ends = [((comps - 1) * count_x + k) * count_y + count_y - 1 for k in ((i + shift) % count_x, i)]
            pairs.append(tuple(ends))
        fars.append(lax.ppermute(high, ("comp", "tx", "ty"), pairs))

    (before,) = scatter_call(own_body, 1, 1, rows, cols, comps, slots, arrived)
    other, before, up, down, south, north, *fars = lax.optimization_barrier(
        (other, before, up, down, south, north, *fars)
    )
    kept, sent = scatter_call(other_body, 2, 2, rows, cols, comps, slots, other, before)
    came = lax.ppermute(sent, "comp", [(g, g ^ 1) for g in range(comps)])
    up, down, south, north, high, kept = lax.optimization_barrier((up, down, south, north, high, kept))
    new_state, new_surface, old_surface = stencil(
        model_state, sea_mask, up, down, south, north, high, fars, fold_map,
        wave_speed, diffusivity, surface_gains, (comps, count_x, count_y),
    )
    return finish(new_state, new_surface, old_surface, kept, came, sea_mask, surface_gains, comps)


def solution(mesh):
    in_specs = (
        P("comp", None, None, "tx", "ty"),
        P("comp", "tx", "ty"),
        P("comp", None),
        P("comp", None),
        P("comp", None),
        P(),
        P("comp", ("tx", "ty"), None, None),
        P("comp", ("tx", "ty"), None, None),
        P("comp", ("tx", "ty"), None, None),
        P("comp", ("tx", "ty"), None),
        P(),
    )
    out_specs = P("comp", None, None, "tx", "ty")
    return jax.shard_map(shards, mesh=mesh, in_specs=in_specs, out_specs=out_specs, check_vma=False)
```

```python
import functools

import jax
import jax.numpy as jnp
from jax import lax
from jax.experimental import pallas as pl
from jax.experimental.pallas import tpu as pltpu
from jax.sharding import PartitionSpec as P

LANES = 128
PACKED = 16
VMEM_BYTES = 28 * 1024 * 1024
F32 = jnp.float32
BF16 = jnp.bfloat16
I32 = jnp.int32
CHANNELS = 5

EDGE_P, SECOND_P, EDGE_VELOCITY, EDGE_T, MASK = range(5)


def iota(shape, dim):
    return lax.broadcasted_iota(I32, shape, dim)


def halo_rows(levels):
    return (4 * levels + 1 + 7) // 8 * 8


def split_two(values):
    high = values.astype(BF16)
    low = (values - high.astype(F32)).astype(BF16)
    return high, low


def packed_ids(count):
    ids = iota((count, LANES), 0).astype(F32).astype(BF16)
    return ids.reshape(count // PACKED, PACKED, LANES)


def spread_row(row):
    return jnp.broadcast_to(row, (PACKED, LANES))


def share_bounds(slots, shares):
    bounds = [0]
    for m in range(shares):
        bounds.append(bounds[-1] + (slots - m + shares - 1) // shares)
    return bounds


def slot_order(slots, shares, sort, half):
    place = iota((8, LANES), 0) * LANES + iota((8, LANES), 1) + half * 8 * LANES
    source = jnp.zeros((8, LANES), I32)
    bounds = share_bounds(slots, shares)
    for m in range(shares):
        inside = jnp.logical_and(place >= bounds[m], place < bounds[m + 1])
        source = jnp.where(inside, (place - bounds[m]) * shares + m, source)
    return jnp.where(sort, source, place)


def pick_rows(ref, n, source):
    total = jnp.zeros((8, LANES), I32)
    for t in range(ref.shape[3] // LANES):
        row = jnp.broadcast_to(ref[0, 0, n : n + 1, t * LANES : (t + 1) * LANES], (8, LANES))
        picked = jnp.take_along_axis(row, source % LANES, axis=1)
        total = jnp.where(source // LANES == t, picked, total)
    return total


def gather_partner(n, rows, cols, comps, refs, out):
    own_ref, target_ref, ids_ref, table_ref, counts_ref, halves_ref, cells_ref, picked_ref, parts_ref = refs
    slots = own_ref.shape[3]
    groups = slots // LANES
    is_ocean = lax.axis_index("comp") == comps - 1

    @pl.when(is_ocean)
    def _():
        for half in range(groups // 8):
            source = slot_order(slots, comps - 1, True, half)
            at = slice(half * 8, (half + 1) * 8)
            cells_ref[at, :] = pick_rows(own_ref, n, source)
            picked_ref[at, :] = pick_rows(ids_ref, n, source)
            out[4 * groups + half * 8 : 4 * groups + (half + 1) * 8, :] = pick_rows(target_ref, n, source).astype(F32)

    @pl.when(jnp.logical_not(is_ocean))
    def _():
        for g in range(groups):
            cut = slice(g * LANES, (g + 1) * LANES)
            cells_ref[g : g + 1, :] = own_ref[0, 0, n : n + 1, cut]
            picked_ref[g : g + 1, :] = ids_ref[0, 0, n : n + 1, cut]
            out[4 * groups + g : 4 * groups + g + 1, :] = target_ref[0, 0, n : n + 1, cut].astype(F32)

    count = jnp.broadcast_to(counts_ref[0, :, n : n + 1], (8, LANES))
    for half in range(groups // 8):
        source = slot_order(slots, comps - 1, is_ocean, half)
        ids = picked_ref[half * 8 : (half + 1) * 8, :]
        weight = jnp.zeros((8, LANES), F32)
        for t in range(table_ref.shape[0]):
            table = jnp.broadcast_to(table_ref[t : t + 1, :], (8, LANES))
            looked = jnp.take_along_axis(table, ids % LANES, axis=1)
            weight = jnp.where(ids // LANES == t, looked, weight)
        out[3 * groups + half * 8 : 3 * groups + (half + 1) * 8, :] = jnp.where(source < count, weight, 0.0)
    col_ids = packed_ids(cols)
    row_ids = iota((rows, LANES), 0)
    one = jnp.ones((), BF16)
    zero = jnp.zeros((), BF16)
    wide, subs = 2, 4

    def some(c, carry):
        for sub in range(subs):
            first = (c * subs + sub) * wide
            cells = [cells_ref[pl.ds(first + g, 1), :] for g in range(wide)]
            picks = []
            for cell in cells:
                col = spread_row(cell % cols).astype(F32).astype(BF16)
                picks.append(jnp.where(col_ids == col[None], one, zero).reshape(cols, LANES))
            picks = jnp.concatenate(picks, axis=1)
            if halves_ref.shape[1] > cols:
                picks = jnp.concatenate([picks, picks], axis=0)
                found = jnp.dot(halves_ref[...], picks, preferred_element_type=F32)
            else:
                found = jnp.dot(halves_ref[...], picks, preferred_element_type=F32)
                found = found[: 3 * rows] + found[3 * rows :]
            for g in range(wide):
                in_row = row_ids == cells[g] // cols
                for place, v in enumerate((2, 0, 1)):
                    block = found[v * rows : (v + 1) * rows, g * LANES : (g + 1) * LANES]
                    block = jnp.where(in_row, block, 0.0).reshape(rows // 8, 8, LANES)
                    start = pl.multiple_of((place * groups + first + g) * 8, 8)
                    parts_ref[pl.ds(start, 8), :] = jnp.sum(block, axis=0)
        return carry

    lax.fori_loop(0, groups // (subs * wide), some, 0)
    weight = out[3 * groups : 4 * groups, :]
    for place in range(3):
        total = jnp.zeros((groups, LANES), F32)
        for i in range(8):
            total += parts_ref[pl.ds(place * groups * 8 + i, groups, stride=8), :]
        out[place * groups : (place + 1) * groups, :] = total * weight


def split_surface(surface_ref, halves_ref, rows, cols):
    for v in range(3):
        high, low = split_two(surface_ref[v])
        if halves_ref.shape[1] > cols:
            halves_ref[v * rows : (v + 1) * rows, :cols] = high
            halves_ref[v * rows : (v + 1) * rows, cols:] = low
        else:
            halves_ref[v * rows : (v + 1) * rows, :] = high
            halves_ref[(v + 3) * rows : (v + 4) * rows, :] = low


def first_body(
    rows, cols, comps,
    state_hbm, own_hbm, target_hbm, ids_hbm, table_hbm, counts_hbm,
    slab1_ref, slab2_ref, slab3_ref,
    surface_ref, own_ref, target_ref, ids_ref, table_ref, counts_ref,
    halves_ref, cells_ref, picked_ref, parts_ref, copies,
):
    sources = (state_hbm.at[0, pl.ds(1, 3), 0], own_hbm, target_hbm, ids_hbm, table_hbm, counts_hbm)
    places = (surface_ref, own_ref, target_ref, ids_ref, table_ref, counts_ref)
    fetches = [
        pltpu.make_async_copy(source, place, copies.at[i])
        for i, (source, place) in enumerate(zip(sources, places))
    ]
    for fetch in fetches:
        fetch.start()
    for fetch in fetches:
        fetch.wait()
    split_surface(surface_ref, halves_ref, rows, cols)
    for n, out in ((3, slab3_ref), (1, slab1_ref), (2, slab2_ref)):
        refs = (own_ref, target_ref, ids_ref, table_ref, counts_ref, halves_ref, cells_ref, picked_ref, parts_ref)
        gather_partner(n, rows, cols, comps, refs, out)


def gather_scratch(rows, cols, slots, stacked):
    return [
        pltpu.VMEM((6 * rows, cols) if stacked else (3 * rows, 2 * cols), BF16),
        pltpu.VMEM((slots // LANES, LANES), I32),
        pltpu.VMEM((slots // LANES, LANES), I32),
        pltpu.VMEM((3 * slots // LANES * 8, LANES), F32),
    ]


def first_side(model_state, slot_arrays, comps):
    rows, cols = model_state.shape[3:]
    near, slots = slot_arrays[0].shape[2:]
    table_shape = slot_arrays[3].shape
    slab = jax.ShapeDtypeStruct((CHANNELS * slots // LANES, LANES), F32)
    vmem = pl.BlockSpec(memory_space=pltpu.VMEM)
    return pl.pallas_call(
        functools.partial(first_body, rows, cols, comps),
        in_specs=[pl.BlockSpec(memory_space=pltpu.HBM)] * 6,
        out_specs=[vmem] * 3,
        out_shape=[slab] * 3,
        scratch_shapes=[pltpu.VMEM((3, rows, cols), F32)]
        + [pltpu.VMEM((1, 1, near, slots), I32)] * 3
        + [pltpu.VMEM(table_shape, F32), pltpu.VMEM((1, 1, near), I32)]
        + gather_scratch(rows, cols, slots, True)
        + [pltpu.SemaphoreType.DMA((6,))],
        compiler_params=pltpu.CompilerParams(vmem_limit_bytes=VMEM_BYTES),
    )(*(pltpu.with_memory_space_constraint(array, pltpu.HBM) for array in (model_state, *slot_arrays)))


def second_body(
    levels, rows, cols, comps, y_pair,
    state_ref, own_ref, target_ref, ids_ref, table_ref, counts_ref, mask_hbm,
    slab0_ref, up_ref, down_ref, high_ref, low_ref, pair_ref,
    halves_ref, cells_ref, picked_ref, parts_ref, mask_ref, copied,
):
    height = halo_rows(levels)
    parts = cols // LANES
    fetch = pltpu.make_async_copy(mask_hbm, mask_ref, copied)
    fetch.start()
    split_surface(state_ref.at[0, pl.ds(1, 3), 0], halves_ref, rows, cols)
    refs = (own_ref, target_ref, ids_ref, table_ref, counts_ref, halves_ref, cells_ref, picked_ref, parts_ref)
    gather_partner(0, rows, cols, comps, refs, slab0_ref)
    fetch.wait()
    sea = mask_ref[0].astype(F32)

    def put_row(ref, q, level, field, at):
        row = q * levels + level
        for part in range(parts):
            cut = slice(part * LANES, (part + 1) * LANES)
            ref[part * height + row : part * height + row + 1, :] = field[at : at + 1, cut]

    for ref, edge, second in ((up_ref, rows - 1, rows - 2), (down_ref, 0, 1)):
        for part in range(parts):
            ref[part * height + 4 * levels : (part + 1) * height, :] = jnp.zeros(
                (height - 4 * levels, LANES), F32
            )
        put_row(ref, 4, 0, sea, edge)
        for l in range(levels):
            put_row(ref, EDGE_P, l, state_ref.at[0, 0, l], edge)
            put_row(ref, SECOND_P, l, state_ref.at[0, 0, l], second)
            put_row(ref, EDGE_VELOCITY, l, state_ref.at[0, 1, l], edge)
            put_row(ref, EDGE_T, l, state_ref.at[0, 3, l], edge)

    lanes = iota((rows, LANES), 1)

    def columns(start, begin):
        edge = 1 if begin else 0
        total = pltpu.roll(sea[:, start : start + LANES], (4 * levels - begin - edge) % LANES, 1)
        for l in range(levels):
            pair = pltpu.roll(state_ref[0, 0, l, :, start : start + LANES], (2 * l - begin) % LANES, 1)
            total = jnp.where(lanes // 2 == l, pair, total)
            for q, v in ((EDGE_VELOCITY, 2), (EDGE_T, 3)):
                at = q * levels + l
                moved = pltpu.roll(state_ref[0, v, l, :, start : start + LANES], (at - begin - edge) % LANES, 1)
                total = jnp.where(lanes == at, moved, total)
        return total.T[:height]

    index_y = lax.axis_index("ty")
    is_ocean = lax.axis_index("comp") == comps - 1
    fold = slice(height * parts, height * (parts + 1))
    if y_pair:
        high_used = jnp.logical_or(index_y == 0, is_ocean)
        low_used = index_y > 0
    else:
        high_used = low_used = index_y >= 0

    @pl.when(high_used)
    def _():
        highest = columns(cols - LANES, LANES - 2)
        for ref in (high_ref, pair_ref, up_ref.at[fold], down_ref.at[fold]):
            ref[...] = highest

    @pl.when(jnp.logical_not(high_used))
    def _():
        for ref in (high_ref, up_ref.at[fold], down_ref.at[fold]):
            ref[...] = jnp.zeros_like(ref)

    @pl.when(low_used)
    def _():
        lowest = columns(0, 0)
        for ref in (low_ref, pair_ref):
            ref[...] = lowest

    @pl.when(jnp.logical_not(low_used))
    def _():
        low_ref[...] = jnp.zeros_like(low_ref)


def second_side(model_state, slot_arrays, sea_mask, comps, y_pair):
    levels, rows, cols = model_state.shape[2:]
    slots = slot_arrays[0].shape[3]
    height = halo_rows(levels)
    tall = height * (cols // LANES) + height
    heights = (CHANNELS * slots // LANES, tall, tall, height, height, height)
    vmem = pl.BlockSpec(memory_space=pltpu.VMEM)
    return pl.pallas_call(
        functools.partial(second_body, levels, rows, cols, comps, y_pair),
        in_specs=[vmem] * 6 + [pl.BlockSpec(memory_space=pltpu.HBM)],
        out_specs=[vmem] * len(heights),
        out_shape=[jax.ShapeDtypeStruct((h, LANES), F32) for h in heights],
        scratch_shapes=gather_scratch(rows, cols, slots, False)
        + [pltpu.VMEM((1, rows, cols), I32), pltpu.SemaphoreType.DMA],
        compiler_params=pltpu.CompilerParams(vmem_limit_bytes=VMEM_BYTES),
    )(model_state, *slot_arrays, pltpu.with_memory_space_constraint(sea_mask, pltpu.HBM))


def stencil_body(
    levels, rows, cols, comps, count_x, count_y,
    state_ref, mask_ref, up_ref, down_ref, south_ref, north_ref, own_ref, fold_ref,
    wave_ref, spread_ref, gains_ref, *rest,
):
    far_refs = rest[: max(count_x - 3, 0)]
    out_ref, new_surface_ref, old_surface_ref = rest[len(far_refs) : len(far_refs) + 3]
    folded_ref, rows_ref, turned_ref, pad_ref, news_ref, stores = rest[len(far_refs) + 3 :]
    height = halo_rows(levels)
    parts = cols // LANES
    index_x = lax.axis_index("tx")
    index_y = lax.axis_index("ty")
    is_ocean = lax.axis_index("comp") == comps - 1
    last_y = index_y == count_y - 1
    has_west = jnp.where(jnp.logical_or(is_ocean, index_x > 0), 1.0, 0.0)
    has_east = jnp.where(jnp.logical_or(is_ocean, index_x < count_x - 1), 1.0, 0.0)
    has_south = jnp.where(index_y > 0, 1.0, 0.0)
    has_north = jnp.where(jnp.logical_or(is_ocean, jnp.logical_not(last_y)), 1.0, 0.0)
    drag = gains_ref[0, 2]
    mask_at = 4 * levels

    def store(l, v):
        return pltpu.make_async_copy(news_ref.at[l, v], out_ref.at[0, v, l], stores.at[l, v])

    fold = fold_ref[pl.ds(index_x, 1), :]
    total = jnp.zeros((height, LANES), F32)
    sources = [(0, own_ref, 0), (-1, up_ref, height * parts), (1, down_ref, height * parts)]
    sources += [(shift, ref, 0) for shift, ref in zip(range(2, count_x - 1), far_refs)]
    for shift, ref, start in sources:
        at = lax.rem(index_x + shift + count_x, count_x)
        chosen = (iota((rows, rows), 0) + at * rows == fold).astype(F32)
        total += jnp.dot(
            ref[start : start + height, :], chosen,
            precision=lax.Precision.HIGHEST, preferred_element_type=F32,
        )
    folded_ref[...] = total

    line = iota((levels, LANES), 0)
    halves = jnp.zeros((levels, LANES), F32)
    for l in range(levels):
        halves = jnp.where(line == l, 0.5 * wave_ref[0, l], halves)

    def keeping(sea_values, drags):
        return jnp.where(is_ocean, sea_values, 1.0 - drags * (1.0 - sea_values))

    drags = jnp.where(line == 0, drag, 0.0)

    def by_level(ref, start, q):
        return ref[start + q * levels : start + (q + 1) * levels, :]

    for side, (ref, sign, has) in enumerate(((up_ref, 1.0, has_west), (down_ref, -1.0, has_east))):
        for p in range(parts):
            start = p * height
            kept = keeping(ref[start + mask_at : start + mask_at + 1, :], drags)
            fixed = kept * (by_level(ref, start, EDGE_VELOCITY) + sign * halves * by_level(ref, start, SECOND_P))
            inner = rows - 1 if side else 0
            own = jnp.concatenate(
                [state_ref[0, 0, l, inner : inner + 1, p * LANES : (p + 1) * LANES] for l in range(levels)], axis=0
            )
            rows_ref[side, p, 0] = has * by_level(ref, start, EDGE_P)
            rows_ref[side, p, 1] = has * by_level(ref, start, EDGE_T)
            rows_ref[side, p, 2] = has * (fixed - sign * kept * halves * own)

    even = lambda ref: ref[pl.ds(0, levels, stride=2), :]
    odd = lambda ref: ref[pl.ds(1, levels, stride=2), :]
    north = [
        jnp.where(last_y, jnp.where(is_ocean, folded, 0.0), low)
        for folded, low in (
            (odd(folded_ref), even(north_ref)),
            (even(folded_ref), odd(north_ref)),
            (-by_level(folded_ref, 0, EDGE_VELOCITY), by_level(north_ref, 0, EDGE_VELOCITY)),
            (by_level(folded_ref, 0, EDGE_T), by_level(north_ref, 0, EDGE_T)),
            (folded_ref[mask_at : mask_at + 1, :], north_ref[mask_at : mask_at + 1, :]),
        )
    ]
    south = [
        odd(south_ref), even(south_ref), by_level(south_ref, 0, EDGE_VELOCITY), by_level(south_ref, 0, EDGE_T),
        south_ref[mask_at : mask_at + 1, :],
    ]
    fill = jnp.zeros((LANES - 4 * levels, LANES), F32)
    for side, ((edge, second, velocity, tracer, sea), sign, has) in enumerate(
        ((south, 1.0, has_south), (north, -1.0, has_north))
    ):
        kept = keeping(sea, drags)
        fixed = has * kept * (velocity + sign * halves * second)
        turned_ref[side] = jnp.concatenate(
            [has * edge, has * tracer, fixed, has * kept * halves, fill], axis=0
        ).T

    sea = mask_ref[0].astype(F32)
    lane = iota((rows, LANES), 1)

    def cut(p):
        return slice(p * LANES, (p + 1) * LANES)

    def south_col(q, level):
        return pltpu.roll(turned_ref[0], lax.rem(LANES - q * levels - level, LANES), 1)

    def north_col(q, level):
        return pltpu.roll(turned_ref[1], LANES - 1 - q * levels - level, 1)

    def from_south(field, edge):
        moved = [pltpu.roll(t, 1, 1) for t in field]
        return [jnp.where(lane == 0, low, t) for low, t in zip([edge] + moved[:-1], moved)]

    def from_north(field, edge):
        moved = [pltpu.roll(t, LANES - 1, 1) for t in field]
        return [jnp.where(lane == LANES - 1, high, t) for high, t in zip(moved[1:] + [edge], moved)]

    def one_level(level, carry):
        half = 0.5 * wave_ref[0, level]
        spread = spread_ref[0, level]
        level_drag = jnp.where(level == 0, drag, 0.0)
        shift = jnp.minimum(level, 0)

        def padded(which, q, field):
            both = []
            for p in range(parts):
                pad_ref[which, p, 8 : 8 + rows, :] = field[p]
                pad_ref[which, p, 7:8, :] = rows_ref[0, p, q, pl.ds(level, 1), :]
                pad_ref[which, p, 8 + rows : 9 + rows, :] = rows_ref[1, p, q, pl.ds(level, 1), :]
                both.append((pad_ref[which, p, pl.ds(7 + shift, rows), :], pad_ref[which, p, pl.ds(9 + shift, rows), :]))
            return both

        pressure, zonal, meridional, tracer = (
            [state_ref[0, v, level, :, cut(p)] for p in range(parts)] for v in range(4)
        )
        keep = [keeping(sea[:, cut(p)], level_drag) for p in range(parts)]
        new_zonal = [
            m * (u - half * (e - w)) for m, u, (w, e) in zip(keep, zonal, padded(0, 0, pressure))
        ]
        new_meridional = [
            m * (v - half * (n - s))
            for m, v, n, s in zip(
                keep, meridional,
                from_north(pressure, north_col(0, level)), from_south(pressure, south_col(0, level)),
            )
        ]
        new_tracer = [
            t + spread * jnp.where(is_ocean, sea[:, cut(p)], 1.0) * (e + w + n + s - 4.0 * t)
            for p, t, (w, e), n, s in zip(
                range(parts), tracer, padded(1, 1, tracer),
                from_north(tracer, north_col(1, level)), from_south(tracer, south_col(1, level)),
            )
        ]
        south_v = south_col(2, level) - south_col(3, level) * pressure[0]
        north_v = north_col(2, level) + north_col(3, level) * pressure[-1]
        new_pressure = [
            q - half * (e - w + n - s)
            for q, (w, e), n, s in zip(
                pressure, padded(2, 2, new_zonal),
                from_north(new_meridional, north_v), from_south(new_meridional, south_v),
            )
        ]
        for p in range(parts):
            for v, field in enumerate((new_pressure, new_zonal, new_meridional, new_tracer)):
                news_ref[level, v, :, cut(p)] = field[p]
        for v in range(4):
            store(level, v).start()

        @pl.when(level == 0)
        def _():
            for v in range(3):
                new_surface_ref[v] = news_ref[0, v + 1]
                old_surface_ref[v] = state_ref[0, v + 1, 0]

        return carry

    lax.fori_loop(0, levels, one_level, 0)
    for l in range(levels):
        for v in range(4):
            store(l, v).wait()


def stencil(model_state, sea_mask, up, down, south, north, own, fars, fold_map, wave_speed, diffusivity, gains, sizes):
    comps, count_x, count_y = sizes
    levels, rows, cols = model_state.shape[2:]
    fold = fold_map.reshape(count_x, rows)
    vmem = pl.BlockSpec(memory_space=pltpu.VMEM)
    scalar = pl.BlockSpec(memory_space=pltpu.SMEM)
    anywhere = pl.BlockSpec(memory_space=pl.ANY)
    surface = jax.ShapeDtypeStruct((3, rows, cols), F32)
    return pl.pallas_call(
        functools.partial(stencil_body, levels, rows, cols, comps, count_x, count_y),
        in_specs=[vmem] * 8 + [scalar] * 3 + [vmem] * len(fars),
        out_specs=[anywhere, vmem, vmem],
        out_shape=[jax.ShapeDtypeStruct(model_state.shape, F32), surface, surface],
        scratch_shapes=[
            pltpu.VMEM(own.shape, F32),
            pltpu.VMEM((2, cols // LANES, 3, levels, LANES), F32),
            pltpu.VMEM((2, rows, LANES), F32),
            pltpu.VMEM((3, cols // LANES, rows + 16, LANES), F32),
            pltpu.VMEM((levels, 4, rows, cols), F32),
            pltpu.SemaphoreType.DMA((levels, 4)),
        ],
        compiler_params=pltpu.CompilerParams(vmem_limit_bytes=VMEM_BYTES),
    )(model_state, sea_mask, up, down, south, north, own, fold, wave_speed, diffusivity, gains, *fars)


def add_slots(rows, cols, groups, slab_ref, total_refs, spread_refs, column_refs, chunks, plan, build_first):
    row_ids = packed_ids(rows)
    col_ids = packed_ids(cols)
    lane = iota((1, LANES), 1)
    one = jnp.ones((), BF16)
    zero = jnp.zeros((), BF16)
    depth = spread_refs[0].shape[1] // LANES

    def build(chunk, buffer, part):
        n, first, low_slot, high_slot = plan(chunk)
        start = n * (CHANNELS * groups) + first
        for g in part:
            cells = slab_ref[pl.ds(start + 4 * groups + g, 1), :].astype(I32)
            slot = lane + (first + g) * LANES
            mine = jnp.logical_and(slot >= low_slot, slot < high_slot)
            row = spread_row(jnp.where(mine, cells // cols, -1)).astype(F32).astype(BF16)
            col = spread_row(cells % cols).astype(F32).astype(BF16)
            cut = slice(g * LANES, (g + 1) * LANES)
            column_refs[buffer][:, cut] = jnp.where(col_ids == col[None], one, zero).reshape(cols, LANES)
            in_row = row_ids == row[None]
            for v in range(4):
                value = spread_row(slab_ref[pl.ds(start + v * groups + g, 1), :])
                high, low = split_two(value)
                spread_refs[buffer][v * rows : (v + 1) * rows, cut] = jnp.where(
                    in_row, high[None], zero
                ).reshape(rows, LANES)
                spread_refs[buffer][(v + 4) * rows : (v + 5) * rows, cut] = jnp.where(
                    in_row, low[None], zero
                ).reshape(rows, LANES)

    def multiply(total_ref, buffer):
        total_ref[...] += lax.dot_general(
            spread_refs[buffer][...], column_refs[buffer][...], (((1,), (1,)), ((), ())),
            preferred_element_type=F32,
        )

    def both(total_ref, used, chunk, buffer):
        if build_first:
            build(chunk, buffer, range(depth))
            multiply(total_ref, used)
        else:
            multiply(total_ref, used)
            build(chunk, buffer, range(depth))

    @pl.when(chunks > 0)
    def _():
        build(0, 0, range(depth))

    done = 0
    for total_ref in total_refs:
        total_ref[...] = jnp.zeros_like(total_ref)

        def pair(c, carry, total_ref=total_ref):
            both(total_ref, 0, 2 * c + 1, 1)
            both(total_ref, 1, jnp.minimum(2 * c + 2, chunks - 1), 0)
            return carry

        step = chunks // 2 // len(total_refs)
        lax.fori_loop(done, done + step, pair, 0)
        done = done + step


def halves_added(total_ref, rows):
    return total_ref[: 4 * rows] + total_ref[4 * rows :]


def own_body(rows, cols, comps, groups, slab_ref, sent_ref, spread0, spread1, column0, column1, total_ref):
    spread_refs, column_refs = (spread0, spread1), (column0, column1)
    here = lax.axis_index("comp")
    depth = spread_refs[0].shape[1] // LANES
    pieces = groups // depth
    near = slab_ref.shape[0] // (CHANNELS * groups)
    bounds = share_bounds(groups * LANES, comps - 1)
    is_ocean = here == comps - 1
    beside = here == comps - 2

    def plan(chunk):
        n = jnp.where(is_ocean, chunk, chunk // pieces)
        first = jnp.where(is_ocean, groups - depth, chunk % pieces * depth)
        return n, first, jnp.where(is_ocean, bounds[comps - 2], 0), groups * LANES

    chunks = jnp.where(is_ocean, near, jnp.where(beside, near * pieces, 0))
    add_slots(rows, cols, groups, slab_ref, [total_ref], spread_refs, column_refs, chunks, plan, False)
    sent_ref[...] = halves_added(total_ref, rows)


def other_body(
    rows, cols, comps, groups, slab_ref, before_ref, kept_ref, sent_ref,
    spread0, spread1, column0, column1, first_ref, second_ref,
):
    spread_refs, column_refs = (spread0, spread1), (column0, column1)
    here = lax.axis_index("comp")
    depth = spread_refs[0].shape[1] // LANES
    pieces = groups // depth
    near = slab_ref.shape[0] // (CHANNELS * groups)
    bounds = share_bounds(groups * LANES, comps - 1)
    is_ocean = here == comps - 1
    beside = here == comps - 2
    for_two = here == comps - 3
    middle = bounds[1] // LANES // 4 * 4

    def plan(chunk):
        mine = chunk >= near
        n = jnp.where(for_two, chunk % near, chunk // pieces)
        first = jnp.where(for_two, jnp.where(mine, middle, 0), chunk % pieces * depth)
        low_slot = jnp.where(jnp.logical_and(for_two, mine), bounds[1], 0)
        high_slot = jnp.where(for_two, jnp.where(mine, bounds[2], bounds[1]), groups * LANES)
        return n, first, low_slot, high_slot

    chunks = jnp.where(here == 0, 0, near * pieces)
    totals = [first_ref, second_ref]
    add_slots(rows, cols, groups, slab_ref, totals, spread_refs, column_refs, chunks, plan, True)
    for start in range(0, 4 * rows, rows):
        first = first_ref[start : start + rows] + first_ref[start + 4 * rows : start + 5 * rows]
        second = second_ref[start : start + rows] + second_ref[start + 4 * rows : start + 5 * rows]
        kept_ref[start : start + rows] = jnp.where(beside, 0.0, second) + jnp.where(is_ocean, first, 0.0)
        sent = jnp.where(is_ocean, 0.0, first) + jnp.where(beside, second, 0.0)
        sent_ref[start : start + rows] = sent + before_ref[start : start + rows]


def scatter_call(body, totals, outs, rows, cols, comps, slots, *operands):
    vmem = pl.BlockSpec(memory_space=pltpu.VMEM)
    depth = 8 * LANES
    return pl.pallas_call(
        functools.partial(body, rows, cols, comps, slots // LANES),
        in_specs=[vmem] * len(operands),
        out_specs=[vmem] * outs,
        out_shape=[jax.ShapeDtypeStruct((4 * rows, cols), F32)] * outs,
        scratch_shapes=[
            pltpu.VMEM((8 * rows, depth), BF16),
            pltpu.VMEM((8 * rows, depth), BF16),
            pltpu.VMEM((cols, depth), BF16),
            pltpu.VMEM((cols, depth), BF16),
        ]
        + [pltpu.VMEM((8 * rows, cols), F32)] * totals,
        compiler_params=pltpu.CompilerParams(vmem_limit_bytes=VMEM_BYTES),
    )(*operands)


def finish_body(rows, comps, state_ref, new_ref, old_ref, kept_ref, came_ref, mask_ref, gains_ref, out_ref, news_ref, copies):
    is_ocean = lax.axis_index("comp") == comps - 1
    tendency = jnp.where(is_ocean, mask_ref[0].astype(F32), 1.0)
    sums = [kept_ref[v * rows : (v + 1) * rows, :] + came_ref[v * rows : (v + 1) * rows, :] for v in range(4)]
    saves = []
    for v, total, gain in ((0, sums[1], 1), (1, sums[2], 1), (2, sums[0], 0)):
        news_ref[v] = new_ref[v] + tendency * gains_ref[0, gain] * (total - sums[3] * old_ref[v])
        saves.append(pltpu.make_async_copy(news_ref.at[v], out_ref.at[0, v + 1, 0], copies.at[v]))
        saves[-1].start()
    for save in saves:
        save.wait()


def finish(state, new_surface, old_surface, kept, came, sea_mask, gains, comps):
    rows, cols = state.shape[3:]
    vmem = pl.BlockSpec(memory_space=pltpu.VMEM)
    anywhere = pl.BlockSpec(memory_space=pl.ANY)
    return pl.pallas_call(
        functools.partial(finish_body, rows, comps),
        in_specs=[anywhere] + [vmem] * 5 + [pl.BlockSpec(memory_space=pltpu.SMEM)],
        out_specs=anywhere,
        out_shape=jax.ShapeDtypeStruct(state.shape, F32),
        scratch_shapes=[pltpu.VMEM((3, rows, cols), F32), pltpu.SemaphoreType.DMA((3,))],
        input_output_aliases={0: 0},
        compiler_params=pltpu.CompilerParams(vmem_limit_bytes=VMEM_BYTES),
    )(state, new_surface, old_surface, kept, came, sea_mask, gains)


def shards(
    model_state, sea_mask, wave_speed, diffusivity, surface_gains, area_table,
    own_cells, target_cells, weight_ids, pair_counts, fold_map,
):
    comps, count_x, count_y = (lax.axis_size(a) for a in ("comp", "tx", "ty"))
    positions = count_x * count_y
    rows, cols = model_state.shape[3:]
    slots = own_cells.shape[3]
    slot_arrays = (own_cells, target_cells, weight_ids, area_table.reshape(-1, LANES), pair_counts)

    def along(block, shift):
        return lax.ppermute(block, ("tx", "ty"), [(s, (s + shift) % positions) for s in range(positions)])

    slab1, slab2, slab3 = first_side(model_state, slot_arrays, comps)
    slab3 = along(slab3, 1 + count_y)
    slab1 = along(slab1, 1)
    slab2 = along(slab2, count_y)
    slab0, up, down, high, low, pair = second_side(model_state, slot_arrays, sea_mask, comps, count_y == 2)
    arrived = jnp.concatenate([slab0, slab1, slab2, slab3])
    other = lax.ppermute(arrived, "comp", [(g, g ^ 2) for g in range(comps)])

    up = along(up, count_y)
    down = along(down, -count_y)
    if count_y == 2:
        south = north = lax.ppermute(pair, "ty", [(0, 1), (1, 0)])
    else:
        south = lax.ppermute(high, "ty", [(j, j + 1) for j in range(count_y - 1)])
        north = lax.ppermute(low, "ty", [(j + 1, j) for j in range(count_y - 1)])
    fars = []
    for shift in range(2, count_x - 1):
        pairs = []
        for i in range(count_x):
            ends = [((comps - 1) * count_x + k) * count_y + count_y - 1 for k in ((i + shift) % count_x, i)]
            pairs.append(tuple(ends))
        fars.append(lax.ppermute(high, ("comp", "tx", "ty"), pairs))

    (before,) = scatter_call(own_body, 1, 1, rows, cols, comps, slots, arrived)
    other, before, up, down, south, north, *fars = lax.optimization_barrier(
        (other, before, up, down, south, north, *fars)
    )
    kept, sent = scatter_call(other_body, 2, 2, rows, cols, comps, slots, other, before)
    came = lax.ppermute(sent, "comp", [(g, g ^ 1) for g in range(comps)])
    up, down, south, north, high, kept = lax.optimization_barrier((up, down, south, north, high, kept))
    new_state, new_surface, old_surface = stencil(
        model_state, sea_mask, up, down, south, north, high, fars, fold_map,
        wave_speed, diffusivity, surface_gains, (comps, count_x, count_y),
    )
    return finish(new_state, new_surface, old_surface, kept, came, sea_mask, surface_gains, comps)


def solution(mesh):
    in_specs = (
        P("comp", None, None, "tx", "ty"),
        P("comp", "tx", "ty"),
        P("comp", None),
        P("comp", None),
        P("comp", None),
        P(),
        P("comp", ("tx", "ty"), None, None),
        P("comp", ("tx", "ty"), None, None),
        P("comp", ("tx", "ty"), None, None),
        P("comp", ("tx", "ty"), None),
        P(),
    )
    out_specs = P("comp", None, None, "tx", "ty")
    return jax.shard_map(shards, mesh=mesh, in_specs=in_specs, out_specs=out_specs, check_vma=False)
```

```python
import functools

import jax
import jax.numpy as jnp
from jax import lax
from jax.experimental import pallas as pl
from jax.experimental.pallas import tpu as pltpu
from jax.sharding import PartitionSpec as P

LANES = 128
DEPTH = 8
PACKED = 16
VMEM_BYTES = 28 * 1024 * 1024
F32 = jnp.float32
BF16 = jnp.bfloat16
I32 = jnp.int32
CHANNELS = 5

EDGE_P, SECOND_P, EDGE_VELOCITY, EDGE_T, MASK = range(5)


def iota(shape, dim):
    return lax.broadcasted_iota(I32, shape, dim)


def halo_rows(levels):
    return (4 * levels + 1 + 7) // 8 * 8


def split_two(values):
    high = values.astype(BF16)
    low = (values - high.astype(F32)).astype(BF16)
    return high, low


def packed_ids(count):
    ids = iota((count, LANES), 0).astype(F32).astype(BF16)
    return ids.reshape(count // PACKED, PACKED, LANES)


def spread_row(row):
    return jnp.broadcast_to(row, (PACKED, LANES))


def share_bounds(slots, shares):
    bounds = [0]
    for m in range(shares):
        bounds.append(bounds[-1] + (slots - m + shares - 1) // shares)
    return bounds


def slot_order(slots, shares, sort, half):
    place = iota((8, LANES), 0) * LANES + iota((8, LANES), 1) + half * 8 * LANES
    source = jnp.zeros((8, LANES), I32)
    bounds = share_bounds(slots, shares)
    for m in range(shares):
        inside = jnp.logical_and(place >= bounds[m], place < bounds[m + 1])
        source = jnp.where(inside, (place - bounds[m]) * shares + m, source)
    return jnp.where(sort, source, place)


def pick_rows(ref, n, source):
    total = jnp.zeros((8, LANES), I32)
    for t in range(ref.shape[3] // LANES):
        row = jnp.broadcast_to(ref[0, 0, n : n + 1, t * LANES : (t + 1) * LANES], (8, LANES))
        picked = jnp.take_along_axis(row, source % LANES, axis=1)
        total = jnp.where(source // LANES == t, picked, total)
    return total


def gather_partner(n, rows, cols, comps, refs, out):
    own_ref, target_ref, ids_ref, table_ref, counts_ref, halves_ref, cells_ref, picked_ref, parts_ref = refs
    slots = own_ref.shape[3]
    groups = slots // LANES
    is_ocean = lax.axis_index("comp") == comps - 1

    @pl.when(is_ocean)
    def _():
        for half in range(groups // 8):
            source = slot_order(slots, comps - 1, True, half)
            at = slice(half * 8, (half + 1) * 8)
            cells_ref[at, :] = pick_rows(own_ref, n, source)
            picked_ref[at, :] = pick_rows(ids_ref, n, source)
            out[4 * groups + half * 8 : 4 * groups + (half + 1) * 8, :] = pick_rows(target_ref, n, source).astype(F32)

    @pl.when(jnp.logical_not(is_ocean))
    def _():
        for g in range(groups):
            cut = slice(g * LANES, (g + 1) * LANES)
            cells_ref[g : g + 1, :] = own_ref[0, 0, n : n + 1, cut]
            picked_ref[g : g + 1, :] = ids_ref[0, 0, n : n + 1, cut]
            out[4 * groups + g : 4 * groups + g + 1, :] = target_ref[0, 0, n : n + 1, cut].astype(F32)

    count = jnp.broadcast_to(counts_ref[0, :, n : n + 1], (8, LANES))
    for half in range(groups // 8):
        source = slot_order(slots, comps - 1, is_ocean, half)
        ids = picked_ref[half * 8 : (half + 1) * 8, :]
        weight = jnp.zeros((8, LANES), F32)
        for t in range(table_ref.shape[0]):
            table = jnp.broadcast_to(table_ref[t : t + 1, :], (8, LANES))
            looked = jnp.take_along_axis(table, ids % LANES, axis=1)
            weight = jnp.where(ids // LANES == t, looked, weight)
        out[3 * groups + half * 8 : 3 * groups + (half + 1) * 8, :] = jnp.where(source < count, weight, 0.0)
    col_ids = packed_ids(cols)
    row_ids = iota((rows, LANES), 0)
    one = jnp.ones((), BF16)
    zero = jnp.zeros((), BF16)
    wide, subs = 2, 4

    def some(c, carry):
        for sub in range(subs):
            first = (c * subs + sub) * wide
            cells = [cells_ref[pl.ds(first + g, 1), :] for g in range(wide)]
            picks = []
            for cell in cells:
                col = spread_row(cell % cols).astype(F32).astype(BF16)
                picks.append(jnp.where(col_ids == col[None], one, zero).reshape(cols, LANES))
            picks = jnp.concatenate(picks, axis=1)
            if halves_ref.shape[1] > cols:
                picks = jnp.concatenate([picks, picks], axis=0)
                found = jnp.dot(halves_ref[...], picks, preferred_element_type=F32)
            else:
                found = jnp.dot(halves_ref[...], picks, preferred_element_type=F32)
                found = found[: 3 * rows] + found[3 * rows :]
            for g in range(wide):
                in_row = row_ids == cells[g] // cols
                for place, v in enumerate((2, 0, 1)):
                    block = found[v * rows : (v + 1) * rows, g * LANES : (g + 1) * LANES]
                    block = jnp.where(in_row, block, 0.0).reshape(rows // 8, 8, LANES)
                    start = pl.multiple_of((place * groups + first + g) * 8, 8)
                    parts_ref[pl.ds(start, 8), :] = jnp.sum(block, axis=0)
        return carry

    lax.fori_loop(0, groups // (subs * wide), some, 0)
    weight = out[3 * groups : 4 * groups, :]
    for place in range(3):
        total = jnp.zeros((groups, LANES), F32)
        for i in range(8):
            total += parts_ref[pl.ds(place * groups * 8 + i, groups, stride=8), :]
        out[place * groups : (place + 1) * groups, :] = total * weight


def split_surface(surface_ref, halves_ref, rows, cols):
    for v in range(3):
        high, low = split_two(surface_ref[v])
        if halves_ref.shape[1] > cols:
            halves_ref[v * rows : (v + 1) * rows, :cols] = high
            halves_ref[v * rows : (v + 1) * rows, cols:] = low
        else:
            halves_ref[v * rows : (v + 1) * rows, :] = high
            halves_ref[(v + 3) * rows : (v + 4) * rows, :] = low


def put_rows(ref, start, levels, cols, fields, sea, edge, second):
    height = halo_rows(levels)
    for p in range(cols // LANES):
        cut = slice(p * LANES, (p + 1) * LANES)
        base = start + p * height
        ref[base + 4 * levels : base + height, :] = jnp.zeros((height - 4 * levels, LANES), F32)
        ref[base + 4 * levels : base + 4 * levels + 1, :] = sea[edge : edge + 1, cut].astype(F32)
        for q, v, at in ((EDGE_P, 0, edge), (SECOND_P, 0, second), (EDGE_VELOCITY, 1, edge), (EDGE_T, 3, edge)):
            for l in range(levels):
                row = base + q * levels + l
                ref[row : row + 1, :] = fields(v, l)[at : at + 1, cut]


def turned_columns(levels, rows, fields, sea, begin):
    edge = 1 if begin else 0
    lanes = iota((rows, LANES), 1)
    total = pltpu.roll(sea.astype(F32), (4 * levels - begin - edge) % LANES, 1)
    for l in range(levels):
        total = jnp.where(lanes // 2 == l, pltpu.roll(fields(0, l), (2 * l - begin) % LANES, 1), total)
        for q, v in ((EDGE_VELOCITY, 2), (EDGE_T, 3)):
            at = q * levels + l
            moved = pltpu.roll(fields(v, l), (at - begin - edge) % LANES, 1)
            total = jnp.where(lanes == at, moved, total)
    return total.T[: halo_rows(levels)]


def first_body(
    levels, rows, cols, comps,
    state_hbm, own_hbm, target_hbm, ids_hbm, table_hbm, counts_hbm, mask_hbm,
    slab1_ref, up_ref, slab3_ref, fold_ref,
    surface_ref, own_ref, target_ref, ids_ref, table_ref, counts_ref, edge_ref, sea_edge_ref, mask_ref, columns_ref,
    halves_ref, cells_ref, picked_ref, parts_ref, copies, column_copies,
):
    sources = (
        state_hbm.at[0, pl.ds(1, 3), 0], own_hbm, target_hbm, ids_hbm, table_hbm, counts_hbm,
        state_hbm.at[0, :, :, pl.ds(rows - 8, 8), :], mask_hbm.at[0, pl.ds(rows - 8, 8), :],
    )
    places = (surface_ref, own_ref, target_ref, ids_ref, table_ref, counts_ref, edge_ref, sea_edge_ref)
    fetches = [
        pltpu.make_async_copy(source, place, copies.at[i])
        for i, (source, place) in enumerate(zip(sources, places))
    ]
    outer = pl.ds(cols - LANES, LANES)
    for_fold = [
        pltpu.make_async_copy(state_hbm.at[0, v, :, :, outer], columns_ref.at[i], column_copies.at[i])
        for i, v in enumerate((0, 2, 3))
    ] + [pltpu.make_async_copy(mask_hbm.at[0, :, outer], mask_ref, column_copies.at[3])]
    northern = lax.axis_index("ty") == lax.axis_size("ty") - 1
    folds = jnp.logical_and(lax.axis_index("comp") == comps - 1, northern)
    for fetch in fetches:
        fetch.start()

    @pl.when(folds)
    def _():
        for fetch in for_fold:
            fetch.start()

    for fetch in fetches:
        fetch.wait()
    slab_rows = slab1_ref.shape[0]
    tall = halo_rows(levels) * (cols // LANES)
    put_rows(up_ref, slab_rows, levels, cols, lambda v, l: edge_ref.at[v, l], sea_edge_ref, 7, 6)

    @pl.when(folds)
    def _():
        for fetch in for_fold:
            fetch.wait()
        places = {0: 0, 2: 1, 3: 2}
        fold_ref[...] = turned_columns(
            levels, rows, lambda v, l: columns_ref[places[v], l], mask_ref[...], LANES - 2
        )

    @pl.when(jnp.logical_not(folds))
    def _():
        fold_ref[...] = jnp.zeros_like(fold_ref)

    up_ref[slab_rows + tall :, :] = fold_ref[...]
    slab3_ref[slab_rows:, :] = fold_ref[...]
    split_surface(surface_ref, halves_ref, rows, cols)
    refs = (own_ref, target_ref, ids_ref, table_ref, counts_ref, halves_ref, cells_ref, picked_ref, parts_ref)
    for n, out in ((3, slab3_ref), (1, slab1_ref), (2, up_ref)):
        gather_partner(n, rows, cols, comps, refs, out)


def gather_scratch(rows, cols, slots, stacked):
    return [
        pltpu.VMEM((6 * rows, cols) if stacked else (3 * rows, 2 * cols), BF16),
        pltpu.VMEM((slots // LANES, LANES), I32),
        pltpu.VMEM((slots // LANES, LANES), I32),
        pltpu.VMEM((3 * slots // LANES * 8, LANES), F32),
    ]


def first_side(model_state, slot_arrays, sea_mask, comps):
    levels, rows, cols = model_state.shape[2:]
    near, slots = slot_arrays[0].shape[2:]
    table_shape = slot_arrays[3].shape
    slab = CHANNELS * slots // LANES
    height = halo_rows(levels)
    heights = (slab, slab + height * (cols // LANES) + height, slab + height, height)
    vmem = pl.BlockSpec(memory_space=pltpu.VMEM)
    arrays = (model_state, *slot_arrays, sea_mask)
    return pl.pallas_call(
        functools.partial(first_body, levels, rows, cols, comps),
        in_specs=[pl.BlockSpec(memory_space=pltpu.HBM)] * len(arrays),
        out_specs=[vmem] * len(heights),
        out_shape=[jax.ShapeDtypeStruct((h, LANES), F32) for h in heights],
        scratch_shapes=[pltpu.VMEM((3, rows, cols), F32)]
        + [pltpu.VMEM((1, 1, near, slots), I32)] * 3
        + [pltpu.VMEM(table_shape, F32), pltpu.VMEM((1, 1, near), I32)]
        + [
            pltpu.VMEM((4, levels, 8, cols), F32),
            pltpu.VMEM((8, cols), I32),
            pltpu.VMEM((rows, LANES), I32),
            pltpu.VMEM((3, levels, rows, LANES), F32),
        ]
        + gather_scratch(rows, cols, slots, True)
        + [pltpu.SemaphoreType.DMA((8,)), pltpu.SemaphoreType.DMA((4,))],
        compiler_params=pltpu.CompilerParams(vmem_limit_bytes=VMEM_BYTES),
    )(*(pltpu.with_memory_space_constraint(array, pltpu.HBM) for array in arrays))


def second_body(
    levels, rows, cols, comps, y_pair,
    state_ref, own_ref, target_ref, ids_ref, table_ref, counts_ref, fold_ref, mask_hbm,
    slab0_ref, down_ref, high_ref, low_ref, pair_ref,
    halves_ref, cells_ref, picked_ref, parts_ref, mask_ref, copied,
):
    fetch = pltpu.make_async_copy(mask_hbm, mask_ref, copied)
    fetch.start()
    split_surface(state_ref.at[0, pl.ds(1, 3), 0], halves_ref, rows, cols)
    refs = (own_ref, target_ref, ids_ref, table_ref, counts_ref, halves_ref, cells_ref, picked_ref, parts_ref)
    gather_partner(0, rows, cols, comps, refs, slab0_ref)
    fetch.wait()
    put_rows(down_ref, 0, levels, cols, lambda v, l: state_ref.at[0, v, l], mask_ref.at[0], 0, 1)
    down_ref[halo_rows(levels) * (cols // LANES) :, :] = fold_ref[...]
    index_y = lax.axis_index("ty")
    high_used = index_y == 0 if y_pair else index_y >= 0
    low_used = index_y > 0 if y_pair else index_y >= 0

    def columns(start, begin):
        cut = slice(start, start + LANES)
        return turned_columns(levels, rows, lambda v, l: state_ref[0, v, l, :, cut], mask_ref[0, :, cut], begin)

    @pl.when(high_used)
    def _():
        highest = columns(cols - LANES, LANES - 2)
        high_ref[...] = highest
        pair_ref[...] = highest

    @pl.when(jnp.logical_not(high_used))
    def _():
        high_ref[...] = jnp.zeros_like(high_ref)

    @pl.when(low_used)
    def _():
        lowest = columns(0, 0)
        low_ref[...] = lowest
        pair_ref[...] = lowest

    @pl.when(jnp.logical_not(low_used))
    def _():
        low_ref[...] = jnp.zeros_like(low_ref)


def second_side(model_state, slot_arrays, fold, sea_mask, comps, y_pair):
    levels, rows, cols = model_state.shape[2:]
    slots = slot_arrays[0].shape[3]
    height = halo_rows(levels)
    heights = (CHANNELS * slots // LANES, height * (cols // LANES) + height, height, height, height)
    vmem = pl.BlockSpec(memory_space=pltpu.VMEM)
    return pl.pallas_call(
        functools.partial(second_body, levels, rows, cols, comps, y_pair),
        in_specs=[vmem] * 7 + [pl.BlockSpec(memory_space=pltpu.HBM)],
        out_specs=[vmem] * len(heights),
        out_shape=[jax.ShapeDtypeStruct((h, LANES), F32) for h in heights],
        scratch_shapes=gather_scratch(rows, cols, slots, False)
        + [pltpu.VMEM((1, rows, cols), I32), pltpu.SemaphoreType.DMA],
        compiler_params=pltpu.CompilerParams(vmem_limit_bytes=VMEM_BYTES),
    )(model_state, *slot_arrays, fold, pltpu.with_memory_space_constraint(sea_mask, pltpu.HBM))


def stencil_body(
    levels, rows, cols, comps, count_x, count_y,
    state_ref, mask_ref, up_ref, down_ref, south_ref, north_ref, own_ref, fold_ref,
    wave_ref, spread_ref, gains_ref, *rest,
):
    far_refs = rest[: max(count_x - 3, 0)]
    out_ref, new_surface_ref, old_surface_ref = rest[len(far_refs) : len(far_refs) + 3]
    folded_ref, rows_ref, turned_ref, pad_ref, news_ref, stores = rest[len(far_refs) + 3 :]
    height = halo_rows(levels)
    parts = cols // LANES
    index_x = lax.axis_index("tx")
    index_y = lax.axis_index("ty")
    is_ocean = lax.axis_index("comp") == comps - 1
    last_y = index_y == count_y - 1
    has_west = jnp.where(jnp.logical_or(is_ocean, index_x > 0), 1.0, 0.0)
    has_east = jnp.where(jnp.logical_or(is_ocean, index_x < count_x - 1), 1.0, 0.0)
    has_south = jnp.where(index_y > 0, 1.0, 0.0)
    has_north = jnp.where(jnp.logical_or(is_ocean, jnp.logical_not(last_y)), 1.0, 0.0)
    drag = gains_ref[0, 2]
    mask_at = 4 * levels

    def store(l, v):
        return pltpu.make_async_copy(news_ref.at[l, v], out_ref.at[0, v, l], stores.at[l, v])

    fold = fold_ref[pl.ds(index_x, 1), :]
    total = jnp.zeros((height, LANES), F32)
    up_start = up_ref.shape[0] - height * (parts + 1)
    sources = [(0, own_ref, 0), (-1, up_ref, up_start + height * parts), (1, down_ref, height * parts)]
    sources += [(shift, ref, 0) for shift, ref in zip(range(2, count_x - 1), far_refs)]
    for shift, ref, start in sources:
        at = lax.rem(index_x + shift + count_x, count_x)
        chosen = (iota((rows, rows), 0) + at * rows == fold).astype(F32)
        total += jnp.dot(
            ref[start : start + height, :], chosen,
            precision=lax.Precision.HIGHEST, preferred_element_type=F32,
        )
    folded_ref[...] = total

    line = iota((levels, LANES), 0)
    halves = jnp.zeros((levels, LANES), F32)
    for l in range(levels):
        halves = jnp.where(line == l, 0.5 * wave_ref[0, l], halves)

    def keeping(sea_values, drags):
        return jnp.where(is_ocean, sea_values, 1.0 - drags * (1.0 - sea_values))

    drags = jnp.where(line == 0, drag, 0.0)

    def by_level(ref, start, q):
        return ref[start + q * levels : start + (q + 1) * levels, :]

    for side, (ref, begin, sign, has) in enumerate(
        ((up_ref, up_start, 1.0, has_west), (down_ref, 0, -1.0, has_east))
    ):
        for p in range(parts):
            start = begin + p * height
            kept = keeping(ref[start + mask_at : start + mask_at + 1, :], drags)
            fixed = kept * (by_level(ref, start, EDGE_VELOCITY) + sign * halves * by_level(ref, start, SECOND_P))
            inner = rows - 1 if side else 0
            own = jnp.concatenate(
                [state_ref[0, 0, l, inner : inner + 1, p * LANES : (p + 1) * LANES] for l in range(levels)], axis=0
            )
            rows_ref[side, p, 0] = has * by_level(ref, start, EDGE_P)
            rows_ref[side, p, 1] = has * by_level(ref, start, EDGE_T)
            rows_ref[side, p, 2] = has * (fixed - sign * kept * halves * own)

    even = lambda ref: ref[pl.ds(0, levels, stride=2), :]
    odd = lambda ref: ref[pl.ds(1, levels, stride=2), :]
    north = [
        jnp.where(last_y, jnp.where(is_ocean, folded, 0.0), low)
        for folded, low in (
            (odd(folded_ref), even(north_ref)),
            (even(folded_ref), odd(north_ref)),
            (-by_level(folded_ref, 0, EDGE_VELOCITY), by_level(north_ref, 0, EDGE_VELOCITY)),
            (by_level(folded_ref, 0, EDGE_T), by_level(north_ref, 0, EDGE_T)),
            (folded_ref[mask_at : mask_at + 1, :], north_ref[mask_at : mask_at + 1, :]),
        )
    ]
    south = [
        odd(south_ref), even(south_ref), by_level(south_ref, 0, EDGE_VELOCITY), by_level(south_ref, 0, EDGE_T),
        south_ref[mask_at : mask_at + 1, :],
    ]
    fill = jnp.zeros((LANES - 4 * levels, LANES), F32)
    for side, ((edge, second, velocity, tracer, sea), sign, has) in enumerate(
        ((south, 1.0, has_south), (north, -1.0, has_north))
    ):
        kept = keeping(sea, drags)
        fixed = has * kept * (velocity + sign * halves * second)
        turned_ref[side] = jnp.concatenate(
            [has * edge, has * tracer, fixed, has * kept * halves, fill], axis=0
        ).T

    sea = mask_ref[0].astype(F32)
    lane = iota((rows, LANES), 1)

    def cut(p):
        return slice(p * LANES, (p + 1) * LANES)

    def south_col(q, level):
        return pltpu.roll(turned_ref[0], lax.rem(LANES - q * levels - level, LANES), 1)

    def north_col(q, level):
        return pltpu.roll(turned_ref[1], LANES - 1 - q * levels - level, 1)

    def from_south(field, edge):
        moved = [pltpu.roll(t, 1, 1) for t in field]
        return [jnp.where(lane == 0, low, t) for low, t in zip([edge] + moved[:-1], moved)]

    def from_north(field, edge):
        moved = [pltpu.roll(t, LANES - 1, 1) for t in field]
        return [jnp.where(lane == LANES - 1, high, t) for high, t in zip(moved[1:] + [edge], moved)]

    def one_level(level, carry):
        half = 0.5 * wave_ref[0, level]
        spread = spread_ref[0, level]
        level_drag = jnp.where(level == 0, drag, 0.0)
        shift = jnp.minimum(level, 0)

        def padded(which, q, field):
            both = []
            for p in range(parts):
                pad_ref[which, p, 8 : 8 + rows, :] = field[p]
                pad_ref[which, p, 7:8, :] = rows_ref[0, p, q, pl.ds(level, 1), :]
                pad_ref[which, p, 8 + rows : 9 + rows, :] = rows_ref[1, p, q, pl.ds(level, 1), :]
                both.append((pad_ref[which, p, pl.ds(7 + shift, rows), :], pad_ref[which, p, pl.ds(9 + shift, rows), :]))
            return both

        pressure, zonal, meridional, tracer = (
            [state_ref[0, v, level, :, cut(p)] for p in range(parts)] for v in range(4)
        )
        keep = [keeping(sea[:, cut(p)], level_drag) for p in range(parts)]
        new_zonal = [
            m * (u - half * (e - w)) for m, u, (w, e) in zip(keep, zonal, padded(0, 0, pressure))
        ]
        new_meridional = [
            m * (v - half * (n - s))
            for m, v, n, s in zip(
                keep, meridional,
                from_north(pressure, north_col(0, level)), from_south(pressure, south_col(0, level)),
            )
        ]
        new_tracer = [
            t + spread * jnp.where(is_ocean, sea[:, cut(p)], 1.0) * (e + w + n + s - 4.0 * t)
            for p, t, (w, e), n, s in zip(
                range(parts), tracer, padded(1, 1, tracer),
                from_north(tracer, north_col(1, level)), from_south(tracer, south_col(1, level)),
            )
        ]
        south_v = south_col(2, level) - south_col(3, level) * pressure[0]
        north_v = north_col(2, level) + north_col(3, level) * pressure[-1]
        new_pressure = [
            q - half * (e - w + n - s)
            for q, (w, e), n, s in zip(
                pressure, padded(2, 2, new_zonal),
                from_north(new_meridional, north_v), from_south(new_meridional, south_v),
            )
        ]
        for p in range(parts):
            for v, field in enumerate((new_pressure, new_zonal, new_meridional, new_tracer)):
                news_ref[level, v, :, cut(p)] = field[p]
        for v in range(4):
            store(level, v).start()

        @pl.when(level == 0)
        def _():
            for v in range(3):
                new_surface_ref[v] = news_ref[0, v + 1]
                old_surface_ref[v] = state_ref[0, v + 1, 0]

        return carry

    lax.fori_loop(0, levels, one_level, 0)
    for l in range(levels):
        for v in range(4):
            store(l, v).wait()


def stencil(model_state, sea_mask, up, down, south, north, own, fars, fold_map, wave_speed, diffusivity, gains, sizes):
    comps, count_x, count_y = sizes
    levels, rows, cols = model_state.shape[2:]
    fold = fold_map.reshape(count_x, rows)
    vmem = pl.BlockSpec(memory_space=pltpu.VMEM)
    scalar = pl.BlockSpec(memory_space=pltpu.SMEM)
    anywhere = pl.BlockSpec(memory_space=pl.ANY)
    surface = jax.ShapeDtypeStruct((3, rows, cols), F32)
    return pl.pallas_call(
        functools.partial(stencil_body, levels, rows, cols, comps, count_x, count_y),
        in_specs=[vmem] * 8 + [scalar] * 3 + [vmem] * len(fars),
        out_specs=[anywhere, vmem, vmem],
        out_shape=[jax.ShapeDtypeStruct(model_state.shape, F32), surface, surface],
        scratch_shapes=[
            pltpu.VMEM(own.shape, F32),
            pltpu.VMEM((2, cols // LANES, 3, levels, LANES), F32),
            pltpu.VMEM((2, rows, LANES), F32),
            pltpu.VMEM((3, cols // LANES, rows + 16, LANES), F32),
            pltpu.VMEM((levels, 4, rows, cols), F32),
            pltpu.SemaphoreType.DMA((levels, 4)),
        ],
        compiler_params=pltpu.CompilerParams(vmem_limit_bytes=VMEM_BYTES),
    )(model_state, sea_mask, up, down, south, north, own, fold, wave_speed, diffusivity, gains, *fars)


def add_slots(rows, cols, groups, slab_ref, total_refs, chunks, plan, block):
    row_ids = packed_ids(rows)
    col_ids = packed_ids(cols)
    lane = iota((1, LANES), 1)
    one = jnp.ones((), BF16)
    zero = jnp.zeros((), BF16)

    def one_chunk(total_ref, chunk):
        n, first, low_slot, high_slot = plan(chunk)
        start = n * (CHANNELS * groups) + first
        for begin in range(0, DEPTH, block):
            columns, spreads = [], []
            for g in range(begin, begin + block):
                cells = slab_ref[pl.ds(start + 4 * groups + g, 1), :].astype(I32)
                slot = lane + (first + g) * LANES
                mine = jnp.logical_and(slot >= low_slot, slot < high_slot)
                row = spread_row(jnp.where(mine, cells // cols, -1)).astype(F32).astype(BF16)
                col = spread_row(cells % cols).astype(F32).astype(BF16)
                columns.append(jnp.where(col_ids == col[None], one, zero).reshape(cols, LANES))
                in_row = row_ids == row[None]
                highs, lows = [], []
                for v in range(4):
                    value = spread_row(slab_ref[pl.ds(start + v * groups + g, 1), :])
                    high, low = split_two(value)
                    highs.append(jnp.where(in_row, high[None], zero).reshape(rows, LANES))
                    lows.append(jnp.where(in_row, low[None], zero).reshape(rows, LANES))
                spreads.append(jnp.concatenate(highs + lows, axis=0))
            total_ref[...] += lax.dot_general(
                jnp.concatenate(spreads, axis=1), jnp.concatenate(columns, axis=1), (((1,), (1,)), ((), ())),
                preferred_element_type=F32,
            )

    done = 0
    for total_ref in total_refs:
        total_ref[...] = jnp.zeros_like(total_ref)

        def some(c, carry, total_ref=total_ref):
            one_chunk(total_ref, c)
            return carry

        step = chunks // len(total_refs)
        lax.fori_loop(done, done + step, some, 0)
        done = done + step


def halves_added(total_ref, rows):
    return total_ref[: 4 * rows] + total_ref[4 * rows :]


def own_body(rows, cols, comps, groups, slab_ref, sent_ref, total_ref):
    here = lax.axis_index("comp")
    pieces = groups // DEPTH
    near = slab_ref.shape[0] // (CHANNELS * groups)
    bounds = share_bounds(groups * LANES, comps - 1)
    is_ocean = here == comps - 1
    beside = here == comps - 2

    def plan(chunk):
        n = jnp.where(is_ocean, chunk, chunk // pieces)
        first = jnp.where(is_ocean, groups - DEPTH, chunk % pieces * DEPTH)
        return n, first, jnp.where(is_ocean, bounds[comps - 2], 0), groups * LANES

    chunks = jnp.where(is_ocean, near, jnp.where(beside, near * pieces, 0))
    add_slots(rows, cols, groups, slab_ref, [total_ref], chunks, plan, 4)
    sent_ref[...] = halves_added(total_ref, rows)


def other_body(
    rows, cols, comps, groups, slab_ref, before_ref, kept_ref, sent_ref,
    first_ref, second_ref,
):
    here = lax.axis_index("comp")
    pieces = groups // DEPTH
    near = slab_ref.shape[0] // (CHANNELS * groups)
    bounds = share_bounds(groups * LANES, comps - 1)
    is_ocean = here == comps - 1
    beside = here == comps - 2
    for_two = here == comps - 3
    middle = bounds[1] // LANES // 4 * 4

    def plan(chunk):
        mine = chunk >= near
        n = jnp.where(for_two, chunk % near, chunk // pieces)
        first = jnp.where(for_two, jnp.where(mine, middle, 0), chunk % pieces * DEPTH)
        low_slot = jnp.where(jnp.logical_and(for_two, mine), bounds[1], 0)
        high_slot = jnp.where(for_two, jnp.where(mine, bounds[2], bounds[1]), groups * LANES)
        return n, first, low_slot, high_slot

    chunks = jnp.where(here == 0, 0, near * pieces)
    totals = [first_ref, second_ref]
    add_slots(rows, cols, groups, slab_ref, totals, chunks, plan, 2)
    for start in range(0, 4 * rows, rows):
        first = first_ref[start : start + rows] + first_ref[start + 4 * rows : start + 5 * rows]
        second = second_ref[start : start + rows] + second_ref[start + 4 * rows : start + 5 * rows]
        kept_ref[start : start + rows] = jnp.where(beside, 0.0, second) + jnp.where(is_ocean, first, 0.0)
        sent = jnp.where(is_ocean, 0.0, first) + jnp.where(beside, second, 0.0)
        sent_ref[start : start + rows] = sent + before_ref[start : start + rows]


def scatter_call(body, totals, outs, rows, cols, comps, slots, *operands):
    vmem = pl.BlockSpec(memory_space=pltpu.VMEM)
    return pl.pallas_call(
        functools.partial(body, rows, cols, comps, slots // LANES),
        in_specs=[vmem] * len(operands),
        out_specs=[vmem] * outs,
        out_shape=[jax.ShapeDtypeStruct((4 * rows, cols), F32)] * outs,
        scratch_shapes=[pltpu.VMEM((8 * rows, cols), F32)] * totals,
        compiler_params=pltpu.CompilerParams(vmem_limit_bytes=VMEM_BYTES),
    )(*operands)


def finish_body(rows, comps, state_ref, new_ref, old_ref, kept_ref, came_ref, mask_ref, gains_ref, out_ref, news_ref, copies):
    is_ocean = lax.axis_index("comp") == comps - 1
    tendency = jnp.where(is_ocean, mask_ref[0].astype(F32), 1.0)
    sums = [kept_ref[v * rows : (v + 1) * rows, :] + came_ref[v * rows : (v + 1) * rows, :] for v in range(4)]
    saves = []
    for v, total, gain in ((0, sums[1], 1), (1, sums[2], 1), (2, sums[0], 0)):
        news_ref[v] = new_ref[v] + tendency * gains_ref[0, gain] * (total - sums[3] * old_ref[v])
        saves.append(pltpu.make_async_copy(news_ref.at[v], out_ref.at[0, v + 1, 0], copies.at[v]))
        saves[-1].start()
    for save in saves:
        save.wait()


def finish(state, new_surface, old_surface, kept, came, sea_mask, gains, comps):
    rows, cols = state.shape[3:]
    vmem = pl.BlockSpec(memory_space=pltpu.VMEM)
    anywhere = pl.BlockSpec(memory_space=pl.ANY)
    return pl.pallas_call(
        functools.partial(finish_body, rows, comps),
        in_specs=[anywhere] + [vmem] * 5 + [pl.BlockSpec(memory_space=pltpu.SMEM)],
        out_specs=anywhere,
        out_shape=jax.ShapeDtypeStruct(state.shape, F32),
        scratch_shapes=[pltpu.VMEM((3, rows, cols), F32), pltpu.SemaphoreType.DMA((3,))],
        input_output_aliases={0: 0},
        compiler_params=pltpu.CompilerParams(vmem_limit_bytes=VMEM_BYTES),
    )(state, new_surface, old_surface, kept, came, sea_mask, gains)


def shards(
    model_state, sea_mask, wave_speed, diffusivity, surface_gains, area_table,
    own_cells, target_cells, weight_ids, pair_counts, fold_map,
):
    comps, count_x, count_y = (lax.axis_size(a) for a in ("comp", "tx", "ty"))
    positions = count_x * count_y
    rows, cols = model_state.shape[3:]
    slots = own_cells.shape[3]
    slot_arrays = (own_cells, target_cells, weight_ids, area_table.reshape(-1, LANES), pair_counts)

    def along(block, shift):
        return lax.ppermute(block, ("tx", "ty"), [(s, (s + shift) % positions) for s in range(positions)])

    y_pair = count_y == 2
    slab_rows = CHANNELS * slots // LANES
    slab1, up, slab3, fold = first_side(model_state, slot_arrays, sea_mask, comps)
    slab3 = along(slab3, 1 + count_y)
    slab1 = along(slab1, 1)
    up = along(up, count_y)
    slab0, down, high, low, pair = second_side(model_state, slot_arrays, fold, sea_mask, comps, y_pair)
    arrived = jnp.concatenate([slab0, slab1, up[:slab_rows], slab3[:slab_rows]])
    other = lax.ppermute(arrived, "comp", [(g, g ^ 2) for g in range(comps)])

    down = along(down, -count_y)
    fars = []
    if y_pair and count_x == 4:
        pair = lax.ppermute(jnp.concatenate([pair, slab3[slab_rows:]]), "ty", [(0, 1), (1, 0)])
        south = north = pair[: fold.shape[0]]
        fars.append(pair[fold.shape[0] :])
    else:
        south = lax.ppermute(high, "ty", [(j, j + 1) for j in range(count_y - 1)])
        north = lax.ppermute(low, "ty", [(j + 1, j) for j in range(count_y - 1)])
        for shift in range(2, count_x - 1):
            pairs = []
            for i in range(count_x):
                ends = [((comps - 1) * count_x + k) * count_y + count_y - 1 for k in ((i + shift) % count_x, i)]
                pairs.append(tuple(ends))
            fars.append(lax.ppermute(fold, ("comp", "tx", "ty"), pairs))

    (before,) = scatter_call(own_body, 1, 1, rows, cols, comps, slots, arrived)
    other, before, up, down, south, north, *fars = lax.optimization_barrier(
        (other, before, up, down, south, north, *fars)
    )
    kept, sent = scatter_call(other_body, 2, 2, rows, cols, comps, slots, other, before)
    came = lax.ppermute(sent, "comp", [(g, g ^ 1) for g in range(comps)])
    up, down, south, north, fold, kept = lax.optimization_barrier((up, down, south, north, fold, kept))
    new_state, new_surface, old_surface = stencil(
        model_state, sea_mask, up, down, south, north, fold, fars, fold_map,
        wave_speed, diffusivity, surface_gains, (comps, count_x, count_y),
    )
    return finish(new_state, new_surface, old_surface, kept, came, sea_mask, surface_gains, comps)


def solution(mesh):
    in_specs = (
        P("comp", None, None, "tx", "ty"),
        P("comp", "tx", "ty"),
        P("comp", None),
        P("comp", None),
        P("comp", None),
        P(),
        P("comp", ("tx", "ty"), None, None),
        P("comp", ("tx", "ty"), None, None),
        P("comp", ("tx", "ty"), None, None),
        P("comp", ("tx", "ty"), None),
        P(),
    )
    out_specs = P("comp", None, None, "tx", "ty")
    return jax.shard_map(shards, mesh=mesh, in_specs=in_specs, out_specs=out_specs, check_vma=False)
```

```python
import functools

import jax
import jax.numpy as jnp
from jax import lax
from jax.experimental import pallas as pl
from jax.experimental.pallas import tpu as pltpu
from jax.sharding import PartitionSpec as P

LANES = 128
DEPTH = 8
PACKED = 16
VMEM_BYTES = 28 * 1024 * 1024
F32 = jnp.float32
BF16 = jnp.bfloat16
I32 = jnp.int32
CHANNELS = 5

EDGE_P, SECOND_P, EDGE_VELOCITY, EDGE_T, MASK = range(5)


def iota(shape, dim):
    return lax.broadcasted_iota(I32, shape, dim)


def halo_rows(levels):
    return (4 * levels + 1 + 7) // 8 * 8


def split_two(values):
    high = values.astype(BF16)
    low = (values - high.astype(F32)).astype(BF16)
    return high, low


def packed_ids(count):
    ids = iota((count, LANES), 0).astype(F32).astype(BF16)
    return ids.reshape(count // PACKED, PACKED, LANES)


def spread_row(row):
    return jnp.broadcast_to(row, (PACKED, LANES))


def share_bounds(slots, shares):
    bounds = [0]
    for m in range(shares):
        bounds.append(bounds[-1] + (slots - m + shares - 1) // shares)
    return bounds


def slot_order(slots, shares, sort, half):
    place = iota((8, LANES), 0) * LANES + iota((8, LANES), 1) + half * 8 * LANES
    source = jnp.zeros((8, LANES), I32)
    bounds = share_bounds(slots, shares)
    for m in range(shares):
        inside = jnp.logical_and(place >= bounds[m], place < bounds[m + 1])
        source = jnp.where(inside, (place - bounds[m]) * shares + m, source)
    return jnp.where(sort, source, place)


def pick_rows(ref, n, source):
    total = jnp.zeros((8, LANES), I32)
    for t in range(ref.shape[3] // LANES):
        row = jnp.broadcast_to(ref[0, 0, n : n + 1, t * LANES : (t + 1) * LANES], (8, LANES))
        picked = jnp.take_along_axis(row, source % LANES, axis=1)
        total = jnp.where(source // LANES == t, picked, total)
    return total


def gather_partner(n, rows, cols, comps, refs, out):
    own_ref, target_ref, ids_ref, table_ref, counts_ref, halves_ref, cells_ref, picked_ref, parts_ref = refs
    slots = own_ref.shape[3]
    groups = slots // LANES
    is_ocean = lax.axis_index("comp") == comps - 1

    @pl.when(is_ocean)
    def _():
        for half in range(groups // 8):
            source = slot_order(slots, comps - 1, True, half)
            at = slice(half * 8, (half + 1) * 8)
            cells_ref[at, :] = pick_rows(own_ref, n, source)
            picked_ref[at, :] = pick_rows(ids_ref, n, source)
            out[4 * groups + half * 8 : 4 * groups + (half + 1) * 8, :] = pick_rows(target_ref, n, source).astype(F32)

    @pl.when(jnp.logical_not(is_ocean))
    def _():
        for g in range(groups):
            cut = slice(g * LANES, (g + 1) * LANES)
            cells_ref[g : g + 1, :] = own_ref[0, 0, n : n + 1, cut]
            picked_ref[g : g + 1, :] = ids_ref[0, 0, n : n + 1, cut]
            out[4 * groups + g : 4 * groups + g + 1, :] = target_ref[0, 0, n : n + 1, cut].astype(F32)

    count = jnp.broadcast_to(counts_ref[0, :, n : n + 1], (8, LANES))
    for half in range(groups // 8):
        source = slot_order(slots, comps - 1, is_ocean, half)
        ids = picked_ref[half * 8 : (half + 1) * 8, :]
        weight = jnp.zeros((8, LANES), F32)
        for t in range(table_ref.shape[0]):
            table = jnp.broadcast_to(table_ref[t : t + 1, :], (8, LANES))
            looked = jnp.take_along_axis(table, ids % LANES, axis=1)
            weight = jnp.where(ids // LANES == t, looked, weight)
        out[3 * groups + half * 8 : 3 * groups + (half + 1) * 8, :] = jnp.where(source < count, weight, 0.0)
    col_ids = packed_ids(cols)
    row_ids = iota((rows, LANES), 0)
    one = jnp.ones((), BF16)
    zero = jnp.zeros((), BF16)
    wide, subs = 2, 4

    def some(c, carry):
        for sub in range(subs):
            first = (c * subs + sub) * wide
            cells = [cells_ref[pl.ds(first + g, 1), :] for g in range(wide)]
            picks = []
            for cell in cells:
                col = spread_row(cell % cols).astype(F32).astype(BF16)
                picks.append(jnp.where(col_ids == col[None], one, zero).reshape(cols, LANES))
            picks = jnp.concatenate(picks, axis=1)
            if halves_ref.shape[1] > cols:
                picks = jnp.concatenate([picks, picks], axis=0)
                found = jnp.dot(halves_ref[...], picks, preferred_element_type=F32)
            else:
                found = jnp.dot(halves_ref[...], picks, preferred_element_type=F32)
                found = found[: 3 * rows] + found[3 * rows :]
            for g in range(wide):
                in_row = row_ids == cells[g] // cols
                for place, v in enumerate((2, 0, 1)):
                    block = found[v * rows : (v + 1) * rows, g * LANES : (g + 1) * LANES]
                    block = jnp.where(in_row, block, 0.0).reshape(rows // 8, 8, LANES)
                    start = pl.multiple_of((place * groups + first + g) * 8, 8)
                    parts_ref[pl.ds(start, 8), :] = jnp.sum(block, axis=0)
        return carry

    lax.fori_loop(0, groups // (subs * wide), some, 0)
    weight = out[3 * groups : 4 * groups, :]
    for place in range(3):
        total = jnp.zeros((groups, LANES), F32)
        for i in range(8):
            total += parts_ref[pl.ds(place * groups * 8 + i, groups, stride=8), :]
        out[place * groups : (place + 1) * groups, :] = total * weight


def split_surface(surface_ref, halves_ref, rows, cols):
    for v in range(3):
        high, low = split_two(surface_ref[v])
        if halves_ref.shape[1] > cols:
            halves_ref[v * rows : (v + 1) * rows, :cols] = high
            halves_ref[v * rows : (v + 1) * rows, cols:] = low
        else:
            halves_ref[v * rows : (v + 1) * rows, :] = high
            halves_ref[(v + 3) * rows : (v + 4) * rows, :] = low


def put_rows(ref, start, levels, cols, fields, sea, edge, second):
    height = halo_rows(levels)
    for p in range(cols // LANES):
        cut = slice(p * LANES, (p + 1) * LANES)
        base = start + p * height
        ref[base + 4 * levels : base + height, :] = jnp.zeros((height - 4 * levels, LANES), F32)
        ref[base + 4 * levels : base + 4 * levels + 1, :] = sea[edge : edge + 1, cut].astype(F32)
        for q, v, at in ((EDGE_P, 0, edge), (SECOND_P, 0, second), (EDGE_VELOCITY, 1, edge), (EDGE_T, 3, edge)):
            for l in range(levels):
                row = base + q * levels + l
                ref[row : row + 1, :] = fields(v, l)[at : at + 1, cut]


def turned_columns(levels, rows, fields, sea, begin):
    edge = 1 if begin else 0
    lanes = iota((rows, LANES), 1)
    total = pltpu.roll(sea.astype(F32), (4 * levels - begin - edge) % LANES, 1)
    for l in range(levels):
        total = jnp.where(lanes // 2 == l, pltpu.roll(fields(0, l), (2 * l - begin) % LANES, 1), total)
        for q, v in ((EDGE_VELOCITY, 2), (EDGE_T, 3)):
            at = q * levels + l
            moved = pltpu.roll(fields(v, l), (at - begin - edge) % LANES, 1)
            total = jnp.where(lanes == at, moved, total)
    return total.T[: halo_rows(levels)]


def first_body(
    levels, rows, cols, comps,
    state_hbm, own_hbm, target_hbm, ids_hbm, table_hbm, counts_hbm, mask_hbm,
    slab1_ref, up_ref, slab3_ref, fold_ref,
    surface_ref, own_ref, target_ref, ids_ref, table_ref, counts_ref, edge_ref, sea_edge_ref, mask_ref, columns_ref,
    halves_ref, cells_ref, picked_ref, parts_ref, copies, column_copies,
):
    sources = (
        state_hbm.at[0, pl.ds(1, 3), 0], own_hbm, target_hbm, ids_hbm, table_hbm, counts_hbm,
        state_hbm.at[0, :, :, pl.ds(rows - 8, 8), :], mask_hbm.at[0, pl.ds(rows - 8, 8), :],
    )
    places = (surface_ref, own_ref, target_ref, ids_ref, table_ref, counts_ref, edge_ref, sea_edge_ref)
    fetches = [
        pltpu.make_async_copy(source, place, copies.at[i])
        for i, (source, place) in enumerate(zip(sources, places))
    ]
    outer = pl.ds(cols - LANES, LANES)
    for_fold = [
        pltpu.make_async_copy(state_hbm.at[0, v, :, :, outer], columns_ref.at[i], column_copies.at[i])
        for i, v in enumerate((0, 2, 3))
    ] + [pltpu.make_async_copy(mask_hbm.at[0, :, outer], mask_ref, column_copies.at[3])]
    northern = lax.axis_index("ty") == lax.axis_size("ty") - 1
    folds = jnp.logical_and(lax.axis_index("comp") == comps - 1, northern)
    for fetch in fetches:
        fetch.start()

    @pl.when(folds)
    def _():
        for fetch in for_fold:
            fetch.start()

    for fetch in fetches:
        fetch.wait()
    slab_rows = slab1_ref.shape[0]
    tall = halo_rows(levels) * (cols // LANES)
    put_rows(up_ref, slab_rows, levels, cols, lambda v, l: edge_ref.at[v, l], sea_edge_ref, 7, 6)

    @pl.when(folds)
    def _():
        for fetch in for_fold:
            fetch.wait()
        places = {0: 0, 2: 1, 3: 2}
        fold_ref[...] = turned_columns(
            levels, rows, lambda v, l: columns_ref[places[v], l], mask_ref[...], LANES - 2
        )

    @pl.when(jnp.logical_not(folds))
    def _():
        fold_ref[...] = jnp.zeros_like(fold_ref)

    up_ref[slab_rows + tall :, :] = fold_ref[...]
    slab3_ref[slab_rows:, :] = fold_ref[...]
    split_surface(surface_ref, halves_ref, rows, cols)
    refs = (own_ref, target_ref, ids_ref, table_ref, counts_ref, halves_ref, cells_ref, picked_ref, parts_ref)
    for n, out in ((3, slab3_ref), (1, slab1_ref), (2, up_ref)):
        gather_partner(n, rows, cols, comps, refs, out)


def gather_scratch(rows, cols, slots, stacked):
    return [
        pltpu.VMEM((6 * rows, cols) if stacked else (3 * rows, 2 * cols), BF16),
        pltpu.VMEM((slots // LANES, LANES), I32),
        pltpu.VMEM((slots // LANES, LANES), I32),
        pltpu.VMEM((3 * slots // LANES * 8, LANES), F32),
    ]


def first_side(model_state, slot_arrays, sea_mask, comps):
    levels, rows, cols = model_state.shape[2:]
    near, slots = slot_arrays[0].shape[2:]
    table_shape = slot_arrays[3].shape
    slab = CHANNELS * slots // LANES
    height = halo_rows(levels)
    heights = (slab, slab + height * (cols // LANES) + height, slab + height, height)
    vmem = pl.BlockSpec(memory_space=pltpu.VMEM)
    arrays = (model_state, *slot_arrays, sea_mask)
    return pl.pallas_call(
        functools.partial(first_body, levels, rows, cols, comps),
        in_specs=[pl.BlockSpec(memory_space=pltpu.HBM)] * len(arrays),
        out_specs=[vmem] * len(heights),
        out_shape=[jax.ShapeDtypeStruct((h, LANES), F32) for h in heights],
        scratch_shapes=[pltpu.VMEM((3, rows, cols), F32)]
        + [pltpu.VMEM((1, 1, near, slots), I32)] * 3
        + [pltpu.VMEM(table_shape, F32), pltpu.VMEM((1, 1, near), I32)]
        + [
            pltpu.VMEM((4, levels, 8, cols), F32),
            pltpu.VMEM((8, cols), I32),
            pltpu.VMEM((rows, LANES), I32),
            pltpu.VMEM((3, levels, rows, LANES), F32),
        ]
        + gather_scratch(rows, cols, slots, True)
        + [pltpu.SemaphoreType.DMA((8,)), pltpu.SemaphoreType.DMA((4,))],
        compiler_params=pltpu.CompilerParams(vmem_limit_bytes=VMEM_BYTES),
    )(*(pltpu.with_memory_space_constraint(array, pltpu.HBM) for array in arrays))


def second_body(
    levels, rows, cols, comps, y_pair,
    state_ref, own_ref, target_ref, ids_ref, table_ref, counts_ref, fold_ref, mask_hbm,
    slab0_ref, down_ref, high_ref, low_ref, pair_ref,
    halves_ref, cells_ref, picked_ref, parts_ref, mask_ref, copied,
):
    fetch = pltpu.make_async_copy(mask_hbm, mask_ref, copied)
    fetch.start()
    split_surface(state_ref.at[0, pl.ds(1, 3), 0], halves_ref, rows, cols)
    refs = (own_ref, target_ref, ids_ref, table_ref, counts_ref, halves_ref, cells_ref, picked_ref, parts_ref)
    gather_partner(0, rows, cols, comps, refs, slab0_ref)
    fetch.wait()
    put_rows(down_ref, 0, levels, cols, lambda v, l: state_ref.at[0, v, l], mask_ref.at[0], 0, 1)
    down_ref[halo_rows(levels) * (cols // LANES) :, :] = fold_ref[...]
    index_y = lax.axis_index("ty")
    high_used = index_y == 0 if y_pair else index_y >= 0
    low_used = index_y > 0 if y_pair else index_y >= 0

    def columns(start, begin):
        cut = slice(start, start + LANES)
        return turned_columns(levels, rows, lambda v, l: state_ref[0, v, l, :, cut], mask_ref[0, :, cut], begin)

    @pl.when(high_used)
    def _():
        highest = columns(cols - LANES, LANES - 2)
        high_ref[...] = highest
        pair_ref[...] = highest

    @pl.when(jnp.logical_not(high_used))
    def _():
        high_ref[...] = jnp.zeros_like(high_ref)

    @pl.when(low_used)
    def _():
        lowest = columns(0, 0)
        low_ref[...] = lowest
        pair_ref[...] = lowest

    @pl.when(jnp.logical_not(low_used))
    def _():
        low_ref[...] = jnp.zeros_like(low_ref)


def second_side(model_state, slot_arrays, fold, sea_mask, comps, y_pair):
    levels, rows, cols = model_state.shape[2:]
    slots = slot_arrays[0].shape[3]
    height = halo_rows(levels)
    heights = (CHANNELS * slots // LANES, height * (cols // LANES) + height, height, height, height)
    vmem = pl.BlockSpec(memory_space=pltpu.VMEM)
    return pl.pallas_call(
        functools.partial(second_body, levels, rows, cols, comps, y_pair),
        in_specs=[vmem] * 7 + [pl.BlockSpec(memory_space=pltpu.HBM)],
        out_specs=[vmem] * len(heights),
        out_shape=[jax.ShapeDtypeStruct((h, LANES), F32) for h in heights],
        scratch_shapes=gather_scratch(rows, cols, slots, False)
        + [pltpu.VMEM((1, rows, cols), I32), pltpu.SemaphoreType.DMA],
        compiler_params=pltpu.CompilerParams(vmem_limit_bytes=VMEM_BYTES),
    )(model_state, *slot_arrays, fold, pltpu.with_memory_space_constraint(sea_mask, pltpu.HBM))


def stencil_body(
    levels, rows, cols, comps, count_x, count_y,
    state_ref, mask_ref, up_ref, down_ref, south_ref, north_ref, own_ref, fold_ref,
    wave_ref, spread_ref, gains_ref, *rest,
):
    height = halo_rows(levels)
    relayed = north_ref.shape[0] > height
    far_refs = rest[: 0 if relayed else max(count_x - 3, 0)]
    out_ref, new_surface_ref, old_surface_ref = rest[len(far_refs) : len(far_refs) + 3]
    folded_ref, rows_ref, turned_ref, pad_ref, news_ref, stores = rest[len(far_refs) + 3 :]
    parts = cols // LANES
    index_x = lax.axis_index("tx")
    index_y = lax.axis_index("ty")
    is_ocean = lax.axis_index("comp") == comps - 1
    last_y = index_y == count_y - 1
    has_west = jnp.where(jnp.logical_or(is_ocean, index_x > 0), 1.0, 0.0)
    has_east = jnp.where(jnp.logical_or(is_ocean, index_x < count_x - 1), 1.0, 0.0)
    has_south = jnp.where(index_y > 0, 1.0, 0.0)
    has_north = jnp.where(jnp.logical_or(is_ocean, jnp.logical_not(last_y)), 1.0, 0.0)
    drag = gains_ref[0, 2]
    mask_at = 4 * levels

    def store(l, v):
        return pltpu.make_async_copy(news_ref.at[l, v], out_ref.at[0, v, l], stores.at[l, v])

    fold = fold_ref[pl.ds(index_x, 1), :]
    total = jnp.zeros((height, LANES), F32)
    up_start = up_ref.shape[0] - height * (parts + 1)
    sources = [(0, own_ref, 0), (-1, up_ref, up_start + height * parts), (1, down_ref, height * parts)]
    if relayed:
        sources.append((2, north_ref, height))
    else:
        sources += [(shift, ref, 0) for shift, ref in zip(range(2, count_x - 1), far_refs)]
    for shift, ref, start in sources:
        at = lax.rem(index_x + shift + count_x, count_x)
        chosen = (iota((rows, rows), 0) + at * rows == fold).astype(F32)
        total += jnp.dot(
            ref[start : start + height, :], chosen,
            precision=lax.Precision.HIGHEST, preferred_element_type=F32,
        )
    folded_ref[...] = total

    line = iota((levels, LANES), 0)
    halves = jnp.zeros((levels, LANES), F32)
    for l in range(levels):
        halves = jnp.where(line == l, 0.5 * wave_ref[0, l], halves)

    def keeping(sea_values, drags):
        return jnp.where(is_ocean, sea_values, 1.0 - drags * (1.0 - sea_values))

    drags = jnp.where(line == 0, drag, 0.0)

    def by_level(ref, start, q):
        return ref[start + q * levels : start + (q + 1) * levels, :]

    for side, (ref, begin, sign, has) in enumerate(
        ((up_ref, up_start, 1.0, has_west), (down_ref, 0, -1.0, has_east))
    ):
        for p in range(parts):
            start = begin + p * height
            kept = keeping(ref[start + mask_at : start + mask_at + 1, :], drags)
            fixed = kept * (by_level(ref, start, EDGE_VELOCITY) + sign * halves * by_level(ref, start, SECOND_P))
            inner = rows - 1 if side else 0
            own = jnp.concatenate(
                [state_ref[0, 0, l, inner : inner + 1, p * LANES : (p + 1) * LANES] for l in range(levels)], axis=0
            )
            rows_ref[side, p, 0] = has * by_level(ref, start, EDGE_P)
            rows_ref[side, p, 1] = has * by_level(ref, start, EDGE_T)
            rows_ref[side, p, 2] = has * (fixed - sign * kept * halves * own)

    even = lambda ref: ref[pl.ds(0, levels, stride=2), :]
    odd = lambda ref: ref[pl.ds(1, levels, stride=2), :]
    north = [
        jnp.where(last_y, jnp.where(is_ocean, folded, 0.0), low)
        for folded, low in (
            (odd(folded_ref), even(north_ref)),
            (even(folded_ref), odd(north_ref)),
            (-by_level(folded_ref, 0, EDGE_VELOCITY), by_level(north_ref, 0, EDGE_VELOCITY)),
            (by_level(folded_ref, 0, EDGE_T), by_level(north_ref, 0, EDGE_T)),
            (folded_ref[mask_at : mask_at + 1, :], north_ref[mask_at : mask_at + 1, :]),
        )
    ]
    south = [
        odd(south_ref), even(south_ref), by_level(south_ref, 0, EDGE_VELOCITY), by_level(south_ref, 0, EDGE_T),
        south_ref[mask_at : mask_at + 1, :],
    ]
    fill = jnp.zeros((LANES - 4 * levels, LANES), F32)
    for side, ((edge, second, velocity, tracer, sea), sign, has) in enumerate(
        ((south, 1.0, has_south), (north, -1.0, has_north))
    ):
        kept = keeping(sea, drags)
        fixed = has * kept * (velocity + sign * halves * second)
        turned_ref[side] = jnp.concatenate(
            [has * edge, has * tracer, fixed, has * kept * halves, fill], axis=0
        ).T

    sea = mask_ref[0].astype(F32)
    lane = iota((rows, LANES), 1)

    def cut(p):
        return slice(p * LANES, (p + 1) * LANES)

    def south_col(q, level):
        return pltpu.roll(turned_ref[0], lax.rem(LANES - q * levels - level, LANES), 1)

    def north_col(q, level):
        return pltpu.roll(turned_ref[1], LANES - 1 - q * levels - level, 1)

    def from_south(field, edge):
        moved = [pltpu.roll(t, 1, 1) for t in field]
        return [jnp.where(lane == 0, low, t) for low, t in zip([edge] + moved[:-1], moved)]

    def from_north(field, edge):
        moved = [pltpu.roll(t, LANES - 1, 1) for t in field]
        return [jnp.where(lane == LANES - 1, high, t) for high, t in zip(moved[1:] + [edge], moved)]

    def one_level(level, carry):
        half = 0.5 * wave_ref[0, level]
        spread = spread_ref[0, level]
        level_drag = jnp.where(level == 0, drag, 0.0)
        shift = jnp.minimum(level, 0)

        def padded(which, q, field):
            both = []
            for p in range(parts):
                pad_ref[which, p, 8 : 8 + rows, :] = field[p]
                pad_ref[which, p, 7:8, :] = rows_ref[0, p, q, pl.ds(level, 1), :]
                pad_ref[which, p, 8 + rows : 9 + rows, :] = rows_ref[1, p, q, pl.ds(level, 1), :]
                both.append((pad_ref[which, p, pl.ds(7 + shift, rows), :], pad_ref[which, p, pl.ds(9 + shift, rows), :]))
            return both

        pressure, zonal, meridional, tracer = (
            [state_ref[0, v, level, :, cut(p)] for p in range(parts)] for v in range(4)
        )
        keep = [keeping(sea[:, cut(p)], level_drag) for p in range(parts)]
        new_zonal = [
            m * (u - half * (e - w)) for m, u, (w, e) in zip(keep, zonal, padded(0, 0, pressure))
        ]
        new_meridional = [
            m * (v - half * (n - s))
            for m, v, n, s in zip(
                keep, meridional,
                from_north(pressure, north_col(0, level)), from_south(pressure, south_col(0, level)),
            )
        ]
        new_tracer = [
            t + spread * jnp.where(is_ocean, sea[:, cut(p)], 1.0) * (e + w + n + s - 4.0 * t)
            for p, t, (w, e), n, s in zip(
                range(parts), tracer, padded(1, 1, tracer),
                from_north(tracer, north_col(1, level)), from_south(tracer, south_col(1, level)),
            )
        ]
        south_v = south_col(2, level) - south_col(3, level) * pressure[0]
        north_v = north_col(2, level) + north_col(3, level) * pressure[-1]
        new_pressure = [
            q - half * (e - w + n - s)
            for q, (w, e), n, s in zip(
                pressure, padded(2, 2, new_zonal),
                from_north(new_meridional, north_v), from_south(new_meridional, south_v),
            )
        ]
        for p in range(parts):
            for v, field in enumerate((new_pressure, new_zonal, new_meridional, new_tracer)):
                news_ref[level, v, :, cut(p)] = field[p]
        for v in range(4):
            store(level, v).start()

        @pl.when(level == 0)
        def _():
            for v in range(3):
                new_surface_ref[v] = news_ref[0, v + 1]
                old_surface_ref[v] = state_ref[0, v + 1, 0]

        return carry

    lax.fori_loop(0, levels, one_level, 0)
    for l in range(levels):
        for v in range(4):
            store(l, v).wait()


def stencil(model_state, sea_mask, up, down, south, north, own, fars, fold_map, wave_speed, diffusivity, gains, sizes):
    comps, count_x, count_y = sizes
    levels, rows, cols = model_state.shape[2:]
    fold = fold_map.reshape(count_x, rows)
    vmem = pl.BlockSpec(memory_space=pltpu.VMEM)
    scalar = pl.BlockSpec(memory_space=pltpu.SMEM)
    anywhere = pl.BlockSpec(memory_space=pl.ANY)
    surface = jax.ShapeDtypeStruct((3, rows, cols), F32)
    return pl.pallas_call(
        functools.partial(stencil_body, levels, rows, cols, comps, count_x, count_y),
        in_specs=[vmem] * 8 + [scalar] * 3 + [vmem] * len(fars),
        out_specs=[anywhere, vmem, vmem],
        out_shape=[jax.ShapeDtypeStruct(model_state.shape, F32), surface, surface],
        scratch_shapes=[
            pltpu.VMEM(own.shape, F32),
            pltpu.VMEM((2, cols // LANES, 3, levels, LANES), F32),
            pltpu.VMEM((2, rows, LANES), F32),
            pltpu.VMEM((3, cols // LANES, rows + 16, LANES), F32),
            pltpu.VMEM((levels, 4, rows, cols), F32),
            pltpu.SemaphoreType.DMA((levels, 4)),
        ],
        compiler_params=pltpu.CompilerParams(vmem_limit_bytes=VMEM_BYTES),
    )(model_state, sea_mask, up, down, south, north, own, fold, wave_speed, diffusivity, gains, *fars)


def add_slots(rows, cols, groups, slab_ref, total_ref, begin, end, plan, channels):
    row_ids = packed_ids(rows)
    col_ids = packed_ids(cols)
    lane = iota((1, LANES), 1)
    one = jnp.ones((), BF16)
    zero = jnp.zeros((), BF16)
    block = 4

    def some(chunk, carry):
        n, first, low_slot, high_slot = plan(chunk)
        start = n * (CHANNELS * groups) + first
        for at in range(0, DEPTH, block):
            columns, spreads = [], []
            for g in range(at, at + block):
                cells = slab_ref[pl.ds(start + 4 * groups + g, 1), :].astype(I32)
                slot = lane + (first + g) * LANES
                mine = jnp.logical_and(slot >= low_slot, slot < high_slot)
                row = spread_row(jnp.where(mine, cells // cols, -1)).astype(F32).astype(BF16)
                col = spread_row(cells % cols).astype(F32).astype(BF16)
                columns.append(jnp.where(col_ids == col[None], one, zero).reshape(cols, LANES))
                in_row = row_ids == row[None]
                highs, lows = [], []
                for v in channels:
                    value = spread_row(slab_ref[pl.ds(start + v * groups + g, 1), :])
                    high, low = split_two(value)
                    highs.append(jnp.where(in_row, high[None], zero).reshape(rows, LANES))
                    lows.append(jnp.where(in_row, low[None], zero).reshape(rows, LANES))
                spreads.append(jnp.concatenate(highs + lows, axis=0))
            total_ref[...] += lax.dot_general(
                jnp.concatenate(spreads, axis=1), jnp.concatenate(columns, axis=1), (((1,), (1,)), ((), ())),
                preferred_element_type=F32,
            )
        return carry

    total_ref[...] = jnp.zeros_like(total_ref)
    lax.fori_loop(begin, end, some, 0)


def halves_added(total_ref):
    half = total_ref.shape[0] // 2
    return total_ref[:half] + total_ref[half:]


ALL, FIRST_TWO, LAST_TWO = (0, 1, 2, 3), (0, 1), (2, 3)


def whole_plan(groups):
    pieces = groups // DEPTH
    return lambda chunk: (chunk // pieces, chunk % pieces * DEPTH, 0, groups * LANES)


def own_body(rows, cols, comps, groups, slab_ref, sent_ref, lent_ref, total_ref, half_ref):
    here = lax.axis_index("comp")
    near = slab_ref.shape[0] // (CHANNELS * groups)
    pieces = groups // DEPTH
    bounds = share_bounds(groups * LANES, comps - 1)
    is_ocean = here == comps - 1
    beside = here == comps - 2

    def plan(chunk):
        n, first, low_slot, high_slot = whole_plan(groups)(chunk)
        n = jnp.where(is_ocean, chunk, n)
        first = jnp.where(is_ocean, groups - DEPTH, first)
        return n, first, jnp.where(is_ocean, bounds[comps - 2], low_slot), high_slot

    end = jnp.where(is_ocean, near, jnp.where(beside, near * pieces // 2, 0))
    add_slots(rows, cols, groups, slab_ref, total_ref, 0, end, plan, ALL)
    end = jnp.where(here == 0, near * pieces, 0)
    add_slots(rows, cols, groups, slab_ref, half_ref, 0, end, whole_plan(groups), FIRST_TWO)
    sent_ref[...] = halves_added(total_ref)
    lent_ref[...] = halves_added(half_ref)


def other_body(
    rows, cols, comps, groups, slab_ref, own_ref, before_ref, kept_ref, sent_ref, first_ref, second_ref, half_ref
):
    here = lax.axis_index("comp")
    near = slab_ref.shape[0] // (CHANNELS * groups)
    pieces = groups // DEPTH
    chunks = near * pieces
    bounds = share_bounds(groups * LANES, comps - 1)
    is_ocean = here == comps - 1
    beside = here == comps - 2
    for_two = here == comps - 3
    middle = bounds[1] // LANES // 4 * 4

    def plan(chunk):
        n, first, low_slot, high_slot = whole_plan(groups)(chunk)
        mine = chunk >= near
        n = jnp.where(for_two, chunk % near, n)
        first = jnp.where(for_two, jnp.where(mine, middle, 0), first)
        low_slot = jnp.where(jnp.logical_and(for_two, mine), bounds[1], low_slot)
        high_slot = jnp.where(for_two, jnp.where(mine, bounds[2], bounds[1]), high_slot)
        return n, first, low_slot, high_slot

    full = jnp.logical_or(is_ocean, for_two)
    add_slots(rows, cols, groups, slab_ref, first_ref, 0, jnp.where(full, chunks // 2, 0), plan, ALL)
    add_slots(
        rows, cols, groups, slab_ref, second_ref, chunks // 2, jnp.where(full, chunks, chunks // 2), plan, ALL
    )
    add_slots(
        rows, cols, groups, slab_ref, half_ref, 0, jnp.where(beside, chunks, 0), whole_plan(groups), LAST_TWO
    )

    @pl.when(beside)
    def _():
        add_slots(rows, cols, groups, own_ref, second_ref, chunks // 2, chunks, whole_plan(groups), ALL)

    for v in range(4):
        at = slice(v * rows, (v + 1) * rows)
        low = slice((v + 4) * rows, (v + 5) * rows)
        first = first_ref[at] + first_ref[low]
        second = second_ref[at] + second_ref[low]
        kept_ref[at] = jnp.where(beside, 0.0, second) + jnp.where(is_ocean, first, 0.0)
        sent = jnp.where(is_ocean, 0.0, first) + jnp.where(beside, second, 0.0) + before_ref[at]
        if v >= 2:
            sent += half_ref[(v - 2) * rows : (v - 1) * rows] + half_ref[v * rows : (v + 1) * rows]
        sent_ref[at] = sent


def scatter_call(body, heights, outs, rows, cols, comps, slots, *operands):
    vmem = pl.BlockSpec(memory_space=pltpu.VMEM)
    return pl.pallas_call(
        functools.partial(body, rows, cols, comps, slots // LANES),
        in_specs=[vmem] * len(operands),
        out_specs=[vmem] * len(outs),
        out_shape=[jax.ShapeDtypeStruct((h * rows, cols), F32) for h in outs],
        scratch_shapes=[pltpu.VMEM((h * rows, cols), F32) for h in heights],
        cost_estimate=pl.CostEstimate(flops=64 * rows * cols * slots, bytes_accessed=0, transcendentals=0),
        compiler_params=pltpu.CompilerParams(vmem_limit_bytes=VMEM_BYTES),
    )(*operands)


def finish_body(rows, comps, state_ref, new_ref, old_ref, kept_ref, came_ref, mask_ref, gains_ref, out_ref, news_ref, copies):
    is_ocean = lax.axis_index("comp") == comps - 1
    tendency = jnp.where(is_ocean, mask_ref[0].astype(F32), 1.0)
    sums = [kept_ref[v * rows : (v + 1) * rows, :] + came_ref[v * rows : (v + 1) * rows, :] for v in range(4)]
    saves = []
    for v, total, gain in ((0, sums[1], 1), (1, sums[2], 1), (2, sums[0], 0)):
        news_ref[v] = new_ref[v] + tendency * gains_ref[0, gain] * (total - sums[3] * old_ref[v])
        saves.append(pltpu.make_async_copy(news_ref.at[v], out_ref.at[0, v + 1, 0], copies.at[v]))
        saves[-1].start()
    for save in saves:
        save.wait()


def finish(state, new_surface, old_surface, kept, came, sea_mask, gains, comps):
    rows, cols = state.shape[3:]
    vmem = pl.BlockSpec(memory_space=pltpu.VMEM)
    anywhere = pl.BlockSpec(memory_space=pl.ANY)
    return pl.pallas_call(
        functools.partial(finish_body, rows, comps),
        in_specs=[anywhere] + [vmem] * 5 + [pl.BlockSpec(memory_space=pltpu.SMEM)],
        out_specs=anywhere,
        out_shape=jax.ShapeDtypeStruct(state.shape, F32),
        scratch_shapes=[pltpu.VMEM((3, rows, cols), F32), pltpu.SemaphoreType.DMA((3,))],
        input_output_aliases={0: 0},
        compiler_params=pltpu.CompilerParams(vmem_limit_bytes=VMEM_BYTES),
    )(state, new_surface, old_surface, kept, came, sea_mask, gains)


def shards(
    model_state, sea_mask, wave_speed, diffusivity, surface_gains, area_table,
    own_cells, target_cells, weight_ids, pair_counts, fold_map,
):
    comps, count_x, count_y = (lax.axis_size(a) for a in ("comp", "tx", "ty"))
    positions = count_x * count_y
    rows, cols = model_state.shape[3:]
    slots = own_cells.shape[3]
    slot_arrays = (own_cells, target_cells, weight_ids, area_table.reshape(-1, LANES), pair_counts)

    def along(block, shift):
        return lax.ppermute(block, ("tx", "ty"), [(s, (s + shift) % positions) for s in range(positions)])

    y_pair = count_y == 2
    slab_rows = CHANNELS * slots // LANES
    slab1, up, slab3, fold = first_side(model_state, slot_arrays, sea_mask, comps)
    slab3 = along(slab3, 1 + count_y)
    slab1 = along(slab1, 1)
    up = along(up, count_y)
    slab0, down, high, low, pair = second_side(model_state, slot_arrays, fold, sea_mask, comps, y_pair)
    arrived = jnp.concatenate([slab0, slab1, up[:slab_rows], slab3[:slab_rows]])
    other = lax.ppermute(arrived, "comp", [(g, g ^ 2) for g in range(comps)])

    down = along(down, -count_y)
    fars = []
    if y_pair and count_x == 4:
        south = north = lax.ppermute(jnp.concatenate([pair, slab3[slab_rows:]]), "ty", [(0, 1), (1, 0)])
    else:
        south = lax.ppermute(high, "ty", [(j, j + 1) for j in range(count_y - 1)])
        north = lax.ppermute(low, "ty", [(j + 1, j) for j in range(count_y - 1)])
        for shift in range(2, count_x - 1):
            pairs = []
            for i in range(count_x):
                ends = [((comps - 1) * count_x + k) * count_y + count_y - 1 for k in ((i + shift) % count_x, i)]
                pairs.append(tuple(ends))
            fars.append(lax.ppermute(fold, ("comp", "tx", "ty"), pairs))

    before, lent = scatter_call(own_body, (8, 4), (4, 2), rows, cols, comps, slots, arrived)
    other, lent, before, up, down, south, north, *fars = lax.optimization_barrier(
        (other, lent, before, up, down, south, north, *fars)
    )
    lent = lax.ppermute(lent, "comp", [(0, comps - 2), (comps - 2, 0)])
    kept, sent = scatter_call(
        other_body, (8, 8, 4), (4, 4), rows, cols, comps, slots, other, arrived, before
    )
    sent = jnp.concatenate([sent[: 2 * rows] + lent, sent[2 * rows :]])
    came = lax.ppermute(sent, "comp", [(g, g ^ 1) for g in range(comps)])
    up, down, south, north, fold, kept = lax.optimization_barrier((up, down, south, north, fold, kept))
    new_state, new_surface, old_surface = stencil(
        model_state, sea_mask, up, down, south, north, fold, fars, fold_map,
        wave_speed, diffusivity, surface_gains, (comps, count_x, count_y),
    )
    return finish(new_state, new_surface, old_surface, kept, came, sea_mask, surface_gains, comps)


def solution(mesh):
    in_specs = (
        P("comp", None, None, "tx", "ty"),
        P("comp", "tx", "ty"),
        P("comp", None),
        P("comp", None),
        P("comp", None),
        P(),
        P("comp", ("tx", "ty"), None, None),
        P("comp", ("tx", "ty"), None, None),
        P("comp", ("tx", "ty"), None, None),
        P("comp", ("tx", "ty"), None),
        P(),
    )
    out_specs = P("comp", None, None, "tx", "ty")
    return jax.shard_map(shards, mesh=mesh, in_specs=in_specs, out_specs=out_specs, check_vma=False)
```

```python
import functools

import jax
import jax.numpy as jnp
from jax import lax
from jax.experimental import pallas as pl
from jax.experimental.pallas import tpu as pltpu
from jax.sharding import PartitionSpec as P

LANES = 128
DEPTH = 8
PACKED = 16
VMEM_BYTES = 28 * 1024 * 1024
F32 = jnp.float32
BF16 = jnp.bfloat16
I32 = jnp.int32
CHANNELS = 5

EDGE_P, SECOND_P, EDGE_VELOCITY, EDGE_T, MASK = range(5)


def iota(shape, dim):
    return lax.broadcasted_iota(I32, shape, dim)


def halo_rows(levels):
    return (4 * levels + 1 + 7) // 8 * 8


def split_two(values):
    high = values.astype(BF16)
    low = (values - high.astype(F32)).astype(BF16)
    return high, low


def packed_ids(count):
    ids = iota((count, LANES), 0).astype(F32).astype(BF16)
    return ids.reshape(count // PACKED, PACKED, LANES)


def spread_row(row):
    return jnp.broadcast_to(row, (PACKED, LANES))


def share_bounds(slots, shares):
    bounds = [0]
    for m in range(shares):
        bounds.append(bounds[-1] + (slots - m + shares - 1) // shares)
    return bounds


def slot_order(slots, shares, sort, half):
    place = iota((8, LANES), 0) * LANES + iota((8, LANES), 1) + half * 8 * LANES
    source = jnp.zeros((8, LANES), I32)
    bounds = share_bounds(slots, shares)
    for m in range(shares):
        inside = jnp.logical_and(place >= bounds[m], place < bounds[m + 1])
        source = jnp.where(inside, (place - bounds[m]) * shares + m, source)
    return jnp.where(sort, source, place)


def pick_rows(ref, n, source):
    total = jnp.zeros((8, LANES), I32)
    for t in range(ref.shape[3] // LANES):
        row = jnp.broadcast_to(ref[0, 0, n : n + 1, t * LANES : (t + 1) * LANES], (8, LANES))
        picked = jnp.take_along_axis(row, source % LANES, axis=1)
        total = jnp.where(source // LANES == t, picked, total)
    return total


def gather_partner(n, rows, cols, comps, refs, out):
    own_ref, target_ref, ids_ref, table_ref, counts_ref, halves_ref, cells_ref, picked_ref, parts_ref = refs
    slots = own_ref.shape[3]
    groups = slots // LANES
    is_ocean = lax.axis_index("comp") == comps - 1

    @pl.when(is_ocean)
    def _():
        for half in range(groups // 8):
            source = slot_order(slots, comps - 1, True, half)
            at = slice(half * 8, (half + 1) * 8)
            cells_ref[at, :] = pick_rows(own_ref, n, source)
            picked_ref[at, :] = pick_rows(ids_ref, n, source)
            out[4 * groups + half * 8 : 4 * groups + (half + 1) * 8, :] = pick_rows(target_ref, n, source).astype(F32)

    @pl.when(jnp.logical_not(is_ocean))
    def _():
        for g in range(groups):
            cut = slice(g * LANES, (g + 1) * LANES)
            cells_ref[g : g + 1, :] = own_ref[0, 0, n : n + 1, cut]
            picked_ref[g : g + 1, :] = ids_ref[0, 0, n : n + 1, cut]
            out[4 * groups + g : 4 * groups + g + 1, :] = target_ref[0, 0, n : n + 1, cut].astype(F32)

    count = jnp.broadcast_to(counts_ref[0, :, n : n + 1], (8, LANES))
    for half in range(groups // 8):
        source = slot_order(slots, comps - 1, is_ocean, half)
        ids = picked_ref[half * 8 : (half + 1) * 8, :]
        weight = jnp.zeros((8, LANES), F32)
        for t in range(table_ref.shape[0]):
            table = jnp.broadcast_to(table_ref[t : t + 1, :], (8, LANES))
            looked = jnp.take_along_axis(table, ids % LANES, axis=1)
            weight = jnp.where(ids // LANES == t, looked, weight)
        out[3 * groups + half * 8 : 3 * groups + (half + 1) * 8, :] = jnp.where(source < count, weight, 0.0)
    col_ids = packed_ids(cols)
    row_ids = iota((rows, LANES), 0)
    one = jnp.ones((), BF16)
    zero = jnp.zeros((), BF16)
    wide, subs = 2, 4

    def some(c, carry):
        for sub in range(subs):
            first = (c * subs + sub) * wide
            cells = [cells_ref[pl.ds(first + g, 1), :] for g in range(wide)]
            picks = []
            for cell in cells:
                col = spread_row(cell % cols).astype(F32).astype(BF16)
                picks.append(jnp.where(col_ids == col[None], one, zero).reshape(cols, LANES))
            picks = jnp.concatenate(picks, axis=1)
            if halves_ref.shape[1] > cols:
                picks = jnp.concatenate([picks, picks], axis=0)
                found = jnp.dot(halves_ref[...], picks, preferred_element_type=F32)
            else:
                found = jnp.dot(halves_ref[...], picks, preferred_element_type=F32)
                found = found[: 3 * rows] + found[3 * rows :]
            for g in range(wide):
                in_row = row_ids == cells[g] // cols
                for place, v in enumerate((2, 0, 1)):
                    block = found[v * rows : (v + 1) * rows, g * LANES : (g + 1) * LANES]
                    block = jnp.where(in_row, block, 0.0).reshape(rows // 8, 8, LANES)
                    start = pl.multiple_of((place * groups + first + g) * 8, 8)
                    parts_ref[pl.ds(start, 8), :] = jnp.sum(block, axis=0)
        return carry

    lax.fori_loop(0, groups // (subs * wide), some, 0)
    weight = out[3 * groups : 4 * groups, :]
    for place in range(3):
        total = jnp.zeros((groups, LANES), F32)
        for i in range(8):
            total += parts_ref[pl.ds(place * groups * 8 + i, groups, stride=8), :]
        out[place * groups : (place + 1) * groups, :] = total * weight


def split_surface(surface_ref, halves_ref, rows, cols):
    for v in range(3):
        high, low = split_two(surface_ref[v])
        if halves_ref.shape[1] > cols:
            halves_ref[v * rows : (v + 1) * rows, :cols] = high
            halves_ref[v * rows : (v + 1) * rows, cols:] = low
        else:
            halves_ref[v * rows : (v + 1) * rows, :] = high
            halves_ref[(v + 3) * rows : (v + 4) * rows, :] = low


def put_rows(ref, start, levels, cols, fields, sea, edge, second):
    height = halo_rows(levels)
    for p in range(cols // LANES):
        cut = slice(p * LANES, (p + 1) * LANES)
        base = start + p * height
        ref[base + 4 * levels : base + height, :] = jnp.zeros((height - 4 * levels, LANES), F32)
        ref[base + 4 * levels : base + 4 * levels + 1, :] = sea[edge : edge + 1, cut].astype(F32)
        for q, v, at in ((EDGE_P, 0, edge), (SECOND_P, 0, second), (EDGE_VELOCITY, 1, edge), (EDGE_T, 3, edge)):
            for l in range(levels):
                row = base + q * levels + l
                ref[row : row + 1, :] = fields(v, l)[at : at + 1, cut]


def turned_columns(levels, rows, fields, sea, begin):
    edge = 1 if begin else 0
    lanes = iota((rows, LANES), 1)
    total = pltpu.roll(sea.astype(F32), (4 * levels - begin - edge) % LANES, 1)
    for l in range(levels):
        total = jnp.where(lanes // 2 == l, pltpu.roll(fields(0, l), (2 * l - begin) % LANES, 1), total)
        for q, v in ((EDGE_VELOCITY, 2), (EDGE_T, 3)):
            at = q * levels + l
            moved = pltpu.roll(fields(v, l), (at - begin - edge) % LANES, 1)
            total = jnp.where(lanes == at, moved, total)
    return total.T[: halo_rows(levels)]


def first_body(
    levels, rows, cols, comps,
    state_hbm, own_hbm, target_hbm, ids_hbm, table_hbm, counts_hbm, mask_hbm,
    slab1_ref, up_ref, slab3_ref, fold_ref,
    surface_ref, own_ref, target_ref, ids_ref, table_ref, counts_ref, edge_ref, sea_edge_ref, mask_ref, columns_ref,
    halves_ref, cells_ref, picked_ref, parts_ref, copies, column_copies,
):
    sources = (
        state_hbm.at[0, pl.ds(1, 3), 0], own_hbm, target_hbm, ids_hbm, table_hbm, counts_hbm,
        state_hbm.at[0, :, :, pl.ds(rows - 8, 8), :], mask_hbm.at[0, pl.ds(rows - 8, 8), :],
    )
    places = (surface_ref, own_ref, target_ref, ids_ref, table_ref, counts_ref, edge_ref, sea_edge_ref)
    fetches = [
        pltpu.make_async_copy(source, place, copies.at[i])
        for i, (source, place) in enumerate(zip(sources, places))
    ]
    outer = pl.ds(cols - LANES, LANES)
    for_fold = [
        pltpu.make_async_copy(state_hbm.at[0, v, :, :, outer], columns_ref.at[i], column_copies.at[i])
        for i, v in enumerate((0, 2, 3))
    ] + [pltpu.make_async_copy(mask_hbm.at[0, :, outer], mask_ref, column_copies.at[3])]
    northern = lax.axis_index("ty") == lax.axis_size("ty") - 1
    folds = jnp.logical_and(lax.axis_index("comp") == comps - 1, northern)
    for fetch in fetches:
        fetch.start()

    @pl.when(folds)
    def _():
        for fetch in for_fold:
            fetch.start()

    for fetch in fetches:
        fetch.wait()
    slab_rows = slab1_ref.shape[0]
    tall = halo_rows(levels) * (cols // LANES)
    put_rows(up_ref, slab_rows, levels, cols, lambda v, l: edge_ref.at[v, l], sea_edge_ref, 7, 6)

    @pl.when(folds)
    def _():
        for fetch in for_fold:
            fetch.wait()
        places = {0: 0, 2: 1, 3: 2}
        fold_ref[...] = turned_columns(
            levels, rows, lambda v, l: columns_ref[places[v], l], mask_ref[...], LANES - 2
        )

    @pl.when(jnp.logical_not(folds))
    def _():
        fold_ref[...] = jnp.zeros_like(fold_ref)

    up_ref[slab_rows + tall :, :] = fold_ref[...]
    slab3_ref[slab_rows:, :] = fold_ref[...]
    split_surface(surface_ref, halves_ref, rows, cols)
    refs = (own_ref, target_ref, ids_ref, table_ref, counts_ref, halves_ref, cells_ref, picked_ref, parts_ref)
    for n, out in ((3, slab3_ref), (1, slab1_ref), (2, up_ref)):
        gather_partner(n, rows, cols, comps, refs, out)


def gather_scratch(rows, cols, slots, stacked):
    return [
        pltpu.VMEM((6 * rows, cols) if stacked else (3 * rows, 2 * cols), BF16),
        pltpu.VMEM((slots // LANES, LANES), I32),
        pltpu.VMEM((slots // LANES, LANES), I32),
        pltpu.VMEM((3 * slots // LANES * 8, LANES), F32),
    ]


def first_side(model_state, slot_arrays, sea_mask, comps):
    levels, rows, cols = model_state.shape[2:]
    near, slots = slot_arrays[0].shape[2:]
    table_shape = slot_arrays[3].shape
    slab = CHANNELS * slots // LANES
    height = halo_rows(levels)
    heights = (slab, slab + height * (cols // LANES) + height, slab + height, height)
    vmem = pl.BlockSpec(memory_space=pltpu.VMEM)
    arrays = (model_state, *slot_arrays, sea_mask)
    return pl.pallas_call(
        functools.partial(first_body, levels, rows, cols, comps),
        in_specs=[pl.BlockSpec(memory_space=pltpu.HBM)] * len(arrays),
        out_specs=[vmem] * len(heights),
        out_shape=[jax.ShapeDtypeStruct((h, LANES), F32) for h in heights],
        scratch_shapes=[pltpu.VMEM((3, rows, cols), F32)]
        + [pltpu.VMEM((1, 1, near, slots), I32)] * 3
        + [pltpu.VMEM(table_shape, F32), pltpu.VMEM((1, 1, near), I32)]
        + [
            pltpu.VMEM((4, levels, 8, cols), F32),
            pltpu.VMEM((8, cols), I32),
            pltpu.VMEM((rows, LANES), I32),
            pltpu.VMEM((3, levels, rows, LANES), F32),
        ]
        + gather_scratch(rows, cols, slots, True)
        + [pltpu.SemaphoreType.DMA((8,)), pltpu.SemaphoreType.DMA((4,))],
        compiler_params=pltpu.CompilerParams(vmem_limit_bytes=VMEM_BYTES),
    )(*(pltpu.with_memory_space_constraint(array, pltpu.HBM) for array in arrays))


def second_body(
    levels, rows, cols, comps, y_pair,
    state_ref, own_ref, target_ref, ids_ref, table_ref, counts_ref, fold_ref, mask_hbm,
    slab0_ref, down_ref, high_ref, low_ref, pair_ref,
    halves_ref, cells_ref, picked_ref, parts_ref, mask_ref, copied,
):
    fetch = pltpu.make_async_copy(mask_hbm, mask_ref, copied)
    fetch.start()
    split_surface(state_ref.at[0, pl.ds(1, 3), 0], halves_ref, rows, cols)
    refs = (own_ref, target_ref, ids_ref, table_ref, counts_ref, halves_ref, cells_ref, picked_ref, parts_ref)
    gather_partner(0, rows, cols, comps, refs, slab0_ref)
    fetch.wait()
    put_rows(down_ref, 0, levels, cols, lambda v, l: state_ref.at[0, v, l], mask_ref.at[0], 0, 1)
    down_ref[halo_rows(levels) * (cols // LANES) :, :] = fold_ref[...]
    index_y = lax.axis_index("ty")
    high_used = index_y == 0 if y_pair else index_y >= 0
    low_used = index_y > 0 if y_pair else index_y >= 0

    def columns(start, begin):
        cut = slice(start, start + LANES)
        return turned_columns(levels, rows, lambda v, l: state_ref[0, v, l, :, cut], mask_ref[0, :, cut], begin)

    @pl.when(high_used)
    def _():
        highest = columns(cols - LANES, LANES - 2)
        high_ref[...] = highest
        pair_ref[...] = highest

    @pl.when(jnp.logical_not(high_used))
    def _():
        high_ref[...] = jnp.zeros_like(high_ref)

    @pl.when(low_used)
    def _():
        lowest = columns(0, 0)
        low_ref[...] = lowest
        pair_ref[...] = lowest

    @pl.when(jnp.logical_not(low_used))
    def _():
        low_ref[...] = jnp.zeros_like(low_ref)


def second_side(model_state, slot_arrays, fold, sea_mask, comps, y_pair):
    levels, rows, cols = model_state.shape[2:]
    slots = slot_arrays[0].shape[3]
    height = halo_rows(levels)
    heights = (CHANNELS * slots // LANES, height * (cols // LANES) + height, height, height, height)
    vmem = pl.BlockSpec(memory_space=pltpu.VMEM)
    return pl.pallas_call(
        functools.partial(second_body, levels, rows, cols, comps, y_pair),
        in_specs=[vmem] * 7 + [pl.BlockSpec(memory_space=pltpu.HBM)],
        out_specs=[vmem] * len(heights),
        out_shape=[jax.ShapeDtypeStruct((h, LANES), F32) for h in heights],
        scratch_shapes=gather_scratch(rows, cols, slots, False)
        + [pltpu.VMEM((1, rows, cols), I32), pltpu.SemaphoreType.DMA],
        compiler_params=pltpu.CompilerParams(vmem_limit_bytes=VMEM_BYTES),
    )(model_state, *slot_arrays, fold, pltpu.with_memory_space_constraint(sea_mask, pltpu.HBM))


def stencil_halos(
    levels, rows, cols, comps, count_x, count_y,
    state_ref, up_ref, down_ref, south_ref, north_ref, own_ref, fold_ref, far_refs, wave_ref, gains_ref,
    folded_ref, rows_ref, turned_ref,
):
    height = halo_rows(levels)
    parts = cols // LANES
    index_x = lax.axis_index("tx")
    index_y = lax.axis_index("ty")
    is_ocean = lax.axis_index("comp") == comps - 1
    last_y = index_y == count_y - 1
    has_west = jnp.where(jnp.logical_or(is_ocean, index_x > 0), 1.0, 0.0)
    has_east = jnp.where(jnp.logical_or(is_ocean, index_x < count_x - 1), 1.0, 0.0)
    has_south = jnp.where(index_y > 0, 1.0, 0.0)
    has_north = jnp.where(jnp.logical_or(is_ocean, jnp.logical_not(last_y)), 1.0, 0.0)
    drag = gains_ref[0, 2]
    mask_at = 4 * levels

    fold = fold_ref[pl.ds(index_x, 1), :]
    total = jnp.zeros((height, LANES), F32)
    up_start = up_ref.shape[0] - height * (parts + 1)
    sources = [(0, own_ref, 0), (-1, up_ref, up_start + height * parts), (1, down_ref, height * parts)]
    if north_ref.shape[0] > height:
        sources.append((2, north_ref, height))
    else:
        sources += [(shift, ref, 0) for shift, ref in zip(range(2, count_x - 1), far_refs)]
    for shift, ref, start in sources:
        at = lax.rem(index_x + shift + count_x, count_x)
        chosen = (iota((rows, rows), 0) + at * rows == fold).astype(F32)
        total += jnp.dot(
            ref[start : start + height, :], chosen,
            precision=lax.Precision.HIGHEST, preferred_element_type=F32,
        )
    folded_ref[...] = total

    line = iota((levels, LANES), 0)
    halves = jnp.zeros((levels, LANES), F32)
    for l in range(levels):
        halves = jnp.where(line == l, 0.5 * wave_ref[0, l], halves)

    def keeping(sea_values, drags):
        return jnp.where(is_ocean, sea_values, 1.0 - drags * (1.0 - sea_values))

    drags = jnp.where(line == 0, drag, 0.0)

    def by_level(ref, start, q):
        return ref[start + q * levels : start + (q + 1) * levels, :]

    for side, (ref, begin, sign, has) in enumerate(
        ((up_ref, up_start, 1.0, has_west), (down_ref, 0, -1.0, has_east))
    ):
        for p in range(parts):
            start = begin + p * height
            kept = keeping(ref[start + mask_at : start + mask_at + 1, :], drags)
            fixed = kept * (by_level(ref, start, EDGE_VELOCITY) + sign * halves * by_level(ref, start, SECOND_P))
            inner = rows - 1 if side else 0
            own = jnp.concatenate(
                [state_ref[0, 0, l, inner : inner + 1, p * LANES : (p + 1) * LANES] for l in range(levels)], axis=0
            )
            rows_ref[side, p, 0] = has * by_level(ref, start, EDGE_P)
            rows_ref[side, p, 1] = has * by_level(ref, start, EDGE_T)
            rows_ref[side, p, 2] = has * (fixed - sign * kept * halves * own)

    even = lambda ref: ref[pl.ds(0, levels, stride=2), :]
    odd = lambda ref: ref[pl.ds(1, levels, stride=2), :]
    north = [
        jnp.where(last_y, jnp.where(is_ocean, folded, 0.0), low)
        for folded, low in (
            (odd(folded_ref), even(north_ref)),
            (even(folded_ref), odd(north_ref)),
            (-by_level(folded_ref, 0, EDGE_VELOCITY), by_level(north_ref, 0, EDGE_VELOCITY)),
            (by_level(folded_ref, 0, EDGE_T), by_level(north_ref, 0, EDGE_T)),
            (folded_ref[mask_at : mask_at + 1, :], north_ref[mask_at : mask_at + 1, :]),
        )
    ]
    south = [
        odd(south_ref), even(south_ref), by_level(south_ref, 0, EDGE_VELOCITY), by_level(south_ref, 0, EDGE_T),
        south_ref[mask_at : mask_at + 1, :],
    ]
    fill = jnp.zeros((LANES - 4 * levels, LANES), F32)
    for side, ((edge, second, velocity, tracer, sea), sign, has) in enumerate(
        ((south, 1.0, has_south), (north, -1.0, has_north))
    ):
        kept = keeping(sea, drags)
        fixed = has * kept * (velocity + sign * halves * second)
        turned_ref[side] = jnp.concatenate(
            [has * edge, has * tracer, fixed, has * kept * halves, fill], axis=0
        ).T


def stencil_levels(
    rows, cols, comps, begin, end, state_ref, mask_ref, rows_ref, turned_ref, wave_ref, spread_ref, gains_ref,
    pad_ref, news_ref, after,
):
    levels = state_ref.shape[2]
    parts = cols // LANES
    is_ocean = lax.axis_index("comp") == comps - 1
    drag = gains_ref[0, 2]

    def keeping(sea_values, drags):
        return jnp.where(is_ocean, sea_values, 1.0 - drags * (1.0 - sea_values))

    sea = mask_ref[0].astype(F32)
    lane = iota((rows, LANES), 1)

    def cut(p):
        return slice(p * LANES, (p + 1) * LANES)

    def south_col(q, level):
        return pltpu.roll(turned_ref[0], lax.rem(LANES - q * levels - level, LANES), 1)

    def north_col(q, level):
        return pltpu.roll(turned_ref[1], LANES - 1 - q * levels - level, 1)

    def from_south(field, edge):
        moved = [pltpu.roll(t, 1, 1) for t in field]
        return [jnp.where(lane == 0, low, t) for low, t in zip([edge] + moved[:-1], moved)]

    def from_north(field, edge):
        moved = [pltpu.roll(t, LANES - 1, 1) for t in field]
        return [jnp.where(lane == LANES - 1, high, t) for high, t in zip(moved[1:] + [edge], moved)]

    def one_level(level, carry):
        half = 0.5 * wave_ref[0, level]
        spread = spread_ref[0, level]
        level_drag = jnp.where(level == 0, drag, 0.0)
        shift = jnp.minimum(level, 0)

        def padded(which, q, field):
            both = []
            for p in range(parts):
                pad_ref[which, p, 8 : 8 + rows, :] = field[p]
                pad_ref[which, p, 7:8, :] = rows_ref[0, p, q, pl.ds(level, 1), :]
                pad_ref[which, p, 8 + rows : 9 + rows, :] = rows_ref[1, p, q, pl.ds(level, 1), :]
                both.append((pad_ref[which, p, pl.ds(7 + shift, rows), :], pad_ref[which, p, pl.ds(9 + shift, rows), :]))
            return both

        pressure, zonal, meridional, tracer = (
            [state_ref[0, v, level, :, cut(p)] for p in range(parts)] for v in range(4)
        )
        keep = [keeping(sea[:, cut(p)], level_drag) for p in range(parts)]
        new_zonal = [
            m * (u - half * (e - w)) for m, u, (w, e) in zip(keep, zonal, padded(0, 0, pressure))
        ]
        new_meridional = [
            m * (v - half * (n - s))
            for m, v, n, s in zip(
                keep, meridional,
                from_north(pressure, north_col(0, level)), from_south(pressure, south_col(0, level)),
            )
        ]
        new_tracer = [
            t + spread * jnp.where(is_ocean, sea[:, cut(p)], 1.0) * (e + w + n + s - 4.0 * t)
            for p, t, (w, e), n, s in zip(
                range(parts), tracer, padded(1, 1, tracer),
                from_north(tracer, north_col(1, level)), from_south(tracer, south_col(1, level)),
            )
        ]
        south_v = south_col(2, level) - south_col(3, level) * pressure[0]
        north_v = north_col(2, level) + north_col(3, level) * pressure[-1]
        new_pressure = [
            q - half * (e - w + n - s)
            for q, (w, e), n, s in zip(
                pressure, padded(2, 2, new_zonal),
                from_north(new_meridional, north_v), from_south(new_meridional, south_v),
            )
        ]
        for p in range(parts):
            for v, field in enumerate((new_pressure, new_zonal, new_meridional, new_tracer)):
                news_ref[v, level - begin, :, cut(p)] = field[p]
        after(level)
        return carry

    lax.fori_loop(begin, end, one_level, 0)


def deep_body(
    sizes, begin,
    state_ref, mask_ref, up_ref, down_ref, south_ref, north_ref, own_ref, fold_ref,
    wave_ref, spread_ref, gains_ref, *rest,
):
    levels, rows, cols, comps, count_x, count_y = sizes
    far_refs, (news_ref, rows_ref, turned_ref, folded_ref, pad_ref) = rest[:-5], rest[-5:]
    stencil_halos(
        *sizes, state_ref, up_ref, down_ref, south_ref, north_ref, own_ref, fold_ref, far_refs, wave_ref, gains_ref,
        folded_ref, rows_ref, turned_ref,
    )
    stencil_levels(
        rows, cols, comps, begin, levels, state_ref, mask_ref, rows_ref, turned_ref, wave_ref, spread_ref, gains_ref,
        pad_ref, news_ref, lambda level: None,
    )


def upper_body(
    sizes, end, begun_ref, state_ref, mask_ref, rows_ref, turned_ref, wave_ref, spread_ref, gains_ref,
    out_ref, new_surface_ref, old_surface_ref, pad_ref, news_ref, stores,
):
    levels, rows, cols, comps, count_x, count_y = sizes

    def store(l, v):
        return pltpu.make_async_copy(news_ref.at[v, l], out_ref.at[0, v, l], stores.at[l, v])

    def after(level):
        for v in range(4):
            store(level, v).start()

    stencil_levels(
        rows, cols, comps, 0, end, state_ref, mask_ref, rows_ref, turned_ref, wave_ref, spread_ref, gains_ref,
        pad_ref, news_ref, after,
    )
    for v in range(3):
        new_surface_ref[v] = news_ref[v + 1, 0]
        old_surface_ref[v] = state_ref[0, v + 1, 0]
    for l in range(end):
        for v in range(4):
            store(l, v).wait()


def deep_levels(model_state, sea_mask, halos, fars, fold_map, wave_speed, diffusivity, gains, sizes, begin):
    levels, rows, cols, comps, count_x, count_y = sizes
    parts = cols // LANES
    fold = fold_map.reshape(count_x, rows)
    vmem = pl.BlockSpec(memory_space=pltpu.VMEM)
    scalar = pl.BlockSpec(memory_space=pltpu.SMEM)
    shapes = ((4, levels - begin, rows, cols), (2, parts, 3, levels, LANES), (2, rows, LANES))
    return pl.pallas_call(
        functools.partial(deep_body, sizes, begin),
        in_specs=[vmem] * 8 + [scalar] * 3 + [vmem] * len(fars),
        out_specs=[vmem] * 3,
        out_shape=[jax.ShapeDtypeStruct(shape, F32) for shape in shapes],
        scratch_shapes=[
            pltpu.VMEM((halo_rows(levels), LANES), F32),
            pltpu.VMEM((3, parts, rows + 16, LANES), F32),
        ],
        compiler_params=pltpu.CompilerParams(vmem_limit_bytes=VMEM_BYTES),
    )(model_state, sea_mask, *halos, fold, wave_speed, diffusivity, gains, *fars)


def upper_levels(begun, model_state, sea_mask, edge_rows, edge_columns, wave_speed, diffusivity, gains, sizes, end):
    levels, rows, cols, comps, count_x, count_y = sizes
    vmem = pl.BlockSpec(memory_space=pltpu.VMEM)
    scalar = pl.BlockSpec(memory_space=pltpu.SMEM)
    anywhere = pl.BlockSpec(memory_space=pl.ANY)
    surface = jax.ShapeDtypeStruct((3, rows, cols), F32)
    return pl.pallas_call(
        functools.partial(upper_body, sizes, end),
        in_specs=[anywhere] + [vmem] * 4 + [scalar] * 3,
        out_specs=[anywhere, vmem, vmem],
        out_shape=[jax.ShapeDtypeStruct(begun.shape, F32), surface, surface],
        scratch_shapes=[
            pltpu.VMEM((3, cols // LANES, rows + 16, LANES), F32),
            pltpu.VMEM((4, end, rows, cols), F32),
            pltpu.SemaphoreType.DMA((end, 4)),
        ],
        input_output_aliases={0: 0},
        compiler_params=pltpu.CompilerParams(vmem_limit_bytes=VMEM_BYTES),
    )(begun, model_state, sea_mask, edge_rows, edge_columns, wave_speed, diffusivity, gains)


def add_slots(rows, cols, groups, slab_ref, total_refs, chunks, plan, block, upright):
    row_ids = packed_ids(rows)
    col_ids = packed_ids(cols)
    lane = iota((1, LANES), 1)
    one = jnp.ones((), BF16)
    zero = jnp.zeros((), BF16)

    def one_chunk(total_ref, chunk):
        n, first, low_slot, high_slot = plan(chunk)
        start = n * (CHANNELS * groups) + first
        if upright:
            at = slab_ref[pl.ds(start + 4 * groups, DEPTH), :].astype(I32) % cols
            at = jnp.concatenate([at.astype(F32), jnp.zeros((LANES - DEPTH, LANES), F32)], axis=0).T
            lanes = iota((LANES, cols), 1).astype(F32)
        for begin in range(0, DEPTH, block):
            columns, spreads = [], []
            for g in range(begin, begin + block):
                cells = slab_ref[pl.ds(start + 4 * groups + g, 1), :].astype(I32)
                slot = lane + (first + g) * LANES
                mine = jnp.logical_and(slot >= low_slot, slot < high_slot)
                row = spread_row(jnp.where(mine, cells // cols, -1)).astype(F32).astype(BF16)
                if upright:
                    columns.append(jnp.where(lanes == at[:, g : g + 1], 1.0, 0.0).astype(BF16))
                else:
                    col = spread_row(cells % cols).astype(F32).astype(BF16)
                    columns.append(jnp.where(col_ids == col[None], one, zero).reshape(cols, LANES))
                in_row = row_ids == row[None]
                highs, lows = [], []
                for v in range(4):
                    value = spread_row(slab_ref[pl.ds(start + v * groups + g, 1), :])
                    high, low = split_two(value)
                    highs.append(jnp.where(in_row, high[None], zero).reshape(rows, LANES))
                    lows.append(jnp.where(in_row, low[None], zero).reshape(rows, LANES))
                spreads.append(jnp.concatenate(highs + lows, axis=0))
            side = 0 if upright else 1
            total_ref[...] += lax.dot_general(
                jnp.concatenate(spreads, axis=1), jnp.concatenate(columns, axis=side), (((1,), (side,)), ((), ())),
                preferred_element_type=F32,
            )

    done = 0
    for total_ref in total_refs:
        total_ref[...] = jnp.zeros_like(total_ref)

        def some(c, carry, total_ref=total_ref):
            one_chunk(total_ref, c)
            return carry

        step = chunks // len(total_refs)
        lax.fori_loop(done, done + step, some, 0)
        done = done + step


def halves_added(total_ref, rows):
    return total_ref[: 4 * rows] + total_ref[4 * rows :]


def own_body(rows, cols, comps, groups, slab_ref, sent_ref, total_ref):
    here = lax.axis_index("comp")
    pieces = groups // DEPTH
    near = slab_ref.shape[0] // (CHANNELS * groups)
    bounds = share_bounds(groups * LANES, comps - 1)
    is_ocean = here == comps - 1
    beside = here == comps - 2

    def plan(chunk):
        n = jnp.where(is_ocean, chunk, chunk // pieces)
        first = jnp.where(is_ocean, groups - DEPTH, chunk % pieces * DEPTH)
        return n, first, jnp.where(is_ocean, bounds[comps - 2], 0), groups * LANES

    chunks = jnp.where(is_ocean, near, jnp.where(beside, near * pieces, 0))
    add_slots(rows, cols, groups, slab_ref, [total_ref], chunks, plan, 4, True)
    sent_ref[...] = halves_added(total_ref, rows)


def other_body(
    rows, cols, comps, groups, slab_ref, before_ref, deep_ref, kept_ref, sent_ref, state_ref,
    first_ref, second_ref, copies,
):
    here = lax.axis_index("comp")
    pieces = groups // DEPTH
    near = slab_ref.shape[0] // (CHANNELS * groups)
    bounds = share_bounds(groups * LANES, comps - 1)
    is_ocean = here == comps - 1
    beside = here == comps - 2
    for_two = here == comps - 3
    middle = bounds[1] // LANES // 4 * 4
    count = deep_ref.shape[1]
    stores = [
        pltpu.make_async_copy(
            deep_ref.at[v], state_ref.at[0, v, pl.ds(state_ref.shape[2] - count, count)], copies.at[v]
        )
        for v in range(4)
    ]
    for store in stores:
        store.start()

    def plan(chunk):
        mine = chunk >= near
        n = jnp.where(for_two, chunk % near, chunk // pieces)
        first = jnp.where(for_two, jnp.where(mine, middle, 0), chunk % pieces * DEPTH)
        low_slot = jnp.where(jnp.logical_and(for_two, mine), bounds[1], 0)
        high_slot = jnp.where(for_two, jnp.where(mine, bounds[2], bounds[1]), groups * LANES)
        return n, first, low_slot, high_slot

    chunks = jnp.where(here == 0, 0, near * pieces)
    totals = [first_ref, second_ref]
    add_slots(rows, cols, groups, slab_ref, totals, chunks, plan, 4, False)
    for start in range(0, 4 * rows, rows):
        first = first_ref[start : start + rows] + first_ref[start + 4 * rows : start + 5 * rows]
        second = second_ref[start : start + rows] + second_ref[start + 4 * rows : start + 5 * rows]
        kept_ref[start : start + rows] = jnp.where(beside, 0.0, second) + jnp.where(is_ocean, first, 0.0)
        sent = jnp.where(is_ocean, 0.0, first) + jnp.where(beside, second, 0.0)
        sent_ref[start : start + rows] = sent + before_ref[start : start + rows]
    for store in stores:
        store.wait()


def scatter_own(arrived, rows, cols, comps, slots):
    vmem = pl.BlockSpec(memory_space=pltpu.VMEM)
    return pl.pallas_call(
        functools.partial(own_body, rows, cols, comps, slots // LANES),
        in_specs=[vmem],
        out_specs=vmem,
        out_shape=jax.ShapeDtypeStruct((4 * rows, cols), F32),
        scratch_shapes=[pltpu.VMEM((8 * rows, cols), F32)],
        compiler_params=pltpu.CompilerParams(vmem_limit_bytes=VMEM_BYTES),
    )(arrived)


def scatter_other(other, before, deep, state_shape, rows, cols, comps, slots):
    vmem = pl.BlockSpec(memory_space=pltpu.VMEM)
    sums = jax.ShapeDtypeStruct((4 * rows, cols), F32)
    return pl.pallas_call(
        functools.partial(other_body, rows, cols, comps, slots // LANES),
        in_specs=[vmem] * 3,
        out_specs=[vmem, vmem, pl.BlockSpec(memory_space=pl.ANY)],
        out_shape=[sums, sums, jax.ShapeDtypeStruct(state_shape, F32)],
        scratch_shapes=[pltpu.VMEM((8 * rows, cols), F32)] * 2 + [pltpu.SemaphoreType.DMA((4,))],
        compiler_params=pltpu.CompilerParams(vmem_limit_bytes=VMEM_BYTES),
    )(other, before, deep)


def finish_body(rows, comps, state_ref, new_ref, old_ref, kept_ref, came_ref, mask_ref, gains_ref, out_ref, news_ref, copies):
    is_ocean = lax.axis_index("comp") == comps - 1
    tendency = jnp.where(is_ocean, mask_ref[0].astype(F32), 1.0)
    sums = [kept_ref[v * rows : (v + 1) * rows, :] + came_ref[v * rows : (v + 1) * rows, :] for v in range(4)]
    saves = []
    for v, total, gain in ((0, sums[1], 1), (1, sums[2], 1), (2, sums[0], 0)):
        news_ref[v] = new_ref[v] + tendency * gains_ref[0, gain] * (total - sums[3] * old_ref[v])
        saves.append(pltpu.make_async_copy(news_ref.at[v], out_ref.at[0, v + 1, 0], copies.at[v]))
        saves[-1].start()
    for save in saves:
        save.wait()


def finish(state, new_surface, old_surface, kept, came, sea_mask, gains, comps):
    rows, cols = state.shape[3:]
    vmem = pl.BlockSpec(memory_space=pltpu.VMEM)
    anywhere = pl.BlockSpec(memory_space=pl.ANY)
    return pl.pallas_call(
        functools.partial(finish_body, rows, comps),
        in_specs=[anywhere] + [vmem] * 5 + [pl.BlockSpec(memory_space=pltpu.SMEM)],
        out_specs=anywhere,
        out_shape=jax.ShapeDtypeStruct(state.shape, F32),
        scratch_shapes=[pltpu.VMEM((3, rows, cols), F32), pltpu.SemaphoreType.DMA((3,))],
        input_output_aliases={0: 0},
        compiler_params=pltpu.CompilerParams(vmem_limit_bytes=VMEM_BYTES),
    )(state, new_surface, old_surface, kept, came, sea_mask, gains)


def shards(
    model_state, sea_mask, wave_speed, diffusivity, surface_gains, area_table,
    own_cells, target_cells, weight_ids, pair_counts, fold_map,
):
    comps, count_x, count_y = (lax.axis_size(a) for a in ("comp", "tx", "ty"))
    positions = count_x * count_y
    rows, cols = model_state.shape[3:]
    slots = own_cells.shape[3]
    slot_arrays = (own_cells, target_cells, weight_ids, area_table.reshape(-1, LANES), pair_counts)

    def along(block, shift):
        return lax.ppermute(block, ("tx", "ty"), [(s, (s + shift) % positions) for s in range(positions)])

    y_pair = count_y == 2
    slab_rows = CHANNELS * slots // LANES
    slab1, up, slab3, fold = first_side(model_state, slot_arrays, sea_mask, comps)
    slab3 = along(slab3, 1 + count_y)
    slab1 = along(slab1, 1)
    up = along(up, count_y)
    slab0, down, high, low, pair = second_side(model_state, slot_arrays, fold, sea_mask, comps, y_pair)
    arrived = jnp.concatenate([slab0, slab1, up[:slab_rows], slab3[:slab_rows]])
    other = lax.ppermute(arrived, "comp", [(g, g ^ 2) for g in range(comps)])

    down = along(down, -count_y)
    fars = []
    if y_pair and count_x == 4:
        south = north = lax.ppermute(jnp.concatenate([pair, slab3[slab_rows:]]), "ty", [(0, 1), (1, 0)])
    else:
        south = lax.ppermute(high, "ty", [(j, j + 1) for j in range(count_y - 1)])
        north = lax.ppermute(low, "ty", [(j + 1, j) for j in range(count_y - 1)])
        for shift in range(2, count_x - 1):
            pairs = []
            for i in range(count_x):
                ends = [((comps - 1) * count_x + k) * count_y + count_y - 1 for k in ((i + shift) % count_x, i)]
                pairs.append(tuple(ends))
            fars.append(lax.ppermute(fold, ("comp", "tx", "ty"), pairs))

    sizes = (*model_state.shape[2:], comps, count_x, count_y)
    cut = sizes[0] // 2
    before = scatter_own(arrived, rows, cols, comps, slots)
    deep, edge_rows, edge_columns = deep_levels(
        model_state, sea_mask, (up, down, south, north, fold), fars, fold_map,
        wave_speed, diffusivity, surface_gains, sizes, cut,
    )
    kept, sent, begun = scatter_other(other, before, deep, model_state.shape, rows, cols, comps, slots)
    came = lax.ppermute(sent, "comp", [(g, g ^ 1) for g in range(comps)])
    new_state, new_surface, old_surface = upper_levels(
        begun, model_state, sea_mask, edge_rows, edge_columns, wave_speed, diffusivity, surface_gains, sizes, cut
    )
    return finish(new_state, new_surface, old_surface, kept, came, sea_mask, surface_gains, comps)


def solution(mesh):
    in_specs = (
        P("comp", None, None, "tx", "ty"),
        P("comp", "tx", "ty"),
        P("comp", None),
        P("comp", None),
        P("comp", None),
        P(),
        P("comp", ("tx", "ty"), None, None),
        P("comp", ("tx", "ty"), None, None),
        P("comp", ("tx", "ty"), None, None),
        P("comp", ("tx", "ty"), None),
        P(),
    )
    out_specs = P("comp", None, None, "tx", "ty")
    return jax.shard_map(shards, mesh=mesh, in_specs=in_specs, out_specs=out_specs, check_vma=False)
```

```python
import functools

import jax
import jax.numpy as jnp
from jax import lax
from jax.experimental import pallas as pl
from jax.experimental.pallas import tpu as pltpu
from jax.sharding import PartitionSpec as P

LANES = 128
DEPTH = 8
PACKED = 16
VMEM_BYTES = 28 * 1024 * 1024
F32 = jnp.float32
BF16 = jnp.bfloat16
I32 = jnp.int32
CHANNELS = 5

EDGE_P, SECOND_P, EDGE_VELOCITY, EDGE_T, MASK = range(5)


def iota(shape, dim):
    return lax.broadcasted_iota(I32, shape, dim)


def halo_rows(levels):
    return (4 * levels + 1 + 7) // 8 * 8


def split_two(values):
    high = values.astype(BF16)
    low = (values - high.astype(F32)).astype(BF16)
    return high, low


def packed_ids(count):
    ids = iota((count, LANES), 0).astype(F32).astype(BF16)
    return ids.reshape(count // PACKED, PACKED, LANES)


def spread_row(row):
    return jnp.broadcast_to(row, (PACKED, LANES))


def share_bounds(slots, shares):
    bounds = [0]
    for m in range(shares):
        bounds.append(bounds[-1] + (slots - m + shares - 1) // shares)
    return bounds


def slot_order(slots, shares, sort, half):
    place = iota((8, LANES), 0) * LANES + iota((8, LANES), 1) + half * 8 * LANES
    source = jnp.zeros((8, LANES), I32)
    bounds = share_bounds(slots, shares)
    for m in range(shares):
        inside = jnp.logical_and(place >= bounds[m], place < bounds[m + 1])
        source = jnp.where(inside, (place - bounds[m]) * shares + m, source)
    return jnp.where(sort, source, place)


def pick_rows(ref, n, source):
    total = jnp.zeros((8, LANES), I32)
    for t in range(ref.shape[3] // LANES):
        row = jnp.broadcast_to(ref[0, 0, n : n + 1, t * LANES : (t + 1) * LANES], (8, LANES))
        picked = jnp.take_along_axis(row, source % LANES, axis=1)
        total = jnp.where(source // LANES == t, picked, total)
    return total


def gather_partner(n, rows, cols, comps, refs, out):
    own_ref, target_ref, ids_ref, table_ref, counts_ref, halves_ref, cells_ref, picked_ref, parts_ref = refs
    slots = own_ref.shape[3]
    groups = slots // LANES
    is_ocean = lax.axis_index("comp") == comps - 1

    @pl.when(is_ocean)
    def _():
        for half in range(groups // 8):
            source = slot_order(slots, comps - 1, True, half)
            at = slice(half * 8, (half + 1) * 8)
            cells_ref[at, :] = pick_rows(own_ref, n, source)
            picked_ref[at, :] = pick_rows(ids_ref, n, source)
            out[4 * groups + half * 8 : 4 * groups + (half + 1) * 8, :] = pick_rows(target_ref, n, source).astype(F32)

    @pl.when(jnp.logical_not(is_ocean))
    def _():
        for g in range(groups):
            cut = slice(g * LANES, (g + 1) * LANES)
            cells_ref[g : g + 1, :] = own_ref[0, 0, n : n + 1, cut]
            picked_ref[g : g + 1, :] = ids_ref[0, 0, n : n + 1, cut]
            out[4 * groups + g : 4 * groups + g + 1, :] = target_ref[0, 0, n : n + 1, cut].astype(F32)

    count = jnp.broadcast_to(counts_ref[0, :, n : n + 1], (8, LANES))
    for half in range(groups // 8):
        source = slot_order(slots, comps - 1, is_ocean, half)
        ids = picked_ref[half * 8 : (half + 1) * 8, :]
        weight = jnp.zeros((8, LANES), F32)
        for t in range(table_ref.shape[0]):
            table = jnp.broadcast_to(table_ref[t : t + 1, :], (8, LANES))
            looked = jnp.take_along_axis(table, ids % LANES, axis=1)
            weight = jnp.where(ids // LANES == t, looked, weight)
        out[3 * groups + half * 8 : 3 * groups + (half + 1) * 8, :] = jnp.where(source < count, weight, 0.0)
    col_ids = packed_ids(cols)
    row_ids = iota((rows, LANES), 0)
    one = jnp.ones((), BF16)
    zero = jnp.zeros((), BF16)
    wide, subs = 2, 4

    def some(c, carry):
        for sub in range(subs):
            first = (c * subs + sub) * wide
            cells = [cells_ref[pl.ds(first + g, 1), :] for g in range(wide)]
            picks = []
            for cell in cells:
                col = spread_row(cell % cols).astype(F32).astype(BF16)
                picks.append(jnp.where(col_ids == col[None], one, zero).reshape(cols, LANES))
            picks = jnp.concatenate(picks, axis=1)
            if halves_ref.shape[1] > cols:
                picks = jnp.concatenate([picks, picks], axis=0)
                found = jnp.dot(halves_ref[...], picks, preferred_element_type=F32)
            else:
                found = jnp.dot(halves_ref[...], picks, preferred_element_type=F32)
                found = found[: 3 * rows] + found[3 * rows :]
            for g in range(wide):
                in_row = row_ids == cells[g] // cols
                for place, v in enumerate((2, 0, 1)):
                    block = found[v * rows : (v + 1) * rows, g * LANES : (g + 1) * LANES]
                    block = jnp.where(in_row, block, 0.0).reshape(rows // 8, 8, LANES)
                    start = pl.multiple_of((place * groups + first + g) * 8, 8)
                    parts_ref[pl.ds(start, 8), :] = jnp.sum(block, axis=0)
        return carry

    lax.fori_loop(0, groups // (subs * wide), some, 0)
    weight = out[3 * groups : 4 * groups, :]
    for place in range(3):
        total = jnp.zeros((groups, LANES), F32)
        for i in range(8):
            total += parts_ref[pl.ds(place * groups * 8 + i, groups, stride=8), :]
        out[place * groups : (place + 1) * groups, :] = total * weight


def split_surface(surface_ref, halves_ref, rows, cols):
    for v in range(3):
        high, low = split_two(surface_ref[v])
        if halves_ref.shape[1] > cols:
            halves_ref[v * rows : (v + 1) * rows, :cols] = high
            halves_ref[v * rows : (v + 1) * rows, cols:] = low
        else:
            halves_ref[v * rows : (v + 1) * rows, :] = high
            halves_ref[(v + 3) * rows : (v + 4) * rows, :] = low


def put_rows(ref, start, levels, cols, fields, sea, edge, second):
    height = halo_rows(levels)
    for p in range(cols // LANES):
        cut = slice(p * LANES, (p + 1) * LANES)
        base = start + p * height
        ref[base + 4 * levels : base + height, :] = jnp.zeros((height - 4 * levels, LANES), F32)
        ref[base + 4 * levels : base + 4 * levels + 1, :] = sea[edge : edge + 1, cut].astype(F32)
        for q, v, at in ((EDGE_P, 0, edge), (SECOND_P, 0, second), (EDGE_VELOCITY, 1, edge), (EDGE_T, 3, edge)):
            for l in range(levels):
                row = base + q * levels + l
                ref[row : row + 1, :] = fields(v, l)[at : at + 1, cut]


def turned_columns(levels, rows, fields, sea, begin):
    edge = 1 if begin else 0
    lanes = iota((rows, LANES), 1)
    total = pltpu.roll(sea.astype(F32), (4 * levels - begin - edge) % LANES, 1)
    for l in range(levels):
        total = jnp.where(lanes // 2 == l, pltpu.roll(fields(0, l), (2 * l - begin) % LANES, 1), total)
        for q, v in ((EDGE_VELOCITY, 2), (EDGE_T, 3)):
            at = q * levels + l
            moved = pltpu.roll(fields(v, l), (at - begin - edge) % LANES, 1)
            total = jnp.where(lanes == at, moved, total)
    return total.T[: halo_rows(levels)]


def first_body(
    levels, rows, cols, comps,
    state_hbm, own_hbm, target_hbm, ids_hbm, table_hbm, counts_hbm, mask_hbm,
    slab1_ref, up_ref, slab3_ref, fold_ref,
    surface_ref, own_ref, target_ref, ids_ref, table_ref, counts_ref, edge_ref, sea_edge_ref, mask_ref, columns_ref,
    halves_ref, cells_ref, picked_ref, parts_ref, copies, column_copies,
):
    sources = (
        state_hbm.at[0, pl.ds(1, 3), 0], own_hbm, target_hbm, ids_hbm, table_hbm, counts_hbm,
        state_hbm.at[0, :, :, pl.ds(rows - 8, 8), :], mask_hbm.at[0, pl.ds(rows - 8, 8), :],
    )
    places = (surface_ref, own_ref, target_ref, ids_ref, table_ref, counts_ref, edge_ref, sea_edge_ref)
    fetches = [
        pltpu.make_async_copy(source, place, copies.at[i])
        for i, (source, place) in enumerate(zip(sources, places))
    ]
    outer = pl.ds(cols - LANES, LANES)
    for_fold = [
        pltpu.make_async_copy(state_hbm.at[0, v, :, :, outer], columns_ref.at[i], column_copies.at[i])
        for i, v in enumerate((0, 2, 3))
    ] + [pltpu.make_async_copy(mask_hbm.at[0, :, outer], mask_ref, column_copies.at[3])]
    northern = lax.axis_index("ty") == lax.axis_size("ty") - 1
    folds = jnp.logical_and(lax.axis_index("comp") == comps - 1, northern)
    for fetch in fetches:
        fetch.start()

    @pl.when(folds)
    def _():
        for fetch in for_fold:
            fetch.start()

    for fetch in fetches:
        fetch.wait()
    slab_rows = slab1_ref.shape[0]
    tall = halo_rows(levels) * (cols // LANES)
    put_rows(up_ref, slab_rows, levels, cols, lambda v, l: edge_ref.at[v, l], sea_edge_ref, 7, 6)

    @pl.when(folds)
    def _():
        for fetch in for_fold:
            fetch.wait()
        places = {0: 0, 2: 1, 3: 2}
        fold_ref[...] = turned_columns(
            levels, rows, lambda v, l: columns_ref[places[v], l], mask_ref[...], LANES - 2
        )

    @pl.when(jnp.logical_not(folds))
    def _():
        fold_ref[...] = jnp.zeros_like(fold_ref)

    up_ref[slab_rows + tall :, :] = fold_ref[...]
    slab3_ref[slab_rows:, :] = fold_ref[...]
    split_surface(surface_ref, halves_ref, rows, cols)
    refs = (own_ref, target_ref, ids_ref, table_ref, counts_ref, halves_ref, cells_ref, picked_ref, parts_ref)
    for n, out in ((3, slab3_ref), (1, slab1_ref), (2, up_ref)):
        gather_partner(n, rows, cols, comps, refs, out)


def gather_scratch(rows, cols, slots, stacked):
    return [
        pltpu.VMEM((6 * rows, cols) if stacked else (3 * rows, 2 * cols), BF16),
        pltpu.VMEM((slots // LANES, LANES), I32),
        pltpu.VMEM((slots // LANES, LANES), I32),
        pltpu.VMEM((3 * slots // LANES * 8, LANES), F32),
    ]


def first_side(model_state, slot_arrays, sea_mask, comps):
    levels, rows, cols = model_state.shape[2:]
    near, slots = slot_arrays[0].shape[2:]
    table_shape = slot_arrays[3].shape
    slab = CHANNELS * slots // LANES
    height = halo_rows(levels)
    heights = (slab, slab + height * (cols // LANES) + height, slab + height, height)
    vmem = pl.BlockSpec(memory_space=pltpu.VMEM)
    arrays = (model_state, *slot_arrays, sea_mask)
    return pl.pallas_call(
        functools.partial(first_body, levels, rows, cols, comps),
        in_specs=[pl.BlockSpec(memory_space=pltpu.HBM)] * len(arrays),
        out_specs=[vmem] * len(heights),
        out_shape=[jax.ShapeDtypeStruct((h, LANES), F32) for h in heights],
        scratch_shapes=[pltpu.VMEM((3, rows, cols), F32)]
        + [pltpu.VMEM((1, 1, near, slots), I32)] * 3
        + [pltpu.VMEM(table_shape, F32), pltpu.VMEM((1, 1, near), I32)]
        + [
            pltpu.VMEM((4, levels, 8, cols), F32),
            pltpu.VMEM((8, cols), I32),
            pltpu.VMEM((rows, LANES), I32),
            pltpu.VMEM((3, levels, rows, LANES), F32),
        ]
        + gather_scratch(rows, cols, slots, True)
        + [pltpu.SemaphoreType.DMA((8,)), pltpu.SemaphoreType.DMA((4,))],
        compiler_params=pltpu.CompilerParams(vmem_limit_bytes=VMEM_BYTES),
    )(*(pltpu.with_memory_space_constraint(array, pltpu.HBM) for array in arrays))


def second_body(
    levels, rows, cols, comps, y_pair,
    state_ref, own_ref, target_ref, ids_ref, table_ref, counts_ref, fold_ref, mask_hbm,
    slab0_ref, down_ref, high_ref, low_ref, pair_ref, sent_ref,
    halves_ref, cells_ref, picked_ref, parts_ref, mask_ref, total_ref, copied,
):
    fetch = pltpu.make_async_copy(mask_hbm, mask_ref, copied)
    fetch.start()
    split_surface(state_ref.at[0, pl.ds(1, 3), 0], halves_ref, rows, cols)
    refs = (own_ref, target_ref, ids_ref, table_ref, counts_ref, halves_ref, cells_ref, picked_ref, parts_ref)
    gather_partner(0, rows, cols, comps, refs, slab0_ref)
    fetch.wait()
    put_rows(down_ref, 0, levels, cols, lambda v, l: state_ref.at[0, v, l], mask_ref.at[0], 0, 1)
    down_ref[halo_rows(levels) * (cols // LANES) :, :] = fold_ref[...]
    index_y = lax.axis_index("ty")
    high_used = index_y == 0 if y_pair else index_y >= 0
    low_used = index_y > 0 if y_pair else index_y >= 0

    def columns(start, begin):
        cut = slice(start, start + LANES)
        return turned_columns(levels, rows, lambda v, l: state_ref[0, v, l, :, cut], mask_ref[0, :, cut], begin)

    @pl.when(high_used)
    def _():
        highest = columns(cols - LANES, LANES - 2)
        high_ref[...] = highest
        pair_ref[...] = highest

    @pl.when(jnp.logical_not(high_used))
    def _():
        high_ref[...] = jnp.zeros_like(high_ref)

    @pl.when(low_used)
    def _():
        lowest = columns(0, 0)
        low_ref[...] = lowest
        pair_ref[...] = lowest

    @pl.when(jnp.logical_not(low_used))
    def _():
        low_ref[...] = jnp.zeros_like(low_ref)

    add_own(rows, cols, comps, own_ref.shape[3] // LANES, slab0_ref, total_ref)
    sent_ref[...] = halves_added(total_ref, rows)


def second_side(model_state, slot_arrays, fold, sea_mask, comps, y_pair):
    levels, rows, cols = model_state.shape[2:]
    slots = slot_arrays[0].shape[3]
    height = halo_rows(levels)
    heights = (CHANNELS * slots // LANES, height * (cols // LANES) + height, height, height, height)
    vmem = pl.BlockSpec(memory_space=pltpu.VMEM)
    return pl.pallas_call(
        functools.partial(second_body, levels, rows, cols, comps, y_pair),
        in_specs=[vmem] * 7 + [pl.BlockSpec(memory_space=pltpu.HBM)],
        out_specs=[vmem] * (len(heights) + 1),
        out_shape=[jax.ShapeDtypeStruct((h, LANES), F32) for h in heights]
        + [jax.ShapeDtypeStruct((4 * rows, cols), F32)],
        scratch_shapes=gather_scratch(rows, cols, slots, False)
        + [pltpu.VMEM((1, rows, cols), I32), pltpu.VMEM((8 * rows, cols), F32), pltpu.SemaphoreType.DMA],
        compiler_params=pltpu.CompilerParams(vmem_limit_bytes=VMEM_BYTES),
    )(model_state, *slot_arrays, fold, pltpu.with_memory_space_constraint(sea_mask, pltpu.HBM))


def stencil_halos(
    levels, rows, cols, comps, count_x, count_y,
    state_ref, up_ref, down_ref, south_ref, north_ref, own_ref, fold_ref, far_refs, wave_ref, gains_ref,
    folded_ref, rows_ref, turned_ref,
):
    height = halo_rows(levels)
    parts = cols // LANES
    index_x = lax.axis_index("tx")
    index_y = lax.axis_index("ty")
    is_ocean = lax.axis_index("comp") == comps - 1
    last_y = index_y == count_y - 1
    has_west = jnp.where(jnp.logical_or(is_ocean, index_x > 0), 1.0, 0.0)
    has_east = jnp.where(jnp.logical_or(is_ocean, index_x < count_x - 1), 1.0, 0.0)
    has_south = jnp.where(index_y > 0, 1.0, 0.0)
    has_north = jnp.where(jnp.logical_or(is_ocean, jnp.logical_not(last_y)), 1.0, 0.0)
    drag = gains_ref[0, 2]
    mask_at = 4 * levels

    fold = fold_ref[pl.ds(index_x, 1), :]
    total = jnp.zeros((height, LANES), F32)
    up_start = up_ref.shape[0] - height * (parts + 1)
    sources = [(0, own_ref, 0), (-1, up_ref, up_start + height * parts), (1, down_ref, height * parts)]
    if north_ref.shape[0] > height:
        sources.append((2, north_ref, height))
    else:
        sources += [(shift, ref, 0) for shift, ref in zip(range(2, count_x - 1), far_refs)]
    for shift, ref, start in sources:
        at = lax.rem(index_x + shift + count_x, count_x)
        chosen = (iota((rows, rows), 0) + at * rows == fold).astype(F32)
        total += jnp.dot(
            ref[start : start + height, :], chosen,
            precision=lax.Precision.HIGHEST, preferred_element_type=F32,
        )
    folded_ref[...] = total

    line = iota((levels, LANES), 0)
    halves = jnp.zeros((levels, LANES), F32)
    for l in range(levels):
        halves = jnp.where(line == l, 0.5 * wave_ref[0, l], halves)

    def keeping(sea_values, drags):
        return jnp.where(is_ocean, sea_values, 1.0 - drags * (1.0 - sea_values))

    drags = jnp.where(line == 0, drag, 0.0)

    def by_level(ref, start, q):
        return ref[start + q * levels : start + (q + 1) * levels, :]

    for side, (ref, begin, sign, has) in enumerate(
        ((up_ref, up_start, 1.0, has_west), (down_ref, 0, -1.0, has_east))
    ):
        for p in range(parts):
            start = begin + p * height
            kept = keeping(ref[start + mask_at : start + mask_at + 1, :], drags)
            fixed = kept * (by_level(ref, start, EDGE_VELOCITY) + sign * halves * by_level(ref, start, SECOND_P))
            inner = rows - 1 if side else 0
            own = jnp.concatenate(
                [state_ref[0, 0, l, inner : inner + 1, p * LANES : (p + 1) * LANES] for l in range(levels)], axis=0
            )
            rows_ref[side, p, 0] = has * by_level(ref, start, EDGE_P)
            rows_ref[side, p, 1] = has * by_level(ref, start, EDGE_T)
            rows_ref[side, p, 2] = has * (fixed - sign * kept * halves * own)

    even = lambda ref: ref[pl.ds(0, levels, stride=2), :]
    odd = lambda ref: ref[pl.ds(1, levels, stride=2), :]
    north = [
        jnp.where(last_y, jnp.where(is_ocean, folded, 0.0), low)
        for folded, low in (
            (odd(folded_ref), even(north_ref)),
            (even(folded_ref), odd(north_ref)),
            (-by_level(folded_ref, 0, EDGE_VELOCITY), by_level(north_ref, 0, EDGE_VELOCITY)),
            (by_level(folded_ref, 0, EDGE_T), by_level(north_ref, 0, EDGE_T)),
            (folded_ref[mask_at : mask_at + 1, :], north_ref[mask_at : mask_at + 1, :]),
        )
    ]
    south = [
        odd(south_ref), even(south_ref), by_level(south_ref, 0, EDGE_VELOCITY), by_level(south_ref, 0, EDGE_T),
        south_ref[mask_at : mask_at + 1, :],
    ]
    fill = jnp.zeros((LANES - 4 * levels, LANES), F32)
    for side, ((edge, second, velocity, tracer, sea), sign, has) in enumerate(
        ((south, 1.0, has_south), (north, -1.0, has_north))
    ):
        kept = keeping(sea, drags)
        fixed = has * kept * (velocity + sign * halves * second)
        turned_ref[side] = jnp.concatenate(
            [has * edge, has * tracer, fixed, has * kept * halves, fill], axis=0
        ).T


def stencil_levels(
    rows, cols, comps, begin, end, state_ref, mask_ref, rows_ref, turned_ref, wave_ref, spread_ref, gains_ref,
    pad_refs, news_ref, after,
):
    levels = state_ref.shape[2]
    parts = cols // LANES
    is_ocean = lax.axis_index("comp") == comps - 1
    drag = gains_ref[0, 2]

    def keeping(sea_values, drags):
        return jnp.where(is_ocean, sea_values, 1.0 - drags * (1.0 - sea_values))

    deep = 16
    lane = iota((deep, LANES), 1)
    pressure_ref, tracer_ref, zonal_ref = pad_refs

    def cut(p):
        return slice(p * LANES, (p + 1) * LANES)

    def from_south(field, edge):
        moved = [pltpu.roll(t, 1, 1) for t in field]
        return [jnp.where(lane == 0, low, t) for low, t in zip([edge] + moved[:-1], moved)]

    def from_north(field, edge):
        moved = [pltpu.roll(t, LANES - 1, 1) for t in field]
        return [jnp.where(lane == LANES - 1, high, t) for high, t in zip(moved[1:] + [edge], moved)]

    def one_level(level, carry):
        half = 0.5 * wave_ref[0, level]
        spread = spread_ref[0, level]
        level_drag = jnp.where(level == 0, drag, 0.0)
        shift = jnp.minimum(level, 0)
        now = level - begin

        def edged(pad_ref, q):
            for p in range(parts):
                pad_ref[p, 7:8, :] = rows_ref[0, p, q, pl.ds(level, 1), :]
                pad_ref[p, 8 + rows : 9 + rows, :] = rows_ref[1, p, q, pl.ds(level, 1), :]

        def beside(pad_ref, p, at):
            return pad_ref[p, pl.ds(7 + at + shift, deep), :], pad_ref[p, pl.ds(9 + at + shift, deep), :]

        for p in range(parts):
            pressure_ref[p, 8 : 8 + rows, :] = state_ref[0, 0, level, :, cut(p)]
            tracer_ref[p, 8 : 8 + rows, :] = state_ref[0, 3, level, :, cut(p)]
        edged(pressure_ref, 0)
        edged(tracer_ref, 1)
        edged(zonal_ref, 2)
        for at in range(0, rows, deep):
            for p in range(parts):
                line = slice(at, at + deep)
                keep = keeping(mask_ref[0, line, cut(p)].astype(F32), level_drag)
                w, e = beside(pressure_ref, p, at)
                new_zonal = keep * (state_ref[0, 1, level, line, cut(p)] - half * (e - w))
                zonal_ref[p, 8 + at : 8 + at + deep, :] = new_zonal
                news_ref[1, now, line, cut(p)] = new_zonal
        for at in range(0, rows, deep):
            line = slice(at, at + deep)
            sea = [mask_ref[0, line, cut(p)].astype(F32) for p in range(parts)]
            pressure, meridional, tracer = (
                [state_ref[0, v, level, line, cut(p)] for p in range(parts)] for v in (0, 2, 3)
            )

            def south_col(q, line=line):
                return pltpu.roll(turned_ref[0, line, :], lax.rem(LANES - q * levels - level, LANES), 1)

            def north_col(q, line=line):
                return pltpu.roll(turned_ref[1, line, :], LANES - 1 - q * levels - level, 1)

            new_meridional = [
                keeping(m, level_drag) * (v - half * (n - s))
                for m, v, n, s in zip(
                    sea, meridional, from_north(pressure, north_col(0)), from_south(pressure, south_col(0))
                )
            ]
            south_v = south_col(2) - south_col(3) * pressure[0]
            north_v = north_col(2) + north_col(3) * pressure[-1]
            norths = from_north(new_meridional, north_v)
            souths = from_south(new_meridional, south_v)
            warm = from_north(tracer, north_col(1))
            cold = from_south(tracer, south_col(1))
            for p in range(parts):
                w, e = beside(zonal_ref, p, at)
                news_ref[0, now, line, cut(p)] = pressure[p] - half * (e - w + norths[p] - souths[p])
                news_ref[2, now, line, cut(p)] = new_meridional[p]
                w, e = beside(tracer_ref, p, at)
                news_ref[3, now, line, cut(p)] = tracer[p] + spread * jnp.where(is_ocean, sea[p], 1.0) * (
                    e + w + warm[p] + cold[p] - 4.0 * tracer[p]
                )
        after(level)
        return carry

    lax.fori_loop(begin, end, one_level, 0)


def deep_body(
    sizes, begin,
    state_ref, mask_ref, up_ref, down_ref, south_ref, north_ref, own_ref, fold_ref,
    wave_ref, spread_ref, gains_ref, *rest,
):
    levels, rows, cols, comps, count_x, count_y = sizes
    far_refs, (news_ref, rows_ref, turned_ref, folded_ref, *pad_refs) = rest[:-7], rest[-7:]
    stencil_halos(
        *sizes, state_ref, up_ref, down_ref, south_ref, north_ref, own_ref, fold_ref, far_refs, wave_ref, gains_ref,
        folded_ref, rows_ref, turned_ref,
    )
    stencil_levels(
        rows, cols, comps, begin, levels, state_ref, mask_ref, rows_ref, turned_ref, wave_ref, spread_ref, gains_ref,
        pad_refs, news_ref, lambda level: None,
    )


def upper_body(
    sizes, end, begun_ref, state_ref, mask_ref, rows_ref, turned_ref, wave_ref, spread_ref, gains_ref,
    out_ref, new_surface_ref, old_surface_ref, pad0, pad1, pad2, news_ref, stores,
):
    levels, rows, cols, comps, count_x, count_y = sizes

    def store(l, v):
        return pltpu.make_async_copy(news_ref.at[v, l], out_ref.at[0, v, l], stores.at[l, v])

    def after(level):
        for v in range(4):
            store(level, v).start()

    stencil_levels(
        rows, cols, comps, 0, end, state_ref, mask_ref, rows_ref, turned_ref, wave_ref, spread_ref, gains_ref,
        (pad0, pad1, pad2), news_ref, after,
    )
    for v in range(3):
        new_surface_ref[v] = news_ref[v + 1, 0]
        old_surface_ref[v] = state_ref[0, v + 1, 0]
    for l in range(end):
        for v in range(4):
            store(l, v).wait()


def deep_levels(model_state, sea_mask, halos, fars, fold_map, wave_speed, diffusivity, gains, sizes, begin):
    levels, rows, cols, comps, count_x, count_y = sizes
    parts = cols // LANES
    fold = fold_map.reshape(count_x, rows)
    vmem = pl.BlockSpec(memory_space=pltpu.VMEM)
    scalar = pl.BlockSpec(memory_space=pltpu.SMEM)
    shapes = ((4, levels - begin, rows, cols), (2, parts, 3, levels, LANES), (2, rows, LANES))
    return pl.pallas_call(
        functools.partial(deep_body, sizes, begin),
        in_specs=[vmem] * 8 + [scalar] * 3 + [vmem] * len(fars),
        out_specs=[vmem] * 3,
        out_shape=[jax.ShapeDtypeStruct(shape, F32) for shape in shapes],
        scratch_shapes=[
            pltpu.VMEM((halo_rows(levels), LANES), F32),
        ]
        + [pltpu.VMEM((parts, rows + 16, LANES), F32)] * 3,
        compiler_params=pltpu.CompilerParams(vmem_limit_bytes=VMEM_BYTES),
    )(model_state, sea_mask, *halos, fold, wave_speed, diffusivity, gains, *fars)


def upper_levels(begun, model_state, sea_mask, edge_rows, edge_columns, wave_speed, diffusivity, gains, sizes, end):
    levels, rows, cols, comps, count_x, count_y = sizes
    vmem = pl.BlockSpec(memory_space=pltpu.VMEM)
    scalar = pl.BlockSpec(memory_space=pltpu.SMEM)
    anywhere = pl.BlockSpec(memory_space=pl.ANY)
    surface = jax.ShapeDtypeStruct((3, rows, cols), F32)
    return pl.pallas_call(
        functools.partial(upper_body, sizes, end),
        in_specs=[anywhere] + [vmem] * 4 + [scalar] * 3,
        out_specs=[anywhere, vmem, vmem],
        out_shape=[jax.ShapeDtypeStruct(begun.shape, F32), surface, surface],
        scratch_shapes=[pltpu.VMEM((cols // LANES, rows + 16, LANES), F32)] * 3
        + [pltpu.VMEM((4, end, rows, cols), F32), pltpu.SemaphoreType.DMA((end, 4))],
        input_output_aliases={0: 0},
        compiler_params=pltpu.CompilerParams(vmem_limit_bytes=VMEM_BYTES),
    )(begun, model_state, sea_mask, edge_rows, edge_columns, wave_speed, diffusivity, gains)


def add_slots(rows, cols, groups, slab_ref, total_refs, chunks, plan):
    row_ids = packed_ids(rows)
    col_ids = packed_ids(cols)
    lane = iota((1, LANES), 1)
    one = jnp.ones((), BF16)
    zero = jnp.zeros((), BF16)
    block = 4

    def one_chunk(total_ref, chunk):
        n, first, low_slot, high_slot = plan(chunk)
        start = n * (CHANNELS * groups) + first
        for begin in range(0, DEPTH, block):
            columns, spreads = [], []
            for g in range(begin, begin + block):
                cells = slab_ref[pl.ds(start + 4 * groups + g, 1), :].astype(I32)
                slot = lane + (first + g) * LANES
                mine = jnp.logical_and(slot >= low_slot, slot < high_slot)
                row = spread_row(jnp.where(mine, cells // cols, -1)).astype(F32).astype(BF16)
                col = spread_row(cells % cols).astype(F32).astype(BF16)
                columns.append(jnp.where(col_ids == col[None], one, zero).reshape(cols, LANES))
                in_row = row_ids == row[None]
                highs, lows = [], []
                for v in range(4):
                    value = spread_row(slab_ref[pl.ds(start + v * groups + g, 1), :])
                    high, low = split_two(value)
                    highs.append(jnp.where(in_row, high[None], zero).reshape(rows, LANES))
                    lows.append(jnp.where(in_row, low[None], zero).reshape(rows, LANES))
                spreads.append(jnp.concatenate(highs + lows, axis=0))
            total_ref[...] += lax.dot_general(
                jnp.concatenate(spreads, axis=1), jnp.concatenate(columns, axis=1), (((1,), (1,)), ((), ())),
                preferred_element_type=F32,
            )

    done = 0
    for total_ref in total_refs:
        total_ref[...] = jnp.zeros_like(total_ref)

        def some(c, carry, total_ref=total_ref):
            one_chunk(total_ref, c)
            return carry

        step = chunks // len(total_refs)
        lax.fori_loop(done, done + step, some, 0)
        done = done + step


def halves_added(total_ref, rows):
    return total_ref[: 4 * rows] + total_ref[4 * rows :]


def add_own(rows, cols, comps, groups, slab_ref, total_ref):
    here = lax.axis_index("comp")
    pieces = groups // DEPTH
    near = slab_ref.shape[0] // (CHANNELS * groups)
    bounds = share_bounds(groups * LANES, comps - 1)
    is_ocean = here == comps - 1
    beside = here == comps - 2

    def plan(chunk):
        n = jnp.where(is_ocean, chunk, chunk // pieces)
        first = jnp.where(is_ocean, groups - DEPTH, chunk % pieces * DEPTH)
        return n, first, jnp.where(is_ocean, bounds[comps - 2], 0), groups * LANES

    chunks = jnp.where(is_ocean, near, jnp.where(beside, near * pieces, 0))
    add_slots(rows, cols, groups, slab_ref, [total_ref], chunks, plan)


def own_body(rows, cols, comps, groups, slab_ref, before_ref, sent_ref, total_ref):
    add_own(rows, cols, comps, groups, slab_ref, total_ref)
    sent_ref[...] = before_ref[...] + halves_added(total_ref, rows)


def other_body(
    rows, cols, comps, groups, slab_ref, before_ref, deep_ref, kept_ref, sent_ref, state_ref,
    first_ref, second_ref, copies,
):
    here = lax.axis_index("comp")
    pieces = groups // DEPTH
    near = slab_ref.shape[0] // (CHANNELS * groups)
    bounds = share_bounds(groups * LANES, comps - 1)
    is_ocean = here == comps - 1
    beside = here == comps - 2
    for_two = here == comps - 3
    middle = bounds[1] // LANES // 4 * 4
    count = deep_ref.shape[1]
    stores = [
        pltpu.make_async_copy(
            deep_ref.at[v], state_ref.at[0, v, pl.ds(state_ref.shape[2] - count, count)], copies.at[v]
        )
        for v in range(4)
    ]
    for store in stores:
        store.start()

    def plan(chunk):
        mine = chunk >= near
        n = jnp.where(for_two, chunk % near, chunk // pieces)
        first = jnp.where(for_two, jnp.where(mine, middle, 0), chunk % pieces * DEPTH)
        low_slot = jnp.where(jnp.logical_and(for_two, mine), bounds[1], 0)
        high_slot = jnp.where(for_two, jnp.where(mine, bounds[2], bounds[1]), groups * LANES)
        return n, first, low_slot, high_slot

    chunks = jnp.where(here == 0, 0, near * pieces)
    totals = [first_ref, second_ref]
    add_slots(rows, cols, groups, slab_ref, totals, chunks, plan)
    for start in range(0, 4 * rows, rows):
        first = first_ref[start : start + rows] + first_ref[start + 4 * rows : start + 5 * rows]
        second = second_ref[start : start + rows] + second_ref[start + 4 * rows : start + 5 * rows]
        kept_ref[start : start + rows] = jnp.where(beside, 0.0, second) + jnp.where(is_ocean, first, 0.0)
        sent = jnp.where(is_ocean, 0.0, first) + jnp.where(beside, second, 0.0)
        sent_ref[start : start + rows] = sent + before_ref[start : start + rows]
    for store in stores:
        store.wait()


def scatter_own(arrived, before, rows, cols, comps, slots):
    vmem = pl.BlockSpec(memory_space=pltpu.VMEM)
    return pl.pallas_call(
        functools.partial(own_body, rows, cols, comps, slots // LANES),
        in_specs=[vmem] * 2,
        out_specs=vmem,
        out_shape=jax.ShapeDtypeStruct((4 * rows, cols), F32),
        scratch_shapes=[pltpu.VMEM((8 * rows, cols), F32)],
        compiler_params=pltpu.CompilerParams(vmem_limit_bytes=VMEM_BYTES),
    )(arrived, before)


def scatter_other(other, before, deep, state_shape, rows, cols, comps, slots):
    vmem = pl.BlockSpec(memory_space=pltpu.VMEM)
    sums = jax.ShapeDtypeStruct((4 * rows, cols), F32)
    return pl.pallas_call(
        functools.partial(other_body, rows, cols, comps, slots // LANES),
        in_specs=[vmem] * 3,
        out_specs=[vmem, vmem, pl.BlockSpec(memory_space=pl.ANY)],
        out_shape=[sums, sums, jax.ShapeDtypeStruct(state_shape, F32)],
        scratch_shapes=[pltpu.VMEM((8 * rows, cols), F32)] * 2 + [pltpu.SemaphoreType.DMA((4,))],
        compiler_params=pltpu.CompilerParams(vmem_limit_bytes=VMEM_BYTES),
    )(other, before, deep)


def finish_body(rows, comps, state_ref, new_ref, old_ref, kept_ref, came_ref, mask_ref, gains_ref, out_ref, news_ref, copies):
    is_ocean = lax.axis_index("comp") == comps - 1
    tendency = jnp.where(is_ocean, mask_ref[0].astype(F32), 1.0)
    sums = [kept_ref[v * rows : (v + 1) * rows, :] + came_ref[v * rows : (v + 1) * rows, :] for v in range(4)]
    saves = []
    for v, total, gain in ((0, sums[1], 1), (1, sums[2], 1), (2, sums[0], 0)):
        news_ref[v] = new_ref[v] + tendency * gains_ref[0, gain] * (total - sums[3] * old_ref[v])
        saves.append(pltpu.make_async_copy(news_ref.at[v], out_ref.at[0, v + 1, 0], copies.at[v]))
        saves[-1].start()
    for save in saves:
        save.wait()


def finish(state, new_surface, old_surface, kept, came, sea_mask, gains, comps):
    rows, cols = state.shape[3:]
    vmem = pl.BlockSpec(memory_space=pltpu.VMEM)
    anywhere = pl.BlockSpec(memory_space=pl.ANY)
    return pl.pallas_call(
        functools.partial(finish_body, rows, comps),
        in_specs=[anywhere] + [vmem] * 5 + [pl.BlockSpec(memory_space=pltpu.SMEM)],
        out_specs=anywhere,
        out_shape=jax.ShapeDtypeStruct(state.shape, F32),
        scratch_shapes=[pltpu.VMEM((3, rows, cols), F32), pltpu.SemaphoreType.DMA((3,))],
        input_output_aliases={0: 0},
        compiler_params=pltpu.CompilerParams(vmem_limit_bytes=VMEM_BYTES),
    )(state, new_surface, old_surface, kept, came, sea_mask, gains)


def shards(
    model_state, sea_mask, wave_speed, diffusivity, surface_gains, area_table,
    own_cells, target_cells, weight_ids, pair_counts, fold_map,
):
    comps, count_x, count_y = (lax.axis_size(a) for a in ("comp", "tx", "ty"))
    positions = count_x * count_y
    rows, cols = model_state.shape[3:]
    slots = own_cells.shape[3]
    slot_arrays = (own_cells, target_cells, weight_ids, area_table.reshape(-1, LANES), pair_counts)

    def along(block, shift):
        return lax.ppermute(block, ("tx", "ty"), [(s, (s + shift) % positions) for s in range(positions)])

    y_pair = count_y == 2
    slab_rows = CHANNELS * slots // LANES
    slab1, up, slab3, fold = first_side(model_state, slot_arrays, sea_mask, comps)
    slab3 = along(slab3, 1 + count_y)
    slab1 = along(slab1, 1)
    up = along(up, count_y)
    slab0, down, high, low, pair, before = second_side(model_state, slot_arrays, fold, sea_mask, comps, y_pair)
    others = jnp.concatenate([slab1, up[:slab_rows], slab3[:slab_rows]])
    arrived = jnp.concatenate([slab0, others])
    other = lax.ppermute(arrived, "comp", [(g, g ^ 2) for g in range(comps)])

    down = along(down, -count_y)
    fars = []
    if y_pair and count_x == 4:
        south = north = lax.ppermute(jnp.concatenate([pair, slab3[slab_rows:]]), "ty", [(0, 1), (1, 0)])
    else:
        south = lax.ppermute(high, "ty", [(j, j + 1) for j in range(count_y - 1)])
        north = lax.ppermute(low, "ty", [(j + 1, j) for j in range(count_y - 1)])
        for shift in range(2, count_x - 1):
            pairs = []
            for i in range(count_x):
                ends = [((comps - 1) * count_x + k) * count_y + count_y - 1 for k in ((i + shift) % count_x, i)]
                pairs.append(tuple(ends))
            fars.append(lax.ppermute(fold, ("comp", "tx", "ty"), pairs))

    sizes = (*model_state.shape[2:], comps, count_x, count_y)
    cut = sizes[0] // 2
    before = scatter_own(others, before, rows, cols, comps, slots)
    deep, edge_rows, edge_columns = deep_levels(
        model_state, sea_mask, (up, down, south, north, fold), fars, fold_map,
        wave_speed, diffusivity, surface_gains, sizes, cut,
    )
    kept, sent, begun = scatter_other(other, before, deep, model_state.shape, rows, cols, comps, slots)
    came = lax.ppermute(sent, "comp", [(g, g ^ 1) for g in range(comps)])
    new_state, new_surface, old_surface = upper_levels(
        begun, model_state, sea_mask, edge_rows, edge_columns, wave_speed, diffusivity, surface_gains, sizes, cut
    )
    return finish(new_state, new_surface, old_surface, kept, came, sea_mask, surface_gains, comps)


def solution(mesh):
    in_specs = (
        P("comp", None, None, "tx", "ty"),
        P("comp", "tx", "ty"),
        P("comp", None),
        P("comp", None),
        P("comp", None),
        P(),
        P("comp", ("tx", "ty"), None, None),
        P("comp", ("tx", "ty"), None, None),
        P("comp", ("tx", "ty"), None, None),
        P("comp", ("tx", "ty"), None),
        P(),
    )
    out_specs = P("comp", None, None, "tx", "ty")
    return jax.shard_map(shards, mesh=mesh, in_specs=in_specs, out_specs=out_specs, check_vma=False)
```

```python
import functools

import jax
import jax.numpy as jnp
import numpy
from jax import lax
from jax.experimental import pallas as pl
from jax.experimental.pallas import tpu as pltpu
from jax.sharding import PartitionSpec as P

LANES = 128
DEPTH = 8
PACKED = 16
VMEM_BYTES = 28 * 1024 * 1024
F32 = jnp.float32
BF16 = jnp.bfloat16
I32 = jnp.int32
CHANNELS = 5

EDGE_P, SECOND_P, EDGE_VELOCITY, EDGE_T, MASK = range(5)


def iota(shape, dim):
    return lax.broadcasted_iota(I32, shape, dim)


def halo_rows(levels):
    return (4 * levels + 1 + 7) // 8 * 8


def split_two(values):
    high = values.astype(BF16)
    low = (values - high.astype(F32)).astype(BF16)
    return high, low


def packed_ids(count):
    ids = iota((count, LANES), 0).astype(F32).astype(BF16)
    return ids.reshape(count // PACKED, PACKED, LANES)


def spread_row(row):
    return jnp.broadcast_to(row, (PACKED, LANES))


def share_bounds(slots, shares):
    bounds = [0]
    for m in range(shares):
        bounds.append(bounds[-1] + (slots - m + shares - 1) // shares)
    return bounds


def slot_order(slots, shares, sort, half):
    place = iota((8, LANES), 0) * LANES + iota((8, LANES), 1) + half * 8 * LANES
    source = jnp.zeros((8, LANES), I32)
    bounds = share_bounds(slots, shares)
    for m in range(shares):
        inside = jnp.logical_and(place >= bounds[m], place < bounds[m + 1])
        source = jnp.where(inside, (place - bounds[m]) * shares + m, source)
    return jnp.where(sort, source, place)


def pick_rows(ref, n, source):
    total = jnp.zeros((8, LANES), I32)
    for t in range(ref.shape[3] // LANES):
        row = jnp.broadcast_to(ref[0, 0, n : n + 1, t * LANES : (t + 1) * LANES], (8, LANES))
        picked = jnp.take_along_axis(row, source % LANES, axis=1)
        total = jnp.where(source // LANES == t, picked, total)
    return total


def gather_partner(n, rows, cols, comps, refs, out):
    own_ref, target_ref, ids_ref, table_ref, counts_ref, halves_ref, cells_ref, picked_ref, parts_ref = refs
    slots = own_ref.shape[3]
    groups = slots // LANES
    is_ocean = lax.axis_index("comp") == comps - 1

    @pl.when(is_ocean)
    def _():
        for half in range(groups // 8):
            source = slot_order(slots, comps - 1, True, half)
            at = slice(half * 8, (half + 1) * 8)
            cells_ref[at, :] = pick_rows(own_ref, n, source)
            picked_ref[at, :] = pick_rows(ids_ref, n, source)
            out[4 * groups + half * 8 : 4 * groups + (half + 1) * 8, :] = pick_rows(target_ref, n, source).astype(F32)

    @pl.when(jnp.logical_not(is_ocean))
    def _():
        for g in range(groups):
            cut = slice(g * LANES, (g + 1) * LANES)
            cells_ref[g : g + 1, :] = own_ref[0, 0, n : n + 1, cut]
            picked_ref[g : g + 1, :] = ids_ref[0, 0, n : n + 1, cut]
            out[4 * groups + g : 4 * groups + g + 1, :] = target_ref[0, 0, n : n + 1, cut].astype(F32)

    count = jnp.broadcast_to(counts_ref[0, :, n : n + 1], (8, LANES))
    for half in range(groups // 8):
        source = slot_order(slots, comps - 1, is_ocean, half)
        ids = picked_ref[half * 8 : (half + 1) * 8, :]
        weight = jnp.zeros((8, LANES), F32)
        for t in range(table_ref.shape[0]):
            table = jnp.broadcast_to(table_ref[t : t + 1, :], (8, LANES))
            looked = jnp.take_along_axis(table, ids % LANES, axis=1)
            weight = jnp.where(ids // LANES == t, looked, weight)
        out[3 * groups + half * 8 : 3 * groups + (half + 1) * 8, :] = jnp.where(source < count, weight, 0.0)
    col_ids = packed_ids(cols)
    row_ids = iota((rows, LANES), 0)
    one = jnp.ones((), BF16)
    zero = jnp.zeros((), BF16)
    wide, subs = 2, 4

    def some(c, carry):
        for sub in range(subs):
            first = (c * subs + sub) * wide
            cells = [cells_ref[pl.ds(first + g, 1), :] for g in range(wide)]
            picks = []
            for cell in cells:
                col = spread_row(cell % cols).astype(F32).astype(BF16)
                picks.append(jnp.where(col_ids == col[None], one, zero).reshape(cols, LANES))
            picks = jnp.concatenate(picks, axis=1)
            if halves_ref.shape[1] > cols:
                picks = jnp.concatenate([picks, picks], axis=0)
                found = jnp.dot(halves_ref[...], picks, preferred_element_type=F32)
            else:
                found = jnp.dot(halves_ref[...], picks, preferred_element_type=F32)
                found = found[: 3 * rows] + found[3 * rows :]
            for g in range(wide):
                in_row = row_ids == cells[g] // cols
                for place, v in enumerate((2, 0, 1)):
                    block = found[v * rows : (v + 1) * rows, g * LANES : (g + 1) * LANES]
                    block = jnp.where(in_row, block, 0.0).reshape(rows // 8, 8, LANES)
                    start = pl.multiple_of((place * groups + first + g) * 8, 8)
                    parts_ref[pl.ds(start, 8), :] = jnp.sum(block, axis=0)
        return carry

    lax.fori_loop(0, groups // (subs * wide), some, 0)
    weight = out[3 * groups : 4 * groups, :]
    for place in range(3):
        total = jnp.zeros((groups, LANES), F32)
        for i in range(8):
            total += parts_ref[pl.ds(place * groups * 8 + i, groups, stride=8), :]
        out[place * groups : (place + 1) * groups, :] = total * weight


def split_surface(surface_ref, halves_ref, rows, cols):
    for v in range(3):
        high, low = split_two(surface_ref[v])
        if halves_ref.shape[1] > cols:
            halves_ref[v * rows : (v + 1) * rows, :cols] = high
            halves_ref[v * rows : (v + 1) * rows, cols:] = low
        else:
            halves_ref[v * rows : (v + 1) * rows, :] = high
            halves_ref[(v + 3) * rows : (v + 4) * rows, :] = low


def put_rows(ref, start, levels, cols, fields, sea, edge, second):
    height = halo_rows(levels)
    for p in range(cols // LANES):
        cut = slice(p * LANES, (p + 1) * LANES)
        base = start + p * height
        ref[base + 4 * levels : base + height, :] = jnp.zeros((height - 4 * levels, LANES), F32)
        ref[base + 4 * levels : base + 4 * levels + 1, :] = sea[edge : edge + 1, cut].astype(F32)
        for q, v, at in ((EDGE_P, 0, edge), (SECOND_P, 0, second), (EDGE_VELOCITY, 1, edge), (EDGE_T, 3, edge)):
            for l in range(levels):
                row = base + q * levels + l
                ref[row : row + 1, :] = fields(v, l)[at : at + 1, cut]


def turned_columns(levels, rows, fields, sea, begin):
    edge = 1 if begin else 0
    lanes = iota((rows, LANES), 1)
    total = pltpu.roll(sea.astype(F32), (4 * levels - begin - edge) % LANES, 1)
    for l in range(levels):
        total = jnp.where(lanes // 2 == l, pltpu.roll(fields(0, l), (2 * l - begin) % LANES, 1), total)
        for q, v in ((EDGE_VELOCITY, 2), (EDGE_T, 3)):
            at = q * levels + l
            moved = pltpu.roll(fields(v, l), (at - begin - edge) % LANES, 1)
            total = jnp.where(lanes == at, moved, total)
    return total.T[: halo_rows(levels)]


def first_body(
    levels, rows, cols, comps,
    state_hbm, own_hbm, target_hbm, ids_hbm, table_hbm, counts_hbm, mask_hbm,
    slab1_ref, up_ref, slab3_ref, fold_ref,
    surface_ref, own_ref, target_ref, ids_ref, table_ref, counts_ref, edge_ref, sea_edge_ref, mask_ref, columns_ref,
    halves_ref, cells_ref, picked_ref, parts_ref, copies, column_copies,
):
    sources = (
        state_hbm.at[0, pl.ds(1, 3), 0], own_hbm, target_hbm, ids_hbm, table_hbm, counts_hbm,
        state_hbm.at[0, :, :, pl.ds(rows - 8, 8), :], mask_hbm.at[0, pl.ds(rows - 8, 8), :],
    )
    places = (surface_ref, own_ref, target_ref, ids_ref, table_ref, counts_ref, edge_ref, sea_edge_ref)
    fetches = [
        pltpu.make_async_copy(source, place, copies.at[i])
        for i, (source, place) in enumerate(zip(sources, places))
    ]
    outer = pl.ds(cols - LANES, LANES)
    for_fold = [
        pltpu.make_async_copy(state_hbm.at[0, v, :, :, outer], columns_ref.at[i], column_copies.at[i])
        for i, v in enumerate((0, 2, 3))
    ] + [pltpu.make_async_copy(mask_hbm.at[0, :, outer], mask_ref, column_copies.at[3])]
    northern = lax.axis_index("ty") == lax.axis_size("ty") - 1
    folds = jnp.logical_and(lax.axis_index("comp") == comps - 1, northern)
    for fetch in fetches:
        fetch.start()

    @pl.when(folds)
    def _():
        for fetch in for_fold:
            fetch.start()

    for fetch in fetches:
        fetch.wait()
    slab_rows = slab1_ref.shape[0]
    tall = halo_rows(levels) * (cols // LANES)
    put_rows(up_ref, slab_rows, levels, cols, lambda v, l: edge_ref.at[v, l], sea_edge_ref, 7, 6)

    @pl.when(folds)
    def _():
        for fetch in for_fold:
            fetch.wait()
        places = {0: 0, 2: 1, 3: 2}
        fold_ref[...] = turned_columns(
            levels, rows, lambda v, l: columns_ref[places[v], l], mask_ref[...], LANES - 2
        )

    @pl.when(jnp.logical_not(folds))
    def _():
        fold_ref[...] = jnp.zeros_like(fold_ref)

    up_ref[slab_rows + tall :, :] = fold_ref[...]
    slab3_ref[slab_rows:, :] = fold_ref[...]
    split_surface(surface_ref, halves_ref, rows, cols)
    refs = (own_ref, target_ref, ids_ref, table_ref, counts_ref, halves_ref, cells_ref, picked_ref, parts_ref)
    for n, out in ((3, slab3_ref), (1, slab1_ref), (2, up_ref)):
        gather_partner(n, rows, cols, comps, refs, out)


def gather_scratch(rows, cols, slots, stacked):
    return [
        pltpu.VMEM((6 * rows, cols) if stacked else (3 * rows, 2 * cols), BF16),
        pltpu.VMEM((slots // LANES, LANES), I32),
        pltpu.VMEM((slots // LANES, LANES), I32),
        pltpu.VMEM((3 * slots // LANES * 8, LANES), F32),
    ]


def first_side(model_state, slot_arrays, sea_mask, comps):
    levels, rows, cols = model_state.shape[2:]
    near, slots = slot_arrays[0].shape[2:]
    table_shape = slot_arrays[3].shape
    slab = CHANNELS * slots // LANES
    height = halo_rows(levels)
    heights = (slab, slab + height * (cols // LANES) + height, slab + height, height)
    vmem = pl.BlockSpec(memory_space=pltpu.VMEM)
    arrays = (model_state, *slot_arrays, sea_mask)
    return pl.pallas_call(
        functools.partial(first_body, levels, rows, cols, comps),
        in_specs=[pl.BlockSpec(memory_space=pltpu.HBM)] * len(arrays),
        out_specs=[vmem] * len(heights),
        out_shape=[jax.ShapeDtypeStruct((h, LANES), F32) for h in heights],
        scratch_shapes=[pltpu.VMEM((3, rows, cols), F32)]
        + [pltpu.VMEM((1, 1, near, slots), I32)] * 3
        + [pltpu.VMEM(table_shape, F32), pltpu.VMEM((1, 1, near), I32)]
        + [
            pltpu.VMEM((4, levels, 8, cols), F32),
            pltpu.VMEM((8, cols), I32),
            pltpu.VMEM((rows, LANES), I32),
            pltpu.VMEM((3, levels, rows, LANES), F32),
        ]
        + gather_scratch(rows, cols, slots, True)
        + [pltpu.SemaphoreType.DMA((8,)), pltpu.SemaphoreType.DMA((4,))],
        compiler_params=pltpu.CompilerParams(vmem_limit_bytes=VMEM_BYTES),
    )(*(pltpu.with_memory_space_constraint(array, pltpu.HBM) for array in arrays))


def second_body(
    levels, rows, cols, comps, y_pair,
    state_ref, own_ref, target_ref, ids_ref, table_ref, counts_ref, fold_ref, mask_hbm,
    slab0_ref, down_ref, high_ref, low_ref, pair_ref, sent_ref,
    halves_ref, cells_ref, picked_ref, parts_ref, mask_ref, total_ref, copied,
):
    fetch = pltpu.make_async_copy(mask_hbm, mask_ref, copied)
    fetch.start()
    split_surface(state_ref.at[0, pl.ds(1, 3), 0], halves_ref, rows, cols)
    refs = (own_ref, target_ref, ids_ref, table_ref, counts_ref, halves_ref, cells_ref, picked_ref, parts_ref)
    gather_partner(0, rows, cols, comps, refs, slab0_ref)
    fetch.wait()
    put_rows(down_ref, 0, levels, cols, lambda v, l: state_ref.at[0, v, l], mask_ref.at[0], 0, 1)
    down_ref[halo_rows(levels) * (cols // LANES) :, :] = fold_ref[...]
    index_y = lax.axis_index("ty")
    high_used = index_y == 0 if y_pair else index_y >= 0
    low_used = index_y > 0 if y_pair else index_y >= 0

    def columns(start, begin):
        cut = slice(start, start + LANES)
        return turned_columns(levels, rows, lambda v, l: state_ref[0, v, l, :, cut], mask_ref[0, :, cut], begin)

    @pl.when(high_used)
    def _():
        highest = columns(cols - LANES, LANES - 2)
        high_ref[...] = highest
        pair_ref[...] = highest

    @pl.when(jnp.logical_not(high_used))
    def _():
        high_ref[...] = jnp.zeros_like(high_ref)

    @pl.when(low_used)
    def _():
        lowest = columns(0, 0)
        low_ref[...] = lowest
        pair_ref[...] = lowest

    @pl.when(jnp.logical_not(low_used))
    def _():
        low_ref[...] = jnp.zeros_like(low_ref)

    add_own(rows, cols, comps, own_ref.shape[3] // LANES, slab0_ref, total_ref)
    sent_ref[...] = halves_added(total_ref, rows)


def second_side(model_state, slot_arrays, fold, sea_mask, comps, y_pair):
    levels, rows, cols = model_state.shape[2:]
    slots = slot_arrays[0].shape[3]
    height = halo_rows(levels)
    heights = (CHANNELS * slots // LANES, height * (cols // LANES) + height, height, height, height)
    vmem = pl.BlockSpec(memory_space=pltpu.VMEM)
    return pl.pallas_call(
        functools.partial(second_body, levels, rows, cols, comps, y_pair),
        in_specs=[vmem] * 7 + [pl.BlockSpec(memory_space=pltpu.HBM)],
        out_specs=[vmem] * (len(heights) + 1),
        out_shape=[jax.ShapeDtypeStruct((h, LANES), F32) for h in heights]
        + [jax.ShapeDtypeStruct((4 * rows, cols), F32)],
        scratch_shapes=gather_scratch(rows, cols, slots, False)
        + [pltpu.VMEM((1, rows, cols), I32), pltpu.VMEM((8 * rows, cols), F32), pltpu.SemaphoreType.DMA],
        compiler_params=pltpu.CompilerParams(vmem_limit_bytes=VMEM_BYTES),
    )(model_state, *slot_arrays, fold, pltpu.with_memory_space_constraint(sea_mask, pltpu.HBM))


def stencil_halos(
    levels, rows, cols, comps, count_x, count_y,
    state_ref, up_ref, down_ref, south_ref, north_ref, own_ref, fold_ref, far_refs, wave_ref, gains_ref,
    folded_ref, rows_ref, turned_ref,
):
    height = halo_rows(levels)
    parts = cols // LANES
    index_x = lax.axis_index("tx")
    index_y = lax.axis_index("ty")
    is_ocean = lax.axis_index("comp") == comps - 1
    last_y = index_y == count_y - 1
    has_west = jnp.where(jnp.logical_or(is_ocean, index_x > 0), 1.0, 0.0)
    has_east = jnp.where(jnp.logical_or(is_ocean, index_x < count_x - 1), 1.0, 0.0)
    has_south = jnp.where(index_y > 0, 1.0, 0.0)
    has_north = jnp.where(jnp.logical_or(is_ocean, jnp.logical_not(last_y)), 1.0, 0.0)
    drag = gains_ref[0, 2]
    mask_at = 4 * levels

    fold = fold_ref[pl.ds(index_x, 1), :]
    total = jnp.zeros((height, LANES), F32)
    up_start = up_ref.shape[0] - height * (parts + 1)
    sources = [(0, own_ref, 0), (-1, up_ref, up_start + height * parts), (1, down_ref, height * parts)]
    if north_ref.shape[0] > height:
        sources.append((2, north_ref, height))
    else:
        sources += [(shift, ref, 0) for shift, ref in zip(range(2, count_x - 1), far_refs)]
    for shift, ref, start in sources:
        at = lax.rem(index_x + shift + count_x, count_x)
        chosen = (iota((rows, rows), 0) + at * rows == fold).astype(F32)
        total += jnp.dot(
            ref[start : start + height, :], chosen,
            precision=lax.Precision.HIGHEST, preferred_element_type=F32,
        )
    folded_ref[...] = total

    line = iota((levels, LANES), 0)
    halves = jnp.zeros((levels, LANES), F32)
    for l in range(levels):
        halves = jnp.where(line == l, 0.5 * wave_ref[0, l], halves)

    def keeping(sea_values, drags):
        return jnp.where(is_ocean, sea_values, 1.0 - drags * (1.0 - sea_values))

    drags = jnp.where(line == 0, drag, 0.0)

    def by_level(ref, start, q):
        return ref[start + q * levels : start + (q + 1) * levels, :]

    for side, (ref, begin, sign, has) in enumerate(
        ((up_ref, up_start, 1.0, has_west), (down_ref, 0, -1.0, has_east))
    ):
        for p in range(parts):
            start = begin + p * height
            kept = keeping(ref[start + mask_at : start + mask_at + 1, :], drags)
            fixed = kept * (by_level(ref, start, EDGE_VELOCITY) + sign * halves * by_level(ref, start, SECOND_P))
            inner = rows - 1 if side else 0
            own = jnp.concatenate(
                [state_ref[0, 0, l, inner : inner + 1, p * LANES : (p + 1) * LANES] for l in range(levels)], axis=0
            )
            rows_ref[side, p, 0] = has * by_level(ref, start, EDGE_P)
            rows_ref[side, p, 1] = has * by_level(ref, start, EDGE_T)
            rows_ref[side, p, 2] = has * (fixed - sign * kept * halves * own)

    even = lambda ref: ref[pl.ds(0, levels, stride=2), :]
    odd = lambda ref: ref[pl.ds(1, levels, stride=2), :]
    north = [
        jnp.where(last_y, jnp.where(is_ocean, folded, 0.0), low)
        for folded, low in (
            (odd(folded_ref), even(north_ref)),
            (even(folded_ref), odd(north_ref)),
            (-by_level(folded_ref, 0, EDGE_VELOCITY), by_level(north_ref, 0, EDGE_VELOCITY)),
            (by_level(folded_ref, 0, EDGE_T), by_level(north_ref, 0, EDGE_T)),
            (folded_ref[mask_at : mask_at + 1, :], north_ref[mask_at : mask_at + 1, :]),
        )
    ]
    south = [
        odd(south_ref), even(south_ref), by_level(south_ref, 0, EDGE_VELOCITY), by_level(south_ref, 0, EDGE_T),
        south_ref[mask_at : mask_at + 1, :],
    ]
    fill = jnp.zeros((LANES // 2 - 4 * levels, LANES), F32)
    lines = []
    for (edge, second, velocity, tracer, sea), sign, has in (
        (south, 1.0, has_south), (north, -1.0, has_north)
    ):
        kept = keeping(sea, drags)
        fixed = has * kept * (velocity + sign * halves * second)
        lines += [has * edge, has * tracer, fixed, has * kept * halves, fill]
    high, low = split_two(jnp.concatenate(lines, axis=0).T)
    turned_ref[:, :LANES] = high
    turned_ref[:, LANES:] = low


def stencil_matrices(rows, cols):
    steps = [[numpy.eye(n, k=k, dtype=numpy.float32) for k in (1, -1, 0)] for n in (rows, cols)]
    after, before, _ = steps[0]
    along = [numpy.concatenate([m, m], axis=1) for m in (after - before, after + before)]
    before, after, centre = steps[1]
    across = [numpy.concatenate([m, m], axis=0) for m in (after - before, after + before - 4 * centre)]
    return jnp.asarray(numpy.stack(along), BF16), jnp.asarray(numpy.stack(across), BF16)


def stencil_levels(
    rows, cols, comps, begin, end, state_ref, mask_ref, rows_ref, turned_ref, wave_ref, spread_ref, gains_ref,
    along_ref, across_ref, place_refs, news_ref, after,
):
    levels = state_ref.shape[2]
    parts = cols // LANES
    is_ocean = lax.axis_index("comp") == comps - 1
    drag = gains_ref[0, 2]
    for ref in place_refs:
        ref[...] = jnp.zeros_like(ref)
    sea = mask_ref[0].astype(F32)
    tendency = jnp.where(is_ocean, sea, 1.0)
    first = iota((8, cols), 0) == 0
    last = iota((8, cols), 0) == 7
    places, lanes = iota((4 * levels, LANES), 0), iota((4 * levels, LANES), 1)

    def product(left, right):
        return jnp.dot(left, right, preferred_element_type=F32)

    def one_level(level, place_ref):
        half = 0.5 * wave_ref[0, level]
        spread = spread_ref[0, level]
        level_drag = jnp.where(level == 0, drag, 0.0)
        for q, sign in enumerate((-1.0, 1.0, -1.0, 1.0)):
            found = places == q * levels + level
            south = jnp.where(jnp.logical_and(found, lanes == 0), sign, 0.0).astype(BF16)
            north = jnp.where(jnp.logical_and(found, lanes == LANES - 1), 1.0, 0.0).astype(BF16)
            for term in range(2):
                at = term * LANES
                place_ref[q, at : at + 4 * levels, :LANES] = south
                at += LANES // 2
                place_ref[q, at : at + 4 * levels, cols - LANES :] = north

        def across(which, q, field):
            inner = product(jnp.concatenate(split_two(field), axis=1), across_ref[which])
            return inner + product(turned_ref[...], place_ref[q])

        def along(which, q, field):
            found = product(along_ref[which], jnp.concatenate(split_two(field), axis=0))
            west, east = (
                jnp.concatenate([rows_ref[side, p, q, pl.ds(level, 1), :] for p in range(parts)], axis=1)
                for side in range(2)
            )
            if which == 0:
                west = -west
            upper = found[:8] + jnp.where(first, west, 0.0)
            lower = found[rows - 8 :] + jnp.where(last, east, 0.0)
            return jnp.concatenate([upper, found[8 : rows - 8], lower], axis=0)

        pressure, zonal, meridional, tracer = (state_ref[0, v, level] for v in range(4))
        keep = jnp.where(is_ocean, sea, 1.0 - level_drag * (1.0 - sea))
        new_zonal = keep * (zonal - half * along(0, 0, pressure))
        new_meridional = keep * (meridional - half * across(0, 0, pressure))
        new_tracer = tracer + spread * tendency * (along(1, 1, tracer) + across(1, 1, tracer))
        beyond = product(turned_ref[...], place_ref[3]) * pressure
        divergence = along(0, 2, new_zonal) + across(0, 2, new_meridional) + beyond
        now = level - begin
        news_ref[0, now] = pressure - half * divergence
        news_ref[1, now] = new_zonal
        news_ref[2, now] = new_meridional
        news_ref[3, now] = new_tracer
        after(level)

    def some(c, carry):
        for i, place_ref in enumerate(place_refs):
            one_level(begin + c * len(place_refs) + i, place_ref)
        return carry

    lax.fori_loop(0, (end - begin) // len(place_refs), some, 0)


def place_scratch(cols):
    return [pltpu.VMEM((4, 2 * LANES, cols), BF16)] * 2


def deep_body(
    sizes, begin,
    state_ref, mask_ref, up_ref, down_ref, south_ref, north_ref, own_ref, fold_ref,
    wave_ref, spread_ref, gains_ref, along_ref, across_ref, *rest,
):
    levels, rows, cols, comps, count_x, count_y = sizes
    far_refs, (news_ref, rows_ref, turned_ref, folded_ref, *place_refs) = rest[:-6], rest[-6:]
    stencil_halos(
        *sizes, state_ref, up_ref, down_ref, south_ref, north_ref, own_ref, fold_ref, far_refs, wave_ref, gains_ref,
        folded_ref, rows_ref, turned_ref,
    )
    stencil_levels(
        rows, cols, comps, begin, levels, state_ref, mask_ref, rows_ref, turned_ref, wave_ref, spread_ref, gains_ref,
        along_ref, across_ref, place_refs, news_ref, lambda level: None,
    )


def upper_body(
    sizes, end, begun_ref, state_ref, mask_ref, rows_ref, turned_ref, wave_ref, spread_ref, gains_ref,
    along_ref, across_ref, out_ref, new_surface_ref, old_surface_ref, place0, place1, news_ref, stores,
):
    levels, rows, cols, comps, count_x, count_y = sizes

    def store(l, v):
        return pltpu.make_async_copy(news_ref.at[v, l], out_ref.at[0, v, l], stores.at[l, v])

    def after(level):
        for v in range(4):
            store(level, v).start()

    stencil_levels(
        rows, cols, comps, 0, end, state_ref, mask_ref, rows_ref, turned_ref, wave_ref, spread_ref, gains_ref,
        along_ref, across_ref, (place0, place1), news_ref, after,
    )
    for v in range(3):
        new_surface_ref[v] = news_ref[v + 1, 0]
        old_surface_ref[v] = state_ref[0, v + 1, 0]
    for l in range(end):
        for v in range(4):
            store(l, v).wait()


def deep_levels(model_state, sea_mask, halos, fars, fold_map, wave_speed, diffusivity, gains, matrices, sizes, begin):
    levels, rows, cols, comps, count_x, count_y = sizes
    parts = cols // LANES
    fold = fold_map.reshape(count_x, rows)
    vmem = pl.BlockSpec(memory_space=pltpu.VMEM)
    scalar = pl.BlockSpec(memory_space=pltpu.SMEM)
    shapes = ((4, levels - begin, rows, cols), (2, parts, 3, levels, LANES), (rows, 2 * LANES))
    return pl.pallas_call(
        functools.partial(deep_body, sizes, begin),
        in_specs=[vmem] * 8 + [scalar] * 3 + [vmem] * (2 + len(fars)),
        out_specs=[vmem] * 3,
        out_shape=[jax.ShapeDtypeStruct(shape, kind) for shape, kind in zip(shapes, (F32, F32, BF16))],
        scratch_shapes=[
            pltpu.VMEM((halo_rows(levels), LANES), F32),
        ]
        + place_scratch(cols),
        compiler_params=pltpu.CompilerParams(vmem_limit_bytes=VMEM_BYTES),
    )(model_state, sea_mask, *halos, fold, wave_speed, diffusivity, gains, *matrices, *fars)


def upper_levels(
    begun, model_state, sea_mask, edge_rows, edge_columns, wave_speed, diffusivity, gains, matrices, sizes, end
):
    levels, rows, cols, comps, count_x, count_y = sizes
    vmem = pl.BlockSpec(memory_space=pltpu.VMEM)
    scalar = pl.BlockSpec(memory_space=pltpu.SMEM)
    anywhere = pl.BlockSpec(memory_space=pl.ANY)
    surface = jax.ShapeDtypeStruct((3, rows, cols), F32)
    return pl.pallas_call(
        functools.partial(upper_body, sizes, end),
        in_specs=[anywhere] + [vmem] * 4 + [scalar] * 3 + [vmem] * 2,
        out_specs=[anywhere, vmem, vmem],
        out_shape=[jax.ShapeDtypeStruct(begun.shape, F32), surface, surface],
        scratch_shapes=place_scratch(cols)
        + [pltpu.VMEM((4, end, rows, cols), F32), pltpu.SemaphoreType.DMA((end, 4))],
        input_output_aliases={0: 0},
        compiler_params=pltpu.CompilerParams(vmem_limit_bytes=VMEM_BYTES),
    )(begun, model_state, sea_mask, edge_rows, edge_columns, wave_speed, diffusivity, gains, *matrices)


def add_slots(rows, cols, groups, slab_ref, total_refs, chunks, plan):
    row_ids = packed_ids(rows)
    col_ids = packed_ids(cols)
    lane = iota((1, LANES), 1)
    one = jnp.ones((), BF16)
    zero = jnp.zeros((), BF16)
    block = 4

    def one_chunk(total_ref, chunk):
        n, first, low_slot, high_slot = plan(chunk)
        start = n * (CHANNELS * groups) + first
        for begin in range(0, DEPTH, block):
            columns, spreads = [], []
            for g in range(begin, begin + block):
                cells = slab_ref[pl.ds(start + 4 * groups + g, 1), :].astype(I32)
                slot = lane + (first + g) * LANES
                mine = jnp.logical_and(slot >= low_slot, slot < high_slot)
                row = spread_row(jnp.where(mine, cells // cols, -1)).astype(F32).astype(BF16)
                col = spread_row(cells % cols).astype(F32).astype(BF16)
                columns.append(jnp.where(col_ids == col[None], one, zero).reshape(cols, LANES))
                in_row = row_ids == row[None]
                highs, lows = [], []
                for v in range(4):
                    value = spread_row(slab_ref[pl.ds(start + v * groups + g, 1), :])
                    high, low = split_two(value)
                    highs.append(jnp.where(in_row, high[None], zero).reshape(rows, LANES))
                    lows.append(jnp.where(in_row, low[None], zero).reshape(rows, LANES))
                spreads.append(jnp.concatenate(highs + lows, axis=0))
            total_ref[...] += lax.dot_general(
                jnp.concatenate(spreads, axis=1), jnp.concatenate(columns, axis=1), (((1,), (1,)), ((), ())),
                preferred_element_type=F32,
            )

    done = 0
    for total_ref in total_refs:
        total_ref[...] = jnp.zeros_like(total_ref)

        def some(c, carry, total_ref=total_ref):
            one_chunk(total_ref, c)
            return carry

        step = chunks // len(total_refs)
        lax.fori_loop(done, done + step, some, 0)
        done = done + step


def halves_added(total_ref, rows):
    return total_ref[: 4 * rows] + total_ref[4 * rows :]


def add_own(rows, cols, comps, groups, slab_ref, total_ref):
    here = lax.axis_index("comp")
    pieces = groups // DEPTH
    near = slab_ref.shape[0] // (CHANNELS * groups)
    bounds = share_bounds(groups * LANES, comps - 1)
    is_ocean = here == comps - 1
    beside = here == comps - 2

    def plan(chunk):
        n = jnp.where(is_ocean, chunk, chunk // pieces)
        first = jnp.where(is_ocean, groups - DEPTH, chunk % pieces * DEPTH)
        return n, first, jnp.where(is_ocean, bounds[comps - 2], 0), groups * LANES

    chunks = jnp.where(is_ocean, near, jnp.where(beside, near * pieces, 0))
    add_slots(rows, cols, groups, slab_ref, [total_ref], chunks, plan)


def own_body(rows, cols, comps, groups, slab_ref, before_ref, sent_ref, total_ref):
    add_own(rows, cols, comps, groups, slab_ref, total_ref)
    sent_ref[...] = before_ref[...] + halves_added(total_ref, rows)


def other_body(
    rows, cols, comps, groups, slab_ref, before_ref, deep_ref, kept_ref, sent_ref, state_ref,
    first_ref, second_ref, copies,
):
    here = lax.axis_index("comp")
    pieces = groups // DEPTH
    near = slab_ref.shape[0] // (CHANNELS * groups)
    bounds = share_bounds(groups * LANES, comps - 1)
    is_ocean = here == comps - 1
    beside = here == comps - 2
    for_two = here == comps - 3
    middle = bounds[1] // LANES // 4 * 4
    count = deep_ref.shape[1]
    stores = [
        pltpu.make_async_copy(
            deep_ref.at[v], state_ref.at[0, v, pl.ds(state_ref.shape[2] - count, count)], copies.at[v]
        )
        for v in range(4)
    ]
    for store in stores:
        store.start()

    def plan(chunk):
        mine = chunk >= near
        n = jnp.where(for_two, chunk % near, chunk // pieces)
        first = jnp.where(for_two, jnp.where(mine, middle, 0), chunk % pieces * DEPTH)
        low_slot = jnp.where(jnp.logical_and(for_two, mine), bounds[1], 0)
        high_slot = jnp.where(for_two, jnp.where(mine, bounds[2], bounds[1]), groups * LANES)
        return n, first, low_slot, high_slot

    chunks = jnp.where(here == 0, 0, near * pieces)
    totals = [first_ref, second_ref]
    add_slots(rows, cols, groups, slab_ref, totals, chunks, plan)
    for start in range(0, 4 * rows, rows):
        first = first_ref[start : start + rows] + first_ref[start + 4 * rows : start + 5 * rows]
        second = second_ref[start : start + rows] + second_ref[start + 4 * rows : start + 5 * rows]
        kept_ref[start : start + rows] = jnp.where(beside, 0.0, second) + jnp.where(is_ocean, first, 0.0)
        sent = jnp.where(is_ocean, 0.0, first) + jnp.where(beside, second, 0.0)
        sent_ref[start : start + rows] = sent + before_ref[start : start + rows]
    for store in stores:
        store.wait()


def scatter_own(arrived, before, rows, cols, comps, slots):
    vmem = pl.BlockSpec(memory_space=pltpu.VMEM)
    return pl.pallas_call(
        functools.partial(own_body, rows, cols, comps, slots // LANES),
        in_specs=[vmem] * 2,
        out_specs=vmem,
        out_shape=jax.ShapeDtypeStruct((4 * rows, cols), F32),
        scratch_shapes=[pltpu.VMEM((8 * rows, cols), F32)],
        compiler_params=pltpu.CompilerParams(vmem_limit_bytes=VMEM_BYTES),
    )(arrived, before)


def scatter_other(other, before, deep, state_shape, rows, cols, comps, slots):
    vmem = pl.BlockSpec(memory_space=pltpu.VMEM)
    sums = jax.ShapeDtypeStruct((4 * rows, cols), F32)
    return pl.pallas_call(
        functools.partial(other_body, rows, cols, comps, slots // LANES),
        in_specs=[vmem] * 3,
        out_specs=[vmem, vmem, pl.BlockSpec(memory_space=pl.ANY)],
        out_shape=[sums, sums, jax.ShapeDtypeStruct(state_shape, F32)],
        scratch_shapes=[pltpu.VMEM((8 * rows, cols), F32)] * 2 + [pltpu.SemaphoreType.DMA((4,))],
        compiler_params=pltpu.CompilerParams(vmem_limit_bytes=VMEM_BYTES),
    )(other, before, deep)


def finish_body(rows, comps, state_ref, new_ref, old_ref, kept_ref, came_ref, mask_ref, gains_ref, out_ref, news_ref, copies):
    is_ocean = lax.axis_index("comp") == comps - 1
    tendency = jnp.where(is_ocean, mask_ref[0].astype(F32), 1.0)
    sums = [kept_ref[v * rows : (v + 1) * rows, :] + came_ref[v * rows : (v + 1) * rows, :] for v in range(4)]
    saves = []
    for v, total, gain in ((0, sums[1], 1), (1, sums[2], 1), (2, sums[0], 0)):
        news_ref[v] = new_ref[v] + tendency * gains_ref[0, gain] * (total - sums[3] * old_ref[v])
        saves.append(pltpu.make_async_copy(news_ref.at[v], out_ref.at[0, v + 1, 0], copies.at[v]))
        saves[-1].start()
    for save in saves:
        save.wait()


def finish(state, new_surface, old_surface, kept, came, sea_mask, gains, comps):
    rows, cols = state.shape[3:]
    vmem = pl.BlockSpec(memory_space=pltpu.VMEM)
    anywhere = pl.BlockSpec(memory_space=pl.ANY)
    return pl.pallas_call(
        functools.partial(finish_body, rows, comps),
        in_specs=[anywhere] + [vmem] * 5 + [pl.BlockSpec(memory_space=pltpu.SMEM)],
        out_specs=anywhere,
        out_shape=jax.ShapeDtypeStruct(state.shape, F32),
        scratch_shapes=[pltpu.VMEM((3, rows, cols), F32), pltpu.SemaphoreType.DMA((3,))],
        input_output_aliases={0: 0},
        compiler_params=pltpu.CompilerParams(vmem_limit_bytes=VMEM_BYTES),
    )(state, new_surface, old_surface, kept, came, sea_mask, gains)


def shards(
    model_state, sea_mask, wave_speed, diffusivity, surface_gains, area_table,
    own_cells, target_cells, weight_ids, pair_counts, fold_map,
):
    comps, count_x, count_y = (lax.axis_size(a) for a in ("comp", "tx", "ty"))
    positions = count_x * count_y
    rows, cols = model_state.shape[3:]
    slots = own_cells.shape[3]
    slot_arrays = (own_cells, target_cells, weight_ids, area_table.reshape(-1, LANES), pair_counts)

    def along(block, shift):
        return lax.ppermute(block, ("tx", "ty"), [(s, (s + shift) % positions) for s in range(positions)])

    y_pair = count_y == 2
    slab_rows = CHANNELS * slots // LANES
    slab1, up, slab3, fold = first_side(model_state, slot_arrays, sea_mask, comps)
    slab3 = along(slab3, 1 + count_y)
    slab1 = along(slab1, 1)
    up = along(up, count_y)
    slab0, down, high, low, pair, before = second_side(model_state, slot_arrays, fold, sea_mask, comps, y_pair)
    others = jnp.concatenate([slab1, up[:slab_rows], slab3[:slab_rows]])
    arrived = jnp.concatenate([slab0, others])
    other = lax.ppermute(arrived, "comp", [(g, g ^ 2) for g in range(comps)])

    down = along(down, -count_y)
    fars = []
    if y_pair and count_x == 4:
        south = north = lax.ppermute(jnp.concatenate([pair, slab3[slab_rows:]]), "ty", [(0, 1), (1, 0)])
    else:
        south = lax.ppermute(high, "ty", [(j, j + 1) for j in range(count_y - 1)])
        north = lax.ppermute(low, "ty", [(j + 1, j) for j in range(count_y - 1)])
        for shift in range(2, count_x - 1):
            pairs = []
            for i in range(count_x):
                ends = [((comps - 1) * count_x + k) * count_y + count_y - 1 for k in ((i + shift) % count_x, i)]
                pairs.append(tuple(ends))
            fars.append(lax.ppermute(fold, ("comp", "tx", "ty"), pairs))

    sizes = (*model_state.shape[2:], comps, count_x, count_y)
    cut = sizes[0] // 2
    matrices = stencil_matrices(rows, cols)
    before = scatter_own(others, before, rows, cols, comps, slots)
    deep, edge_rows, edge_columns = deep_levels(
        model_state, sea_mask, (up, down, south, north, fold), fars, fold_map,
        wave_speed, diffusivity, surface_gains, matrices, sizes, cut,
    )
    kept, sent, begun = scatter_other(other, before, deep, model_state.shape, rows, cols, comps, slots)
    came = lax.ppermute(sent, "comp", [(g, g ^ 1) for g in range(comps)])
    new_state, new_surface, old_surface = upper_levels(
        begun, model_state, sea_mask, edge_rows, edge_columns, wave_speed, diffusivity, surface_gains,
        matrices, sizes, cut,
    )
    return finish(new_state, new_surface, old_surface, kept, came, sea_mask, surface_gains, comps)


def solution(mesh):
    in_specs = (
        P("comp", None, None, "tx", "ty"),
        P("comp", "tx", "ty"),
        P("comp", None),
        P("comp", None),
        P("comp", None),
        P(),
        P("comp", ("tx", "ty"), None, None),
        P("comp", ("tx", "ty"), None, None),
        P("comp", ("tx", "ty"), None, None),
        P("comp", ("tx", "ty"), None),
        P(),
    )
    out_specs = P("comp", None, None, "tx", "ty")
    return jax.shard_map(shards, mesh=mesh, in_specs=in_specs, out_specs=out_specs, check_vma=False)
```

```python
import functools

import jax
import jax.numpy as jnp
import numpy
from jax import lax
from jax.experimental import pallas as pl
from jax.experimental.pallas import tpu as pltpu
from jax.sharding import PartitionSpec as P

LANES = 128
DEPTH = 8
PACKED = 16
VMEM_BYTES = 28 * 1024 * 1024
F32 = jnp.float32
BF16 = jnp.bfloat16
I32 = jnp.int32
CHANNELS = 5

EDGE_P, SECOND_P, EDGE_VELOCITY, EDGE_T, MASK = range(5)


def iota(shape, dim):
    return lax.broadcasted_iota(I32, shape, dim)


def halo_rows(levels):
    return (4 * levels + 1 + 7) // 8 * 8


def split_two(values):
    high = values.astype(BF16)
    low = (values - high.astype(F32)).astype(BF16)
    return high, low


def packed_ids(count):
    ids = iota((count, LANES), 0).astype(F32).astype(BF16)
    return ids.reshape(count // PACKED, PACKED, LANES)


def spread_row(row):
    return jnp.broadcast_to(row, (PACKED, LANES))


def share_bounds(slots, shares):
    bounds = [0]
    for m in range(shares):
        bounds.append(bounds[-1] + (slots - m + shares - 1) // shares)
    return bounds


def slot_order(slots, shares, sort, half):
    place = iota((8, LANES), 0) * LANES + iota((8, LANES), 1) + half * 8 * LANES
    source = jnp.zeros((8, LANES), I32)
    bounds = share_bounds(slots, shares)
    for m in range(shares):
        inside = jnp.logical_and(place >= bounds[m], place < bounds[m + 1])
        source = jnp.where(inside, (place - bounds[m]) * shares + m, source)
    return jnp.where(sort, source, place)


def pick_rows(ref, n, source):
    total = jnp.zeros((8, LANES), I32)
    for t in range(ref.shape[3] // LANES):
        row = jnp.broadcast_to(ref[0, 0, n : n + 1, t * LANES : (t + 1) * LANES], (8, LANES))
        picked = jnp.take_along_axis(row, source % LANES, axis=1)
        total = jnp.where(source // LANES == t, picked, total)
    return total


def prepare_partner(n, comps, refs, cells_ref, out):
    own_ref, target_ref, ids_ref, table_ref, counts_ref, picked_ref = refs
    slots = own_ref.shape[3]
    groups = slots // LANES
    is_ocean = lax.axis_index("comp") == comps - 1

    @pl.when(is_ocean)
    def _():
        for half in range(groups // 8):
            source = slot_order(slots, comps - 1, True, half)
            at = slice(half * 8, (half + 1) * 8)
            cells_ref[at, :] = pick_rows(own_ref, n, source)
            picked_ref[at, :] = pick_rows(ids_ref, n, source)
            out[4 * groups + half * 8 : 4 * groups + (half + 1) * 8, :] = pick_rows(target_ref, n, source).astype(F32)

    @pl.when(jnp.logical_not(is_ocean))
    def _():
        for g in range(groups):
            cut = slice(g * LANES, (g + 1) * LANES)
            cells_ref[g : g + 1, :] = own_ref[0, 0, n : n + 1, cut]
            picked_ref[g : g + 1, :] = ids_ref[0, 0, n : n + 1, cut]
            out[4 * groups + g : 4 * groups + g + 1, :] = target_ref[0, 0, n : n + 1, cut].astype(F32)

    count = jnp.broadcast_to(counts_ref[0, :, n : n + 1], (8, LANES))
    for half in range(groups // 8):
        source = slot_order(slots, comps - 1, is_ocean, half)
        ids = picked_ref[half * 8 : (half + 1) * 8, :]
        weight = jnp.zeros((8, LANES), F32)
        for t in range(table_ref.shape[0]):
            table = jnp.broadcast_to(table_ref[t : t + 1, :], (8, LANES))
            looked = jnp.take_along_axis(table, ids % LANES, axis=1)
            weight = jnp.where(ids // LANES == t, looked, weight)
        out[3 * groups + half * 8 : 3 * groups + (half + 1) * 8, :] = jnp.where(source < count, weight, 0.0)


def gather_partner(rows, cols, halves_ref, cells_ref, parts_ref, out):
    groups = cells_ref.shape[0]
    col_ids = packed_ids(cols)
    row_ids = iota((rows, LANES), 0)
    one = jnp.ones((), BF16)
    zero = jnp.zeros((), BF16)
    wide, subs = 2, 4

    def some(c, carry):
        for sub in range(subs):
            first = (c * subs + sub) * wide
            cells = [cells_ref[pl.ds(first + g, 1), :] for g in range(wide)]
            picks = []
            for cell in cells:
                col = spread_row(cell % cols).astype(F32).astype(BF16)
                picks.append(jnp.where(col_ids == col[None], one, zero).reshape(cols, LANES))
            picks = jnp.concatenate(picks, axis=1)
            if halves_ref.shape[1] > cols:
                picks = jnp.concatenate([picks, picks], axis=0)
                found = jnp.dot(halves_ref[...], picks, preferred_element_type=F32)
            else:
                found = jnp.dot(halves_ref[...], picks, preferred_element_type=F32)
                found = found[: 3 * rows] + found[3 * rows :]
            for g in range(wide):
                in_row = row_ids == cells[g] // cols
                for place, v in enumerate((2, 0, 1)):
                    block = found[v * rows : (v + 1) * rows, g * LANES : (g + 1) * LANES]
                    block = jnp.where(in_row, block, 0.0).reshape(rows // 8, 8, LANES)
                    start = pl.multiple_of((place * groups + first + g) * 8, 8)
                    parts_ref[pl.ds(start, 8), :] = jnp.sum(block, axis=0)
        return carry

    lax.fori_loop(0, groups // (subs * wide), some, 0)
    weight = out[3 * groups : 4 * groups, :]
    for place in range(3):
        total = jnp.zeros((groups, LANES), F32)
        for i in range(8):
            total += parts_ref[pl.ds(place * groups * 8 + i, groups, stride=8), :]
        out[place * groups : (place + 1) * groups, :] = total * weight


def split_surface(surface_ref, halves_ref, rows, cols):
    for v in range(3):
        high, low = split_two(surface_ref[v])
        if halves_ref.shape[1] > cols:
            halves_ref[v * rows : (v + 1) * rows, :cols] = high
            halves_ref[v * rows : (v + 1) * rows, cols:] = low
        else:
            halves_ref[v * rows : (v + 1) * rows, :] = high
            halves_ref[(v + 3) * rows : (v + 4) * rows, :] = low


def put_rows(ref, start, levels, cols, fields, sea, edge, second):
    height = halo_rows(levels)
    for p in range(cols // LANES):
        cut = slice(p * LANES, (p + 1) * LANES)
        base = start + p * height
        ref[base + 4 * levels : base + height, :] = jnp.zeros((height - 4 * levels, LANES), F32)
        ref[base + 4 * levels : base + 4 * levels + 1, :] = sea[edge : edge + 1, cut].astype(F32)
        for q, v, at in ((EDGE_P, 0, edge), (SECOND_P, 0, second), (EDGE_VELOCITY, 1, edge), (EDGE_T, 3, edge)):
            for l in range(levels):
                row = base + q * levels + l
                ref[row : row + 1, :] = fields(v, l)[at : at + 1, cut]


def turned_columns(levels, rows, fields, sea, begin):
    edge = 1 if begin else 0
    lanes = iota((rows, LANES), 1)
    total = pltpu.roll(sea.astype(F32), (4 * levels - begin - edge) % LANES, 1)
    for l in range(levels):
        total = jnp.where(lanes // 2 == l, pltpu.roll(fields(0, l), (2 * l - begin) % LANES, 1), total)
        for q, v in ((EDGE_VELOCITY, 2), (EDGE_T, 3)):
            at = q * levels + l
            moved = pltpu.roll(fields(v, l), (at - begin - edge) % LANES, 1)
            total = jnp.where(lanes == at, moved, total)
    return total.T[: halo_rows(levels)]


def first_body(
    levels, rows, cols, comps,
    state_hbm, own_hbm, target_hbm, ids_hbm, table_hbm, counts_hbm, mask_hbm,
    slab1_ref, up_ref, slab3_ref, fold_ref,
    surface_ref, own_ref, target_ref, ids_ref, table_ref, counts_ref, edge_ref, sea_edge_ref, mask_ref, columns_ref,
    halves_ref, cells_ref, picked_ref, parts_ref, copies, column_copies,
):
    sources = (
        own_hbm, target_hbm, ids_hbm, table_hbm, counts_hbm, state_hbm.at[0, pl.ds(1, 3), 0],
        state_hbm.at[0, :, :, pl.ds(rows - 8, 8), :], mask_hbm.at[0, pl.ds(rows - 8, 8), :],
    )
    places = (own_ref, target_ref, ids_ref, table_ref, counts_ref, surface_ref, edge_ref, sea_edge_ref)
    fetches = [
        pltpu.make_async_copy(source, place, copies.at[i])
        for i, (source, place) in enumerate(zip(sources, places))
    ]
    outer = pl.ds(cols - LANES, LANES)
    for_fold = [
        pltpu.make_async_copy(state_hbm.at[0, v, :, :, outer], columns_ref.at[i], column_copies.at[i])
        for i, v in enumerate((0, 2, 3))
    ] + [pltpu.make_async_copy(mask_hbm.at[0, :, outer], mask_ref, column_copies.at[3])]
    northern = lax.axis_index("ty") == lax.axis_size("ty") - 1
    folds = jnp.logical_and(lax.axis_index("comp") == comps - 1, northern)
    for fetch in fetches:
        fetch.start()

    @pl.when(folds)
    def _():
        for fetch in for_fold:
            fetch.start()

    for fetch in fetches[:5]:
        fetch.wait()
    refs = (own_ref, target_ref, ids_ref, table_ref, counts_ref, picked_ref)
    slabs = ((3, slab3_ref), (1, slab1_ref), (2, up_ref))
    for i, (n, out) in enumerate(slabs):
        prepare_partner(n, comps, refs, cells_ref.at[i], out)
    fetches[5].wait()
    split_surface(surface_ref, halves_ref, rows, cols)
    for i, (n, out) in enumerate(slabs):
        gather_partner(rows, cols, halves_ref, cells_ref.at[i], parts_ref, out)
    for fetch in fetches[6:]:
        fetch.wait()
    slab_rows = slab1_ref.shape[0]
    tall = halo_rows(levels) * (cols // LANES)
    put_rows(up_ref, slab_rows, levels, cols, lambda v, l: edge_ref.at[v, l], sea_edge_ref, 7, 6)

    @pl.when(folds)
    def _():
        for fetch in for_fold:
            fetch.wait()
        places = {0: 0, 2: 1, 3: 2}
        fold_ref[...] = turned_columns(
            levels, rows, lambda v, l: columns_ref[places[v], l], mask_ref[...], LANES - 2
        )

    @pl.when(jnp.logical_not(folds))
    def _():
        fold_ref[...] = jnp.zeros_like(fold_ref)

    up_ref[slab_rows + tall :, :] = fold_ref[...]
    slab3_ref[slab_rows:, :] = fold_ref[...]


def gather_scratch(rows, cols, slots, stacked):
    return [
        pltpu.VMEM((6 * rows, cols) if stacked else (3 * rows, 2 * cols), BF16),
        pltpu.VMEM((3, slots // LANES, LANES), I32),
        pltpu.VMEM((slots // LANES, LANES), I32),
        pltpu.VMEM((3 * slots // LANES * 8, LANES), F32),
    ]


def first_side(model_state, slot_arrays, sea_mask, comps):
    levels, rows, cols = model_state.shape[2:]
    near, slots = slot_arrays[0].shape[2:]
    table_shape = slot_arrays[3].shape
    slab = CHANNELS * slots // LANES
    height = halo_rows(levels)
    heights = (slab, slab + height * (cols // LANES) + height, slab + height, height)
    vmem = pl.BlockSpec(memory_space=pltpu.VMEM)
    arrays = (model_state, *slot_arrays, sea_mask)
    return pl.pallas_call(
        functools.partial(first_body, levels, rows, cols, comps),
        in_specs=[pl.BlockSpec(memory_space=pltpu.HBM)] * len(arrays),
        out_specs=[vmem] * len(heights),
        out_shape=[jax.ShapeDtypeStruct((h, LANES), F32) for h in heights],
        scratch_shapes=[pltpu.VMEM((3, rows, cols), F32)]
        + [pltpu.VMEM((1, 1, near, slots), I32)] * 3
        + [pltpu.VMEM(table_shape, F32), pltpu.VMEM((1, 1, near), I32)]
        + [
            pltpu.VMEM((4, levels, 8, cols), F32),
            pltpu.VMEM((8, cols), I32),
            pltpu.VMEM((rows, LANES), I32),
            pltpu.VMEM((3, levels, rows, LANES), F32),
        ]
        + gather_scratch(rows, cols, slots, True)
        + [pltpu.SemaphoreType.DMA((8,)), pltpu.SemaphoreType.DMA((4,))],
        compiler_params=pltpu.CompilerParams(vmem_limit_bytes=VMEM_BYTES),
    )(*(pltpu.with_memory_space_constraint(array, pltpu.HBM) for array in arrays))


def second_body(
    levels, rows, cols, comps, y_pair,
    state_ref, own_ref, target_ref, ids_ref, table_ref, counts_ref, fold_ref, mask_hbm,
    slab0_ref, down_ref, high_ref, low_ref, pair_ref, sent_ref,
    halves_ref, cells_ref, picked_ref, parts_ref, mask_ref, total_ref, copied,
):
    fetch = pltpu.make_async_copy(mask_hbm, mask_ref, copied)
    fetch.start()
    split_surface(state_ref.at[0, pl.ds(1, 3), 0], halves_ref, rows, cols)
    refs = (own_ref, target_ref, ids_ref, table_ref, counts_ref, picked_ref)
    prepare_partner(0, comps, refs, cells_ref.at[0], slab0_ref)
    gather_partner(rows, cols, halves_ref, cells_ref.at[0], parts_ref, slab0_ref)
    fetch.wait()
    put_rows(down_ref, 0, levels, cols, lambda v, l: state_ref.at[0, v, l], mask_ref.at[0], 0, 1)
    down_ref[halo_rows(levels) * (cols // LANES) :, :] = fold_ref[...]
    index_y = lax.axis_index("ty")
    high_used = index_y == 0 if y_pair else index_y >= 0
    low_used = index_y > 0 if y_pair else index_y >= 0

    def columns(start, begin):
        cut = slice(start, start + LANES)
        return turned_columns(levels, rows, lambda v, l: state_ref[0, v, l, :, cut], mask_ref[0, :, cut], begin)

    @pl.when(high_used)
    def _():
        highest = columns(cols - LANES, LANES - 2)
        high_ref[...] = highest
        pair_ref[...] = highest

    @pl.when(jnp.logical_not(high_used))
    def _():
        high_ref[...] = jnp.zeros_like(high_ref)

    @pl.when(low_used)
    def _():
        lowest = columns(0, 0)
        low_ref[...] = lowest
        pair_ref[...] = lowest

    @pl.when(jnp.logical_not(low_used))
    def _():
        low_ref[...] = jnp.zeros_like(low_ref)

    add_own(rows, cols, comps, own_ref.shape[3] // LANES, slab0_ref, total_ref, 0)
    sent_ref[...] = halves_added(total_ref, rows)


def second_side(model_state, slot_arrays, fold, sea_mask, comps, y_pair):
    levels, rows, cols = model_state.shape[2:]
    slots = slot_arrays[0].shape[3]
    height = halo_rows(levels)
    heights = (CHANNELS * slots // LANES, height * (cols // LANES) + height, height, height, height)
    vmem = pl.BlockSpec(memory_space=pltpu.VMEM)
    return pl.pallas_call(
        functools.partial(second_body, levels, rows, cols, comps, y_pair),
        in_specs=[vmem] * 7 + [pl.BlockSpec(memory_space=pltpu.HBM)],
        out_specs=[vmem] * (len(heights) + 1),
        out_shape=[jax.ShapeDtypeStruct((h, LANES), F32) for h in heights]
        + [jax.ShapeDtypeStruct((4 * rows, cols), F32)],
        scratch_shapes=gather_scratch(rows, cols, slots, False)
        + [pltpu.VMEM((1, rows, cols), I32), pltpu.VMEM((8 * rows, cols), F32), pltpu.SemaphoreType.DMA],
        compiler_params=pltpu.CompilerParams(vmem_limit_bytes=VMEM_BYTES),
    )(model_state, *slot_arrays, fold, pltpu.with_memory_space_constraint(sea_mask, pltpu.HBM))


def stencil_halos(
    levels, rows, cols, comps, count_x, count_y,
    state_ref, up_ref, down_ref, south_ref, north_ref, own_ref, fold_ref, far_refs, wave_ref, gains_ref,
    folded_ref, rows_ref, turned_ref,
):
    height = halo_rows(levels)
    parts = cols // LANES
    index_x = lax.axis_index("tx")
    index_y = lax.axis_index("ty")
    is_ocean = lax.axis_index("comp") == comps - 1
    last_y = index_y == count_y - 1
    has_west = jnp.where(jnp.logical_or(is_ocean, index_x > 0), 1.0, 0.0)
    has_east = jnp.where(jnp.logical_or(is_ocean, index_x < count_x - 1), 1.0, 0.0)
    has_south = jnp.where(index_y > 0, 1.0, 0.0)
    has_north = jnp.where(jnp.logical_or(is_ocean, jnp.logical_not(last_y)), 1.0, 0.0)
    drag = gains_ref[0, 2]
    mask_at = 4 * levels

    fold = fold_ref[pl.ds(index_x, 1), :]
    total = jnp.zeros((height, LANES), F32)
    up_start = up_ref.shape[0] - height * (parts + 1)
    sources = [(0, own_ref, 0), (-1, up_ref, up_start + height * parts), (1, down_ref, height * parts)]
    if north_ref.shape[0] > height:
        sources.append((2, north_ref, height))
    else:
        sources += [(shift, ref, 0) for shift, ref in zip(range(2, count_x - 1), far_refs)]
    for shift, ref, start in sources:
        at = lax.rem(index_x + shift + count_x, count_x)
        chosen = (iota((rows, rows), 0) + at * rows == fold).astype(F32)
        total += jnp.dot(
            ref[start : start + height, :], chosen,
            precision=lax.Precision.HIGHEST, preferred_element_type=F32,
        )
    folded_ref[...] = total

    line = iota((levels, LANES), 0)
    halves = jnp.zeros((levels, LANES), F32)
    for l in range(levels):
        halves = jnp.where(line == l, 0.5 * wave_ref[0, l], halves)

    def keeping(sea_values, drags):
        return jnp.where(is_ocean, sea_values, 1.0 - drags * (1.0 - sea_values))

    drags = jnp.where(line == 0, drag, 0.0)

    def by_level(ref, start, q):
        return ref[start + q * levels : start + (q + 1) * levels, :]

    for side, (ref, begin, sign, has) in enumerate(
        ((up_ref, up_start, 1.0, has_west), (down_ref, 0, -1.0, has_east))
    ):
        for p in range(parts):
            start = begin + p * height
            kept = keeping(ref[start + mask_at : start + mask_at + 1, :], drags)
            fixed = kept * (by_level(ref, start, EDGE_VELOCITY) + sign * halves * by_level(ref, start, SECOND_P))
            inner = rows - 1 if side else 0
            own = jnp.concatenate(
                [state_ref[0, 0, l, inner : inner + 1, p * LANES : (p + 1) * LANES] for l in range(levels)], axis=0
            )
            rows_ref[side, p, 0] = has * by_level(ref, start, EDGE_P)
            rows_ref[side, p, 1] = has * by_level(ref, start, EDGE_T)
            rows_ref[side, p, 2] = has * (fixed - sign * kept * halves * own)

    even = lambda ref: ref[pl.ds(0, levels, stride=2), :]
    odd = lambda ref: ref[pl.ds(1, levels, stride=2), :]
    north = [
        jnp.where(last_y, jnp.where(is_ocean, folded, 0.0), low)
        for folded, low in (
            (odd(folded_ref), even(north_ref)),
            (even(folded_ref), odd(north_ref)),
            (-by_level(folded_ref, 0, EDGE_VELOCITY), by_level(north_ref, 0, EDGE_VELOCITY)),
            (by_level(folded_ref, 0, EDGE_T), by_level(north_ref, 0, EDGE_T)),
            (folded_ref[mask_at : mask_at + 1, :], north_ref[mask_at : mask_at + 1, :]),
        )
    ]
    south = [
        odd(south_ref), even(south_ref), by_level(south_ref, 0, EDGE_VELOCITY), by_level(south_ref, 0, EDGE_T),
        south_ref[mask_at : mask_at + 1, :],
    ]
    fill = jnp.zeros((LANES // 2 - 4 * levels, LANES), F32)
    lines = []
    for (edge, second, velocity, tracer, sea), sign, has in (
        (south, 1.0, has_south), (north, -1.0, has_north)
    ):
        kept = keeping(sea, drags)
        fixed = has * kept * (velocity + sign * halves * second)
        lines += [has * edge, has * tracer, fixed, has * kept * halves, fill]
    high, low = split_two(jnp.concatenate(lines, axis=0).T)
    turned_ref[:, :LANES] = high
    turned_ref[:, LANES:] = low


def stencil_matrices(rows, cols):
    steps = [[numpy.eye(n, k=k, dtype=numpy.float32) for k in (1, -1, 0)] for n in (rows, cols)]
    after, before, _ = steps[0]
    along = [numpy.concatenate([m, m], axis=1) for m in (after - before, after + before)]
    before, after, centre = steps[1]
    across = [numpy.concatenate([m, m], axis=0) for m in (after - before, after + before - 4 * centre)]
    return jnp.asarray(numpy.stack(along), BF16), jnp.asarray(numpy.stack(across), BF16)


def stencil_levels(
    rows, cols, comps, begin, end, state_ref, mask_ref, rows_ref, turned_ref, wave_ref, spread_ref, gains_ref,
    along_ref, across_ref, place_refs, news_ref, after,
):
    levels = state_ref.shape[2]
    parts = cols // LANES
    is_ocean = lax.axis_index("comp") == comps - 1
    drag = gains_ref[0, 2]
    for ref in place_refs:
        ref[...] = jnp.zeros_like(ref)
    sea = mask_ref[0].astype(F32)
    tendency = jnp.where(is_ocean, sea, 1.0)
    first = iota((8, cols), 0) == 0
    last = iota((8, cols), 0) == 7
    places, lanes = iota((4 * levels, LANES), 0), iota((4 * levels, LANES), 1)

    def product(left, right):
        return jnp.dot(left, right, preferred_element_type=F32)

    def one_level(level, place_ref):
        half = 0.5 * wave_ref[0, level]
        spread = spread_ref[0, level]
        level_drag = jnp.where(level == 0, drag, 0.0)
        for q, sign in enumerate((-1.0, 1.0, -1.0, 1.0)):
            found = places == q * levels + level
            south = jnp.where(jnp.logical_and(found, lanes == 0), sign, 0.0).astype(BF16)
            north = jnp.where(jnp.logical_and(found, lanes == LANES - 1), 1.0, 0.0).astype(BF16)
            for term in range(2):
                at = term * LANES
                place_ref[q, at : at + 4 * levels, :LANES] = south
                at += LANES // 2
                place_ref[q, at : at + 4 * levels, cols - LANES :] = north

        def across(which, q, field):
            inner = product(jnp.concatenate(split_two(field), axis=1), across_ref[which])
            return inner + product(turned_ref[...], place_ref[q])

        def along(which, q, field):
            found = product(along_ref[which], jnp.concatenate(split_two(field), axis=0))
            west, east = (
                jnp.concatenate([rows_ref[side, p, q, pl.ds(level, 1), :] for p in range(parts)], axis=1)
                for side in range(2)
            )
            if which == 0:
                west = -west
            upper = found[:8] + jnp.where(first, west, 0.0)
            lower = found[rows - 8 :] + jnp.where(last, east, 0.0)
            return jnp.concatenate([upper, found[8 : rows - 8], lower], axis=0)

        pressure, zonal, meridional, tracer = (state_ref[0, v, level] for v in range(4))
        keep = jnp.where(is_ocean, sea, 1.0 - level_drag * (1.0 - sea))
        new_zonal = keep * (zonal - half * along(0, 0, pressure))
        new_meridional = keep * (meridional - half * across(0, 0, pressure))
        new_tracer = tracer + spread * tendency * (along(1, 1, tracer) + across(1, 1, tracer))
        beyond = product(turned_ref[...], place_ref[3]) * pressure
        divergence = along(0, 2, new_zonal) + across(0, 2, new_meridional) + beyond
        now = level - begin
        news_ref[0, now] = pressure - half * divergence
        news_ref[1, now] = new_zonal
        news_ref[2, now] = new_meridional
        news_ref[3, now] = new_tracer
        after(level)

    def some(c, carry):
        for i, place_ref in enumerate(place_refs):
            one_level(begin + c * len(place_refs) + i, place_ref)
        return carry

    lax.fori_loop(0, (end - begin) // len(place_refs), some, 0)


def place_scratch(cols):
    return [pltpu.VMEM((4, 2 * LANES, cols), BF16)] * 2


def deep_body(
    sizes, begin,
    state_ref, mask_ref, up_ref, down_ref, south_ref, north_ref, own_ref, fold_ref,
    wave_ref, spread_ref, gains_ref, along_ref, across_ref, *rest,
):
    levels, rows, cols, comps, count_x, count_y = sizes
    far_refs, (news_ref, rows_ref, turned_ref, folded_ref, *place_refs) = rest[:-6], rest[-6:]
    stencil_halos(
        *sizes, state_ref, up_ref, down_ref, south_ref, north_ref, own_ref, fold_ref, far_refs, wave_ref, gains_ref,
        folded_ref, rows_ref, turned_ref,
    )
    stencil_levels(
        rows, cols, comps, begin, levels, state_ref, mask_ref, rows_ref, turned_ref, wave_ref, spread_ref, gains_ref,
        along_ref, across_ref, place_refs, news_ref, lambda level: None,
    )


def upper_body(
    sizes, end, begun_ref, state_ref, mask_ref, rows_ref, turned_ref, wave_ref, spread_ref, gains_ref,
    along_ref, across_ref, out_ref, new_surface_ref, old_surface_ref, place0, place1, news_ref, stores,
):
    levels, rows, cols, comps, count_x, count_y = sizes

    def store(l, v):
        return pltpu.make_async_copy(news_ref.at[v, l], out_ref.at[0, v, l], stores.at[l, v])

    def after(level):
        for v in range(4):
            store(level, v).start()

    stencil_levels(
        rows, cols, comps, 0, end, state_ref, mask_ref, rows_ref, turned_ref, wave_ref, spread_ref, gains_ref,
        along_ref, across_ref, (place0, place1), news_ref, after,
    )
    for v in range(3):
        new_surface_ref[v] = news_ref[v + 1, 0]
        old_surface_ref[v] = state_ref[0, v + 1, 0]
    for l in range(end):
        for v in range(4):
            store(l, v).wait()


def deep_levels(model_state, sea_mask, halos, fars, fold_map, wave_speed, diffusivity, gains, matrices, sizes, begin):
    levels, rows, cols, comps, count_x, count_y = sizes
    parts = cols // LANES
    fold = fold_map.reshape(count_x, rows)
    vmem = pl.BlockSpec(memory_space=pltpu.VMEM)
    scalar = pl.BlockSpec(memory_space=pltpu.SMEM)
    shapes = ((4, levels - begin, rows, cols), (2, parts, 3, levels, LANES), (rows, 2 * LANES))
    return pl.pallas_call(
        functools.partial(deep_body, sizes, begin),
        in_specs=[vmem] * 8 + [scalar] * 3 + [vmem] * (2 + len(fars)),
        out_specs=[vmem] * 3,
        out_shape=[jax.ShapeDtypeStruct(shape, kind) for shape, kind in zip(shapes, (F32, F32, BF16))],
        scratch_shapes=[
            pltpu.VMEM((halo_rows(levels), LANES), F32),
        ]
        + place_scratch(cols),
        compiler_params=pltpu.CompilerParams(vmem_limit_bytes=VMEM_BYTES),
    )(model_state, sea_mask, *halos, fold, wave_speed, diffusivity, gains, *matrices, *fars)


def upper_levels(
    begun, model_state, sea_mask, edge_rows, edge_columns, wave_speed, diffusivity, gains, matrices, sizes, end
):
    levels, rows, cols, comps, count_x, count_y = sizes
    vmem = pl.BlockSpec(memory_space=pltpu.VMEM)
    scalar = pl.BlockSpec(memory_space=pltpu.SMEM)
    anywhere = pl.BlockSpec(memory_space=pl.ANY)
    surface = jax.ShapeDtypeStruct((3, rows, cols), F32)
    return pl.pallas_call(
        functools.partial(upper_body, sizes, end),
        in_specs=[anywhere] + [vmem] * 4 + [scalar] * 3 + [vmem] * 2,
        out_specs=[anywhere, vmem, vmem],
        out_shape=[jax.ShapeDtypeStruct(begun.shape, F32), surface, surface],
        scratch_shapes=place_scratch(cols)
        + [pltpu.VMEM((4, end, rows, cols), F32), pltpu.SemaphoreType.DMA((end, 4))],
        input_output_aliases={0: 0},
        compiler_params=pltpu.CompilerParams(vmem_limit_bytes=VMEM_BYTES),
    )(begun, model_state, sea_mask, edge_rows, edge_columns, wave_speed, diffusivity, gains, *matrices)


def add_slots(rows, cols, groups, slab_ref, total_refs, chunks, plan, odd):
    row_ids = packed_ids(rows)
    col_ids = packed_ids(cols)
    lane = iota((1, LANES), 1)
    one = jnp.ones((), BF16)
    zero = jnp.zeros((), BF16)
    block = 4

    def one_chunk(total_ref, chunk):
        n, first, low_slot, high_slot = plan(chunk)
        start = n * (CHANNELS * groups) + first
        for begin in range(0, DEPTH, block):
            columns, spreads = [], []
            for g in range(begin, begin + block):
                cells = slab_ref[pl.ds(start + 4 * groups + g, 1), :].astype(I32)
                slot = lane + (first + g) * LANES
                mine = jnp.logical_and(slot >= low_slot, slot < high_slot)
                row = spread_row(jnp.where(mine, cells // cols, -1)).astype(F32).astype(BF16)
                col = spread_row(cells % cols).astype(F32).astype(BF16)
                columns.append(jnp.where(col_ids == col[None], one, zero).reshape(cols, LANES))
                in_row = row_ids == row[None]
                highs, lows = [], []
                for v in range(4):
                    value = spread_row(slab_ref[pl.ds(start + v * groups + g, 1), :])
                    high, low = split_two(value)
                    highs.append(jnp.where(in_row, high[None], zero).reshape(rows, LANES))
                    lows.append(jnp.where(in_row, low[None], zero).reshape(rows, LANES))
                spreads.append(jnp.concatenate(highs + lows, axis=0))
            total_ref[...] += lax.dot_general(
                jnp.concatenate(spreads, axis=1), jnp.concatenate(columns, axis=1), (((1,), (1,)), ((), ())),
                preferred_element_type=F32,
            )

    done = 0
    for total_ref in total_refs:
        total_ref[...] = jnp.zeros_like(total_ref)

        def two(c, carry, total_ref=total_ref, done=done):
            one_chunk(total_ref, done + 2 * c)
            one_chunk(total_ref, done + 2 * c + 1)
            return carry

        def single(c, carry, total_ref=total_ref):
            one_chunk(total_ref, c)
            return carry

        step = chunks // len(total_refs)
        lax.fori_loop(0, step // 2, two, 0)
        if odd:
            lax.fori_loop(done + step // 2 * 2, done + step, single, 0)
        done = done + step


def halves_added(total_ref, rows):
    return total_ref[: 4 * rows] + total_ref[4 * rows :]


def add_own(rows, cols, comps, groups, slab_ref, total_ref, skipped):
    here = lax.axis_index("comp")
    pieces = groups // DEPTH
    near = slab_ref.shape[0] // (CHANNELS * groups) - skipped
    bounds = share_bounds(groups * LANES, comps - 1)
    is_ocean = here == comps - 1
    beside = here == comps - 2

    def plan(chunk):
        n = skipped + jnp.where(is_ocean, chunk, chunk // pieces)
        first = jnp.where(is_ocean, groups - DEPTH, chunk % pieces * DEPTH)
        return n, first, jnp.where(is_ocean, bounds[comps - 2], 0), groups * LANES

    chunks = jnp.where(is_ocean, near, jnp.where(beside, near * pieces, 0))
    add_slots(rows, cols, groups, slab_ref, [total_ref], chunks, plan, near % 2 == 1)


def own_body(rows, cols, comps, groups, slab_ref, before_ref, sent_ref, total_ref):
    add_own(rows, cols, comps, groups, slab_ref, total_ref, 1)
    sent_ref[...] = before_ref[...] + halves_added(total_ref, rows)


def other_body(
    rows, cols, comps, groups, slab_ref, before_ref, deep_ref, kept_ref, sent_ref, state_ref,
    first_ref, second_ref, copies,
):
    here = lax.axis_index("comp")
    pieces = groups // DEPTH
    near = slab_ref.shape[0] // (CHANNELS * groups)
    bounds = share_bounds(groups * LANES, comps - 1)
    is_ocean = here == comps - 1
    beside = here == comps - 2
    for_two = here == comps - 3
    middle = bounds[1] // LANES // 4 * 4
    count = deep_ref.shape[1]
    stores = [
        pltpu.make_async_copy(
            deep_ref.at[v], state_ref.at[0, v, pl.ds(state_ref.shape[2] - count, count)], copies.at[v]
        )
        for v in range(4)
    ]
    for store in stores:
        store.start()

    def plan(chunk):
        mine = chunk >= near
        n = jnp.where(for_two, chunk % near, chunk // pieces)
        first = jnp.where(for_two, jnp.where(mine, middle, 0), chunk % pieces * DEPTH)
        low_slot = jnp.where(jnp.logical_and(for_two, mine), bounds[1], 0)
        high_slot = jnp.where(for_two, jnp.where(mine, bounds[2], bounds[1]), groups * LANES)
        return n, first, low_slot, high_slot

    chunks = jnp.where(here == 0, 0, near * pieces)
    totals = [first_ref, second_ref]
    add_slots(rows, cols, groups, slab_ref, totals, chunks, plan, near * pieces // 2 % 2 == 1)
    for start in range(0, 4 * rows, rows):
        first = first_ref[start : start + rows] + first_ref[start + 4 * rows : start + 5 * rows]
        second = second_ref[start : start + rows] + second_ref[start + 4 * rows : start + 5 * rows]
        kept_ref[start : start + rows] = jnp.where(beside, 0.0, second) + jnp.where(is_ocean, first, 0.0)
        sent = jnp.where(is_ocean, 0.0, first) + jnp.where(beside, second, 0.0)
        sent_ref[start : start + rows] = sent + before_ref[start : start + rows]
    for store in stores:
        store.wait()


def scatter_own(arrived, before, rows, cols, comps, slots):
    vmem = pl.BlockSpec(memory_space=pltpu.VMEM)
    return pl.pallas_call(
        functools.partial(own_body, rows, cols, comps, slots // LANES),
        in_specs=[vmem] * 2,
        out_specs=vmem,
        out_shape=jax.ShapeDtypeStruct((4 * rows, cols), F32),
        scratch_shapes=[pltpu.VMEM((8 * rows, cols), F32)],
        compiler_params=pltpu.CompilerParams(vmem_limit_bytes=VMEM_BYTES),
    )(arrived, before)


def scatter_other(other, before, deep, state_shape, rows, cols, comps, slots):
    vmem = pl.BlockSpec(memory_space=pltpu.VMEM)
    sums = jax.ShapeDtypeStruct((4 * rows, cols), F32)
    return pl.pallas_call(
        functools.partial(other_body, rows, cols, comps, slots // LANES),
        in_specs=[vmem] * 3,
        out_specs=[vmem, vmem, pl.BlockSpec(memory_space=pl.ANY)],
        out_shape=[sums, sums, jax.ShapeDtypeStruct(state_shape, F32)],
        scratch_shapes=[pltpu.VMEM((8 * rows, cols), F32)] * 2 + [pltpu.SemaphoreType.DMA((4,))],
        compiler_params=pltpu.CompilerParams(vmem_limit_bytes=VMEM_BYTES),
    )(other, before, deep)


def finish_body(rows, comps, state_ref, new_ref, old_ref, kept_ref, came_ref, mask_ref, gains_ref, out_ref, news_ref, copies):
    is_ocean = lax.axis_index("comp") == comps - 1
    tendency = jnp.where(is_ocean, mask_ref[0].astype(F32), 1.0)
    sums = [kept_ref[v * rows : (v + 1) * rows, :] + came_ref[v * rows : (v + 1) * rows, :] for v in range(4)]
    saves = []
    for v, total, gain in ((0, sums[1], 1), (1, sums[2], 1), (2, sums[0], 0)):
        news_ref[v] = new_ref[v] + tendency * gains_ref[0, gain] * (total - sums[3] * old_ref[v])
        saves.append(pltpu.make_async_copy(news_ref.at[v], out_ref.at[0, v + 1, 0], copies.at[v]))
        saves[-1].start()
    for save in saves:
        save.wait()


def finish(state, new_surface, old_surface, kept, came, sea_mask, gains, comps):
    rows, cols = state.shape[3:]
    vmem = pl.BlockSpec(memory_space=pltpu.VMEM)
    anywhere = pl.BlockSpec(memory_space=pl.ANY)
    return pl.pallas_call(
        functools.partial(finish_body, rows, comps),
        in_specs=[anywhere] + [vmem] * 5 + [pl.BlockSpec(memory_space=pltpu.SMEM)],
        out_specs=anywhere,
        out_shape=jax.ShapeDtypeStruct(state.shape, F32),
        scratch_shapes=[pltpu.VMEM((3, rows, cols), F32), pltpu.SemaphoreType.DMA((3,))],
        input_output_aliases={0: 0},
        compiler_params=pltpu.CompilerParams(vmem_limit_bytes=VMEM_BYTES),
    )(state, new_surface, old_surface, kept, came, sea_mask, gains)


def shards(
    model_state, sea_mask, wave_speed, diffusivity, surface_gains, area_table,
    own_cells, target_cells, weight_ids, pair_counts, fold_map,
):
    comps, count_x, count_y = (lax.axis_size(a) for a in ("comp", "tx", "ty"))
    positions = count_x * count_y
    rows, cols = model_state.shape[3:]
    slots = own_cells.shape[3]
    slot_arrays = (own_cells, target_cells, weight_ids, area_table.reshape(-1, LANES), pair_counts)

    def along(block, shift):
        return lax.ppermute(block, ("tx", "ty"), [(s, (s + shift) % positions) for s in range(positions)])

    y_pair = count_y == 2
    slab_rows = CHANNELS * slots // LANES
    slab1, up, slab3, fold = first_side(model_state, slot_arrays, sea_mask, comps)
    slab3 = along(slab3, 1 + count_y)
    slab1 = along(slab1, 1)
    up = along(up, count_y)
    slab0, down, high, low, pair, before = second_side(model_state, slot_arrays, fold, sea_mask, comps, y_pair)
    arrived = jnp.concatenate([slab0, slab1, up[:slab_rows], slab3[:slab_rows]])
    down = along(down, -count_y)
    fars = []
    if y_pair and count_x == 4:
        south = north = lax.ppermute(jnp.concatenate([pair, slab3[slab_rows:]]), "ty", [(0, 1), (1, 0)])
    else:
        south = lax.ppermute(high, "ty", [(j, j + 1) for j in range(count_y - 1)])
        north = lax.ppermute(low, "ty", [(j + 1, j) for j in range(count_y - 1)])
        for shift in range(2, count_x - 1):
            pairs = []
            for i in range(count_x):
                ends = [((comps - 1) * count_x + k) * count_y + count_y - 1 for k in ((i + shift) % count_x, i)]
                pairs.append(tuple(ends))
            fars.append(lax.ppermute(fold, ("comp", "tx", "ty"), pairs))

    other = lax.ppermute(arrived, "comp", [(g, g ^ 2) for g in range(comps)])

    sizes = (*model_state.shape[2:], comps, count_x, count_y)
    cut = sizes[0] // 2
    matrices = stencil_matrices(rows, cols)
    before = scatter_own(arrived, before, rows, cols, comps, slots)
    other, before, up, down, south, north, *fars = lax.optimization_barrier(
        (other, before, up, down, south, north, *fars)
    )
    deep, edge_rows, edge_columns = deep_levels(
        model_state, sea_mask, (up, down, south, north, fold), fars, fold_map,
        wave_speed, diffusivity, surface_gains, matrices, sizes, cut,
    )
    kept, sent, begun = scatter_other(other, before, deep, model_state.shape, rows, cols, comps, slots)
    came = lax.ppermute(sent, "comp", [(g, g ^ 1) for g in range(comps)])
    new_state, new_surface, old_surface = upper_levels(
        begun, model_state, sea_mask, edge_rows, edge_columns, wave_speed, diffusivity, surface_gains,
        matrices, sizes, cut,
    )
    return finish(new_state, new_surface, old_surface, kept, came, sea_mask, surface_gains, comps)


def solution(mesh):
    in_specs = (
        P("comp", None, None, "tx", "ty"),
        P("comp", "tx", "ty"),
        P("comp", None),
        P("comp", None),
        P("comp", None),
        P(),
        P("comp", ("tx", "ty"), None, None),
        P("comp", ("tx", "ty"), None, None),
        P("comp", ("tx", "ty"), None, None),
        P("comp", ("tx", "ty"), None),
        P(),
    )
    out_specs = P("comp", None, None, "tx", "ty")
    return jax.shard_map(shards, mesh=mesh, in_specs=in_specs, out_specs=out_specs, check_vma=False)
```

```python
import functools

import jax
import jax.numpy as jnp
import numpy
from jax import lax
from jax.experimental import pallas as pl
from jax.experimental.pallas import tpu as pltpu
from jax.sharding import PartitionSpec as P

LANES = 128
DEPTH = 8
PACKED = 16
VMEM_BYTES = 28 * 1024 * 1024
F32 = jnp.float32
BF16 = jnp.bfloat16
I32 = jnp.int32
CHANNELS = 5

EDGE_P, SECOND_P, EDGE_VELOCITY, EDGE_T, MASK = range(5)


def iota(shape, dim):
    return lax.broadcasted_iota(I32, shape, dim)


def halo_rows(levels):
    return (4 * levels + 1 + 7) // 8 * 8


def split_two(values):
    high = values.astype(BF16)
    low = (values - high.astype(F32)).astype(BF16)
    return high, low


def packed_ids(count):
    ids = iota((count, LANES), 0).astype(F32).astype(BF16)
    return ids.reshape(count // PACKED, PACKED, LANES)


def spread_row(row):
    return jnp.broadcast_to(row, (PACKED, LANES))


def share_bounds(slots, shares):
    bounds = [0]
    for m in range(shares):
        bounds.append(bounds[-1] + (slots - m + shares - 1) // shares)
    return bounds


def slot_order(slots, shares, sort, half):
    place = iota((8, LANES), 0) * LANES + iota((8, LANES), 1) + half * 8 * LANES
    source = jnp.zeros((8, LANES), I32)
    bounds = share_bounds(slots, shares)
    for m in range(shares):
        inside = jnp.logical_and(place >= bounds[m], place < bounds[m + 1])
        source = jnp.where(inside, (place - bounds[m]) * shares + m, source)
    return jnp.where(sort, source, place)


def pick_rows(ref, n, source):
    total = jnp.zeros((8, LANES), I32)
    for t in range(ref.shape[3] // LANES):
        row = jnp.broadcast_to(ref[0, 0, n : n + 1, t * LANES : (t + 1) * LANES], (8, LANES))
        picked = jnp.take_along_axis(row, source % LANES, axis=1)
        total = jnp.where(source // LANES == t, picked, total)
    return total


def prepare_partner(n, comps, refs, cells_ref, out):
    own_ref, target_ref, ids_ref, table_ref, counts_ref, picked_ref = refs
    slots = own_ref.shape[3]
    groups = slots // LANES
    is_ocean = lax.axis_index("comp") == comps - 1

    @pl.when(is_ocean)
    def _():
        for half in range(groups // 8):
            source = slot_order(slots, comps - 1, True, half)
            at = slice(half * 8, (half + 1) * 8)
            cells_ref[at, :] = pick_rows(own_ref, n, source)
            picked_ref[at, :] = pick_rows(ids_ref, n, source)
            out[4 * groups + half * 8 : 4 * groups + (half + 1) * 8, :] = pick_rows(target_ref, n, source).astype(F32)

    @pl.when(jnp.logical_not(is_ocean))
    def _():
        for g in range(groups):
            cut = slice(g * LANES, (g + 1) * LANES)
            cells_ref[g : g + 1, :] = own_ref[0, 0, n : n + 1, cut]
            picked_ref[g : g + 1, :] = ids_ref[0, 0, n : n + 1, cut]
            out[4 * groups + g : 4 * groups + g + 1, :] = target_ref[0, 0, n : n + 1, cut].astype(F32)

    count = jnp.broadcast_to(counts_ref[0, :, n : n + 1], (8, LANES))
    for half in range(groups // 8):
        source = slot_order(slots, comps - 1, is_ocean, half)
        ids = picked_ref[half * 8 : (half + 1) * 8, :]
        weight = jnp.zeros((8, LANES), F32)
        for t in range(table_ref.shape[0]):
            table = jnp.broadcast_to(table_ref[t : t + 1, :], (8, LANES))
            looked = jnp.take_along_axis(table, ids % LANES, axis=1)
            weight = jnp.where(ids // LANES == t, looked, weight)
        out[3 * groups + half * 8 : 3 * groups + (half + 1) * 8, :] = jnp.where(source < count, weight, 0.0)


def gather_partner(rows, cols, halves_ref, cells_ref, parts_ref, out):
    groups = cells_ref.shape[0]
    col_ids = packed_ids(cols)
    row_ids = iota((rows, LANES), 0)
    one = jnp.ones((), BF16)
    zero = jnp.zeros((), BF16)
    wide = 2
    subs = groups // wide

    def some(c, carry):
        for sub in range(subs):
            first = (c * subs + sub) * wide
            cells = [cells_ref[pl.ds(first + g, 1), :] for g in range(wide)]
            picks = []
            for cell in cells:
                col = spread_row(cell % cols).astype(F32).astype(BF16)
                picks.append(jnp.where(col_ids == col[None], one, zero).reshape(cols, LANES))
            picks = jnp.concatenate(picks, axis=1)
            if halves_ref.shape[1] > cols:
                picks = jnp.concatenate([picks, picks], axis=0)
                found = jnp.dot(halves_ref[...], picks, preferred_element_type=F32)
            else:
                found = jnp.dot(halves_ref[...], picks, preferred_element_type=F32)
                found = found[: 3 * rows] + found[3 * rows :]
            for g in range(wide):
                in_row = row_ids == cells[g] // cols
                for place, v in enumerate((2, 0, 1)):
                    block = found[v * rows : (v + 1) * rows, g * LANES : (g + 1) * LANES]
                    block = jnp.where(in_row, block, 0.0).reshape(rows // 8, 8, LANES)
                    start = pl.multiple_of((place * groups + first + g) * 8, 8)
                    parts_ref[pl.ds(start, 8), :] = jnp.sum(block, axis=0)
        return carry

    lax.fori_loop(0, groups // (subs * wide), some, 0)
    weight = out[3 * groups : 4 * groups, :]
    for place in range(3):
        total = jnp.zeros((groups, LANES), F32)
        for i in range(8):
            total += parts_ref[pl.ds(place * groups * 8 + i, groups, stride=8), :]
        out[place * groups : (place + 1) * groups, :] = total * weight


def split_surface(surface_ref, halves_ref, rows, cols):
    for v in range(3):
        high, low = split_two(surface_ref[v])
        if halves_ref.shape[1] > cols:
            halves_ref[v * rows : (v + 1) * rows, :cols] = high
            halves_ref[v * rows : (v + 1) * rows, cols:] = low
        else:
            halves_ref[v * rows : (v + 1) * rows, :] = high
            halves_ref[(v + 3) * rows : (v + 4) * rows, :] = low


def put_rows(ref, start, levels, cols, fields, sea, edge, second):
    height = halo_rows(levels)
    for p in range(cols // LANES):
        cut = slice(p * LANES, (p + 1) * LANES)
        base = start + p * height
        ref[base + 4 * levels : base + height, :] = jnp.zeros((height - 4 * levels, LANES), F32)
        ref[base + 4 * levels : base + 4 * levels + 1, :] = sea[edge : edge + 1, cut].astype(F32)
        for q, v, at in ((EDGE_P, 0, edge), (SECOND_P, 0, second), (EDGE_VELOCITY, 1, edge), (EDGE_T, 3, edge)):
            for l in range(levels):
                row = base + q * levels + l
                ref[row : row + 1, :] = fields(v, l)[at : at + 1, cut]


def turned_columns(levels, rows, fields, sea, begin):
    edge = 1 if begin else 0
    lanes = iota((rows, LANES), 1)
    total = pltpu.roll(sea.astype(F32), (4 * levels - begin - edge) % LANES, 1)
    for l in range(levels):
        total = jnp.where(lanes // 2 == l, pltpu.roll(fields(0, l), (2 * l - begin) % LANES, 1), total)
        for q, v in ((EDGE_VELOCITY, 2), (EDGE_T, 3)):
            at = q * levels + l
            moved = pltpu.roll(fields(v, l), (at - begin - edge) % LANES, 1)
            total = jnp.where(lanes == at, moved, total)
    return total.T[: halo_rows(levels)]


def first_body(
    levels, rows, cols, comps,
    state_hbm, own_hbm, target_hbm, ids_hbm, table_hbm, counts_hbm, mask_hbm,
    slab1_ref, up_ref, slab3_ref, fold_ref,
    surface_ref, own_ref, target_ref, ids_ref, table_ref, counts_ref, edge_ref, sea_edge_ref, mask_ref, columns_ref,
    halves_ref, cells_ref, picked_ref, parts_ref, copies, column_copies,
):
    sources = (
        own_hbm, target_hbm, ids_hbm, table_hbm, counts_hbm, state_hbm.at[0, pl.ds(1, 3), 0],
        state_hbm.at[0, :, :, pl.ds(rows - 8, 8), :], mask_hbm.at[0, pl.ds(rows - 8, 8), :],
    )
    places = (own_ref, target_ref, ids_ref, table_ref, counts_ref, surface_ref, edge_ref, sea_edge_ref)
    fetches = [
        pltpu.make_async_copy(source, place, copies.at[i])
        for i, (source, place) in enumerate(zip(sources, places))
    ]
    outer = pl.ds(cols - LANES, LANES)
    for_fold = [
        pltpu.make_async_copy(state_hbm.at[0, v, :, :, outer], columns_ref.at[i], column_copies.at[i])
        for i, v in enumerate((0, 2, 3))
    ] + [pltpu.make_async_copy(mask_hbm.at[0, :, outer], mask_ref, column_copies.at[3])]
    northern = lax.axis_index("ty") == lax.axis_size("ty") - 1
    folds = jnp.logical_and(lax.axis_index("comp") == comps - 1, northern)
    for fetch in fetches:
        fetch.start()

    @pl.when(folds)
    def _():
        for fetch in for_fold:
            fetch.start()

    for fetch in fetches[:5]:
        fetch.wait()
    refs = (own_ref, target_ref, ids_ref, table_ref, counts_ref, picked_ref)
    slabs = ((3, slab3_ref), (1, slab1_ref), (2, up_ref))
    for i, (n, out) in enumerate(slabs):
        prepare_partner(n, comps, refs, cells_ref.at[i], out)
    fetches[5].wait()
    split_surface(surface_ref, halves_ref, rows, cols)
    for i, (n, out) in enumerate(slabs):
        gather_partner(rows, cols, halves_ref, cells_ref.at[i], parts_ref, out)
    for fetch in fetches[6:]:
        fetch.wait()
    slab_rows = slab1_ref.shape[0]
    tall = halo_rows(levels) * (cols // LANES)
    put_rows(up_ref, slab_rows, levels, cols, lambda v, l: edge_ref.at[v, l], sea_edge_ref, 7, 6)

    @pl.when(folds)
    def _():
        for fetch in for_fold:
            fetch.wait()
        places = {0: 0, 2: 1, 3: 2}
        fold_ref[...] = turned_columns(
            levels, rows, lambda v, l: columns_ref[places[v], l], mask_ref[...], LANES - 2
        )

    @pl.when(jnp.logical_not(folds))
    def _():
        fold_ref[...] = jnp.zeros_like(fold_ref)

    up_ref[slab_rows + tall :, :] = fold_ref[...]
    slab3_ref[slab_rows:, :] = fold_ref[...]


def gather_scratch(rows, cols, slots, stacked):
    return [
        pltpu.VMEM((6 * rows, cols) if stacked else (3 * rows, 2 * cols), BF16),
        pltpu.VMEM((3, slots // LANES, LANES), I32),
        pltpu.VMEM((slots // LANES, LANES), I32),
        pltpu.VMEM((3 * slots // LANES * 8, LANES), F32),
    ]


def first_side(model_state, slot_arrays, sea_mask, comps):
    levels, rows, cols = model_state.shape[2:]
    near, slots = slot_arrays[0].shape[2:]
    table_shape = slot_arrays[3].shape
    slab = CHANNELS * slots // LANES
    height = halo_rows(levels)
    heights = (slab, slab + height * (cols // LANES) + height, slab + height, height)
    vmem = pl.BlockSpec(memory_space=pltpu.VMEM)
    arrays = (model_state, *slot_arrays, sea_mask)
    return pl.pallas_call(
        functools.partial(first_body, levels, rows, cols, comps),
        in_specs=[pl.BlockSpec(memory_space=pltpu.HBM)] * len(arrays),
        out_specs=[vmem] * len(heights),
        out_shape=[jax.ShapeDtypeStruct((h, LANES), F32) for h in heights],
        scratch_shapes=[pltpu.VMEM((3, rows, cols), F32)]
        + [pltpu.VMEM((1, 1, near, slots), I32)] * 3
        + [pltpu.VMEM(table_shape, F32), pltpu.VMEM((1, 1, near), I32)]
        + [
            pltpu.VMEM((4, levels, 8, cols), F32),
            pltpu.VMEM((8, cols), I32),
            pltpu.VMEM((rows, LANES), I32),
            pltpu.VMEM((3, levels, rows, LANES), F32),
        ]
        + gather_scratch(rows, cols, slots, True)
        + [pltpu.SemaphoreType.DMA((8,)), pltpu.SemaphoreType.DMA((4,))],
        compiler_params=pltpu.CompilerParams(vmem_limit_bytes=VMEM_BYTES),
    )(*(pltpu.with_memory_space_constraint(array, pltpu.HBM) for array in arrays))


def second_body(
    levels, rows, cols, comps, y_pair,
    state_ref, own_ref, target_ref, ids_ref, table_ref, counts_ref, fold_ref, mask_hbm,
    slab0_ref, down_ref, high_ref, low_ref, pair_ref, sent_ref,
    halves_ref, cells_ref, picked_ref, parts_ref, mask_ref, total_ref, copied,
):
    fetch = pltpu.make_async_copy(mask_hbm, mask_ref, copied)
    fetch.start()
    split_surface(state_ref.at[0, pl.ds(1, 3), 0], halves_ref, rows, cols)
    refs = (own_ref, target_ref, ids_ref, table_ref, counts_ref, picked_ref)
    prepare_partner(0, comps, refs, cells_ref.at[0], slab0_ref)
    gather_partner(rows, cols, halves_ref, cells_ref.at[0], parts_ref, slab0_ref)
    fetch.wait()
    put_rows(down_ref, 0, levels, cols, lambda v, l: state_ref.at[0, v, l], mask_ref.at[0], 0, 1)
    down_ref[halo_rows(levels) * (cols // LANES) :, :] = fold_ref[...]
    index_y = lax.axis_index("ty")
    high_used = index_y == 0 if y_pair else index_y >= 0
    low_used = index_y > 0 if y_pair else index_y >= 0

    def columns(start, begin):
        cut = slice(start, start + LANES)
        return turned_columns(levels, rows, lambda v, l: state_ref[0, v, l, :, cut], mask_ref[0, :, cut], begin)

    @pl.when(high_used)
    def _():
        highest = columns(cols - LANES, LANES - 2)
        high_ref[...] = highest
        pair_ref[...] = highest

    @pl.when(jnp.logical_not(high_used))
    def _():
        high_ref[...] = jnp.zeros_like(high_ref)

    @pl.when(low_used)
    def _():
        lowest = columns(0, 0)
        low_ref[...] = lowest
        pair_ref[...] = lowest

    @pl.when(jnp.logical_not(low_used))
    def _():
        low_ref[...] = jnp.zeros_like(low_ref)

    add_own(rows, cols, comps, own_ref.shape[3] // LANES, slab0_ref, total_ref, 0)
    sent_ref[...] = halves_added(total_ref, rows)


def second_side(model_state, slot_arrays, fold, sea_mask, comps, y_pair):
    levels, rows, cols = model_state.shape[2:]
    slots = slot_arrays[0].shape[3]
    height = halo_rows(levels)
    heights = (CHANNELS * slots // LANES, height * (cols // LANES) + height, height, height, height)
    vmem = pl.BlockSpec(memory_space=pltpu.VMEM)
    return pl.pallas_call(
        functools.partial(second_body, levels, rows, cols, comps, y_pair),
        in_specs=[vmem] * 7 + [pl.BlockSpec(memory_space=pltpu.HBM)],
        out_specs=[vmem] * (len(heights) + 1),
        out_shape=[jax.ShapeDtypeStruct((h, LANES), F32) for h in heights]
        + [jax.ShapeDtypeStruct((4 * rows, cols), F32)],
        scratch_shapes=gather_scratch(rows, cols, slots, False)
        + [pltpu.VMEM((1, rows, cols), I32), pltpu.VMEM((8 * rows, cols), F32), pltpu.SemaphoreType.DMA],
        compiler_params=pltpu.CompilerParams(vmem_limit_bytes=VMEM_BYTES),
    )(model_state, *slot_arrays, fold, pltpu.with_memory_space_constraint(sea_mask, pltpu.HBM))


def stencil_halos(
    levels, rows, cols, comps, count_x, count_y,
    state_ref, up_ref, down_ref, south_ref, north_ref, own_ref, fold_ref, far_refs, wave_ref, gains_ref,
    folded_ref, rows_ref, turned_ref,
):
    height = halo_rows(levels)
    parts = cols // LANES
    index_x = lax.axis_index("tx")
    index_y = lax.axis_index("ty")
    is_ocean = lax.axis_index("comp") == comps - 1
    last_y = index_y == count_y - 1
    has_west = jnp.where(jnp.logical_or(is_ocean, index_x > 0), 1.0, 0.0)
    has_east = jnp.where(jnp.logical_or(is_ocean, index_x < count_x - 1), 1.0, 0.0)
    has_south = jnp.where(index_y > 0, 1.0, 0.0)
    has_north = jnp.where(jnp.logical_or(is_ocean, jnp.logical_not(last_y)), 1.0, 0.0)
    drag = gains_ref[0, 2]
    mask_at = 4 * levels

    fold = fold_ref[pl.ds(index_x, 1), :]
    total = jnp.zeros((height, LANES), F32)
    up_start = up_ref.shape[0] - height * (parts + 1)
    sources = [(0, own_ref, 0), (-1, up_ref, up_start + height * parts), (1, down_ref, height * parts)]
    if north_ref.shape[0] > height:
        sources.append((2, north_ref, height))
    else:
        sources += [(shift, ref, 0) for shift, ref in zip(range(2, count_x - 1), far_refs)]
    for shift, ref, start in sources:
        at = lax.rem(index_x + shift + count_x, count_x)
        chosen = (iota((rows, rows), 0) + at * rows == fold).astype(F32)
        total += jnp.dot(
            ref[start : start + height, :], chosen,
            precision=lax.Precision.HIGHEST, preferred_element_type=F32,
        )
    folded_ref[...] = total

    line = iota((levels, LANES), 0)
    halves = jnp.zeros((levels, LANES), F32)
    for l in range(levels):
        halves = jnp.where(line == l, 0.5 * wave_ref[0, l], halves)

    def keeping(sea_values, drags):
        return jnp.where(is_ocean, sea_values, 1.0 - drags * (1.0 - sea_values))

    drags = jnp.where(line == 0, drag, 0.0)

    def by_level(ref, start, q):
        return ref[start + q * levels : start + (q + 1) * levels, :]

    for side, (ref, begin, sign, has) in enumerate(
        ((up_ref, up_start, 1.0, has_west), (down_ref, 0, -1.0, has_east))
    ):
        for p in range(parts):
            start = begin + p * height
            kept = keeping(ref[start + mask_at : start + mask_at + 1, :], drags)
            fixed = kept * (by_level(ref, start, EDGE_VELOCITY) + sign * halves * by_level(ref, start, SECOND_P))
            inner = rows - 1 if side else 0
            own = jnp.concatenate(
                [state_ref[0, 0, l, inner : inner + 1, p * LANES : (p + 1) * LANES] for l in range(levels)], axis=0
            )
            rows_ref[side, p, 0] = has * by_level(ref, start, EDGE_P)
            rows_ref[side, p, 1] = has * by_level(ref, start, EDGE_T)
            rows_ref[side, p, 2] = has * (fixed - sign * kept * halves * own)

    even = lambda ref: ref[pl.ds(0, levels, stride=2), :]
    odd = lambda ref: ref[pl.ds(1, levels, stride=2), :]
    north = [
        jnp.where(last_y, jnp.where(is_ocean, folded, 0.0), low)
        for folded, low in (
            (odd(folded_ref), even(north_ref)),
            (even(folded_ref), odd(north_ref)),
            (-by_level(folded_ref, 0, EDGE_VELOCITY), by_level(north_ref, 0, EDGE_VELOCITY)),
            (by_level(folded_ref, 0, EDGE_T), by_level(north_ref, 0, EDGE_T)),
            (folded_ref[mask_at : mask_at + 1, :], north_ref[mask_at : mask_at + 1, :]),
        )
    ]
    south = [
        odd(south_ref), even(south_ref), by_level(south_ref, 0, EDGE_VELOCITY), by_level(south_ref, 0, EDGE_T),
        south_ref[mask_at : mask_at + 1, :],
    ]
    fill = jnp.zeros((LANES // 2 - 4 * levels, LANES), F32)
    lines = []
    for (edge, second, velocity, tracer, sea), sign, has in (
        (south, 1.0, has_south), (north, -1.0, has_north)
    ):
        kept = keeping(sea, drags)
        fixed = has * kept * (velocity + sign * halves * second)
        lines += [has * edge, has * tracer, fixed, has * kept * halves, fill]
    high, low = split_two(jnp.concatenate(lines, axis=0).T)
    turned_ref[:, :LANES] = high
    turned_ref[:, LANES:] = low


def stencil_matrices(rows, cols):
    steps = [[numpy.eye(n, k=k, dtype=numpy.float32) for k in (1, -1, 0)] for n in (rows, cols)]
    after, before, _ = steps[0]
    along = [numpy.concatenate([m, m], axis=1) for m in (after - before, after + before)]
    before, after, centre = steps[1]
    across = [numpy.concatenate([m, m], axis=0) for m in (after - before, after + before - 4 * centre)]
    return jnp.asarray(numpy.stack(along), BF16), jnp.asarray(numpy.stack(across), BF16)


def stencil_levels(
    rows, cols, comps, begin, end, state_ref, mask_ref, rows_ref, turned_ref, wave_ref, spread_ref, gains_ref,
    along_ref, across_ref, place_refs, news_ref, after,
):
    levels = state_ref.shape[2]
    parts = cols // LANES
    is_ocean = lax.axis_index("comp") == comps - 1
    drag = gains_ref[0, 2]
    for ref in place_refs:
        ref[...] = jnp.zeros_like(ref)
    sea = mask_ref[0].astype(F32)
    tendency = jnp.where(is_ocean, sea, 1.0)
    first = iota((8, cols), 0) == 0
    last = iota((8, cols), 0) == 7
    places, lanes = iota((4 * levels, LANES), 0), iota((4 * levels, LANES), 1)

    def product(left, right):
        return jnp.dot(left, right, preferred_element_type=F32)

    def one_level(level, place_ref):
        half = 0.5 * wave_ref[0, level]
        spread = spread_ref[0, level]
        level_drag = jnp.where(level == 0, drag, 0.0)
        for q, sign in enumerate((-1.0, 1.0, -1.0, 1.0)):
            found = places == q * levels + level
            south = jnp.where(jnp.logical_and(found, lanes == 0), sign, 0.0).astype(BF16)
            north = jnp.where(jnp.logical_and(found, lanes == LANES - 1), 1.0, 0.0).astype(BF16)
            for term in range(2):
                at = term * LANES
                place_ref[q, at : at + 4 * levels, :LANES] = south
                at += LANES // 2
                place_ref[q, at : at + 4 * levels, cols - LANES :] = north

        def across(which, q, field):
            inner = product(jnp.concatenate(split_two(field), axis=1), across_ref[which])
            return inner + product(turned_ref[...], place_ref[q])

        def along(which, q, field):
            found = product(along_ref[which], jnp.concatenate(split_two(field), axis=0))
            west, east = (
                jnp.concatenate([rows_ref[side, p, q, pl.ds(level, 1), :] for p in range(parts)], axis=1)
                for side in range(2)
            )
            if which == 0:
                west = -west
            upper = found[:8] + jnp.where(first, west, 0.0)
            lower = found[rows - 8 :] + jnp.where(last, east, 0.0)
            return jnp.concatenate([upper, found[8 : rows - 8], lower], axis=0)

        pressure, zonal, meridional, tracer = (state_ref[0, v, level] for v in range(4))
        keep = jnp.where(is_ocean, sea, 1.0 - level_drag * (1.0 - sea))
        new_zonal = keep * (zonal - half * along(0, 0, pressure))
        new_meridional = keep * (meridional - half * across(0, 0, pressure))
        new_tracer = tracer + spread * tendency * (along(1, 1, tracer) + across(1, 1, tracer))
        beyond = product(turned_ref[...], place_ref[3]) * pressure
        divergence = along(0, 2, new_zonal) + across(0, 2, new_meridional) + beyond
        now = level - begin
        news_ref[0, now] = pressure - half * divergence
        news_ref[1, now] = new_zonal
        news_ref[2, now] = new_meridional
        news_ref[3, now] = new_tracer
        after(level)

    def some(c, carry):
        for i in range(length):
            one_level(begin + c * length + i, place_refs[i % len(place_refs)])
        return carry

    length = 4 if (end - begin) % 4 == 0 else 1
    lax.fori_loop(0, (end - begin) // length, some, 0)


def place_scratch(cols):
    return [pltpu.VMEM((4, 2 * LANES, cols), BF16)] * 2


def deep_body(
    sizes, begin,
    state_ref, mask_ref, up_ref, down_ref, south_ref, north_ref, own_ref, fold_ref,
    wave_ref, spread_ref, gains_ref, along_ref, across_ref, *rest,
):
    levels, rows, cols, comps, count_x, count_y = sizes
    far_refs, (news_ref, rows_ref, turned_ref, folded_ref, *place_refs) = rest[:-6], rest[-6:]
    stencil_halos(
        *sizes, state_ref, up_ref, down_ref, south_ref, north_ref, own_ref, fold_ref, far_refs, wave_ref, gains_ref,
        folded_ref, rows_ref, turned_ref,
    )
    stencil_levels(
        rows, cols, comps, begin, levels, state_ref, mask_ref, rows_ref, turned_ref, wave_ref, spread_ref, gains_ref,
        along_ref, across_ref, place_refs, news_ref, lambda level: None,
    )


def upper_body(
    sizes, end, begun_ref, state_ref, mask_ref, rows_ref, turned_ref, wave_ref, spread_ref, gains_ref,
    along_ref, across_ref, out_ref, new_surface_ref, old_surface_ref, place0, place1, news_ref, stores,
):
    levels, rows, cols, comps, count_x, count_y = sizes

    def store(l, v):
        return pltpu.make_async_copy(news_ref.at[v, l], out_ref.at[0, v, l], stores.at[l, v])

    def after(level):
        for v in range(4):
            store(level, v).start()

    stencil_levels(
        rows, cols, comps, 0, end, state_ref, mask_ref, rows_ref, turned_ref, wave_ref, spread_ref, gains_ref,
        along_ref, across_ref, (place0, place1), news_ref, after,
    )
    for v in range(3):
        new_surface_ref[v] = news_ref[v + 1, 0]
        old_surface_ref[v] = state_ref[0, v + 1, 0]
    for l in range(end):
        for v in range(4):
            store(l, v).wait()


def deep_levels(model_state, sea_mask, halos, fars, fold_map, wave_speed, diffusivity, gains, matrices, sizes, begin):
    levels, rows, cols, comps, count_x, count_y = sizes
    parts = cols // LANES
    fold = fold_map.reshape(count_x, rows)
    vmem = pl.BlockSpec(memory_space=pltpu.VMEM)
    scalar = pl.BlockSpec(memory_space=pltpu.SMEM)
    shapes = ((4, levels - begin, rows, cols), (2, parts, 3, levels, LANES), (rows, 2 * LANES))
    return pl.pallas_call(
        functools.partial(deep_body, sizes, begin),
        in_specs=[vmem] * 8 + [scalar] * 3 + [vmem] * (2 + len(fars)),
        out_specs=[vmem] * 3,
        out_shape=[jax.ShapeDtypeStruct(shape, kind) for shape, kind in zip(shapes, (F32, F32, BF16))],
        scratch_shapes=[
            pltpu.VMEM((halo_rows(levels), LANES), F32),
        ]
        + place_scratch(cols),
        compiler_params=pltpu.CompilerParams(vmem_limit_bytes=VMEM_BYTES),
    )(model_state, sea_mask, *halos, fold, wave_speed, diffusivity, gains, *matrices, *fars)


def upper_levels(
    begun, model_state, sea_mask, edge_rows, edge_columns, wave_speed, diffusivity, gains, matrices, sizes, end
):
    levels, rows, cols, comps, count_x, count_y = sizes
    vmem = pl.BlockSpec(memory_space=pltpu.VMEM)
    scalar = pl.BlockSpec(memory_space=pltpu.SMEM)
    anywhere = pl.BlockSpec(memory_space=pl.ANY)
    surface = jax.ShapeDtypeStruct((3, rows, cols), F32)
    return pl.pallas_call(
        functools.partial(upper_body, sizes, end),
        in_specs=[anywhere] + [vmem] * 4 + [scalar] * 3 + [vmem] * 2,
        out_specs=[anywhere, vmem, vmem],
        out_shape=[jax.ShapeDtypeStruct(begun.shape, F32), surface, surface],
        scratch_shapes=place_scratch(cols)
        + [pltpu.VMEM((4, end, rows, cols), F32), pltpu.SemaphoreType.DMA((end, 4))],
        input_output_aliases={0: 0},
        compiler_params=pltpu.CompilerParams(vmem_limit_bytes=VMEM_BYTES),
    )(begun, model_state, sea_mask, edge_rows, edge_columns, wave_speed, diffusivity, gains, *matrices)


def add_slots(rows, cols, groups, slab_ref, total_ref, chunks, plan, length, runs=1):
    row_ids = packed_ids(rows)
    col_ids = packed_ids(cols)
    lane = iota((1, LANES), 1)
    one = jnp.ones((), BF16)
    zero = jnp.zeros((), BF16)
    block = 4

    def one_chunk(total_ref, chunk):
        n, first, low_slot, high_slot = plan(chunk)
        start = n * (CHANNELS * groups) + first
        for begin in range(0, DEPTH, block):
            columns, spreads = [], []
            for g in range(begin, begin + block):
                cells = slab_ref[pl.ds(start + 4 * groups + g, 1), :].astype(I32)
                slot = lane + (first + g) * LANES
                mine = jnp.logical_and(slot >= low_slot, slot < high_slot)
                row = spread_row(jnp.where(mine, cells // cols, -1)).astype(F32).astype(BF16)
                col = spread_row(cells % cols).astype(F32).astype(BF16)
                columns.append(jnp.where(col_ids == col[None], one, zero).reshape(cols, LANES))
                in_row = row_ids == row[None]
                highs, lows = [], []
                for v in range(4):
                    value = spread_row(slab_ref[pl.ds(start + v * groups + g, 1), :])
                    high, low = split_two(value)
                    highs.append(jnp.where(in_row, high[None], zero).reshape(rows, LANES))
                    lows.append(jnp.where(in_row, low[None], zero).reshape(rows, LANES))
                spreads.append(jnp.concatenate(highs + lows, axis=0))
            total_ref[...] += lax.dot_general(
                jnp.concatenate(spreads, axis=1), jnp.concatenate(columns, axis=1), (((1,), (1,)), ((), ())),
                preferred_element_type=F32,
            )

    def turn(c, carry):
        for i in range(length):
            one_chunk(total_ref if runs == 1 else total_ref.at[c], c * length + i)
        return carry

    def single(c, carry):
        one_chunk(total_ref, c)
        return carry

    total_ref[...] = jnp.zeros_like(total_ref)
    turns = chunks // length
    lax.fori_loop(0, turns, turn, 0)
    if runs == 1:
        lax.fori_loop(turns * length, chunks, single, 0)


def halves_added(total_ref, rows):
    return total_ref[: 4 * rows] + total_ref[4 * rows :]


def add_own(rows, cols, comps, groups, slab_ref, total_ref, skipped):
    here = lax.axis_index("comp")
    pieces = groups // DEPTH
    near = slab_ref.shape[0] // (CHANNELS * groups) - skipped
    bounds = share_bounds(groups * LANES, comps - 1)
    is_ocean = here == comps - 1
    beside = here == comps - 2

    def plan(chunk):
        n = skipped + jnp.where(is_ocean, chunk, chunk // pieces)
        first = jnp.where(is_ocean, groups - DEPTH, chunk % pieces * DEPTH)
        return n, first, jnp.where(is_ocean, bounds[comps - 2], 0), groups * LANES

    chunks = jnp.where(is_ocean, near, jnp.where(beside, near * pieces, 0))
    add_slots(rows, cols, groups, slab_ref, total_ref, chunks, plan, 3 if near == 3 else 2)


def own_body(rows, cols, comps, groups, slab_ref, before_ref, sent_ref, total_ref):
    add_own(rows, cols, comps, groups, slab_ref, total_ref, 1)
    sent_ref[...] = before_ref[...] + halves_added(total_ref, rows)


def other_body(
    rows, cols, comps, groups, slab_ref, before_ref, deep_ref, kept_ref, sent_ref, state_ref,
    totals_ref, copies,
):
    here = lax.axis_index("comp")
    pieces = groups // DEPTH
    near = slab_ref.shape[0] // (CHANNELS * groups)
    bounds = share_bounds(groups * LANES, comps - 1)
    is_ocean = here == comps - 1
    beside = here == comps - 2
    for_two = here == comps - 3
    middle = bounds[1] // LANES // 4 * 4
    count = deep_ref.shape[1]
    stores = [
        pltpu.make_async_copy(
            deep_ref.at[v], state_ref.at[0, v, pl.ds(state_ref.shape[2] - count, count)], copies.at[v]
        )
        for v in range(4)
    ]
    for store in stores:
        store.start()

    def plan(chunk):
        mine = chunk >= near
        n = jnp.where(for_two, chunk % near, chunk // pieces)
        first = jnp.where(for_two, jnp.where(mine, middle, 0), chunk % pieces * DEPTH)
        low_slot = jnp.where(jnp.logical_and(for_two, mine), bounds[1], 0)
        high_slot = jnp.where(for_two, jnp.where(mine, bounds[2], bounds[1]), groups * LANES)
        return n, first, low_slot, high_slot

    chunks = jnp.where(here == 0, 0, near * pieces)
    add_slots(rows, cols, groups, slab_ref, totals_ref, chunks, plan, near * pieces // 2, 2)
    first_ref, second_ref = totals_ref.at[0], totals_ref.at[1]
    for start in range(0, 4 * rows, rows):
        first = first_ref[start : start + rows] + first_ref[start + 4 * rows : start + 5 * rows]
        second = second_ref[start : start + rows] + second_ref[start + 4 * rows : start + 5 * rows]
        kept_ref[start : start + rows] = jnp.where(beside, 0.0, second) + jnp.where(is_ocean, first, 0.0)
        sent = jnp.where(is_ocean, 0.0, first) + jnp.where(beside, second, 0.0)
        sent_ref[start : start + rows] = sent + before_ref[start : start + rows]
    for store in stores:
        store.wait()


def scatter_own(arrived, before, rows, cols, comps, slots):
    vmem = pl.BlockSpec(memory_space=pltpu.VMEM)
    return pl.pallas_call(
        functools.partial(own_body, rows, cols, comps, slots // LANES),
        in_specs=[vmem] * 2,
        out_specs=vmem,
        out_shape=jax.ShapeDtypeStruct((4 * rows, cols), F32),
        scratch_shapes=[pltpu.VMEM((8 * rows, cols), F32)],
        compiler_params=pltpu.CompilerParams(vmem_limit_bytes=VMEM_BYTES),
    )(arrived, before)


def scatter_other(other, before, deep, state_shape, rows, cols, comps, slots):
    vmem = pl.BlockSpec(memory_space=pltpu.VMEM)
    sums = jax.ShapeDtypeStruct((4 * rows, cols), F32)
    return pl.pallas_call(
        functools.partial(other_body, rows, cols, comps, slots // LANES),
        in_specs=[vmem] * 3,
        out_specs=[vmem, vmem, pl.BlockSpec(memory_space=pl.ANY)],
        out_shape=[sums, sums, jax.ShapeDtypeStruct(state_shape, F32)],
        scratch_shapes=[pltpu.VMEM((2, 8 * rows, cols), F32), pltpu.SemaphoreType.DMA((4,))],
        compiler_params=pltpu.CompilerParams(vmem_limit_bytes=VMEM_BYTES),
    )(other, before, deep)


def finish_body(rows, comps, state_ref, new_ref, old_ref, kept_ref, came_ref, mask_ref, gains_ref, out_ref, news_ref, copies):
    is_ocean = lax.axis_index("comp") == comps - 1
    tendency = jnp.where(is_ocean, mask_ref[0].astype(F32), 1.0)
    sums = [kept_ref[v * rows : (v + 1) * rows, :] + came_ref[v * rows : (v + 1) * rows, :] for v in range(4)]
    saves = []
    for v, total, gain in ((0, sums[1], 1), (1, sums[2], 1), (2, sums[0], 0)):
        news_ref[v] = new_ref[v] + tendency * gains_ref[0, gain] * (total - sums[3] * old_ref[v])
        saves.append(pltpu.make_async_copy(news_ref.at[v], out_ref.at[0, v + 1, 0], copies.at[v]))
        saves[-1].start()
    for save in saves:
        save.wait()


def finish(state, new_surface, old_surface, kept, came, sea_mask, gains, comps):
    rows, cols = state.shape[3:]
    vmem = pl.BlockSpec(memory_space=pltpu.VMEM)
    anywhere = pl.BlockSpec(memory_space=pl.ANY)
    return pl.pallas_call(
        functools.partial(finish_body, rows, comps),
        in_specs=[anywhere] + [vmem] * 5 + [pl.BlockSpec(memory_space=pltpu.SMEM)],
        out_specs=anywhere,
        out_shape=jax.ShapeDtypeStruct(state.shape, F32),
        scratch_shapes=[pltpu.VMEM((3, rows, cols), F32), pltpu.SemaphoreType.DMA((3,))],
        input_output_aliases={0: 0},
        compiler_params=pltpu.CompilerParams(vmem_limit_bytes=VMEM_BYTES),
    )(state, new_surface, old_surface, kept, came, sea_mask, gains)


def shards(
    model_state, sea_mask, wave_speed, diffusivity, surface_gains, area_table,
    own_cells, target_cells, weight_ids, pair_counts, fold_map,
):
    comps, count_x, count_y = (lax.axis_size(a) for a in ("comp", "tx", "ty"))
    positions = count_x * count_y
    rows, cols = model_state.shape[3:]
    slots = own_cells.shape[3]
    slot_arrays = (own_cells, target_cells, weight_ids, area_table.reshape(-1, LANES), pair_counts)

    def along(block, shift):
        return lax.ppermute(block, ("tx", "ty"), [(s, (s + shift) % positions) for s in range(positions)])

    y_pair = count_y == 2
    slab_rows = CHANNELS * slots // LANES
    slab1, up, slab3, fold = first_side(model_state, slot_arrays, sea_mask, comps)
    slab3 = along(slab3, 1 + count_y)
    slab1 = along(slab1, 1)
    up = along(up, count_y)
    slab0, down, high, low, pair, before = second_side(model_state, slot_arrays, fold, sea_mask, comps, y_pair)
    arrived = jnp.concatenate([slab0, slab1, up[:slab_rows], slab3[:slab_rows]])
    down = along(down, -count_y)
    fars = []
    if y_pair and count_x == 4:
        south = north = lax.ppermute(jnp.concatenate([pair, slab3[slab_rows:]]), "ty", [(0, 1), (1, 0)])
    else:
        south = lax.ppermute(high, "ty", [(j, j + 1) for j in range(count_y - 1)])
        north = lax.ppermute(low, "ty", [(j + 1, j) for j in range(count_y - 1)])
        for shift in range(2, count_x - 1):
            pairs = []
            for i in range(count_x):
                ends = [((comps - 1) * count_x + k) * count_y + count_y - 1 for k in ((i + shift) % count_x, i)]
                pairs.append(tuple(ends))
            fars.append(lax.ppermute(fold, ("comp", "tx", "ty"), pairs))

    other = lax.ppermute(arrived, "comp", [(g, g ^ 2) for g in range(comps)])

    sizes = (*model_state.shape[2:], comps, count_x, count_y)
    cut = sizes[0] // 2
    matrices = stencil_matrices(rows, cols)
    before = scatter_own(arrived, before, rows, cols, comps, slots)
    deep, edge_rows, edge_columns = deep_levels(
        model_state, sea_mask, (up, down, south, north, fold), fars, fold_map,
        wave_speed, diffusivity, surface_gains, matrices, sizes, cut,
    )
    kept, sent, begun = scatter_other(other, before, deep, model_state.shape, rows, cols, comps, slots)
    came = lax.ppermute(sent, "comp", [(g, g ^ 1) for g in range(comps)])
    new_state, new_surface, old_surface = upper_levels(
        begun, model_state, sea_mask, edge_rows, edge_columns, wave_speed, diffusivity, surface_gains,
        matrices, sizes, cut,
    )
    return finish(new_state, new_surface, old_surface, kept, came, sea_mask, surface_gains, comps)


def solution(mesh):
    in_specs = (
        P("comp", None, None, "tx", "ty"),
        P("comp", "tx", "ty"),
        P("comp", None),
        P("comp", None),
        P("comp", None),
        P(),
        P("comp", ("tx", "ty"), None, None),
        P("comp", ("tx", "ty"), None, None),
        P("comp", ("tx", "ty"), None, None),
        P("comp", ("tx", "ty"), None),
        P(),
    )
    out_specs = P("comp", None, None, "tx", "ty")
    return jax.shard_map(shards, mesh=mesh, in_specs=in_specs, out_specs=out_specs, check_vma=False)
```

```python
import functools

import jax
import jax.numpy as jnp
import numpy
from jax import lax
from jax.experimental import pallas as pl
from jax.experimental.pallas import tpu as pltpu
from jax.sharding import PartitionSpec as P

LANES = 128
DEPTH = 8
PACKED = 16
VMEM_BYTES = 28 * 1024 * 1024
F32 = jnp.float32
BF16 = jnp.bfloat16
I32 = jnp.int32
CHANNELS = 5

EDGE_P, SECOND_P, EDGE_VELOCITY, EDGE_T, MASK = range(5)


def iota(shape, dim):
    return lax.broadcasted_iota(I32, shape, dim)


def halo_rows(levels):
    return (4 * levels + 1 + 7) // 8 * 8


def split_two(values):
    high = values.astype(BF16)
    low = (values - high.astype(F32)).astype(BF16)
    return high, low


def packed_ids(count):
    ids = iota((count, LANES), 0).astype(F32).astype(BF16)
    return ids.reshape(count // PACKED, PACKED, LANES)


def spread_row(row):
    return jnp.broadcast_to(row, (PACKED, LANES))


def share_bounds(slots, shares):
    bounds = [0]
    for m in range(shares):
        bounds.append(bounds[-1] + (slots - m + shares - 1) // shares)
    return bounds


def slot_order(slots, shares, sort, half):
    place = iota((8, LANES), 0) * LANES + iota((8, LANES), 1) + half * 8 * LANES
    source = jnp.zeros((8, LANES), I32)
    bounds = share_bounds(slots, shares)
    for m in range(shares):
        inside = jnp.logical_and(place >= bounds[m], place < bounds[m + 1])
        source = jnp.where(inside, (place - bounds[m]) * shares + m, source)
    return jnp.where(sort, source, place)


def pick_rows(ref, n, source):
    total = jnp.zeros((8, LANES), I32)
    for t in range(ref.shape[3] // LANES):
        row = jnp.broadcast_to(ref[0, 0, n : n + 1, t * LANES : (t + 1) * LANES], (8, LANES))
        picked = jnp.take_along_axis(row, source % LANES, axis=1)
        total = jnp.where(source // LANES == t, picked, total)
    return total


def prepare_partner(n, comps, refs, cells_ref, out):
    own_ref, target_ref, ids_ref, table_ref, counts_ref, picked_ref = refs
    slots = own_ref.shape[3]
    groups = slots // LANES
    is_ocean = lax.axis_index("comp") == comps - 1

    @pl.when(is_ocean)
    def _():
        for half in range(groups // 8):
            source = slot_order(slots, comps - 1, True, half)
            at = slice(half * 8, (half + 1) * 8)
            cells_ref[at, :] = pick_rows(own_ref, n, source)
            picked_ref[at, :] = pick_rows(ids_ref, n, source)
            out[4 * groups + half * 8 : 4 * groups + (half + 1) * 8, :] = pick_rows(target_ref, n, source).astype(F32)

    @pl.when(jnp.logical_not(is_ocean))
    def _():
        for g in range(groups):
            cut = slice(g * LANES, (g + 1) * LANES)
            cells_ref[g : g + 1, :] = own_ref[0, 0, n : n + 1, cut]
            picked_ref[g : g + 1, :] = ids_ref[0, 0, n : n + 1, cut]
            out[4 * groups + g : 4 * groups + g + 1, :] = target_ref[0, 0, n : n + 1, cut].astype(F32)

    count = jnp.broadcast_to(counts_ref[0, :, n : n + 1], (8, LANES))
    for half in range(groups // 8):
        source = slot_order(slots, comps - 1, is_ocean, half)
        ids = picked_ref[half * 8 : (half + 1) * 8, :]
        weight = jnp.zeros((8, LANES), F32)
        for t in range(table_ref.shape[0]):
            table = jnp.broadcast_to(table_ref[t : t + 1, :], (8, LANES))
            looked = jnp.take_along_axis(table, ids % LANES, axis=1)
            weight = jnp.where(ids // LANES == t, looked, weight)
        out[3 * groups + half * 8 : 3 * groups + (half + 1) * 8, :] = jnp.where(source < count, weight, 0.0)


def gather_partner(rows, cols, halves_ref, cells_ref, parts_ref, out):
    groups = cells_ref.shape[0]
    col_ids = packed_ids(cols)
    row_ids = iota((rows, LANES), 0)
    one = jnp.ones((), BF16)
    zero = jnp.zeros((), BF16)
    wide = 2
    subs = groups // wide

    def some(c, carry):
        for sub in range(subs):
            first = (c * subs + sub) * wide
            cells = [cells_ref[pl.ds(first + g, 1), :] for g in range(wide)]
            picks = []
            for cell in cells:
                col = spread_row(cell % cols).astype(F32).astype(BF16)
                picks.append(jnp.where(col_ids == col[None], one, zero).reshape(cols, LANES))
            picks = jnp.concatenate(picks, axis=1)
            if halves_ref.shape[1] > cols:
                picks = jnp.concatenate([picks, picks], axis=0)
                found = jnp.dot(halves_ref[...], picks, preferred_element_type=F32)
            else:
                found = jnp.dot(halves_ref[...], picks, preferred_element_type=F32)
                found = found[: 3 * rows] + found[3 * rows :]
            for g in range(wide):
                in_row = row_ids == cells[g] // cols
                for place, v in enumerate((2, 0, 1)):
                    block = found[v * rows : (v + 1) * rows, g * LANES : (g + 1) * LANES]
                    block = jnp.where(in_row, block, 0.0).reshape(rows // 8, 8, LANES)
                    start = pl.multiple_of((place * groups + first + g) * 8, 8)
                    parts_ref[pl.ds(start, 8), :] = jnp.sum(block, axis=0)
        return carry

    lax.fori_loop(0, groups // (subs * wide), some, 0)
    weight = out[3 * groups : 4 * groups, :]
    for place in range(3):
        total = jnp.zeros((groups, LANES), F32)
        for i in range(8):
            total += parts_ref[pl.ds(place * groups * 8 + i, groups, stride=8), :]
        out[place * groups : (place + 1) * groups, :] = total * weight


def split_surface(surface_ref, halves_ref, rows, cols):
    for v in range(3):
        high, low = split_two(surface_ref[v])
        if halves_ref.shape[1] > cols:
            halves_ref[v * rows : (v + 1) * rows, :cols] = high
            halves_ref[v * rows : (v + 1) * rows, cols:] = low
        else:
            halves_ref[v * rows : (v + 1) * rows, :] = high
            halves_ref[(v + 3) * rows : (v + 4) * rows, :] = low


def put_rows(ref, start, levels, cols, fields, sea, edge, second):
    height = halo_rows(levels)
    for p in range(cols // LANES):
        cut = slice(p * LANES, (p + 1) * LANES)
        base = start + p * height
        ref[base + 4 * levels : base + height, :] = jnp.zeros((height - 4 * levels, LANES), F32)
        ref[base + 4 * levels : base + 4 * levels + 1, :] = sea[edge : edge + 1, cut].astype(F32)
        for q, v, at in ((EDGE_P, 0, edge), (SECOND_P, 0, second), (EDGE_VELOCITY, 1, edge), (EDGE_T, 3, edge)):
            for l in range(levels):
                row = base + q * levels + l
                ref[row : row + 1, :] = fields(v, l)[at : at + 1, cut]


def turned_columns(levels, rows, fields, sea, begin):
    edge = 1 if begin else 0
    lanes = iota((rows, LANES), 1)
    total = pltpu.roll(sea.astype(F32), (4 * levels - begin - edge) % LANES, 1)
    for l in range(levels):
        total = jnp.where(lanes // 2 == l, pltpu.roll(fields(0, l), (2 * l - begin) % LANES, 1), total)
        for q, v in ((EDGE_VELOCITY, 2), (EDGE_T, 3)):
            at = q * levels + l
            moved = pltpu.roll(fields(v, l), (at - begin - edge) % LANES, 1)
            total = jnp.where(lanes == at, moved, total)
    return total.T[: halo_rows(levels)]


def first_body(
    levels, rows, cols, comps,
    state_hbm, own_hbm, target_hbm, ids_hbm, table_hbm, counts_hbm, mask_hbm,
    slab1_ref, up_ref, slab3_ref, fold_ref,
    surface_ref, own_ref, target_ref, ids_ref, table_ref, counts_ref, edge_ref, sea_edge_ref, mask_ref, columns_ref,
    halves_ref, cells_ref, picked_ref, parts_ref, copies, column_copies,
):
    sources = (
        own_hbm, target_hbm, ids_hbm, table_hbm, counts_hbm, state_hbm.at[0, pl.ds(1, 3), 0],
        state_hbm.at[0, :, :, pl.ds(rows - 8, 8), :], mask_hbm.at[0, pl.ds(rows - 8, 8), :],
    )
    places = (own_ref, target_ref, ids_ref, table_ref, counts_ref, surface_ref, edge_ref, sea_edge_ref)
    fetches = [
        pltpu.make_async_copy(source, place, copies.at[i])
        for i, (source, place) in enumerate(zip(sources, places))
    ]
    outer = pl.ds(cols - LANES, LANES)
    for_fold = [
        pltpu.make_async_copy(state_hbm.at[0, v, :, :, outer], columns_ref.at[i], column_copies.at[i])
        for i, v in enumerate((0, 2, 3))
    ] + [pltpu.make_async_copy(mask_hbm.at[0, :, outer], mask_ref, column_copies.at[3])]
    northern = lax.axis_index("ty") == lax.axis_size("ty") - 1
    folds = jnp.logical_and(lax.axis_index("comp") == comps - 1, northern)
    for fetch in fetches:
        fetch.start()

    @pl.when(folds)
    def _():
        for fetch in for_fold:
            fetch.start()

    for fetch in fetches[:5]:
        fetch.wait()
    refs = (own_ref, target_ref, ids_ref, table_ref, counts_ref, picked_ref)
    slabs = ((3, slab3_ref), (1, slab1_ref), (2, up_ref))
    for i, (n, out) in enumerate(slabs):
        prepare_partner(n, comps, refs, cells_ref.at[i], out)
    fetches[5].wait()
    split_surface(surface_ref, halves_ref, rows, cols)
    for i, (n, out) in enumerate(slabs):
        gather_partner(rows, cols, halves_ref, cells_ref.at[i], parts_ref, out)
    for fetch in fetches[6:]:
        fetch.wait()
    slab_rows = slab1_ref.shape[0]
    tall = halo_rows(levels) * (cols // LANES)
    put_rows(up_ref, slab_rows, levels, cols, lambda v, l: edge_ref.at[v, l], sea_edge_ref, 7, 6)

    @pl.when(folds)
    def _():
        for fetch in for_fold:
            fetch.wait()
        places = {0: 0, 2: 1, 3: 2}
        fold_ref[...] = turned_columns(
            levels, rows, lambda v, l: columns_ref[places[v], l], mask_ref[...], LANES - 2
        )

    @pl.when(jnp.logical_not(folds))
    def _():
        fold_ref[...] = jnp.zeros_like(fold_ref)

    up_ref[slab_rows + tall :, :] = fold_ref[...]
    slab3_ref[slab_rows:, :] = fold_ref[...]


def gather_scratch(rows, cols, slots, stacked):
    return [
        pltpu.VMEM((6 * rows, cols) if stacked else (3 * rows, 2 * cols), BF16),
        pltpu.VMEM((3, slots // LANES, LANES), I32),
        pltpu.VMEM((slots // LANES, LANES), I32),
        pltpu.VMEM((3 * slots // LANES * 8, LANES), F32),
    ]


def first_side(model_state, slot_arrays, sea_mask, comps):
    levels, rows, cols = model_state.shape[2:]
    near, slots = slot_arrays[0].shape[2:]
    table_shape = slot_arrays[3].shape
    slab = CHANNELS * slots // LANES
    height = halo_rows(levels)
    heights = (slab, slab + height * (cols // LANES) + height, slab + height, height)
    vmem = pl.BlockSpec(memory_space=pltpu.VMEM)
    arrays = (model_state, *slot_arrays, sea_mask)
    return pl.pallas_call(
        functools.partial(first_body, levels, rows, cols, comps),
        in_specs=[pl.BlockSpec(memory_space=pltpu.HBM)] * len(arrays),
        out_specs=[vmem] * len(heights),
        out_shape=[jax.ShapeDtypeStruct((h, LANES), F32) for h in heights],
        scratch_shapes=[pltpu.VMEM((3, rows, cols), F32)]
        + [pltpu.VMEM((1, 1, near, slots), I32)] * 3
        + [pltpu.VMEM(table_shape, F32), pltpu.VMEM((1, 1, near), I32)]
        + [
            pltpu.VMEM((4, levels, 8, cols), F32),
            pltpu.VMEM((8, cols), I32),
            pltpu.VMEM((rows, LANES), I32),
            pltpu.VMEM((3, levels, rows, LANES), F32),
        ]
        + gather_scratch(rows, cols, slots, True)
        + [pltpu.SemaphoreType.DMA((8,)), pltpu.SemaphoreType.DMA((4,))],
        compiler_params=pltpu.CompilerParams(vmem_limit_bytes=VMEM_BYTES),
    )(*(pltpu.with_memory_space_constraint(array, pltpu.HBM) for array in arrays))


def second_body(
    levels, rows, cols, comps, y_pair,
    state_ref, own_ref, target_ref, ids_ref, table_ref, counts_ref, fold_ref, mask_hbm,
    slab0_ref, down_ref, high_ref, low_ref, pair_ref, sent_ref,
    halves_ref, cells_ref, picked_ref, parts_ref, mask_ref, total_ref, copied,
):
    fetch = pltpu.make_async_copy(mask_hbm, mask_ref, copied)
    fetch.start()
    split_surface(state_ref.at[0, pl.ds(1, 3), 0], halves_ref, rows, cols)
    refs = (own_ref, target_ref, ids_ref, table_ref, counts_ref, picked_ref)
    prepare_partner(0, comps, refs, cells_ref.at[0], slab0_ref)
    gather_partner(rows, cols, halves_ref, cells_ref.at[0], parts_ref, slab0_ref)
    fetch.wait()
    put_rows(down_ref, 0, levels, cols, lambda v, l: state_ref.at[0, v, l], mask_ref.at[0], 0, 1)
    down_ref[halo_rows(levels) * (cols // LANES) :, :] = fold_ref[...]
    index_y = lax.axis_index("ty")
    high_used = index_y == 0 if y_pair else index_y >= 0
    low_used = index_y > 0 if y_pair else index_y >= 0

    def columns(start, begin):
        cut = slice(start, start + LANES)
        return turned_columns(levels, rows, lambda v, l: state_ref[0, v, l, :, cut], mask_ref[0, :, cut], begin)

    @pl.when(high_used)
    def _():
        highest = columns(cols - LANES, LANES - 2)
        high_ref[...] = highest
        pair_ref[...] = highest

    @pl.when(jnp.logical_not(high_used))
    def _():
        high_ref[...] = jnp.zeros_like(high_ref)

    @pl.when(low_used)
    def _():
        lowest = columns(0, 0)
        low_ref[...] = lowest
        pair_ref[...] = lowest

    @pl.when(jnp.logical_not(low_used))
    def _():
        low_ref[...] = jnp.zeros_like(low_ref)

    add_own(rows, cols, comps, own_ref.shape[3] // LANES, slab0_ref, total_ref, 0)
    sent_ref[...] = halves_added(total_ref, rows)


def second_side(model_state, slot_arrays, fold, sea_mask, comps, y_pair):
    levels, rows, cols = model_state.shape[2:]
    slots = slot_arrays[0].shape[3]
    height = halo_rows(levels)
    heights = (CHANNELS * slots // LANES, height * (cols // LANES) + height, height, height, height)
    vmem = pl.BlockSpec(memory_space=pltpu.VMEM)
    return pl.pallas_call(
        functools.partial(second_body, levels, rows, cols, comps, y_pair),
        in_specs=[vmem] * 7 + [pl.BlockSpec(memory_space=pltpu.HBM)],
        out_specs=[vmem] * (len(heights) + 1),
        out_shape=[jax.ShapeDtypeStruct((h, LANES), F32) for h in heights]
        + [jax.ShapeDtypeStruct((4 * rows, cols), F32)],
        scratch_shapes=gather_scratch(rows, cols, slots, False)
        + [pltpu.VMEM((1, rows, cols), I32), pltpu.VMEM((8 * rows, cols), F32), pltpu.SemaphoreType.DMA],
        compiler_params=pltpu.CompilerParams(vmem_limit_bytes=VMEM_BYTES),
    )(model_state, *slot_arrays, fold, pltpu.with_memory_space_constraint(sea_mask, pltpu.HBM))


def stencil_halos(
    levels, rows, cols, comps, count_x, count_y,
    state_ref, up_ref, down_ref, south_ref, north_ref, own_ref, fold_ref, far_refs, wave_ref, gains_ref,
    folded_ref, rows_ref, turned_ref,
):
    height = halo_rows(levels)
    parts = cols // LANES
    index_x = lax.axis_index("tx")
    index_y = lax.axis_index("ty")
    is_ocean = lax.axis_index("comp") == comps - 1
    last_y = index_y == count_y - 1
    has_west = jnp.where(jnp.logical_or(is_ocean, index_x > 0), 1.0, 0.0)
    has_east = jnp.where(jnp.logical_or(is_ocean, index_x < count_x - 1), 1.0, 0.0)
    has_south = jnp.where(index_y > 0, 1.0, 0.0)
    has_north = jnp.where(jnp.logical_or(is_ocean, jnp.logical_not(last_y)), 1.0, 0.0)
    drag = gains_ref[0, 2]
    mask_at = 4 * levels

    fold = fold_ref[pl.ds(index_x, 1), :]
    total = jnp.zeros((height, LANES), F32)
    up_start = up_ref.shape[0] - height * (parts + 1)
    sources = [(0, own_ref, 0), (-1, up_ref, up_start + height * parts), (1, down_ref, height * parts)]
    if north_ref.shape[0] > height:
        sources.append((2, north_ref, height))
    else:
        sources += [(shift, ref, 0) for shift, ref in zip(range(2, count_x - 1), far_refs)]
    for shift, ref, start in sources:
        at = lax.rem(index_x + shift + count_x, count_x)
        chosen = (iota((rows, rows), 0) + at * rows == fold).astype(F32)
        total += jnp.dot(
            ref[start : start + height, :], chosen,
            precision=lax.Precision.HIGHEST, preferred_element_type=F32,
        )
    folded_ref[...] = total

    line = iota((levels, LANES), 0)
    halves = jnp.zeros((levels, LANES), F32)
    for l in range(levels):
        halves = jnp.where(line == l, 0.5 * wave_ref[0, l], halves)

    def keeping(sea_values, drags):
        return jnp.where(is_ocean, sea_values, 1.0 - drags * (1.0 - sea_values))

    drags = jnp.where(line == 0, drag, 0.0)

    def by_level(ref, start, q):
        return ref[start + q * levels : start + (q + 1) * levels, :]

    for side, (ref, begin, sign, has) in enumerate(
        ((up_ref, up_start, 1.0, has_west), (down_ref, 0, -1.0, has_east))
    ):
        for p in range(parts):
            start = begin + p * height
            kept = keeping(ref[start + mask_at : start + mask_at + 1, :], drags)
            fixed = kept * (by_level(ref, start, EDGE_VELOCITY) + sign * halves * by_level(ref, start, SECOND_P))
            inner = rows - 1 if side else 0
            own = jnp.concatenate(
                [state_ref[0, 0, l, inner : inner + 1, p * LANES : (p + 1) * LANES] for l in range(levels)], axis=0
            )
            rows_ref[side, p, 0] = has * by_level(ref, start, EDGE_P)
            rows_ref[side, p, 1] = has * by_level(ref, start, EDGE_T)
            rows_ref[side, p, 2] = has * (fixed - sign * kept * halves * own)

    even = lambda ref: ref[pl.ds(0, levels, stride=2), :]
    odd = lambda ref: ref[pl.ds(1, levels, stride=2), :]
    north = [
        jnp.where(last_y, jnp.where(is_ocean, folded, 0.0), low)
        for folded, low in (
            (odd(folded_ref), even(north_ref)),
            (even(folded_ref), odd(north_ref)),
            (-by_level(folded_ref, 0, EDGE_VELOCITY), by_level(north_ref, 0, EDGE_VELOCITY)),
            (by_level(folded_ref, 0, EDGE_T), by_level(north_ref, 0, EDGE_T)),
            (folded_ref[mask_at : mask_at + 1, :], north_ref[mask_at : mask_at + 1, :]),
        )
    ]
    south = [
        odd(south_ref), even(south_ref), by_level(south_ref, 0, EDGE_VELOCITY), by_level(south_ref, 0, EDGE_T),
        south_ref[mask_at : mask_at + 1, :],
    ]
    fill = jnp.zeros((LANES // 2 - 4 * levels, LANES), F32)
    lines = []
    for (edge, second, velocity, tracer, sea), sign, has in (
        (south, 1.0, has_south), (north, -1.0, has_north)
    ):
        kept = keeping(sea, drags)
        fixed = has * kept * (velocity + sign * halves * second)
        lines += [has * edge, has * tracer, fixed, has * kept * halves, fill]
    high, low = split_two(jnp.concatenate(lines, axis=0).T)
    turned_ref[:, :LANES] = high
    turned_ref[:, LANES:] = low


def stencil_matrices(rows, cols):
    steps = [[numpy.eye(n, k=k, dtype=numpy.float32) for k in (1, -1, 0)] for n in (rows, cols)]
    after, before, _ = steps[0]
    along = [numpy.concatenate([m, m], axis=1) for m in (after - before, after + before)]
    before, after, centre = steps[1]
    across = [numpy.concatenate([m, m], axis=0) for m in (after - before, after + before - 4 * centre)]
    return jnp.asarray(numpy.stack(along), BF16), jnp.asarray(numpy.stack(across), BF16)


def halo_places(levels, begin, end):
    count = end - begin
    places = numpy.zeros((2 * LANES, 4 * count * LANES), numpy.float32)
    for q, sign in enumerate((-1.0, 1.0, -1.0, 1.0)):
        for l in range(begin, end):
            tile = (q * count + l - begin) * LANES
            for term in range(2):
                at = term * LANES + q * levels + l
                places[at, tile] = sign
                places[at + LANES // 2, tile + LANES - 1] = 1.0
    return jnp.asarray(places, BF16)


def stencil_levels(
    rows, cols, comps, begin, end, state_ref, mask_ref, rows_ref, turned_ref, wave_ref, spread_ref, gains_ref,
    along_ref, across_ref, places_ref, scratch, news_ref, after,
):
    pressures_ref, tracers_ref, edges_ref, sums_ref, warmths_ref = scratch
    parts = cols // LANES
    count = end - begin
    is_ocean = lax.axis_index("comp") == comps - 1
    drag = gains_ref[0, 2]
    sea = mask_ref[0].astype(F32)
    tendency = jnp.where(is_ocean, sea, 1.0)
    first = iota((8, cols), 0) == 0
    last = iota((8, cols), 0) == 7
    lanes = iota((rows, LANES), 1)
    turns = 2 if count % 2 == 0 else 1

    def product(left, right):
        return jnp.dot(left, right, preferred_element_type=F32)

    def each(body):
        def some(c, carry):
            for i in range(turns):
                body(c * turns + i)
            return carry

        lax.fori_loop(0, count // turns, some, 0)

    def line(now):
        return pl.ds(pl.multiple_of(now * rows, rows), rows)

    def put_terms(ref, now, field):
        high, low = split_two(field)
        ref[line(now), :cols] = high
        ref[line(now), cols:] = low

    def edges(q, now):
        start = pl.multiple_of((q * count + now) * LANES, LANES)
        tile = edges_ref[:, pl.ds(start, LANES)]
        middle = [jnp.zeros((rows, LANES), F32)] * (parts - 2)
        outer = [jnp.where(lanes == at, tile, 0.0) for at in (0, LANES - 1)]
        return jnp.concatenate(outer[:1] + middle + outer[1:], axis=1)

    def along(which, q, level, field):
        found = product(along_ref[which], jnp.concatenate(split_two(field), axis=0))
        west, east = (
            jnp.concatenate([rows_ref[side, p, q, pl.ds(level, 1), :] for p in range(parts)], axis=1)
            for side in range(2)
        )
        if which == 0:
            west = -west
        upper = found[:8] + jnp.where(first, west, 0.0)
        lower = found[rows - 8 :] + jnp.where(last, east, 0.0)
        return jnp.concatenate([upper, found[8 : rows - 8], lower], axis=0)

    def split_fields(now):
        put_terms(pressures_ref, now, state_ref[0, 0, begin + now])
        put_terms(tracers_ref, now, state_ref[0, 3, begin + now])

    def velocities(now):
        level = begin + now
        half = 0.5 * wave_ref[0, level]
        spread = spread_ref[0, level]
        level_drag = jnp.where(level == 0, drag, 0.0)
        pressure, zonal, meridional, tracer = (state_ref[0, v, level] for v in range(4))
        keep = jnp.where(is_ocean, sea, 1.0 - level_drag * (1.0 - sea))
        new_zonal = keep * (zonal - half * along(0, 0, level, pressure))
        new_meridional = keep * (meridional - half * (sums_ref[line(now), :] + edges(0, now)))
        put_terms(pressures_ref, now, new_meridional)
        news_ref[1, now] = new_zonal
        news_ref[2, now] = new_meridional
        news_ref[3, now] = tracer + spread * tendency * (
            along(1, 1, level, tracer) + warmths_ref[line(now), :] + edges(1, now)
        )
        news_ref[0, now] = pressure - half * (along(0, 2, level, new_zonal) + edges(3, now) * pressure)
        after(level, (1, 2, 3))

    def pressures(now):
        level = begin + now
        half = 0.5 * wave_ref[0, level]
        news_ref[0, now] = news_ref[0, now] - half * (sums_ref[line(now), :] + edges(2, now))
        after(level, (0,))

    each(split_fields)
    edges_ref[...] = product(turned_ref[...], places_ref[...])
    sums_ref[...] = product(pressures_ref[...], across_ref[0])
    warmths_ref[...] = product(tracers_ref[...], across_ref[1])
    each(velocities)
    sums_ref[...] = product(pressures_ref[...], across_ref[0])
    each(pressures)


def stencil_scratch(rows, cols, count):
    return [
        pltpu.VMEM((count * rows, 2 * cols), BF16),
        pltpu.VMEM((count * rows, 2 * cols), BF16),
        pltpu.VMEM((rows, 4 * count * LANES), F32),
        pltpu.VMEM((count * rows, cols), F32),
        pltpu.VMEM((count * rows, cols), F32),
    ]


def deep_body(
    sizes, begin,
    state_ref, mask_ref, up_ref, down_ref, south_ref, north_ref, own_ref, fold_ref,
    wave_ref, spread_ref, gains_ref, along_ref, across_ref, places_ref, *rest,
):
    levels, rows, cols, comps, count_x, count_y = sizes
    far_refs, (news_ref, rows_ref, turned_ref, folded_ref, *scratch) = rest[:-9], rest[-9:]
    stencil_halos(
        *sizes, state_ref, up_ref, down_ref, south_ref, north_ref, own_ref, fold_ref, far_refs, wave_ref, gains_ref,
        folded_ref, rows_ref, turned_ref,
    )
    stencil_levels(
        rows, cols, comps, begin, levels, state_ref, mask_ref, rows_ref, turned_ref, wave_ref, spread_ref, gains_ref,
        along_ref, across_ref, places_ref, scratch, news_ref, lambda level, fields: None,
    )


def upper_body(
    sizes, end, begun_ref, state_ref, mask_ref, rows_ref, turned_ref, wave_ref, spread_ref, gains_ref,
    along_ref, across_ref, places_ref, out_ref, new_surface_ref, old_surface_ref, *rest,
):
    levels, rows, cols, comps, count_x, count_y = sizes
    *scratch, news_ref, stores = rest

    def store(l, v):
        return pltpu.make_async_copy(news_ref.at[v, l], out_ref.at[0, v, l], stores.at[l, v])

    def after(level, fields):
        for v in fields:
            store(level, v).start()

    stencil_levels(
        rows, cols, comps, 0, end, state_ref, mask_ref, rows_ref, turned_ref, wave_ref, spread_ref, gains_ref,
        along_ref, across_ref, places_ref, scratch, news_ref, after,
    )
    for v in range(3):
        new_surface_ref[v] = news_ref[v + 1, 0]
        old_surface_ref[v] = state_ref[0, v + 1, 0]
    for l in range(end):
        for v in range(4):
            store(l, v).wait()


def deep_levels(model_state, sea_mask, halos, fars, fold_map, wave_speed, diffusivity, gains, matrices, sizes, begin):
    levels, rows, cols, comps, count_x, count_y = sizes
    parts = cols // LANES
    fold = fold_map.reshape(count_x, rows)
    vmem = pl.BlockSpec(memory_space=pltpu.VMEM)
    scalar = pl.BlockSpec(memory_space=pltpu.SMEM)
    shapes = ((4, levels - begin, rows, cols), (2, parts, 3, levels, LANES), (rows, 2 * LANES))
    return pl.pallas_call(
        functools.partial(deep_body, sizes, begin),
        in_specs=[vmem] * 8 + [scalar] * 3 + [vmem] * (3 + len(fars)),
        out_specs=[vmem] * 3,
        out_shape=[jax.ShapeDtypeStruct(shape, kind) for shape, kind in zip(shapes, (F32, F32, BF16))],
        scratch_shapes=[
            pltpu.VMEM((halo_rows(levels), LANES), F32),
        ]
        + stencil_scratch(rows, cols, levels - begin),
        compiler_params=pltpu.CompilerParams(vmem_limit_bytes=VMEM_BYTES),
    )(model_state, sea_mask, *halos, fold, wave_speed, diffusivity, gains, *matrices, halo_places(levels, begin, levels), *fars)


def upper_levels(
    begun, model_state, sea_mask, edge_rows, edge_columns, wave_speed, diffusivity, gains, matrices, sizes, end
):
    levels, rows, cols, comps, count_x, count_y = sizes
    vmem = pl.BlockSpec(memory_space=pltpu.VMEM)
    scalar = pl.BlockSpec(memory_space=pltpu.SMEM)
    anywhere = pl.BlockSpec(memory_space=pl.ANY)
    surface = jax.ShapeDtypeStruct((3, rows, cols), F32)
    return pl.pallas_call(
        functools.partial(upper_body, sizes, end),
        in_specs=[anywhere] + [vmem] * 4 + [scalar] * 3 + [vmem] * 3,
        out_specs=[anywhere, vmem, vmem],
        out_shape=[jax.ShapeDtypeStruct(begun.shape, F32), surface, surface],
        scratch_shapes=stencil_scratch(rows, cols, end)
        + [pltpu.VMEM((4, end, rows, cols), F32), pltpu.SemaphoreType.DMA((end, 4))],
        input_output_aliases={0: 0},
        compiler_params=pltpu.CompilerParams(vmem_limit_bytes=VMEM_BYTES),
    )(begun, model_state, sea_mask, edge_rows, edge_columns, wave_speed, diffusivity, gains, *matrices, halo_places(levels, 0, end))


def add_slots(rows, cols, groups, slab_ref, total_ref, chunks, plan, length, runs=1):
    row_ids = packed_ids(rows)
    col_ids = packed_ids(cols)
    lane = iota((1, LANES), 1)
    one = jnp.ones((), BF16)
    zero = jnp.zeros((), BF16)
    block = 4

    def one_chunk(total_ref, chunk):
        n, first, low_slot, high_slot = plan(chunk)
        start = n * (CHANNELS * groups) + first
        for begin in range(0, DEPTH, block):
            columns, spreads = [], []
            for g in range(begin, begin + block):
                cells = slab_ref[pl.ds(start + 4 * groups + g, 1), :].astype(I32)
                slot = lane + (first + g) * LANES
                mine = jnp.logical_and(slot >= low_slot, slot < high_slot)
                row = spread_row(jnp.where(mine, cells // cols, -1)).astype(F32).astype(BF16)
                col = spread_row(cells % cols).astype(F32).astype(BF16)
                columns.append(jnp.where(col_ids == col[None], one, zero).reshape(cols, LANES))
                in_row = row_ids == row[None]
                highs, lows = [], []
                for v in range(4):
                    value = spread_row(slab_ref[pl.ds(start + v * groups + g, 1), :])
                    high, low = split_two(value)
                    highs.append(jnp.where(in_row, high[None], zero).reshape(rows, LANES))
                    lows.append(jnp.where(in_row, low[None], zero).reshape(rows, LANES))
                spreads.append(jnp.concatenate(highs + lows, axis=0))
            total_ref[...] += lax.dot_general(
                jnp.concatenate(spreads, axis=1), jnp.concatenate(columns, axis=1), (((1,), (1,)), ((), ())),
                preferred_element_type=F32,
            )

    def turn(c, carry):
        for i in range(length):
            one_chunk(total_ref if runs == 1 else total_ref.at[c], c * length + i)
        return carry

    def single(c, carry):
        one_chunk(total_ref, c)
        return carry

    total_ref[...] = jnp.zeros_like(total_ref)
    turns = chunks // length
    lax.fori_loop(0, turns, turn, 0)
    if runs == 1:
        lax.fori_loop(turns * length, chunks, single, 0)


def halves_added(total_ref, rows):
    return total_ref[: 4 * rows] + total_ref[4 * rows :]


def add_own(rows, cols, comps, groups, slab_ref, total_ref, skipped):
    here = lax.axis_index("comp")
    pieces = groups // DEPTH
    near = slab_ref.shape[0] // (CHANNELS * groups) - skipped
    bounds = share_bounds(groups * LANES, comps - 1)
    is_ocean = here == comps - 1
    beside = here == comps - 2

    def plan(chunk):
        n = skipped + jnp.where(is_ocean, chunk, chunk // pieces)
        first = jnp.where(is_ocean, groups - DEPTH, chunk % pieces * DEPTH)
        return n, first, jnp.where(is_ocean, bounds[comps - 2], 0), groups * LANES

    chunks = jnp.where(is_ocean, near, jnp.where(beside, near * pieces, 0))
    add_slots(rows, cols, groups, slab_ref, total_ref, chunks, plan, 3 if near == 3 else 2)


def own_body(rows, cols, comps, groups, slab_ref, before_ref, sent_ref, total_ref):
    add_own(rows, cols, comps, groups, slab_ref, total_ref, 0)
    sent_ref[...] = before_ref[...] + halves_added(total_ref, rows)


def other_body(
    rows, cols, comps, groups, slab_ref, before_ref, deep_ref, kept_ref, sent_ref, state_ref,
    totals_ref, copies,
):
    here = lax.axis_index("comp")
    pieces = groups // DEPTH
    near = slab_ref.shape[0] // (CHANNELS * groups)
    bounds = share_bounds(groups * LANES, comps - 1)
    is_ocean = here == comps - 1
    beside = here == comps - 2
    for_two = here == comps - 3
    middle = bounds[1] // LANES // 4 * 4
    count = deep_ref.shape[1]
    stores = [
        pltpu.make_async_copy(
            deep_ref.at[v], state_ref.at[0, v, pl.ds(state_ref.shape[2] - count, count)], copies.at[v]
        )
        for v in range(4)
    ]
    for store in stores:
        store.start()

    def plan(chunk):
        mine = chunk >= near
        n = jnp.where(for_two, chunk % near, chunk // pieces)
        first = jnp.where(for_two, jnp.where(mine, middle, 0), chunk % pieces * DEPTH)
        low_slot = jnp.where(jnp.logical_and(for_two, mine), bounds[1], 0)
        high_slot = jnp.where(for_two, jnp.where(mine, bounds[2], bounds[1]), groups * LANES)
        return n, first, low_slot, high_slot

    chunks = jnp.where(here == 0, 0, near * pieces)
    add_slots(rows, cols, groups, slab_ref, totals_ref, chunks, plan, near * pieces // 2, 2)
    first_ref, second_ref = totals_ref.at[0], totals_ref.at[1]
    for start in range(0, 4 * rows, rows):
        first = first_ref[start : start + rows] + first_ref[start + 4 * rows : start + 5 * rows]
        second = second_ref[start : start + rows] + second_ref[start + 4 * rows : start + 5 * rows]
        kept_ref[start : start + rows] = jnp.where(beside, 0.0, second) + jnp.where(is_ocean, first, 0.0)
        sent = jnp.where(is_ocean, 0.0, first) + jnp.where(beside, second, 0.0)
        sent_ref[start : start + rows] = sent + before_ref[start : start + rows]
    for store in stores:
        store.wait()


def scatter_own(arrived, before, rows, cols, comps, slots):
    vmem = pl.BlockSpec(memory_space=pltpu.VMEM)
    return pl.pallas_call(
        functools.partial(own_body, rows, cols, comps, slots // LANES),
        in_specs=[vmem] * 2,
        out_specs=vmem,
        out_shape=jax.ShapeDtypeStruct((4 * rows, cols), F32),
        scratch_shapes=[pltpu.VMEM((8 * rows, cols), F32)],
        compiler_params=pltpu.CompilerParams(vmem_limit_bytes=VMEM_BYTES),
    )(arrived, before)


def scatter_other(other, before, deep, state_shape, rows, cols, comps, slots):
    vmem = pl.BlockSpec(memory_space=pltpu.VMEM)
    sums = jax.ShapeDtypeStruct((4 * rows, cols), F32)
    return pl.pallas_call(
        functools.partial(other_body, rows, cols, comps, slots // LANES),
        in_specs=[vmem] * 3,
        out_specs=[vmem, vmem, pl.BlockSpec(memory_space=pl.ANY)],
        out_shape=[sums, sums, jax.ShapeDtypeStruct(state_shape, F32)],
        scratch_shapes=[pltpu.VMEM((2, 8 * rows, cols), F32), pltpu.SemaphoreType.DMA((4,))],
        compiler_params=pltpu.CompilerParams(vmem_limit_bytes=VMEM_BYTES),
    )(other, before, deep)


def finish_body(rows, comps, state_ref, new_ref, old_ref, kept_ref, came_ref, mask_ref, gains_ref, out_ref, news_ref, copies):
    is_ocean = lax.axis_index("comp") == comps - 1
    tendency = jnp.where(is_ocean, mask_ref[0].astype(F32), 1.0)
    sums = [kept_ref[v * rows : (v + 1) * rows, :] + came_ref[v * rows : (v + 1) * rows, :] for v in range(4)]
    saves = []
    for v, total, gain in ((0, sums[1], 1), (1, sums[2], 1), (2, sums[0], 0)):
        news_ref[v] = new_ref[v] + tendency * gains_ref[0, gain] * (total - sums[3] * old_ref[v])
        saves.append(pltpu.make_async_copy(news_ref.at[v], out_ref.at[0, v + 1, 0], copies.at[v]))
        saves[-1].start()
    for save in saves:
        save.wait()


def finish(state, new_surface, old_surface, kept, came, sea_mask, gains, comps):
    rows, cols = state.shape[3:]
    vmem = pl.BlockSpec(memory_space=pltpu.VMEM)
    anywhere = pl.BlockSpec(memory_space=pl.ANY)
    return pl.pallas_call(
        functools.partial(finish_body, rows, comps),
        in_specs=[anywhere] + [vmem] * 5 + [pl.BlockSpec(memory_space=pltpu.SMEM)],
        out_specs=anywhere,
        out_shape=jax.ShapeDtypeStruct(state.shape, F32),
        scratch_shapes=[pltpu.VMEM((3, rows, cols), F32), pltpu.SemaphoreType.DMA((3,))],
        input_output_aliases={0: 0},
        compiler_params=pltpu.CompilerParams(vmem_limit_bytes=VMEM_BYTES),
    )(state, new_surface, old_surface, kept, came, sea_mask, gains)


def shards(
    model_state, sea_mask, wave_speed, diffusivity, surface_gains, area_table,
    own_cells, target_cells, weight_ids, pair_counts, fold_map,
):
    comps, count_x, count_y = (lax.axis_size(a) for a in ("comp", "tx", "ty"))
    positions = count_x * count_y
    rows, cols = model_state.shape[3:]
    slots = own_cells.shape[3]
    slot_arrays = (own_cells, target_cells, weight_ids, area_table.reshape(-1, LANES), pair_counts)

    def along(block, shift):
        return lax.ppermute(block, ("tx", "ty"), [(s, (s + shift) % positions) for s in range(positions)])

    y_pair = count_y == 2
    slab_rows = CHANNELS * slots // LANES
    slab1, up, slab3, fold = first_side(model_state, slot_arrays, sea_mask, comps)
    slab3 = along(slab3, 1 + count_y)
    slab1 = along(slab1, 1)
    up = along(up, count_y)
    slab0, down, high, low, pair, before = second_side(model_state, slot_arrays, fold, sea_mask, comps, y_pair)
    others = jnp.concatenate([slab1, up[:slab_rows], slab3[:slab_rows]])
    arrived = jnp.concatenate([slab0, others])
    other = lax.ppermute(arrived, "comp", [(g, g ^ 2) for g in range(comps)])

    down = along(down, -count_y)
    fars = []
    if y_pair and count_x == 4:
        south = north = lax.ppermute(jnp.concatenate([pair, slab3[slab_rows:]]), "ty", [(0, 1), (1, 0)])
    else:
        south = lax.ppermute(high, "ty", [(j, j + 1) for j in range(count_y - 1)])
        north = lax.ppermute(low, "ty", [(j + 1, j) for j in range(count_y - 1)])
        for shift in range(2, count_x - 1):
            pairs = []
            for i in range(count_x):
                ends = [((comps - 1) * count_x + k) * count_y + count_y - 1 for k in ((i + shift) % count_x, i)]
                pairs.append(tuple(ends))
            fars.append(lax.ppermute(fold, ("comp", "tx", "ty"), pairs))

    sizes = (*model_state.shape[2:], comps, count_x, count_y)
    cut = sizes[0] // 2
    matrices = stencil_matrices(rows, cols)
    before = scatter_own(others, before, rows, cols, comps, slots)
    deep, edge_rows, edge_columns = deep_levels(
        model_state, sea_mask, (up, down, south, north, fold), fars, fold_map,
        wave_speed, diffusivity, surface_gains, matrices, sizes, cut,
    )
    kept, sent, begun = scatter_other(other, before, deep, model_state.shape, rows, cols, comps, slots)
    came = lax.ppermute(sent, "comp", [(g, g ^ 1) for g in range(comps)])
    new_state, new_surface, old_surface = upper_levels(
        begun, model_state, sea_mask, edge_rows, edge_columns, wave_speed, diffusivity, surface_gains,
        matrices, sizes, cut,
    )
    return finish(new_state, new_surface, old_surface, kept, came, sea_mask, surface_gains, comps)


def solution(mesh):
    in_specs = (
        P("comp", None, None, "tx", "ty"),
        P("comp", "tx", "ty"),
        P("comp", None),
        P("comp", None),
        P("comp", None),
        P(),
        P("comp", ("tx", "ty"), None, None),
        P("comp", ("tx", "ty"), None, None),
        P("comp", ("tx", "ty"), None, None),
        P("comp", ("tx", "ty"), None),
        P(),
    )
    out_specs = P("comp", None, None, "tx", "ty")
    return jax.shard_map(shards, mesh=mesh, in_specs=in_specs, out_specs=out_specs, check_vma=False)
```

```python
import functools

import jax
import jax.numpy as jnp
import numpy
from jax import lax
from jax.experimental import pallas as pl
from jax.experimental.pallas import tpu as pltpu
from jax.sharding import PartitionSpec as P

LANES = 128
DEPTH = 8
PACKED = 16
VMEM_BYTES = 28 * 1024 * 1024
F32 = jnp.float32
BF16 = jnp.bfloat16
I32 = jnp.int32
CHANNELS = 5

EDGE_P, SECOND_P, EDGE_VELOCITY, EDGE_T, MASK = range(5)


def iota(shape, dim):
    return lax.broadcasted_iota(I32, shape, dim)


def halo_rows(levels):
    return (4 * levels + 1 + 7) // 8 * 8


def split_two(values):
    high = values.astype(BF16)
    low = (values - high.astype(F32)).astype(BF16)
    return high, low


def packed_ids(count):
    ids = iota((count, LANES), 0).astype(F32).astype(BF16)
    return ids.reshape(count // PACKED, PACKED, LANES)


def spread_row(row):
    return jnp.broadcast_to(row, (PACKED, LANES))


def share_bounds(slots, shares):
    bounds = [0]
    for m in range(shares):
        bounds.append(bounds[-1] + (slots - m + shares - 1) // shares)
    return bounds


def slot_order(slots, shares, sort, half):
    place = iota((8, LANES), 0) * LANES + iota((8, LANES), 1) + half * 8 * LANES
    source = jnp.zeros((8, LANES), I32)
    bounds = share_bounds(slots, shares)
    for m in range(shares):
        inside = jnp.logical_and(place >= bounds[m], place < bounds[m + 1])
        source = jnp.where(inside, (place - bounds[m]) * shares + m, source)
    return jnp.where(sort, source, place)


def pick_rows(ref, n, source):
    total = jnp.zeros((8, LANES), I32)
    for t in range(ref.shape[3] // LANES):
        row = jnp.broadcast_to(ref[0, 0, n : n + 1, t * LANES : (t + 1) * LANES], (8, LANES))
        picked = jnp.take_along_axis(row, source % LANES, axis=1)
        total = jnp.where(source // LANES == t, picked, total)
    return total


def prepare_partner(n, comps, refs, cells_ref, out):
    own_ref, target_ref, ids_ref, table_ref, counts_ref, picked_ref = refs
    slots = own_ref.shape[3]
    groups = slots // LANES
    is_ocean = lax.axis_index("comp") == comps - 1

    @pl.when(is_ocean)
    def _():
        for half in range(groups // 8):
            source = slot_order(slots, comps - 1, True, half)
            at = slice(half * 8, (half + 1) * 8)
            cells_ref[at, :] = pick_rows(own_ref, n, source)
            picked_ref[at, :] = pick_rows(ids_ref, n, source)
            out[4 * groups + half * 8 : 4 * groups + (half + 1) * 8, :] = pick_rows(target_ref, n, source).astype(F32)

    @pl.when(jnp.logical_not(is_ocean))
    def _():
        for g in range(groups):
            cut = slice(g * LANES, (g + 1) * LANES)
            cells_ref[g : g + 1, :] = own_ref[0, 0, n : n + 1, cut]
            picked_ref[g : g + 1, :] = ids_ref[0, 0, n : n + 1, cut]
            out[4 * groups + g : 4 * groups + g + 1, :] = target_ref[0, 0, n : n + 1, cut].astype(F32)

    count = jnp.broadcast_to(counts_ref[0, :, n : n + 1], (8, LANES))
    for half in range(groups // 8):
        source = slot_order(slots, comps - 1, is_ocean, half)
        ids = picked_ref[half * 8 : (half + 1) * 8, :]
        weight = jnp.zeros((8, LANES), F32)
        for t in range(table_ref.shape[0]):
            table = jnp.broadcast_to(table_ref[t : t + 1, :], (8, LANES))
            looked = jnp.take_along_axis(table, ids % LANES, axis=1)
            weight = jnp.where(ids // LANES == t, looked, weight)
        out[3 * groups + half * 8 : 3 * groups + (half + 1) * 8, :] = jnp.where(source < count, weight, 0.0)


def gather_partner(rows, cols, halves_ref, cells_ref, parts_ref, out):
    groups = cells_ref.shape[0]
    col_ids = packed_ids(cols)
    row_ids = iota((rows, LANES), 0)
    one = jnp.ones((), BF16)
    zero = jnp.zeros((), BF16)
    wide = 2
    subs = groups // wide

    def some(c, carry):
        for sub in range(subs):
            first = (c * subs + sub) * wide
            cells = [cells_ref[pl.ds(first + g, 1), :] for g in range(wide)]
            picks = []
            for cell in cells:
                col = spread_row(cell % cols).astype(F32).astype(BF16)
                picks.append(jnp.where(col_ids == col[None], one, zero).reshape(cols, LANES))
            picks = jnp.concatenate(picks, axis=1)
            if halves_ref.shape[1] > cols:
                picks = jnp.concatenate([picks, picks], axis=0)
                found = jnp.dot(halves_ref[...], picks, preferred_element_type=F32)
            else:
                found = jnp.dot(halves_ref[...], picks, preferred_element_type=F32)
                found = found[: 3 * rows] + found[3 * rows :]
            for g in range(wide):
                in_row = row_ids == cells[g] // cols
                for place, v in enumerate((2, 0, 1)):
                    block = found[v * rows : (v + 1) * rows, g * LANES : (g + 1) * LANES]
                    block = jnp.where(in_row, block, 0.0).reshape(rows // 8, 8, LANES)
                    start = pl.multiple_of((place * groups + first + g) * 8, 8)
                    parts_ref[pl.ds(start, 8), :] = jnp.sum(block, axis=0)
        return carry

    lax.fori_loop(0, groups // (subs * wide), some, 0)
    weight = out[3 * groups : 4 * groups, :]
    for place in range(3):
        total = jnp.zeros((groups, LANES), F32)
        for i in range(8):
            total += parts_ref[pl.ds(place * groups * 8 + i, groups, stride=8), :]
        out[place * groups : (place + 1) * groups, :] = total * weight


def split_surface(surface_ref, halves_ref, rows, cols):
    for v in range(3):
        high, low = split_two(surface_ref[v])
        if halves_ref.shape[1] > cols:
            halves_ref[v * rows : (v + 1) * rows, :cols] = high
            halves_ref[v * rows : (v + 1) * rows, cols:] = low
        else:
            halves_ref[v * rows : (v + 1) * rows, :] = high
            halves_ref[(v + 3) * rows : (v + 4) * rows, :] = low


def put_rows(ref, start, levels, cols, fields, sea, edge, second):
    height = halo_rows(levels)
    for p in range(cols // LANES):
        cut = slice(p * LANES, (p + 1) * LANES)
        base = start + p * height
        ref[base + 4 * levels : base + height, :] = jnp.zeros((height - 4 * levels, LANES), F32)
        ref[base + 4 * levels : base + 4 * levels + 1, :] = sea[edge : edge + 1, cut].astype(F32)
        for q, v, at in ((EDGE_P, 0, edge), (SECOND_P, 0, second), (EDGE_VELOCITY, 1, edge), (EDGE_T, 3, edge)):
            for l in range(levels):
                row = base + q * levels + l
                ref[row : row + 1, :] = fields(v, l)[at : at + 1, cut]


def turned_columns(levels, rows, fields, sea, begin):
    edge = 1 if begin else 0
    lanes = iota((rows, LANES), 1)
    total = pltpu.roll(sea.astype(F32), (4 * levels - begin - edge) % LANES, 1)
    for l in range(levels):
        total = jnp.where(lanes // 2 == l, pltpu.roll(fields(0, l), (2 * l - begin) % LANES, 1), total)
        for q, v in ((EDGE_VELOCITY, 2), (EDGE_T, 3)):
            at = q * levels + l
            moved = pltpu.roll(fields(v, l), (at - begin - edge) % LANES, 1)
            total = jnp.where(lanes == at, moved, total)
    return total.T[: halo_rows(levels)]


def first_body(
    levels, rows, cols, comps,
    state_hbm, own_hbm, target_hbm, ids_hbm, table_hbm, counts_hbm, mask_hbm,
    slab1_ref, up_ref, slab3_ref, fold_ref,
    surface_ref, own_ref, target_ref, ids_ref, table_ref, counts_ref, edge_ref, sea_edge_ref, mask_ref, columns_ref,
    halves_ref, cells_ref, picked_ref, parts_ref, copies, column_copies,
):
    sources = (
        own_hbm, target_hbm, ids_hbm, table_hbm, counts_hbm, state_hbm.at[0, pl.ds(1, 3), 0],
        state_hbm.at[0, :, :, pl.ds(rows - 8, 8), :], mask_hbm.at[0, pl.ds(rows - 8, 8), :],
    )
    places = (own_ref, target_ref, ids_ref, table_ref, counts_ref, surface_ref, edge_ref, sea_edge_ref)
    fetches = [
        pltpu.make_async_copy(source, place, copies.at[i])
        for i, (source, place) in enumerate(zip(sources, places))
    ]
    outer = pl.ds(cols - LANES, LANES)
    for_fold = [
        pltpu.make_async_copy(state_hbm.at[0, v, :, :, outer], columns_ref.at[i], column_copies.at[i])
        for i, v in enumerate((0, 2, 3))
    ] + [pltpu.make_async_copy(mask_hbm.at[0, :, outer], mask_ref, column_copies.at[3])]
    northern = lax.axis_index("ty") == lax.axis_size("ty") - 1
    folds = jnp.logical_and(lax.axis_index("comp") == comps - 1, northern)
    for fetch in fetches:
        fetch.start()

    @pl.when(folds)
    def _():
        for fetch in for_fold:
            fetch.start()

    for fetch in fetches[:5]:
        fetch.wait()
    refs = (own_ref, target_ref, ids_ref, table_ref, counts_ref, picked_ref)
    slabs = ((3, slab3_ref), (1, slab1_ref), (2, up_ref))
    for i, (n, out) in enumerate(slabs):
        prepare_partner(n, comps, refs, cells_ref.at[i], out)
    fetches[5].wait()
    split_surface(surface_ref, halves_ref, rows, cols)
    for i, (n, out) in enumerate(slabs):
        gather_partner(rows, cols, halves_ref, cells_ref.at[i], parts_ref, out)
    for fetch in fetches[6:]:
        fetch.wait()
    slab_rows = slab1_ref.shape[0]
    tall = halo_rows(levels) * (cols // LANES)
    put_rows(up_ref, slab_rows, levels, cols, lambda v, l: edge_ref.at[v, l], sea_edge_ref, 7, 6)

    @pl.when(folds)
    def _():
        for fetch in for_fold:
            fetch.wait()
        places = {0: 0, 2: 1, 3: 2}
        fold_ref[...] = turned_columns(
            levels, rows, lambda v, l: columns_ref[places[v], l], mask_ref[...], LANES - 2
        )

    @pl.when(jnp.logical_not(folds))
    def _():
        fold_ref[...] = jnp.zeros_like(fold_ref)

    up_ref[slab_rows + tall :, :] = fold_ref[...]
    slab3_ref[slab_rows:, :] = fold_ref[...]


def gather_scratch(rows, cols, slots, stacked):
    return [
        pltpu.VMEM((6 * rows, cols) if stacked else (3 * rows, 2 * cols), BF16),
        pltpu.VMEM((3, slots // LANES, LANES), I32),
        pltpu.VMEM((slots // LANES, LANES), I32),
        pltpu.VMEM((3 * slots // LANES * 8, LANES), F32),
    ]


def first_side(model_state, slot_arrays, sea_mask, comps):
    levels, rows, cols = model_state.shape[2:]
    near, slots = slot_arrays[0].shape[2:]
    table_shape = slot_arrays[3].shape
    slab = CHANNELS * slots // LANES
    height = halo_rows(levels)
    heights = (slab, slab + height * (cols // LANES) + height, slab + height, height)
    vmem = pl.BlockSpec(memory_space=pltpu.VMEM)
    arrays = (model_state, *slot_arrays, sea_mask)
    return pl.pallas_call(
        functools.partial(first_body, levels, rows, cols, comps),
        in_specs=[pl.BlockSpec(memory_space=pltpu.HBM)] * len(arrays),
        out_specs=[vmem] * len(heights),
        out_shape=[jax.ShapeDtypeStruct((h, LANES), F32) for h in heights],
        scratch_shapes=[pltpu.VMEM((3, rows, cols), F32)]
        + [pltpu.VMEM((1, 1, near, slots), I32)] * 3
        + [pltpu.VMEM(table_shape, F32), pltpu.VMEM((1, 1, near), I32)]
        + [
            pltpu.VMEM((4, levels, 8, cols), F32),
            pltpu.VMEM((8, cols), I32),
            pltpu.VMEM((rows, LANES), I32),
            pltpu.VMEM((3, levels, rows, LANES), F32),
        ]
        + gather_scratch(rows, cols, slots, True)
        + [pltpu.SemaphoreType.DMA((8,)), pltpu.SemaphoreType.DMA((4,))],
        compiler_params=pltpu.CompilerParams(vmem_limit_bytes=VMEM_BYTES),
    )(*(pltpu.with_memory_space_constraint(array, pltpu.HBM) for array in arrays))


def second_body(
    levels, rows, cols, comps, y_pair,
    state_ref, own_ref, target_ref, ids_ref, table_ref, counts_ref, fold_ref, mask_hbm,
    slab0_ref, down_ref, high_ref, low_ref, pair_ref, sent_ref,
    halves_ref, cells_ref, picked_ref, parts_ref, mask_ref, total_ref, copied,
):
    fetch = pltpu.make_async_copy(mask_hbm, mask_ref, copied)
    fetch.start()
    split_surface(state_ref.at[0, pl.ds(1, 3), 0], halves_ref, rows, cols)
    refs = (own_ref, target_ref, ids_ref, table_ref, counts_ref, picked_ref)
    prepare_partner(0, comps, refs, cells_ref.at[0], slab0_ref)
    gather_partner(rows, cols, halves_ref, cells_ref.at[0], parts_ref, slab0_ref)
    fetch.wait()
    put_rows(down_ref, 0, levels, cols, lambda v, l: state_ref.at[0, v, l], mask_ref.at[0], 0, 1)
    down_ref[halo_rows(levels) * (cols // LANES) :, :] = fold_ref[...]
    index_y = lax.axis_index("ty")
    high_used = index_y == 0 if y_pair else index_y >= 0
    low_used = index_y > 0 if y_pair else index_y >= 0

    def columns(start, begin):
        cut = slice(start, start + LANES)
        return turned_columns(levels, rows, lambda v, l: state_ref[0, v, l, :, cut], mask_ref[0, :, cut], begin)

    @pl.when(high_used)
    def _():
        highest = columns(cols - LANES, LANES - 2)
        high_ref[...] = highest
        pair_ref[...] = highest

    @pl.when(jnp.logical_not(high_used))
    def _():
        high_ref[...] = jnp.zeros_like(high_ref)

    @pl.when(low_used)
    def _():
        lowest = columns(0, 0)
        low_ref[...] = lowest
        pair_ref[...] = lowest

    @pl.when(jnp.logical_not(low_used))
    def _():
        low_ref[...] = jnp.zeros_like(low_ref)

    add_own(rows, cols, comps, own_ref.shape[3] // LANES, slab0_ref, total_ref, 0)
    sent_ref[...] = halves_added(total_ref, rows)


def second_side(model_state, slot_arrays, fold, sea_mask, comps, y_pair):
    levels, rows, cols = model_state.shape[2:]
    slots = slot_arrays[0].shape[3]
    height = halo_rows(levels)
    heights = (CHANNELS * slots // LANES, height * (cols // LANES) + height, height, height, height)
    vmem = pl.BlockSpec(memory_space=pltpu.VMEM)
    return pl.pallas_call(
        functools.partial(second_body, levels, rows, cols, comps, y_pair),
        in_specs=[vmem] * 7 + [pl.BlockSpec(memory_space=pltpu.HBM)],
        out_specs=[vmem] * (len(heights) + 1),
        out_shape=[jax.ShapeDtypeStruct((h, LANES), F32) for h in heights]
        + [jax.ShapeDtypeStruct((4 * rows, cols), F32)],
        scratch_shapes=gather_scratch(rows, cols, slots, False)
        + [pltpu.VMEM((1, rows, cols), I32), pltpu.VMEM((8 * rows, cols), F32), pltpu.SemaphoreType.DMA],
        compiler_params=pltpu.CompilerParams(vmem_limit_bytes=VMEM_BYTES),
    )(model_state, *slot_arrays, fold, pltpu.with_memory_space_constraint(sea_mask, pltpu.HBM))


def stencil_halos(
    levels, rows, cols, comps, count_x, count_y,
    state_ref, up_ref, down_ref, south_ref, north_ref, own_ref, fold_ref, far_refs, wave_ref, gains_ref,
    folded_ref, rows_ref, turned_ref,
):
    height = halo_rows(levels)
    parts = cols // LANES
    index_x = lax.axis_index("tx")
    index_y = lax.axis_index("ty")
    is_ocean = lax.axis_index("comp") == comps - 1
    last_y = index_y == count_y - 1
    has_west = jnp.where(jnp.logical_or(is_ocean, index_x > 0), 1.0, 0.0)
    has_east = jnp.where(jnp.logical_or(is_ocean, index_x < count_x - 1), 1.0, 0.0)
    has_south = jnp.where(index_y > 0, 1.0, 0.0)
    has_north = jnp.where(jnp.logical_or(is_ocean, jnp.logical_not(last_y)), 1.0, 0.0)
    drag = gains_ref[0, 2]
    mask_at = 4 * levels

    fold = fold_ref[pl.ds(index_x, 1), :]
    total = jnp.zeros((height, LANES), F32)
    up_start = up_ref.shape[0] - height * (parts + 1)
    sources = [(0, own_ref, 0), (-1, up_ref, up_start + height * parts), (1, down_ref, height * parts)]
    if north_ref.shape[0] > height:
        sources.append((2, north_ref, height))
    else:
        sources += [(shift, ref, 0) for shift, ref in zip(range(2, count_x - 1), far_refs)]
    for shift, ref, start in sources:
        at = lax.rem(index_x + shift + count_x, count_x)
        chosen = (iota((rows, rows), 0) + at * rows == fold).astype(F32)
        total += jnp.dot(
            ref[start : start + height, :], chosen,
            precision=lax.Precision.HIGHEST, preferred_element_type=F32,
        )
    folded_ref[...] = total

    line = iota((levels, LANES), 0)
    halves = jnp.zeros((levels, LANES), F32)
    for l in range(levels):
        halves = jnp.where(line == l, 0.5 * wave_ref[0, l], halves)

    def keeping(sea_values, drags):
        return jnp.where(is_ocean, sea_values, 1.0 - drags * (1.0 - sea_values))

    drags = jnp.where(line == 0, drag, 0.0)

    def by_level(ref, start, q):
        return ref[start + q * levels : start + (q + 1) * levels, :]

    for side, (ref, begin, sign, has) in enumerate(
        ((up_ref, up_start, 1.0, has_west), (down_ref, 0, -1.0, has_east))
    ):
        for p in range(parts):
            start = begin + p * height
            kept = keeping(ref[start + mask_at : start + mask_at + 1, :], drags)
            fixed = kept * (by_level(ref, start, EDGE_VELOCITY) + sign * halves * by_level(ref, start, SECOND_P))
            inner = rows - 1 if side else 0
            own = jnp.concatenate(
                [state_ref[0, 0, l, inner : inner + 1, p * LANES : (p + 1) * LANES] for l in range(levels)], axis=0
            )
            rows_ref[side, p, 0] = has * by_level(ref, start, EDGE_P)
            rows_ref[side, p, 1] = has * by_level(ref, start, EDGE_T)
            rows_ref[side, p, 2] = has * (fixed - sign * kept * halves * own)

    even = lambda ref: ref[pl.ds(0, levels, stride=2), :]
    odd = lambda ref: ref[pl.ds(1, levels, stride=2), :]
    north = [
        jnp.where(last_y, jnp.where(is_ocean, folded, 0.0), low)
        for folded, low in (
            (odd(folded_ref), even(north_ref)),
            (even(folded_ref), odd(north_ref)),
            (-by_level(folded_ref, 0, EDGE_VELOCITY), by_level(north_ref, 0, EDGE_VELOCITY)),
            (by_level(folded_ref, 0, EDGE_T), by_level(north_ref, 0, EDGE_T)),
            (folded_ref[mask_at : mask_at + 1, :], north_ref[mask_at : mask_at + 1, :]),
        )
    ]
    south = [
        odd(south_ref), even(south_ref), by_level(south_ref, 0, EDGE_VELOCITY), by_level(south_ref, 0, EDGE_T),
        south_ref[mask_at : mask_at + 1, :],
    ]
    fill = jnp.zeros((LANES // 2 - 4 * levels, LANES), F32)
    lines = []
    for (edge, second, velocity, tracer, sea), sign, has in (
        (south, 1.0, has_south), (north, -1.0, has_north)
    ):
        kept = keeping(sea, drags)
        fixed = has * kept * (velocity + sign * halves * second)
        lines += [has * edge, has * tracer, fixed, has * kept * halves, fill]
    high, low = split_two(jnp.concatenate(lines, axis=0).T)
    turned_ref[:, :LANES] = high
    turned_ref[:, LANES:] = low


def stencil_matrices(rows, cols):
    steps = [[numpy.eye(n, k=k, dtype=numpy.float32) for k in (1, -1, 0)] for n in (rows, cols)]
    after, before, _ = steps[0]
    along = [numpy.concatenate([m, m], axis=1) for m in (after - before, after + before)]
    before, after, centre = steps[1]
    across = [numpy.concatenate([m, m], axis=0) for m in (after - before, after + before - 4 * centre)]
    return jnp.asarray(numpy.stack(along), BF16), jnp.asarray(numpy.stack(across), BF16)


def stencil_levels(
    rows, cols, comps, begin, end, state_ref, mask_ref, rows_ref, turned_ref, wave_ref, spread_ref, gains_ref,
    along_ref, across_ref, place_refs, news_ref, after,
):
    levels = state_ref.shape[2]
    parts = cols // LANES
    is_ocean = lax.axis_index("comp") == comps - 1
    drag = gains_ref[0, 2]
    for ref in place_refs:
        ref[...] = jnp.zeros_like(ref)
    sea = mask_ref[0].astype(F32)
    tendency = jnp.where(is_ocean, sea, 1.0)
    first = iota((8, cols), 0) == 0
    last = iota((8, cols), 0) == 7
    places, lanes = iota((4 * levels, LANES), 0), iota((4 * levels, LANES), 1)

    def product(left, right):
        return jnp.dot(left, right, preferred_element_type=F32)

    def one_level(level, place_ref):
        half = 0.5 * wave_ref[0, level]
        spread = spread_ref[0, level]
        level_drag = jnp.where(level == 0, drag, 0.0)
        for q, sign in enumerate((-1.0, 1.0, -1.0, 1.0)):
            found = places == q * levels + level
            south = jnp.where(jnp.logical_and(found, lanes == 0), sign, 0.0).astype(BF16)
            north = jnp.where(jnp.logical_and(found, lanes == LANES - 1), 1.0, 0.0).astype(BF16)
            for term in range(2):
                at = term * LANES
                place_ref[q, at : at + 4 * levels, :LANES] = south
                at += LANES // 2
                place_ref[q, at : at + 4 * levels, cols - LANES :] = north

        def across(which, q, field):
            inner = product(jnp.concatenate(split_two(field), axis=1), across_ref[which])
            return inner + product(turned_ref[...], place_ref[q])

        def along(which, q, field):
            found = product(along_ref[which], jnp.concatenate(split_two(field), axis=0))
            west, east = (
                jnp.concatenate([rows_ref[side, p, q, pl.ds(level, 1), :] for p in range(parts)], axis=1)
                for side in range(2)
            )
            if which == 0:
                west = -west
            upper = found[:8] + jnp.where(first, west, 0.0)
            lower = found[rows - 8 :] + jnp.where(last, east, 0.0)
            return jnp.concatenate([upper, found[8 : rows - 8], lower], axis=0)

        pressure, zonal, meridional, tracer = (state_ref[0, v, level] for v in range(4))
        keep = jnp.where(is_ocean, sea, 1.0 - level_drag * (1.0 - sea))
        new_zonal = keep * (zonal - half * along(0, 0, pressure))
        new_meridional = keep * (meridional - half * across(0, 0, pressure))
        new_tracer = tracer + spread * tendency * (along(1, 1, tracer) + across(1, 1, tracer))
        beyond = product(turned_ref[...], place_ref[3]) * pressure
        divergence = along(0, 2, new_zonal) + across(0, 2, new_meridional) + beyond
        now = level - begin
        news_ref[0, now] = pressure - half * divergence
        news_ref[1, now] = new_zonal
        news_ref[2, now] = new_meridional
        news_ref[3, now] = new_tracer
        after(level)

    def some(c, carry):
        for i in range(length):
            one_level(begin + c * length + i, place_refs[i % len(place_refs)])
        return carry

    length = 2 if (end - begin) % 2 == 0 else 1
    lax.fori_loop(0, (end - begin) // length, some, 0)


def place_scratch(cols):
    return [pltpu.VMEM((4, 2 * LANES, cols), BF16)] * 2


def deep_body(
    sizes, begin,
    state_ref, mask_ref, up_ref, down_ref, south_ref, north_ref, own_ref, fold_ref,
    wave_ref, spread_ref, gains_ref, along_ref, across_ref, *rest,
):
    levels, rows, cols, comps, count_x, count_y = sizes
    far_refs, (news_ref, rows_ref, turned_ref, folded_ref, *place_refs) = rest[:-6], rest[-6:]
    stencil_halos(
        *sizes, state_ref, up_ref, down_ref, south_ref, north_ref, own_ref, fold_ref, far_refs, wave_ref, gains_ref,
        folded_ref, rows_ref, turned_ref,
    )
    stencil_levels(
        rows, cols, comps, begin, levels, state_ref, mask_ref, rows_ref, turned_ref, wave_ref, spread_ref, gains_ref,
        along_ref, across_ref, place_refs, news_ref, lambda level: None,
    )


def upper_body(
    sizes, end, begun_ref, state_ref, mask_ref, rows_ref, turned_ref, wave_ref, spread_ref, gains_ref,
    along_ref, across_ref, out_ref, new_surface_ref, old_surface_ref, place0, place1, news_ref, stores,
):
    levels, rows, cols, comps, count_x, count_y = sizes

    def store(l, v):
        return pltpu.make_async_copy(news_ref.at[v, l], out_ref.at[0, v, l], stores.at[l, v])

    def after(level):
        for v in range(4):
            store(level, v).start()

    stencil_levels(
        rows, cols, comps, 0, end, state_ref, mask_ref, rows_ref, turned_ref, wave_ref, spread_ref, gains_ref,
        along_ref, across_ref, (place0, place1), news_ref, after,
    )
    for v in range(3):
        new_surface_ref[v] = news_ref[v + 1, 0]
        old_surface_ref[v] = state_ref[0, v + 1, 0]
    for l in range(end):
        for v in range(4):
            store(l, v).wait()


def deep_levels(model_state, sea_mask, halos, fars, fold_map, wave_speed, diffusivity, gains, matrices, sizes, begin):
    levels, rows, cols, comps, count_x, count_y = sizes
    parts = cols // LANES
    fold = fold_map.reshape(count_x, rows)
    vmem = pl.BlockSpec(memory_space=pltpu.VMEM)
    scalar = pl.BlockSpec(memory_space=pltpu.SMEM)
    shapes = ((4, levels - begin, rows, cols), (2, parts, 3, levels, LANES), (rows, 2 * LANES))
    return pl.pallas_call(
        functools.partial(deep_body, sizes, begin),
        in_specs=[vmem] * 8 + [scalar] * 3 + [vmem] * (2 + len(fars)),
        out_specs=[vmem] * 3,
        out_shape=[jax.ShapeDtypeStruct(shape, kind) for shape, kind in zip(shapes, (F32, F32, BF16))],
        scratch_shapes=[
            pltpu.VMEM((halo_rows(levels), LANES), F32),
        ]
        + place_scratch(cols),
        compiler_params=pltpu.CompilerParams(vmem_limit_bytes=VMEM_BYTES),
    )(model_state, sea_mask, *halos, fold, wave_speed, diffusivity, gains, *matrices, *fars)


def upper_levels(
    begun, model_state, sea_mask, edge_rows, edge_columns, wave_speed, diffusivity, gains, matrices, sizes, end
):
    levels, rows, cols, comps, count_x, count_y = sizes
    vmem = pl.BlockSpec(memory_space=pltpu.VMEM)
    scalar = pl.BlockSpec(memory_space=pltpu.SMEM)
    anywhere = pl.BlockSpec(memory_space=pl.ANY)
    surface = jax.ShapeDtypeStruct((3, rows, cols), F32)
    return pl.pallas_call(
        functools.partial(upper_body, sizes, end),
        in_specs=[anywhere] + [vmem] * 4 + [scalar] * 3 + [vmem] * 2,
        out_specs=[anywhere, vmem, vmem],
        out_shape=[jax.ShapeDtypeStruct(begun.shape, F32), surface, surface],
        scratch_shapes=place_scratch(cols)
        + [pltpu.VMEM((4, end, rows, cols), F32), pltpu.SemaphoreType.DMA((end, 4))],
        input_output_aliases={0: 0},
        compiler_params=pltpu.CompilerParams(vmem_limit_bytes=VMEM_BYTES),
    )(begun, model_state, sea_mask, edge_rows, edge_columns, wave_speed, diffusivity, gains, *matrices)


def add_slots(rows, cols, groups, slab_ref, total_ref, chunks, plan, length, runs=1):
    row_ids = packed_ids(rows)
    col_ids = packed_ids(cols)
    lane = iota((1, LANES), 1)
    one = jnp.ones((), BF16)
    zero = jnp.zeros((), BF16)
    block = 4

    def one_chunk(total_ref, chunk):
        n, first, low_slot, high_slot = plan(chunk)
        start = n * (CHANNELS * groups) + first
        for begin in range(0, DEPTH, block):
            columns, spreads = [], []
            for g in range(begin, begin + block):
                cells = slab_ref[pl.ds(start + 4 * groups + g, 1), :].astype(I32)
                slot = lane + (first + g) * LANES
                mine = jnp.logical_and(slot >= low_slot, slot < high_slot)
                row = spread_row(jnp.where(mine, cells // cols, -1)).astype(F32).astype(BF16)
                col = spread_row(cells % cols).astype(F32).astype(BF16)
                columns.append(jnp.where(col_ids == col[None], one, zero).reshape(cols, LANES))
                in_row = row_ids == row[None]
                highs, lows = [], []
                for v in range(4):
                    value = spread_row(slab_ref[pl.ds(start + v * groups + g, 1), :])
                    high, low = split_two(value)
                    highs.append(jnp.where(in_row, high[None], zero).reshape(rows, LANES))
                    lows.append(jnp.where(in_row, low[None], zero).reshape(rows, LANES))
                spreads.append(jnp.concatenate(highs + lows, axis=0))
            total_ref[...] += lax.dot_general(
                jnp.concatenate(spreads, axis=1), jnp.concatenate(columns, axis=1), (((1,), (1,)), ((), ())),
                preferred_element_type=F32,
            )

    def turn(c, carry):
        for i in range(length):
            one_chunk(total_ref if runs == 1 else total_ref.at[c], c * length + i)
        return carry

    def single(c, carry):
        one_chunk(total_ref, c)
        return carry

    total_ref[...] = jnp.zeros_like(total_ref)
    turns = chunks // length
    lax.fori_loop(0, turns, turn, 0)
    if runs == 1:
        lax.fori_loop(turns * length, chunks, single, 0)


def halves_added(total_ref, rows):
    return total_ref[: 4 * rows] + total_ref[4 * rows :]


def add_own(rows, cols, comps, groups, slab_ref, total_ref, skipped):
    here = lax.axis_index("comp")
    pieces = groups // DEPTH
    near = slab_ref.shape[0] // (CHANNELS * groups) - skipped
    bounds = share_bounds(groups * LANES, comps - 1)
    is_ocean = here == comps - 1
    beside = here == comps - 2

    def plan(chunk):
        n = skipped + jnp.where(is_ocean, chunk, chunk // pieces)
        first = jnp.where(is_ocean, groups - DEPTH, chunk % pieces * DEPTH)
        return n, first, jnp.where(is_ocean, bounds[comps - 2], 0), groups * LANES

    chunks = jnp.where(is_ocean, near, jnp.where(beside, near * pieces, 0))
    add_slots(rows, cols, groups, slab_ref, total_ref, chunks, plan, 3 if near == 3 else 2)


def own_body(rows, cols, comps, groups, slab_ref, before_ref, sent_ref, total_ref):
    add_own(rows, cols, comps, groups, slab_ref, total_ref, 0)
    sent_ref[...] = before_ref[...] + halves_added(total_ref, rows)


def other_body(
    rows, cols, comps, groups, slab_ref, before_ref, deep_ref, kept_ref, sent_ref, state_ref,
    totals_ref, copies,
):
    here = lax.axis_index("comp")
    pieces = groups // DEPTH
    near = slab_ref.shape[0] // (CHANNELS * groups)
    bounds = share_bounds(groups * LANES, comps - 1)
    is_ocean = here == comps - 1
    beside = here == comps - 2
    for_two = here == comps - 3
    middle = bounds[1] // LANES // 4 * 4
    count = deep_ref.shape[1]
    stores = [
        pltpu.make_async_copy(
            deep_ref.at[v], state_ref.at[0, v, pl.ds(state_ref.shape[2] - count, count)], copies.at[v]
        )
        for v in range(4)
    ]
    for store in stores:
        store.start()

    def plan(chunk):
        mine = chunk >= near
        n = jnp.where(for_two, chunk % near, chunk // pieces)
        first = jnp.where(for_two, jnp.where(mine, middle, 0), chunk % pieces * DEPTH)
        low_slot = jnp.where(jnp.logical_and(for_two, mine), bounds[1], 0)
        high_slot = jnp.where(for_two, jnp.where(mine, bounds[2], bounds[1]), groups * LANES)
        return n, first, low_slot, high_slot

    chunks = jnp.where(here == 0, 0, near * pieces)
    add_slots(rows, cols, groups, slab_ref, totals_ref, chunks, plan, near * pieces // 2, 2)
    first_ref, second_ref = totals_ref.at[0], totals_ref.at[1]
    for start in range(0, 4 * rows, rows):
        first = first_ref[start : start + rows] + first_ref[start + 4 * rows : start + 5 * rows]
        second = second_ref[start : start + rows] + second_ref[start + 4 * rows : start + 5 * rows]
        kept_ref[start : start + rows] = jnp.where(beside, 0.0, second) + jnp.where(is_ocean, first, 0.0)
        sent = jnp.where(is_ocean, 0.0, first) + jnp.where(beside, second, 0.0)
        sent_ref[start : start + rows] = sent + before_ref[start : start + rows]
    for store in stores:
        store.wait()


def scatter_own(arrived, before, rows, cols, comps, slots):
    vmem = pl.BlockSpec(memory_space=pltpu.VMEM)
    return pl.pallas_call(
        functools.partial(own_body, rows, cols, comps, slots // LANES),
        in_specs=[vmem] * 2,
        out_specs=vmem,
        out_shape=jax.ShapeDtypeStruct((4 * rows, cols), F32),
        scratch_shapes=[pltpu.VMEM((8 * rows, cols), F32)],
        compiler_params=pltpu.CompilerParams(vmem_limit_bytes=VMEM_BYTES),
    )(arrived, before)


def scatter_other(other, before, deep, state_shape, rows, cols, comps, slots):
    vmem = pl.BlockSpec(memory_space=pltpu.VMEM)
    sums = jax.ShapeDtypeStruct((4 * rows, cols), F32)
    return pl.pallas_call(
        functools.partial(other_body, rows, cols, comps, slots // LANES),
        in_specs=[vmem] * 3,
        out_specs=[vmem, vmem, pl.BlockSpec(memory_space=pl.ANY)],
        out_shape=[sums, sums, jax.ShapeDtypeStruct(state_shape, F32)],
        scratch_shapes=[pltpu.VMEM((2, 8 * rows, cols), F32), pltpu.SemaphoreType.DMA((4,))],
        compiler_params=pltpu.CompilerParams(vmem_limit_bytes=VMEM_BYTES),
    )(other, before, deep)


def finish_body(rows, comps, state_ref, new_ref, old_ref, kept_ref, came_ref, mask_ref, gains_ref, out_ref, news_ref, copies):
    is_ocean = lax.axis_index("comp") == comps - 1
    tendency = jnp.where(is_ocean, mask_ref[0].astype(F32), 1.0)
    sums = [kept_ref[v * rows : (v + 1) * rows, :] + came_ref[v * rows : (v + 1) * rows, :] for v in range(4)]
    saves = []
    for v, total, gain in ((0, sums[1], 1), (1, sums[2], 1), (2, sums[0], 0)):
        news_ref[v] = new_ref[v] + tendency * gains_ref[0, gain] * (total - sums[3] * old_ref[v])
        saves.append(pltpu.make_async_copy(news_ref.at[v], out_ref.at[0, v + 1, 0], copies.at[v]))
        saves[-1].start()
    for save in saves:
        save.wait()


def finish(state, new_surface, old_surface, kept, came, sea_mask, gains, comps):
    rows, cols = state.shape[3:]
    vmem = pl.BlockSpec(memory_space=pltpu.VMEM)
    anywhere = pl.BlockSpec(memory_space=pl.ANY)
    return pl.pallas_call(
        functools.partial(finish_body, rows, comps),
        in_specs=[anywhere] + [vmem] * 5 + [pl.BlockSpec(memory_space=pltpu.SMEM)],
        out_specs=anywhere,
        out_shape=jax.ShapeDtypeStruct(state.shape, F32),
        scratch_shapes=[pltpu.VMEM((3, rows, cols), F32), pltpu.SemaphoreType.DMA((3,))],
        input_output_aliases={0: 0},
        compiler_params=pltpu.CompilerParams(vmem_limit_bytes=VMEM_BYTES),
    )(state, new_surface, old_surface, kept, came, sea_mask, gains)


def shards(
    model_state, sea_mask, wave_speed, diffusivity, surface_gains, area_table,
    own_cells, target_cells, weight_ids, pair_counts, fold_map,
):
    comps, count_x, count_y = (lax.axis_size(a) for a in ("comp", "tx", "ty"))
    positions = count_x * count_y
    rows, cols = model_state.shape[3:]
    slots = own_cells.shape[3]
    slot_arrays = (own_cells, target_cells, weight_ids, area_table.reshape(-1, LANES), pair_counts)

    def along(block, shift):
        return lax.ppermute(block, ("tx", "ty"), [(s, (s + shift) % positions) for s in range(positions)])

    y_pair = count_y == 2
    slab_rows = CHANNELS * slots // LANES
    slab1, up, slab3, fold = first_side(model_state, slot_arrays, sea_mask, comps)
    slab3 = along(slab3, 1 + count_y)
    slab1 = along(slab1, 1)
    up = along(up, count_y)
    slab0, down, high, low, pair, before = second_side(model_state, slot_arrays, fold, sea_mask, comps, y_pair)
    others = jnp.concatenate([slab1, up[:slab_rows], slab3[:slab_rows]])
    arrived = jnp.concatenate([slab0, others])
    down = along(down, -count_y)
    fars = []
    if y_pair and count_x == 4:
        south = north = lax.ppermute(jnp.concatenate([pair, slab3[slab_rows:]]), "ty", [(0, 1), (1, 0)])
    else:
        south = lax.ppermute(high, "ty", [(j, j + 1) for j in range(count_y - 1)])
        north = lax.ppermute(low, "ty", [(j + 1, j) for j in range(count_y - 1)])
        for shift in range(2, count_x - 1):
            pairs = []
            for i in range(count_x):
                ends = [((comps - 1) * count_x + k) * count_y + count_y - 1 for k in ((i + shift) % count_x, i)]
                pairs.append(tuple(ends))
            fars.append(lax.ppermute(fold, ("comp", "tx", "ty"), pairs))

    if y_pair:
        arrived, south, down = lax.optimization_barrier((arrived, south, down))
        north = south
    other = lax.ppermute(arrived, "comp", [(g, g ^ 2) for g in range(comps)])

    sizes = (*model_state.shape[2:], comps, count_x, count_y)
    cut = sizes[0] // 2
    matrices = stencil_matrices(rows, cols)
    before = scatter_own(others, before, rows, cols, comps, slots)
    deep, edge_rows, edge_columns = deep_levels(
        model_state, sea_mask, (up, down, south, north, fold), fars, fold_map,
        wave_speed, diffusivity, surface_gains, matrices, sizes, cut,
    )
    kept, sent, begun = scatter_other(other, before, deep, model_state.shape, rows, cols, comps, slots)
    came = lax.ppermute(sent, "comp", [(g, g ^ 1) for g in range(comps)])
    new_state, new_surface, old_surface = upper_levels(
        begun, model_state, sea_mask, edge_rows, edge_columns, wave_speed, diffusivity, surface_gains,
        matrices, sizes, cut,
    )
    return finish(new_state, new_surface, old_surface, kept, came, sea_mask, surface_gains, comps)


def solution(mesh):
    in_specs = (
        P("comp", None, None, "tx", "ty"),
        P("comp", "tx", "ty"),
        P("comp", None),
        P("comp", None),
        P("comp", None),
        P(),
        P("comp", ("tx", "ty"), None, None),
        P("comp", ("tx", "ty"), None, None),
        P("comp", ("tx", "ty"), None, None),
        P("comp", ("tx", "ty"), None),
        P(),
    )
    out_specs = P("comp", None, None, "tx", "ty")
    return jax.shard_map(shards, mesh=mesh, in_specs=in_specs, out_specs=out_specs, check_vma=False)
```

```python
import functools

import jax
import jax.numpy as jnp
import numpy
from jax import lax
from jax.experimental import pallas as pl
from jax.experimental.pallas import tpu as pltpu
from jax.sharding import PartitionSpec as P

LANES = 128
DEPTH = 8
PACKED = 16
VMEM_BYTES = 28 * 1024 * 1024
F32 = jnp.float32
BF16 = jnp.bfloat16
I32 = jnp.int32
CHANNELS = 5

EDGE_P, SECOND_P, EDGE_VELOCITY, EDGE_T, MASK = range(5)


def iota(shape, dim):
    return lax.broadcasted_iota(I32, shape, dim)


def halo_rows(levels):
    return (4 * levels + 1 + 7) // 8 * 8


def split_two(values):
    high = values.astype(BF16)
    low = (values - high.astype(F32)).astype(BF16)
    return high, low


def packed_ids(count):
    ids = iota((count, LANES), 0).astype(F32).astype(BF16)
    return ids.reshape(count // PACKED, PACKED, LANES)


def spread_row(row):
    return jnp.broadcast_to(row, (PACKED, LANES))


def share_bounds(slots, shares):
    bounds = [0]
    for m in range(shares):
        bounds.append(bounds[-1] + (slots - m + shares - 1) // shares)
    return bounds


def slot_order(slots, shares, sort, half):
    place = iota((8, LANES), 0) * LANES + iota((8, LANES), 1) + half * 8 * LANES
    source = jnp.zeros((8, LANES), I32)
    bounds = share_bounds(slots, shares)
    for m in range(shares):
        inside = jnp.logical_and(place >= bounds[m], place < bounds[m + 1])
        source = jnp.where(inside, (place - bounds[m]) * shares + m, source)
    return jnp.where(sort, source, place)


def pick_rows(ref, n, source):
    total = jnp.zeros((8, LANES), I32)
    for t in range(ref.shape[3] // LANES):
        row = jnp.broadcast_to(ref[0, 0, n : n + 1, t * LANES : (t + 1) * LANES], (8, LANES))
        picked = jnp.take_along_axis(row, source % LANES, axis=1)
        total = jnp.where(source // LANES == t, picked, total)
    return total


def prepare_partner(n, comps, refs, cells_ref, out):
    own_ref, target_ref, ids_ref, table_ref, counts_ref, picked_ref = refs
    slots = own_ref.shape[3]
    groups = slots // LANES
    is_ocean = lax.axis_index("comp") == comps - 1

    @pl.when(is_ocean)
    def _():
        for half in range(groups // 8):
            source = slot_order(slots, comps - 1, True, half)
            at = slice(half * 8, (half + 1) * 8)
            cells_ref[at, :] = pick_rows(own_ref, n, source)
            picked_ref[at, :] = pick_rows(ids_ref, n, source)
            out[4 * groups + half * 8 : 4 * groups + (half + 1) * 8, :] = pick_rows(target_ref, n, source).astype(F32)

    @pl.when(jnp.logical_not(is_ocean))
    def _():
        for g in range(groups):
            cut = slice(g * LANES, (g + 1) * LANES)
            cells_ref[g : g + 1, :] = own_ref[0, 0, n : n + 1, cut]
            picked_ref[g : g + 1, :] = ids_ref[0, 0, n : n + 1, cut]
            out[4 * groups + g : 4 * groups + g + 1, :] = target_ref[0, 0, n : n + 1, cut].astype(F32)

    count = jnp.broadcast_to(counts_ref[0, :, n : n + 1], (8, LANES))
    for half in range(groups // 8):
        source = slot_order(slots, comps - 1, is_ocean, half)
        ids = picked_ref[half * 8 : (half + 1) * 8, :]
        weight = jnp.zeros((8, LANES), F32)
        for t in range(table_ref.shape[0]):
            table = jnp.broadcast_to(table_ref[t : t + 1, :], (8, LANES))
            looked = jnp.take_along_axis(table, ids % LANES, axis=1)
            weight = jnp.where(ids // LANES == t, looked, weight)
        out[3 * groups + half * 8 : 3 * groups + (half + 1) * 8, :] = jnp.where(source < count, weight, 0.0)


def gather_partner(rows, cols, halves_ref, cells_ref, parts_ref, out):
    groups = cells_ref.shape[0]
    col_ids = packed_ids(cols)
    row_ids = iota((rows, LANES), 0)
    one = jnp.ones((), BF16)
    zero = jnp.zeros((), BF16)
    wide = 2
    subs = groups // wide

    def some(c, carry):
        for sub in range(subs):
            first = (c * subs + sub) * wide
            cells = [cells_ref[pl.ds(first + g, 1), :] for g in range(wide)]
            picks = []
            for cell in cells:
                col = spread_row(cell % cols).astype(F32).astype(BF16)
                picks.append(jnp.where(col_ids == col[None], one, zero).reshape(cols, LANES))
            picks = jnp.concatenate(picks, axis=1)
            if halves_ref.shape[1] > cols:
                picks = jnp.concatenate([picks, picks], axis=0)
                found = jnp.dot(halves_ref[...], picks, preferred_element_type=F32)
            else:
                found = jnp.dot(halves_ref[...], picks, preferred_element_type=F32)
                found = found[: 3 * rows] + found[3 * rows :]
            for g in range(wide):
                in_row = row_ids == cells[g] // cols
                for place, v in enumerate((2, 0, 1)):
                    block = found[v * rows : (v + 1) * rows, g * LANES : (g + 1) * LANES]
                    block = jnp.where(in_row, block, 0.0).reshape(rows // 8, 8, LANES)
                    start = pl.multiple_of((place * groups + first + g) * 8, 8)
                    parts_ref[pl.ds(start, 8), :] = jnp.sum(block, axis=0)
        return carry

    lax.fori_loop(0, groups // (subs * wide), some, 0)
    weight = out[3 * groups : 4 * groups, :]
    for place in range(3):
        total = jnp.zeros((groups, LANES), F32)
        for i in range(8):
            total += parts_ref[pl.ds(place * groups * 8 + i, groups, stride=8), :]
        out[place * groups : (place + 1) * groups, :] = total * weight


def split_surface(surface_ref, halves_ref, rows, cols):
    for v in range(3):
        high, low = split_two(surface_ref[v])
        if halves_ref.shape[1] > cols:
            halves_ref[v * rows : (v + 1) * rows, :cols] = high
            halves_ref[v * rows : (v + 1) * rows, cols:] = low
        else:
            halves_ref[v * rows : (v + 1) * rows, :] = high
            halves_ref[(v + 3) * rows : (v + 4) * rows, :] = low


def put_rows(ref, start, levels, cols, fields, sea, edge, second):
    height = halo_rows(levels)
    for p in range(cols // LANES):
        cut = slice(p * LANES, (p + 1) * LANES)
        base = start + p * height
        ref[base + 4 * levels : base + height, :] = jnp.zeros((height - 4 * levels, LANES), F32)
        ref[base + 4 * levels : base + 4 * levels + 1, :] = sea[edge : edge + 1, cut].astype(F32)
        for q, v, at in ((EDGE_P, 0, edge), (SECOND_P, 0, second), (EDGE_VELOCITY, 1, edge), (EDGE_T, 3, edge)):
            for l in range(levels):
                row = base + q * levels + l
                ref[row : row + 1, :] = fields(v, l)[at : at + 1, cut]


def turned_columns(levels, rows, fields, sea, begin):
    edge = 1 if begin else 0
    lanes = iota((rows, LANES), 1)
    total = pltpu.roll(sea.astype(F32), (4 * levels - begin - edge) % LANES, 1)
    for l in range(levels):
        total = jnp.where(lanes // 2 == l, pltpu.roll(fields(0, l), (2 * l - begin) % LANES, 1), total)
        for q, v in ((EDGE_VELOCITY, 2), (EDGE_T, 3)):
            at = q * levels + l
            moved = pltpu.roll(fields(v, l), (at - begin - edge) % LANES, 1)
            total = jnp.where(lanes == at, moved, total)
    return total.T[: halo_rows(levels)]


def first_body(
    levels, rows, cols, comps,
    state_hbm, own_hbm, target_hbm, ids_hbm, table_hbm, counts_hbm, mask_hbm,
    slab1_ref, up_ref, slab3_ref, fold_ref,
    surface_ref, own_ref, target_ref, ids_ref, table_ref, counts_ref, edge_ref, sea_edge_ref, mask_ref, columns_ref,
    halves_ref, cells_ref, picked_ref, parts_ref, copies, column_copies,
):
    sources = (
        own_hbm, target_hbm, ids_hbm, table_hbm, counts_hbm, state_hbm.at[0, pl.ds(1, 3), 0],
        state_hbm.at[0, :, :, pl.ds(rows - 8, 8), :], mask_hbm.at[0, pl.ds(rows - 8, 8), :],
    )
    places = (own_ref, target_ref, ids_ref, table_ref, counts_ref, surface_ref, edge_ref, sea_edge_ref)
    fetches = [
        pltpu.make_async_copy(source, place, copies.at[i])
        for i, (source, place) in enumerate(zip(sources, places))
    ]
    outer = pl.ds(cols - LANES, LANES)
    for_fold = [
        pltpu.make_async_copy(state_hbm.at[0, v, :, :, outer], columns_ref.at[i], column_copies.at[i])
        for i, v in enumerate((0, 2, 3))
    ] + [pltpu.make_async_copy(mask_hbm.at[0, :, outer], mask_ref, column_copies.at[3])]
    northern = lax.axis_index("ty") == lax.axis_size("ty") - 1
    folds = jnp.logical_and(lax.axis_index("comp") == comps - 1, northern)
    for fetch in fetches:
        fetch.start()

    @pl.when(folds)
    def _():
        for fetch in for_fold:
            fetch.start()

    for fetch in fetches[:5]:
        fetch.wait()
    refs = (own_ref, target_ref, ids_ref, table_ref, counts_ref, picked_ref)
    slabs = ((3, slab3_ref), (1, slab1_ref), (2, up_ref))
    for i, (n, out) in enumerate(slabs):
        prepare_partner(n, comps, refs, cells_ref.at[i], out)
    fetches[5].wait()
    split_surface(surface_ref, halves_ref, rows, cols)
    for i, (n, out) in enumerate(slabs):
        gather_partner(rows, cols, halves_ref, cells_ref.at[i], parts_ref, out)
    for fetch in fetches[6:]:
        fetch.wait()
    slab_rows = slab1_ref.shape[0]
    tall = halo_rows(levels) * (cols // LANES)
    put_rows(up_ref, slab_rows, levels, cols, lambda v, l: edge_ref.at[v, l], sea_edge_ref, 7, 6)

    @pl.when(folds)
    def _():
        for fetch in for_fold:
            fetch.wait()
        places = {0: 0, 2: 1, 3: 2}
        fold_ref[...] = turned_columns(
            levels, rows, lambda v, l: columns_ref[places[v], l], mask_ref[...], LANES - 2
        )

    @pl.when(jnp.logical_not(folds))
    def _():
        fold_ref[...] = jnp.zeros_like(fold_ref)

    up_ref[slab_rows + tall :, :] = fold_ref[...]
    slab3_ref[slab_rows:, :] = fold_ref[...]


def gather_scratch(rows, cols, slots, stacked):
    return [
        pltpu.VMEM((6 * rows, cols) if stacked else (3 * rows, 2 * cols), BF16),
        pltpu.VMEM((3, slots // LANES, LANES), I32),
        pltpu.VMEM((slots // LANES, LANES), I32),
        pltpu.VMEM((3 * slots // LANES * 8, LANES), F32),
    ]


def first_side(model_state, slot_arrays, sea_mask, comps):
    levels, rows, cols = model_state.shape[2:]
    near, slots = slot_arrays[0].shape[2:]
    table_shape = slot_arrays[3].shape
    slab = CHANNELS * slots // LANES
    height = halo_rows(levels)
    heights = (slab, slab + height * (cols // LANES) + height, slab + height, height)
    vmem = pl.BlockSpec(memory_space=pltpu.VMEM)
    arrays = (model_state, *slot_arrays, sea_mask)
    return pl.pallas_call(
        functools.partial(first_body, levels, rows, cols, comps),
        in_specs=[pl.BlockSpec(memory_space=pltpu.HBM)] * len(arrays),
        out_specs=[vmem] * len(heights),
        out_shape=[jax.ShapeDtypeStruct((h, LANES), F32) for h in heights],
        scratch_shapes=[pltpu.VMEM((3, rows, cols), F32)]
        + [pltpu.VMEM((1, 1, near, slots), I32)] * 3
        + [pltpu.VMEM(table_shape, F32), pltpu.VMEM((1, 1, near), I32)]
        + [
            pltpu.VMEM((4, levels, 8, cols), F32),
            pltpu.VMEM((8, cols), I32),
            pltpu.VMEM((rows, LANES), I32),
            pltpu.VMEM((3, levels, rows, LANES), F32),
        ]
        + gather_scratch(rows, cols, slots, True)
        + [pltpu.SemaphoreType.DMA((8,)), pltpu.SemaphoreType.DMA((4,))],
        compiler_params=pltpu.CompilerParams(vmem_limit_bytes=VMEM_BYTES),
    )(*(pltpu.with_memory_space_constraint(array, pltpu.HBM) for array in arrays))


def second_body(
    levels, rows, cols, comps, y_pair,
    state_ref, own_ref, target_ref, ids_ref, table_ref, counts_ref, fold_ref, mask_hbm,
    slab0_ref, down_ref, high_ref, low_ref, pair_ref, sent_ref,
    halves_ref, cells_ref, picked_ref, parts_ref, mask_ref, total_ref, copied,
):
    fetch = pltpu.make_async_copy(mask_hbm, mask_ref, copied)
    fetch.start()
    split_surface(state_ref.at[0, pl.ds(1, 3), 0], halves_ref, rows, cols)
    refs = (own_ref, target_ref, ids_ref, table_ref, counts_ref, picked_ref)
    prepare_partner(0, comps, refs, cells_ref.at[0], slab0_ref)
    gather_partner(rows, cols, halves_ref, cells_ref.at[0], parts_ref, slab0_ref)
    fetch.wait()
    put_rows(down_ref, 0, levels, cols, lambda v, l: state_ref.at[0, v, l], mask_ref.at[0], 0, 1)
    down_ref[halo_rows(levels) * (cols // LANES) :, :] = fold_ref[...]
    index_y = lax.axis_index("ty")
    high_used = index_y == 0 if y_pair else index_y >= 0
    low_used = index_y > 0 if y_pair else index_y >= 0

    def columns(start, begin):
        cut = slice(start, start + LANES)
        return turned_columns(levels, rows, lambda v, l: state_ref[0, v, l, :, cut], mask_ref[0, :, cut], begin)

    @pl.when(high_used)
    def _():
        highest = columns(cols - LANES, LANES - 2)
        high_ref[...] = highest
        pair_ref[...] = highest

    @pl.when(jnp.logical_not(high_used))
    def _():
        high_ref[...] = jnp.zeros_like(high_ref)

    @pl.when(low_used)
    def _():
        lowest = columns(0, 0)
        low_ref[...] = lowest
        pair_ref[...] = lowest

    @pl.when(jnp.logical_not(low_used))
    def _():
        low_ref[...] = jnp.zeros_like(low_ref)

    add_own(rows, cols, comps, own_ref.shape[3] // LANES, slab0_ref, total_ref, 0)
    sent_ref[...] = halves_added(total_ref, rows)


def second_side(model_state, slot_arrays, fold, sea_mask, comps, y_pair):
    levels, rows, cols = model_state.shape[2:]
    slots = slot_arrays[0].shape[3]
    height = halo_rows(levels)
    heights = (CHANNELS * slots // LANES, height * (cols // LANES) + height, height, height, height)
    vmem = pl.BlockSpec(memory_space=pltpu.VMEM)
    return pl.pallas_call(
        functools.partial(second_body, levels, rows, cols, comps, y_pair),
        in_specs=[vmem] * 7 + [pl.BlockSpec(memory_space=pltpu.HBM)],
        out_specs=[vmem] * (len(heights) + 1),
        out_shape=[jax.ShapeDtypeStruct((h, LANES), F32) for h in heights]
        + [jax.ShapeDtypeStruct((4 * rows, cols), F32)],
        scratch_shapes=gather_scratch(rows, cols, slots, False)
        + [pltpu.VMEM((1, rows, cols), I32), pltpu.VMEM((8 * rows, cols), F32), pltpu.SemaphoreType.DMA],
        compiler_params=pltpu.CompilerParams(vmem_limit_bytes=VMEM_BYTES),
    )(model_state, *slot_arrays, fold, pltpu.with_memory_space_constraint(sea_mask, pltpu.HBM))


def stencil_halos(
    levels, rows, cols, comps, count_x, count_y,
    state_ref, up_ref, down_ref, south_ref, north_ref, own_ref, fold_ref, far_refs, wave_ref, gains_ref,
    folded_ref, rows_ref, turned_ref,
):
    height = halo_rows(levels)
    parts = cols // LANES
    index_x = lax.axis_index("tx")
    index_y = lax.axis_index("ty")
    is_ocean = lax.axis_index("comp") == comps - 1
    last_y = index_y == count_y - 1
    has_west = jnp.where(jnp.logical_or(is_ocean, index_x > 0), 1.0, 0.0)
    has_east = jnp.where(jnp.logical_or(is_ocean, index_x < count_x - 1), 1.0, 0.0)
    has_south = jnp.where(index_y > 0, 1.0, 0.0)
    has_north = jnp.where(jnp.logical_or(is_ocean, jnp.logical_not(last_y)), 1.0, 0.0)
    drag = gains_ref[0, 2]
    mask_at = 4 * levels

    fold = fold_ref[pl.ds(index_x, 1), :]
    total = jnp.zeros((height, LANES), F32)
    up_start = up_ref.shape[0] - height * (parts + 1)
    sources = [(0, own_ref, 0), (-1, up_ref, up_start + height * parts), (1, down_ref, height * parts)]
    if north_ref.shape[0] > height:
        sources.append((2, north_ref, height))
    else:
        sources += [(shift, ref, 0) for shift, ref in zip(range(2, count_x - 1), far_refs)]
    for shift, ref, start in sources:
        at = lax.rem(index_x + shift + count_x, count_x)
        chosen = (iota((rows, rows), 0) + at * rows == fold).astype(F32)
        total += jnp.dot(
            ref[start : start + height, :], chosen,
            precision=lax.Precision.HIGHEST, preferred_element_type=F32,
        )
    folded_ref[...] = total

    line = iota((levels, LANES), 0)
    halves = jnp.zeros((levels, LANES), F32)
    for l in range(levels):
        halves = jnp.where(line == l, 0.5 * wave_ref[0, l], halves)

    def keeping(sea_values, drags):
        return jnp.where(is_ocean, sea_values, 1.0 - drags * (1.0 - sea_values))

    drags = jnp.where(line == 0, drag, 0.0)

    def by_level(ref, start, q):
        return ref[start + q * levels : start + (q + 1) * levels, :]

    for side, (ref, begin, sign, has) in enumerate(
        ((up_ref, up_start, 1.0, has_west), (down_ref, 0, -1.0, has_east))
    ):
        for p in range(parts):
            start = begin + p * height
            kept = keeping(ref[start + mask_at : start + mask_at + 1, :], drags)
            fixed = kept * (by_level(ref, start, EDGE_VELOCITY) + sign * halves * by_level(ref, start, SECOND_P))
            inner = rows - 1 if side else 0
            own = jnp.concatenate(
                [state_ref[0, 0, l, inner : inner + 1, p * LANES : (p + 1) * LANES] for l in range(levels)], axis=0
            )
            rows_ref[side, p, 0] = has * by_level(ref, start, EDGE_P)
            rows_ref[side, p, 1] = has * by_level(ref, start, EDGE_T)
            rows_ref[side, p, 2] = has * (fixed - sign * kept * halves * own)

    even = lambda ref: ref[pl.ds(0, levels, stride=2), :]
    odd = lambda ref: ref[pl.ds(1, levels, stride=2), :]
    north = [
        jnp.where(last_y, jnp.where(is_ocean, folded, 0.0), low)
        for folded, low in (
            (odd(folded_ref), even(north_ref)),
            (even(folded_ref), odd(north_ref)),
            (-by_level(folded_ref, 0, EDGE_VELOCITY), by_level(north_ref, 0, EDGE_VELOCITY)),
            (by_level(folded_ref, 0, EDGE_T), by_level(north_ref, 0, EDGE_T)),
            (folded_ref[mask_at : mask_at + 1, :], north_ref[mask_at : mask_at + 1, :]),
        )
    ]
    south = [
        odd(south_ref), even(south_ref), by_level(south_ref, 0, EDGE_VELOCITY), by_level(south_ref, 0, EDGE_T),
        south_ref[mask_at : mask_at + 1, :],
    ]
    fill = jnp.zeros((LANES // 2 - 4 * levels, LANES), F32)
    lines = []
    for (edge, second, velocity, tracer, sea), sign, has in (
        (south, 1.0, has_south), (north, -1.0, has_north)
    ):
        kept = keeping(sea, drags)
        fixed = has * kept * (velocity + sign * halves * second)
        lines += [has * edge, has * tracer, fixed, has * kept * halves, fill]
    high, low = split_two(jnp.concatenate(lines, axis=0).T)
    turned_ref[:, :LANES] = high
    turned_ref[:, LANES:] = low


def stencil_matrices(rows, cols):
    steps = [[numpy.eye(n, k=k, dtype=numpy.float32) for k in (1, -1, 0)] for n in (rows, cols)]
    after, before, _ = steps[0]
    along = [numpy.concatenate([m, m], axis=1) for m in (after - before, after + before)]
    before, after, centre = steps[1]
    across = [numpy.concatenate([m, m], axis=0) for m in (after - before, after + before - 4 * centre)]
    return jnp.asarray(numpy.stack(along), BF16), jnp.asarray(numpy.stack(across), BF16)


def stencil_levels(
    rows, cols, comps, begin, end, state_ref, mask_ref, rows_ref, turned_ref, wave_ref, spread_ref, gains_ref,
    along_ref, across_ref, place_refs, news_ref, after,
):
    levels = state_ref.shape[2]
    parts = cols // LANES
    is_ocean = lax.axis_index("comp") == comps - 1
    drag = gains_ref[0, 2]
    for ref in place_refs:
        ref[...] = jnp.zeros_like(ref)
    sea = mask_ref[0].astype(F32)
    tendency = jnp.where(is_ocean, sea, 1.0)
    first = iota((8, cols), 0) == 0
    last = iota((8, cols), 0) == 7
    places, lanes = iota((4 * levels, LANES), 0), iota((4 * levels, LANES), 1)

    def product(left, right):
        return jnp.dot(left, right, preferred_element_type=F32)

    def one_level(level, place_ref):
        half = 0.5 * wave_ref[0, level]
        spread = spread_ref[0, level]
        level_drag = jnp.where(level == 0, drag, 0.0)
        for q, sign in enumerate((-1.0, 1.0, -1.0, 1.0)):
            found = places == q * levels + level
            south = jnp.where(jnp.logical_and(found, lanes == 0), sign, 0.0).astype(BF16)
            north = jnp.where(jnp.logical_and(found, lanes == LANES - 1), 1.0, 0.0).astype(BF16)
            for term in range(2):
                at = term * LANES
                place_ref[q, at : at + 4 * levels, :LANES] = south
                at += LANES // 2
                place_ref[q, at : at + 4 * levels, cols - LANES :] = north

        def across(which, q, field):
            inner = product(jnp.concatenate(split_two(field), axis=1), across_ref[which])
            return inner + product(turned_ref[...], place_ref[q])

        def along(which, q, field):
            found = product(along_ref[which], jnp.concatenate(split_two(field), axis=0))
            west, east = (
                jnp.concatenate([rows_ref[side, p, q, pl.ds(level, 1), :] for p in range(parts)], axis=1)
                for side in range(2)
            )
            if which == 0:
                west = -west
            upper = found[:8] + jnp.where(first, west, 0.0)
            lower = found[rows - 8 :] + jnp.where(last, east, 0.0)
            return jnp.concatenate([upper, found[8 : rows - 8], lower], axis=0)

        pressure, zonal, meridional, tracer = (state_ref[0, v, level] for v in range(4))
        keep = jnp.where(is_ocean, sea, 1.0 - level_drag * (1.0 - sea))
        new_zonal = keep * (zonal - half * along(0, 0, pressure))
        new_meridional = keep * (meridional - half * across(0, 0, pressure))
        new_tracer = tracer + spread * tendency * (along(1, 1, tracer) + across(1, 1, tracer))
        beyond = product(turned_ref[...], place_ref[3]) * pressure
        divergence = along(0, 2, new_zonal) + across(0, 2, new_meridional) + beyond
        now = level - begin
        news_ref[0, now] = pressure - half * divergence
        news_ref[1, now] = new_zonal
        news_ref[2, now] = new_meridional
        news_ref[3, now] = new_tracer
        after(level)

    def some(c, carry):
        for i in range(length):
            one_level(begin + c * length + i, place_refs[i % len(place_refs)])
        return carry

    length = 2 if (end - begin) % 2 == 0 else 1
    lax.fori_loop(0, (end - begin) // length, some, 0)


def place_scratch(cols):
    return [pltpu.VMEM((4, 2 * LANES, cols), BF16)] * 2


def deep_body(
    sizes, begin,
    state_ref, mask_ref, up_ref, down_ref, south_ref, north_ref, own_ref, fold_ref,
    wave_ref, spread_ref, gains_ref, along_ref, across_ref, *rest,
):
    levels, rows, cols, comps, count_x, count_y = sizes
    far_refs, (news_ref, rows_ref, turned_ref, folded_ref, *place_refs) = rest[:-6], rest[-6:]
    stencil_halos(
        *sizes, state_ref, up_ref, down_ref, south_ref, north_ref, own_ref, fold_ref, far_refs, wave_ref, gains_ref,
        folded_ref, rows_ref, turned_ref,
    )
    stencil_levels(
        rows, cols, comps, begin, levels, state_ref, mask_ref, rows_ref, turned_ref, wave_ref, spread_ref, gains_ref,
        along_ref, across_ref, place_refs, news_ref, lambda level: None,
    )


def upper_body(
    sizes, end, begun_ref, state_ref, mask_ref, rows_ref, turned_ref, wave_ref, spread_ref, gains_ref,
    along_ref, across_ref, out_ref, new_surface_ref, old_surface_ref, place0, place1, news_ref, stores,
):
    levels, rows, cols, comps, count_x, count_y = sizes

    def store(l, v):
        return pltpu.make_async_copy(news_ref.at[v, l], out_ref.at[0, v, l], stores.at[l, v])

    def after(level):
        for v in range(4):
            store(level, v).start()

    stencil_levels(
        rows, cols, comps, 0, end, state_ref, mask_ref, rows_ref, turned_ref, wave_ref, spread_ref, gains_ref,
        along_ref, across_ref, (place0, place1), news_ref, after,
    )
    for v in range(3):
        new_surface_ref[v] = news_ref[v + 1, 0]
        old_surface_ref[v] = state_ref[0, v + 1, 0]
    for l in range(end):
        for v in range(4):
            store(l, v).wait()


def deep_levels(model_state, sea_mask, halos, fars, fold_map, wave_speed, diffusivity, gains, matrices, sizes, begin):
    levels, rows, cols, comps, count_x, count_y = sizes
    parts = cols // LANES
    fold = fold_map.reshape(count_x, rows)
    vmem = pl.BlockSpec(memory_space=pltpu.VMEM)
    scalar = pl.BlockSpec(memory_space=pltpu.SMEM)
    shapes = ((4, levels - begin, rows, cols), (2, parts, 3, levels, LANES), (rows, 2 * LANES))
    return pl.pallas_call(
        functools.partial(deep_body, sizes, begin),
        in_specs=[vmem] * 8 + [scalar] * 3 + [vmem] * (2 + len(fars)),
        out_specs=[vmem] * 3,
        out_shape=[jax.ShapeDtypeStruct(shape, kind) for shape, kind in zip(shapes, (F32, F32, BF16))],
        scratch_shapes=[
            pltpu.VMEM((halo_rows(levels), LANES), F32),
        ]
        + place_scratch(cols),
        compiler_params=pltpu.CompilerParams(vmem_limit_bytes=VMEM_BYTES),
    )(model_state, sea_mask, *halos, fold, wave_speed, diffusivity, gains, *matrices, *fars)


def upper_levels(
    begun, model_state, sea_mask, edge_rows, edge_columns, wave_speed, diffusivity, gains, matrices, sizes, end
):
    levels, rows, cols, comps, count_x, count_y = sizes
    vmem = pl.BlockSpec(memory_space=pltpu.VMEM)
    scalar = pl.BlockSpec(memory_space=pltpu.SMEM)
    anywhere = pl.BlockSpec(memory_space=pl.ANY)
    surface = jax.ShapeDtypeStruct((3, rows, cols), F32)
    return pl.pallas_call(
        functools.partial(upper_body, sizes, end),
        in_specs=[anywhere] + [vmem] * 4 + [scalar] * 3 + [vmem] * 2,
        out_specs=[anywhere, vmem, vmem],
        out_shape=[jax.ShapeDtypeStruct(begun.shape, F32), surface, surface],
        scratch_shapes=place_scratch(cols)
        + [pltpu.VMEM((4, end, rows, cols), F32), pltpu.SemaphoreType.DMA((end, 4))],
        input_output_aliases={0: 0},
        compiler_params=pltpu.CompilerParams(vmem_limit_bytes=VMEM_BYTES),
    )(begun, model_state, sea_mask, edge_rows, edge_columns, wave_speed, diffusivity, gains, *matrices)


def add_slots(rows, cols, groups, slab_ref, total_ref, chunks, plan, length, runs=1):
    row_ids = packed_ids(rows)
    col_ids = packed_ids(cols)
    lane = iota((1, LANES), 1)
    one = jnp.ones((), BF16)
    zero = jnp.zeros((), BF16)
    block = 4

    def one_chunk(total_ref, chunk):
        n, first, low_slot, high_slot = plan(chunk)
        start = n * (CHANNELS * groups) + first
        for begin in range(0, DEPTH, block):
            columns, spreads = [], []
            for g in range(begin, begin + block):
                cells = slab_ref[pl.ds(start + 4 * groups + g, 1), :].astype(I32)
                slot = lane + (first + g) * LANES
                mine = jnp.logical_and(slot >= low_slot, slot < high_slot)
                row = spread_row(jnp.where(mine, cells // cols, -1)).astype(F32).astype(BF16)
                col = spread_row(cells % cols).astype(F32).astype(BF16)
                columns.append(jnp.where(col_ids == col[None], one, zero).reshape(cols, LANES))
                in_row = row_ids == row[None]
                highs, lows = [], []
                for v in range(4):
                    value = spread_row(slab_ref[pl.ds(start + v * groups + g, 1), :])
                    high, low = split_two(value)
                    highs.append(jnp.where(in_row, high[None], zero).reshape(rows, LANES))
                    lows.append(jnp.where(in_row, low[None], zero).reshape(rows, LANES))
                spreads.append(jnp.concatenate(highs + lows, axis=0))
            total_ref[...] += lax.dot_general(
                jnp.concatenate(spreads, axis=1), jnp.concatenate(columns, axis=1), (((1,), (1,)), ((), ())),
                preferred_element_type=F32,
            )

    def turn(c, carry):
        for i in range(length):
            one_chunk(total_ref if runs == 1 else total_ref.at[c], c * length + i)
        return carry

    def single(c, carry):
        one_chunk(total_ref, c)
        return carry

    total_ref[...] = jnp.zeros_like(total_ref)
    turns = chunks // length
    lax.fori_loop(0, turns, turn, 0)
    if runs == 1:
        lax.fori_loop(turns * length, chunks, single, 0)


def halves_added(total_ref, rows):
    return total_ref[: 4 * rows] + total_ref[4 * rows :]


def add_own(rows, cols, comps, groups, slab_ref, total_ref, skipped):
    here = lax.axis_index("comp")
    pieces = groups // DEPTH
    near = slab_ref.shape[0] // (CHANNELS * groups) - skipped
    bounds = share_bounds(groups * LANES, comps - 1)
    is_ocean = here == comps - 1
    beside = here == comps - 2

    def plan(chunk):
        n = skipped + jnp.where(is_ocean, chunk, chunk // pieces)
        first = jnp.where(is_ocean, groups - DEPTH, chunk % pieces * DEPTH)
        return n, first, jnp.where(is_ocean, bounds[comps - 2], 0), groups * LANES

    chunks = jnp.where(is_ocean, near, jnp.where(beside, near * pieces, 0))
    add_slots(rows, cols, groups, slab_ref, total_ref, chunks, plan, 3 if near == 3 else 2)


def own_body(rows, cols, comps, groups, slab_ref, before_ref, sent_ref, total_ref):
    add_own(rows, cols, comps, groups, slab_ref, total_ref, 0)
    sent_ref[...] = before_ref[...] + halves_added(total_ref, rows)


def other_body(
    rows, cols, comps, groups, slab_ref, before_ref, deep_ref, kept_ref, sent_ref, state_ref,
    totals_ref, copies,
):
    here = lax.axis_index("comp")
    pieces = groups // DEPTH
    near = slab_ref.shape[0] // (CHANNELS * groups)
    bounds = share_bounds(groups * LANES, comps - 1)
    is_ocean = here == comps - 1
    beside = here == comps - 2
    for_two = here == comps - 3
    middle = bounds[1] // LANES // 4 * 4
    count = deep_ref.shape[1]
    stores = [
        pltpu.make_async_copy(
            deep_ref.at[v], state_ref.at[0, v, pl.ds(state_ref.shape[2] - count, count)], copies.at[v]
        )
        for v in range(4)
    ]
    for store in stores:
        store.start()

    def plan(chunk):
        mine = chunk >= near
        n = jnp.where(for_two, chunk % near, chunk // pieces)
        first = jnp.where(for_two, jnp.where(mine, middle, 0), chunk % pieces * DEPTH)
        low_slot = jnp.where(jnp.logical_and(for_two, mine), bounds[1], 0)
        high_slot = jnp.where(for_two, jnp.where(mine, bounds[2], bounds[1]), groups * LANES)
        return n, first, low_slot, high_slot

    chunks = jnp.where(here == 0, 0, near * pieces)
    add_slots(rows, cols, groups, slab_ref, totals_ref, chunks, plan, near * pieces // 2, 2)
    first_ref, second_ref = totals_ref.at[0], totals_ref.at[1]
    for start in range(0, 4 * rows, rows):
        first = first_ref[start : start + rows] + first_ref[start + 4 * rows : start + 5 * rows]
        second = second_ref[start : start + rows] + second_ref[start + 4 * rows : start + 5 * rows]
        kept_ref[start : start + rows] = jnp.where(beside, 0.0, second) + jnp.where(is_ocean, first, 0.0)
        sent = jnp.where(is_ocean, 0.0, first) + jnp.where(beside, second, 0.0)
        sent_ref[start : start + rows] = sent + before_ref[start : start + rows]
    for store in stores:
        store.wait()


def scatter_own(arrived, before, rows, cols, comps, slots):
    vmem = pl.BlockSpec(memory_space=pltpu.VMEM)
    return pl.pallas_call(
        functools.partial(own_body, rows, cols, comps, slots // LANES),
        in_specs=[vmem] * 2,
        out_specs=vmem,
        out_shape=jax.ShapeDtypeStruct((4 * rows, cols), F32),
        scratch_shapes=[pltpu.VMEM((8 * rows, cols), F32)],
        compiler_params=pltpu.CompilerParams(vmem_limit_bytes=VMEM_BYTES),
    )(arrived, before)


def scatter_other(other, before, deep, state_shape, rows, cols, comps, slots):
    vmem = pl.BlockSpec(memory_space=pltpu.VMEM)
    sums = jax.ShapeDtypeStruct((4 * rows, cols), F32)
    return pl.pallas_call(
        functools.partial(other_body, rows, cols, comps, slots // LANES),
        in_specs=[vmem] * 3,
        out_specs=[vmem, vmem, pl.BlockSpec(memory_space=pl.ANY)],
        out_shape=[sums, sums, jax.ShapeDtypeStruct(state_shape, F32)],
        scratch_shapes=[pltpu.VMEM((2, 8 * rows, cols), F32), pltpu.SemaphoreType.DMA((4,))],
        compiler_params=pltpu.CompilerParams(vmem_limit_bytes=VMEM_BYTES),
    )(other, before, deep)


def finish_body(rows, comps, state_ref, new_ref, old_ref, kept_ref, came_ref, mask_ref, gains_ref, out_ref, news_ref, copies):
    is_ocean = lax.axis_index("comp") == comps - 1
    tendency = jnp.where(is_ocean, mask_ref[0].astype(F32), 1.0)
    sums = [kept_ref[v * rows : (v + 1) * rows, :] + came_ref[v * rows : (v + 1) * rows, :] for v in range(4)]
    saves = []
    for v, total, gain in ((0, sums[1], 1), (1, sums[2], 1), (2, sums[0], 0)):
        news_ref[v] = new_ref[v] + tendency * gains_ref[0, gain] * (total - sums[3] * old_ref[v])
        saves.append(pltpu.make_async_copy(news_ref.at[v], out_ref.at[0, v + 1, 0], copies.at[v]))
        saves[-1].start()
    for save in saves:
        save.wait()


def finish(state, new_surface, old_surface, kept, came, sea_mask, gains, comps):
    rows, cols = state.shape[3:]
    vmem = pl.BlockSpec(memory_space=pltpu.VMEM)
    anywhere = pl.BlockSpec(memory_space=pl.ANY)
    return pl.pallas_call(
        functools.partial(finish_body, rows, comps),
        in_specs=[anywhere] + [vmem] * 5 + [pl.BlockSpec(memory_space=pltpu.SMEM)],
        out_specs=anywhere,
        out_shape=jax.ShapeDtypeStruct(state.shape, F32),
        scratch_shapes=[pltpu.VMEM((3, rows, cols), F32), pltpu.SemaphoreType.DMA((3,))],
        input_output_aliases={0: 0},
        compiler_params=pltpu.CompilerParams(vmem_limit_bytes=VMEM_BYTES),
    )(state, new_surface, old_surface, kept, came, sea_mask, gains)


def shards(
    model_state, sea_mask, wave_speed, diffusivity, surface_gains, area_table,
    own_cells, target_cells, weight_ids, pair_counts, fold_map,
):
    comps, count_x, count_y = (lax.axis_size(a) for a in ("comp", "tx", "ty"))
    positions = count_x * count_y
    rows, cols = model_state.shape[3:]
    slots = own_cells.shape[3]
    slot_arrays = (own_cells, target_cells, weight_ids, area_table.reshape(-1, LANES), pair_counts)

    def along(block, shift):
        return lax.ppermute(block, ("tx", "ty"), [(s, (s + shift) % positions) for s in range(positions)])

    y_pair = count_y == 2
    slab_rows = CHANNELS * slots // LANES
    slab1, up, slab3, fold = first_side(model_state, slot_arrays, sea_mask, comps)
    slab3 = along(slab3, 1 + count_y)
    slab1 = along(slab1, 1)
    up = along(up, count_y)
    slab0, down, high, low, pair, before = second_side(model_state, slot_arrays, fold, sea_mask, comps, y_pair)
    others = jnp.concatenate([slab1, up[:slab_rows], slab3[:slab_rows]])
    arrived = jnp.concatenate([slab0, others])
    other = lax.ppermute(arrived, "comp", [(g, g ^ 2) for g in range(comps)])

    down = along(down, -count_y)
    fars = []
    if y_pair and count_x == 4:
        south = north = lax.ppermute(jnp.concatenate([pair, slab3[slab_rows:]]), "ty", [(0, 1), (1, 0)])
    else:
        south = lax.ppermute(high, "ty", [(j, j + 1) for j in range(count_y - 1)])
        north = lax.ppermute(low, "ty", [(j + 1, j) for j in range(count_y - 1)])
        for shift in range(2, count_x - 1):
            pairs = []
            for i in range(count_x):
                ends = [((comps - 1) * count_x + k) * count_y + count_y - 1 for k in ((i + shift) % count_x, i)]
                pairs.append(tuple(ends))
            fars.append(lax.ppermute(fold, ("comp", "tx", "ty"), pairs))

    sizes = (*model_state.shape[2:], comps, count_x, count_y)
    cut = sizes[0] // 2
    matrices = stencil_matrices(rows, cols)
    before = scatter_own(others, before, rows, cols, comps, slots)
    deep, edge_rows, edge_columns = deep_levels(
        model_state, sea_mask, (up, down, south, north, fold), fars, fold_map,
        wave_speed, diffusivity, surface_gains, matrices, sizes, cut,
    )
    kept, sent, begun = scatter_other(other, before, deep, model_state.shape, rows, cols, comps, slots)
    came = lax.ppermute(sent, "comp", [(g, g ^ 1) for g in range(comps)])
    new_state, new_surface, old_surface = upper_levels(
        begun, model_state, sea_mask, edge_rows, edge_columns, wave_speed, diffusivity, surface_gains,
        matrices, sizes, cut,
    )
    return finish(new_state, new_surface, old_surface, kept, came, sea_mask, surface_gains, comps)


def solution(mesh):
    in_specs = (
        P("comp", None, None, "tx", "ty"),
        P("comp", "tx", "ty"),
        P("comp", None),
        P("comp", None),
        P("comp", None),
        P(),
        P("comp", ("tx", "ty"), None, None),
        P("comp", ("tx", "ty"), None, None),
        P("comp", ("tx", "ty"), None, None),
        P("comp", ("tx", "ty"), None),
        P(),
    )
    out_specs = P("comp", None, None, "tx", "ty")
    return jax.shard_map(shards, mesh=mesh, in_specs=in_specs, out_specs=out_specs, check_vma=False)
```

```python
import functools

import jax
import jax.numpy as jnp
import numpy
from jax import lax
from jax.experimental import pallas as pl
from jax.experimental.pallas import tpu as pltpu
from jax.sharding import PartitionSpec as P

LANES = 128
DEPTH = 8
PACKED = 16
VMEM_BYTES = 28 * 1024 * 1024
F32 = jnp.float32
BF16 = jnp.bfloat16
I32 = jnp.int32
CHANNELS = 5

EDGE_P, SECOND_P, EDGE_VELOCITY, EDGE_T, MASK = range(5)


def iota(shape, dim):
    return lax.broadcasted_iota(I32, shape, dim)


def halo_rows(levels):
    return (4 * levels + 1 + 7) // 8 * 8


def split_two(values):
    high = values.astype(BF16)
    low = (values - high.astype(F32)).astype(BF16)
    return high, low


def packed_ids(count):
    ids = iota((count, LANES), 0).astype(F32).astype(BF16)
    return ids.reshape(count // PACKED, PACKED, LANES)


def spread_row(row):
    return jnp.broadcast_to(row, (PACKED, LANES))


def share_bounds(slots, shares):
    bounds = [0]
    for m in range(shares):
        bounds.append(bounds[-1] + (slots - m + shares - 1) // shares)
    return bounds


def slot_order(slots, shares, sort, half):
    place = iota((8, LANES), 0) * LANES + iota((8, LANES), 1) + half * 8 * LANES
    source = jnp.zeros((8, LANES), I32)
    bounds = share_bounds(slots, shares)
    for m in range(shares):
        inside = jnp.logical_and(place >= bounds[m], place < bounds[m + 1])
        source = jnp.where(inside, (place - bounds[m]) * shares + m, source)
    return jnp.where(sort, source, place)


def pick_rows(ref, n, source):
    total = jnp.zeros((8, LANES), I32)
    for t in range(ref.shape[3] // LANES):
        row = jnp.broadcast_to(ref[0, 0, n : n + 1, t * LANES : (t + 1) * LANES], (8, LANES))
        picked = jnp.take_along_axis(row, source % LANES, axis=1)
        total = jnp.where(source // LANES == t, picked, total)
    return total


def prepare_partner(n, comps, refs, cells_ref, out):
    own_ref, target_ref, ids_ref, table_ref, counts_ref, picked_ref = refs
    slots = own_ref.shape[3]
    groups = slots // LANES
    is_ocean = lax.axis_index("comp") == comps - 1

    @pl.when(is_ocean)
    def _():
        for half in range(groups // 8):
            source = slot_order(slots, comps - 1, True, half)
            at = slice(half * 8, (half + 1) * 8)
            cells_ref[at, :] = pick_rows(own_ref, n, source)
            picked_ref[at, :] = pick_rows(ids_ref, n, source)
            out[4 * groups + half * 8 : 4 * groups + (half + 1) * 8, :] = pick_rows(target_ref, n, source).astype(F32)

    @pl.when(jnp.logical_not(is_ocean))
    def _():
        for g in range(groups):
            cut = slice(g * LANES, (g + 1) * LANES)
            cells_ref[g : g + 1, :] = own_ref[0, 0, n : n + 1, cut]
            picked_ref[g : g + 1, :] = ids_ref[0, 0, n : n + 1, cut]
            out[4 * groups + g : 4 * groups + g + 1, :] = target_ref[0, 0, n : n + 1, cut].astype(F32)

    count = jnp.broadcast_to(counts_ref[0, :, n : n + 1], (8, LANES))
    for half in range(groups // 8):
        source = slot_order(slots, comps - 1, is_ocean, half)
        ids = picked_ref[half * 8 : (half + 1) * 8, :]
        weight = jnp.zeros((8, LANES), F32)
        for t in range(table_ref.shape[0]):
            table = jnp.broadcast_to(table_ref[t : t + 1, :], (8, LANES))
            looked = jnp.take_along_axis(table, ids % LANES, axis=1)
            weight = jnp.where(ids // LANES == t, looked, weight)
        out[3 * groups + half * 8 : 3 * groups + (half + 1) * 8, :] = jnp.where(source < count, weight, 0.0)


def gather_partner(rows, cols, halves_ref, cells_ref, parts_ref, out):
    groups = cells_ref.shape[0]
    col_ids = packed_ids(cols)
    row_ids = iota((rows, LANES), 0)
    one = jnp.ones((), BF16)
    zero = jnp.zeros((), BF16)
    wide = 2
    subs = groups // wide

    def some(c, carry):
        for sub in range(subs):
            first = (c * subs + sub) * wide
            cells = [cells_ref[pl.ds(first + g, 1), :] for g in range(wide)]
            picks = []
            for cell in cells:
                col = spread_row(cell % cols).astype(F32).astype(BF16)
                picks.append(jnp.where(col_ids == col[None], one, zero).reshape(cols, LANES))
            picks = jnp.concatenate(picks, axis=1)
            if halves_ref.shape[1] > cols:
                picks = jnp.concatenate([picks, picks], axis=0)
                found = jnp.dot(halves_ref[...], picks, preferred_element_type=F32)
            else:
                found = jnp.dot(halves_ref[...], picks, preferred_element_type=F32)
                found = found[: 3 * rows] + found[3 * rows :]
            for g in range(wide):
                in_row = row_ids == cells[g] // cols
                for place, v in enumerate((2, 0, 1)):
                    block = found[v * rows : (v + 1) * rows, g * LANES : (g + 1) * LANES]
                    block = jnp.where(in_row, block, 0.0).reshape(rows // 8, 8, LANES)
                    start = pl.multiple_of((place * groups + first + g) * 8, 8)
                    parts_ref[pl.ds(start, 8), :] = jnp.sum(block, axis=0)
        return carry

    lax.fori_loop(0, groups // (subs * wide), some, 0)
    weight = out[3 * groups : 4 * groups, :]
    for place in range(3):
        total = jnp.zeros((groups, LANES), F32)
        for i in range(8):
            total += parts_ref[pl.ds(place * groups * 8 + i, groups, stride=8), :]
        out[place * groups : (place + 1) * groups, :] = total * weight


def split_surface(surface_ref, halves_ref, rows, cols):
    for v in range(3):
        high, low = split_two(surface_ref[v])
        if halves_ref.shape[1] > cols:
            halves_ref[v * rows : (v + 1) * rows, :cols] = high
            halves_ref[v * rows : (v + 1) * rows, cols:] = low
        else:
            halves_ref[v * rows : (v + 1) * rows, :] = high
            halves_ref[(v + 3) * rows : (v + 4) * rows, :] = low


def put_rows(ref, start, levels, cols, fields, sea, edge, second):
    height = halo_rows(levels)
    for p in range(cols // LANES):
        cut = slice(p * LANES, (p + 1) * LANES)
        base = start + p * height
        ref[base + 4 * levels : base + height, :] = jnp.zeros((height - 4 * levels, LANES), F32)
        ref[base + 4 * levels : base + 4 * levels + 1, :] = sea[edge : edge + 1, cut].astype(F32)
        for q, v, at in ((EDGE_P, 0, edge), (SECOND_P, 0, second), (EDGE_VELOCITY, 1, edge), (EDGE_T, 3, edge)):
            for l in range(levels):
                row = base + q * levels + l
                ref[row : row + 1, :] = fields(v, l)[at : at + 1, cut]


def turned_columns(levels, rows, fields, sea, begin):
    edge = 1 if begin else 0
    lanes = iota((rows, LANES), 1)
    total = pltpu.roll(sea.astype(F32), (4 * levels - begin - edge) % LANES, 1)
    for l in range(levels):
        total = jnp.where(lanes // 2 == l, pltpu.roll(fields(0, l), (2 * l - begin) % LANES, 1), total)
        for q, v in ((EDGE_VELOCITY, 2), (EDGE_T, 3)):
            at = q * levels + l
            moved = pltpu.roll(fields(v, l), (at - begin - edge) % LANES, 1)
            total = jnp.where(lanes == at, moved, total)
    return total.T[: halo_rows(levels)]


def first_body(
    levels, rows, cols, comps,
    state_hbm, own_hbm, target_hbm, ids_hbm, table_hbm, counts_hbm, mask_hbm,
    slab1_ref, up_ref, slab3_ref, fold_ref,
    surface_ref, own_ref, target_ref, ids_ref, table_ref, counts_ref, edge_ref, sea_edge_ref, mask_ref, columns_ref,
    halves_ref, cells_ref, picked_ref, parts_ref, copies, column_copies,
):
    sources = (
        own_hbm, target_hbm, ids_hbm, table_hbm, counts_hbm, state_hbm.at[0, pl.ds(1, 3), 0],
        state_hbm.at[0, :, :, pl.ds(rows - 8, 8), :], mask_hbm.at[0, pl.ds(rows - 8, 8), :],
    )
    places = (own_ref, target_ref, ids_ref, table_ref, counts_ref, surface_ref, edge_ref, sea_edge_ref)
    fetches = [
        pltpu.make_async_copy(source, place, copies.at[i])
        for i, (source, place) in enumerate(zip(sources, places))
    ]
    outer = pl.ds(cols - LANES, LANES)
    for_fold = [
        pltpu.make_async_copy(state_hbm.at[0, v, :, :, outer], columns_ref.at[i], column_copies.at[i])
        for i, v in enumerate((0, 2, 3))
    ] + [pltpu.make_async_copy(mask_hbm.at[0, :, outer], mask_ref, column_copies.at[3])]
    northern = lax.axis_index("ty") == lax.axis_size("ty") - 1
    folds = jnp.logical_and(lax.axis_index("comp") == comps - 1, northern)
    for fetch in fetches:
        fetch.start()

    @pl.when(folds)
    def _():
        for fetch in for_fold:
            fetch.start()

    for fetch in fetches[:5]:
        fetch.wait()
    refs = (own_ref, target_ref, ids_ref, table_ref, counts_ref, picked_ref)
    slabs = ((3, slab3_ref), (1, slab1_ref), (2, up_ref))
    for i, (n, out) in enumerate(slabs):
        prepare_partner(n, comps, refs, cells_ref.at[i], out)
    fetches[5].wait()
    split_surface(surface_ref, halves_ref, rows, cols)
    for i, (n, out) in enumerate(slabs):
        gather_partner(rows, cols, halves_ref, cells_ref.at[i], parts_ref, out)
    for fetch in fetches[6:]:
        fetch.wait()
    slab_rows = slab1_ref.shape[0]
    tall = halo_rows(levels) * (cols // LANES)
    put_rows(up_ref, slab_rows, levels, cols, lambda v, l: edge_ref.at[v, l], sea_edge_ref, 7, 6)

    @pl.when(folds)
    def _():
        for fetch in for_fold:
            fetch.wait()
        places = {0: 0, 2: 1, 3: 2}
        fold_ref[...] = turned_columns(
            levels, rows, lambda v, l: columns_ref[places[v], l], mask_ref[...], LANES - 2
        )

    @pl.when(jnp.logical_not(folds))
    def _():
        fold_ref[...] = jnp.zeros_like(fold_ref)

    up_ref[slab_rows + tall :, :] = fold_ref[...]
    slab3_ref[slab_rows:, :] = fold_ref[...]


def gather_scratch(rows, cols, slots, stacked):
    return [
        pltpu.VMEM((6 * rows, cols) if stacked else (3 * rows, 2 * cols), BF16),
        pltpu.VMEM((3, slots // LANES, LANES), I32),
        pltpu.VMEM((slots // LANES, LANES), I32),
        pltpu.VMEM((3 * slots // LANES * 8, LANES), F32),
    ]


def first_side(model_state, slot_arrays, sea_mask, comps):
    levels, rows, cols = model_state.shape[2:]
    near, slots = slot_arrays[0].shape[2:]
    table_shape = slot_arrays[3].shape
    slab = CHANNELS * slots // LANES
    height = halo_rows(levels)
    heights = (slab, slab + height * (cols // LANES) + height, slab + height, height)
    vmem = pl.BlockSpec(memory_space=pltpu.VMEM)
    arrays = (model_state, *slot_arrays, sea_mask)
    return pl.pallas_call(
        functools.partial(first_body, levels, rows, cols, comps),
        in_specs=[pl.BlockSpec(memory_space=pltpu.HBM)] * len(arrays),
        out_specs=[vmem] * len(heights),
        out_shape=[jax.ShapeDtypeStruct((h, LANES), F32) for h in heights],
        scratch_shapes=[pltpu.VMEM((3, rows, cols), F32)]
        + [pltpu.VMEM((1, 1, near, slots), I32)] * 3
        + [pltpu.VMEM(table_shape, F32), pltpu.VMEM((1, 1, near), I32)]
        + [
            pltpu.VMEM((4, levels, 8, cols), F32),
            pltpu.VMEM((8, cols), I32),
            pltpu.VMEM((rows, LANES), I32),
            pltpu.VMEM((3, levels, rows, LANES), F32),
        ]
        + gather_scratch(rows, cols, slots, True)
        + [pltpu.SemaphoreType.DMA((8,)), pltpu.SemaphoreType.DMA((4,))],
        compiler_params=pltpu.CompilerParams(vmem_limit_bytes=VMEM_BYTES),
    )(*(pltpu.with_memory_space_constraint(array, pltpu.HBM) for array in arrays))


def second_body(
    levels, rows, cols, comps, y_pair,
    state_ref, own_ref, target_ref, ids_ref, table_ref, counts_ref, fold_ref, mask_hbm,
    slab0_ref, down_ref, high_ref, low_ref, pair_ref, sent_ref,
    halves_ref, cells_ref, picked_ref, parts_ref, mask_ref, total_ref, copied,
):
    fetch = pltpu.make_async_copy(mask_hbm, mask_ref, copied)
    fetch.start()
    split_surface(state_ref.at[0, pl.ds(1, 3), 0], halves_ref, rows, cols)
    refs = (own_ref, target_ref, ids_ref, table_ref, counts_ref, picked_ref)
    prepare_partner(0, comps, refs, cells_ref.at[0], slab0_ref)
    gather_partner(rows, cols, halves_ref, cells_ref.at[0], parts_ref, slab0_ref)
    fetch.wait()
    put_rows(down_ref, 0, levels, cols, lambda v, l: state_ref.at[0, v, l], mask_ref.at[0], 0, 1)
    down_ref[halo_rows(levels) * (cols // LANES) :, :] = fold_ref[...]
    index_y = lax.axis_index("ty")
    high_used = index_y == 0 if y_pair else index_y >= 0
    low_used = index_y > 0 if y_pair else index_y >= 0

    def columns(start, begin):
        cut = slice(start, start + LANES)
        return turned_columns(levels, rows, lambda v, l: state_ref[0, v, l, :, cut], mask_ref[0, :, cut], begin)

    @pl.when(high_used)
    def _():
        highest = columns(cols - LANES, LANES - 2)
        high_ref[...] = highest
        pair_ref[...] = highest

    @pl.when(jnp.logical_not(high_used))
    def _():
        high_ref[...] = jnp.zeros_like(high_ref)

    @pl.when(low_used)
    def _():
        lowest = columns(0, 0)
        low_ref[...] = lowest
        pair_ref[...] = lowest

    @pl.when(jnp.logical_not(low_used))
    def _():
        low_ref[...] = jnp.zeros_like(low_ref)

    add_own(rows, cols, comps, own_ref.shape[3] // LANES, slab0_ref, total_ref, 0)
    sent_ref[...] = halves_added(total_ref, rows)


def second_side(model_state, slot_arrays, fold, sea_mask, comps, y_pair):
    levels, rows, cols = model_state.shape[2:]
    slots = slot_arrays[0].shape[3]
    height = halo_rows(levels)
    heights = (CHANNELS * slots // LANES, height * (cols // LANES) + height, height, height, height)
    vmem = pl.BlockSpec(memory_space=pltpu.VMEM)
    return pl.pallas_call(
        functools.partial(second_body, levels, rows, cols, comps, y_pair),
        in_specs=[vmem] * 7 + [pl.BlockSpec(memory_space=pltpu.HBM)],
        out_specs=[vmem] * (len(heights) + 1),
        out_shape=[jax.ShapeDtypeStruct((h, LANES), F32) for h in heights]
        + [jax.ShapeDtypeStruct((4 * rows, cols), F32)],
        scratch_shapes=gather_scratch(rows, cols, slots, False)
        + [pltpu.VMEM((1, rows, cols), I32), pltpu.VMEM((8 * rows, cols), F32), pltpu.SemaphoreType.DMA],
        compiler_params=pltpu.CompilerParams(vmem_limit_bytes=VMEM_BYTES),
    )(model_state, *slot_arrays, fold, pltpu.with_memory_space_constraint(sea_mask, pltpu.HBM))


def stencil_halos(
    levels, rows, cols, comps, count_x, count_y,
    state_ref, up_ref, down_ref, south_ref, north_ref, own_ref, fold_ref, far_refs, wave_ref, gains_ref,
    folded_ref, rows_ref, turned_ref,
):
    height = halo_rows(levels)
    parts = cols // LANES
    index_x = lax.axis_index("tx")
    index_y = lax.axis_index("ty")
    is_ocean = lax.axis_index("comp") == comps - 1
    last_y = index_y == count_y - 1
    has_west = jnp.where(jnp.logical_or(is_ocean, index_x > 0), 1.0, 0.0)
    has_east = jnp.where(jnp.logical_or(is_ocean, index_x < count_x - 1), 1.0, 0.0)
    has_south = jnp.where(index_y > 0, 1.0, 0.0)
    has_north = jnp.where(jnp.logical_or(is_ocean, jnp.logical_not(last_y)), 1.0, 0.0)
    drag = gains_ref[0, 2]
    mask_at = 4 * levels

    fold = fold_ref[pl.ds(index_x, 1), :]
    total = jnp.zeros((height, LANES), F32)
    up_start = up_ref.shape[0] - height * (parts + 1)
    sources = [(0, own_ref, 0), (-1, up_ref, up_start + height * parts), (1, down_ref, height * parts)]
    if north_ref.shape[0] > height:
        sources.append((2, north_ref, height))
    else:
        sources += [(shift, ref, 0) for shift, ref in zip(range(2, count_x - 1), far_refs)]
    for shift, ref, start in sources:
        at = lax.rem(index_x + shift + count_x, count_x)
        chosen = (iota((rows, rows), 0) + at * rows == fold).astype(F32)
        total += jnp.dot(
            ref[start : start + height, :], chosen,
            precision=lax.Precision.HIGHEST, preferred_element_type=F32,
        )
    folded_ref[...] = total

    line = iota((levels, LANES), 0)
    halves = jnp.zeros((levels, LANES), F32)
    for l in range(levels):
        halves = jnp.where(line == l, 0.5 * wave_ref[0, l], halves)

    def keeping(sea_values, drags):
        return jnp.where(is_ocean, sea_values, 1.0 - drags * (1.0 - sea_values))

    drags = jnp.where(line == 0, drag, 0.0)

    def by_level(ref, start, q):
        return ref[start + q * levels : start + (q + 1) * levels, :]

    for side, (ref, begin, sign, has) in enumerate(
        ((up_ref, up_start, 1.0, has_west), (down_ref, 0, -1.0, has_east))
    ):
        for p in range(parts):
            start = begin + p * height
            kept = keeping(ref[start + mask_at : start + mask_at + 1, :], drags)
            fixed = kept * (by_level(ref, start, EDGE_VELOCITY) + sign * halves * by_level(ref, start, SECOND_P))
            inner = rows - 1 if side else 0
            own = jnp.concatenate(
                [state_ref[0, 0, l, inner : inner + 1, p * LANES : (p + 1) * LANES] for l in range(levels)], axis=0
            )
            rows_ref[side, p, 0] = has * by_level(ref, start, EDGE_P)
            rows_ref[side, p, 1] = has * by_level(ref, start, EDGE_T)
            rows_ref[side, p, 2] = has * (fixed - sign * kept * halves * own)

    even = lambda ref: ref[pl.ds(0, levels, stride=2), :]
    odd = lambda ref: ref[pl.ds(1, levels, stride=2), :]
    north = [
        jnp.where(last_y, jnp.where(is_ocean, folded, 0.0), low)
        for folded, low in (
            (odd(folded_ref), even(north_ref)),
            (even(folded_ref), odd(north_ref)),
            (-by_level(folded_ref, 0, EDGE_VELOCITY), by_level(north_ref, 0, EDGE_VELOCITY)),
            (by_level(folded_ref, 0, EDGE_T), by_level(north_ref, 0, EDGE_T)),
            (folded_ref[mask_at : mask_at + 1, :], north_ref[mask_at : mask_at + 1, :]),
        )
    ]
    south = [
        odd(south_ref), even(south_ref), by_level(south_ref, 0, EDGE_VELOCITY), by_level(south_ref, 0, EDGE_T),
        south_ref[mask_at : mask_at + 1, :],
    ]
    fill = jnp.zeros((LANES // 2 - 4 * levels, LANES), F32)
    lines = []
    for (edge, second, velocity, tracer, sea), sign, has in (
        (south, 1.0, has_south), (north, -1.0, has_north)
    ):
        kept = keeping(sea, drags)
        fixed = has * kept * (velocity + sign * halves * second)
        lines += [has * edge, has * tracer, fixed, has * kept * halves, fill]
    high, low = split_two(jnp.concatenate(lines, axis=0).T)
    turned_ref[:, :LANES] = high
    turned_ref[:, LANES:] = low


def stencil_matrices(rows, cols):
    steps = [[numpy.eye(n, k=k, dtype=numpy.float32) for k in (1, -1, 0)] for n in (rows, cols)]
    after, before, _ = steps[0]
    along = [numpy.concatenate([m, m], axis=1) for m in (after - before, after + before)]
    before, after, centre = steps[1]
    across = [numpy.concatenate([m, m], axis=0) for m in (after - before, after + before - 4 * centre)]
    return jnp.asarray(numpy.stack(along), BF16), jnp.asarray(numpy.stack(across), BF16)


def stencil_levels(
    rows, cols, comps, begin, end, state_ref, mask_ref, rows_ref, turned_ref, wave_ref, spread_ref, gains_ref,
    along_ref, across_ref, place_refs, news_ref, after,
):
    levels = state_ref.shape[2]
    parts = cols // LANES
    is_ocean = lax.axis_index("comp") == comps - 1
    drag = gains_ref[0, 2]
    for ref in place_refs:
        ref[...] = jnp.zeros_like(ref)
    sea = mask_ref[0].astype(F32)
    tendency = jnp.where(is_ocean, sea, 1.0)
    first = iota((8, cols), 0) == 0
    last = iota((8, cols), 0) == 7
    places, lanes = iota((4 * levels, LANES), 0), iota((4 * levels, LANES), 1)

    def product(left, right):
        return jnp.dot(left, right, preferred_element_type=F32)

    def one_level(level, place_ref):
        half = 0.5 * wave_ref[0, level]
        spread = spread_ref[0, level]
        level_drag = jnp.where(level == 0, drag, 0.0)
        for q, sign in enumerate((-1.0, 1.0, -1.0, 1.0)):
            found = places == q * levels + level
            south = jnp.where(jnp.logical_and(found, lanes == 0), sign, 0.0).astype(BF16)
            north = jnp.where(jnp.logical_and(found, lanes == LANES - 1), 1.0, 0.0).astype(BF16)
            for term in range(2):
                at = term * LANES
                place_ref[q, at : at + 4 * levels, :LANES] = south
                at += LANES // 2
                place_ref[q, at : at + 4 * levels, cols - LANES :] = north

        def across(which, q, field):
            inner = product(jnp.concatenate(split_two(field), axis=1), across_ref[which])
            return inner + product(turned_ref[...], place_ref[q])

        def along(which, q, field):
            found = product(along_ref[which], jnp.concatenate(split_two(field), axis=0))
            west, east = (
                jnp.concatenate([rows_ref[side, p, q, pl.ds(level, 1), :] for p in range(parts)], axis=1)
                for side in range(2)
            )
            if which == 0:
                west = -west
            upper = found[:8] + jnp.where(first, west, 0.0)
            lower = found[rows - 8 :] + jnp.where(last, east, 0.0)
            return jnp.concatenate([upper, found[8 : rows - 8], lower], axis=0)

        pressure, zonal, meridional, tracer = (state_ref[0, v, level] for v in range(4))
        keep = jnp.where(is_ocean, sea, 1.0 - level_drag * (1.0 - sea))
        new_zonal = keep * (zonal - half * along(0, 0, pressure))
        new_meridional = keep * (meridional - half * across(0, 0, pressure))
        new_tracer = tracer + spread * tendency * (along(1, 1, tracer) + across(1, 1, tracer))
        beyond = product(turned_ref[...], place_ref[3]) * pressure
        divergence = along(0, 2, new_zonal) + across(0, 2, new_meridional) + beyond
        now = level - begin
        news_ref[0, now] = pressure - half * divergence
        news_ref[1, now] = new_zonal
        news_ref[2, now] = new_meridional
        news_ref[3, now] = new_tracer
        after(level)

    def some(c, carry):
        for i in range(length):
            one_level(begin + c * length + i, place_refs[i % len(place_refs)])
        return carry

    length = 2 if (end - begin) % 2 == 0 else 1
    lax.fori_loop(0, (end - begin) // length, some, 0)


def place_scratch(cols):
    return [pltpu.VMEM((4, 2 * LANES, cols), BF16)] * 2


def deep_body(
    sizes, begin,
    state_ref, mask_ref, up_ref, down_ref, south_ref, north_ref, own_ref, fold_ref,
    wave_ref, spread_ref, gains_ref, along_ref, across_ref, *rest,
):
    levels, rows, cols, comps, count_x, count_y = sizes
    far_refs, (news_ref, rows_ref, turned_ref, folded_ref, *place_refs) = rest[:-6], rest[-6:]
    stencil_halos(
        *sizes, state_ref, up_ref, down_ref, south_ref, north_ref, own_ref, fold_ref, far_refs, wave_ref, gains_ref,
        folded_ref, rows_ref, turned_ref,
    )
    stencil_levels(
        rows, cols, comps, begin, levels, state_ref, mask_ref, rows_ref, turned_ref, wave_ref, spread_ref, gains_ref,
        along_ref, across_ref, place_refs, news_ref, lambda level: None,
    )


def upper_body(
    sizes, end, begun_ref, state_ref, mask_ref, rows_ref, turned_ref, wave_ref, spread_ref, gains_ref,
    along_ref, across_ref, out_ref, new_surface_ref, old_surface_ref, place0, place1, news_ref, stores,
):
    levels, rows, cols, comps, count_x, count_y = sizes

    def store(l, v):
        return pltpu.make_async_copy(news_ref.at[v, l], out_ref.at[0, v, l], stores.at[l, v])

    def after(level):
        for v in range(4):
            store(level, v).start()

    stencil_levels(
        rows, cols, comps, 0, end, state_ref, mask_ref, rows_ref, turned_ref, wave_ref, spread_ref, gains_ref,
        along_ref, across_ref, (place0, place1), news_ref, after,
    )
    for v in range(3):
        new_surface_ref[v] = news_ref[v + 1, 0]
        old_surface_ref[v] = state_ref[0, v + 1, 0]
    for l in range(end):
        for v in range(4):
            store(l, v).wait()


def deep_levels(model_state, sea_mask, halos, fars, fold_map, wave_speed, diffusivity, gains, matrices, sizes, begin):
    levels, rows, cols, comps, count_x, count_y = sizes
    parts = cols // LANES
    fold = fold_map.reshape(count_x, rows)
    vmem = pl.BlockSpec(memory_space=pltpu.VMEM)
    scalar = pl.BlockSpec(memory_space=pltpu.SMEM)
    shapes = ((4, levels - begin, rows, cols), (2, parts, 3, levels, LANES), (rows, 2 * LANES))
    return pl.pallas_call(
        functools.partial(deep_body, sizes, begin),
        in_specs=[vmem] * 8 + [scalar] * 3 + [vmem] * (2 + len(fars)),
        out_specs=[vmem] * 3,
        out_shape=[jax.ShapeDtypeStruct(shape, kind) for shape, kind in zip(shapes, (F32, F32, BF16))],
        scratch_shapes=[
            pltpu.VMEM((halo_rows(levels), LANES), F32),
        ]
        + place_scratch(cols),
        compiler_params=pltpu.CompilerParams(vmem_limit_bytes=VMEM_BYTES),
    )(model_state, sea_mask, *halos, fold, wave_speed, diffusivity, gains, *matrices, *fars)


def upper_levels(
    begun, model_state, sea_mask, edge_rows, edge_columns, wave_speed, diffusivity, gains, matrices, sizes, end
):
    levels, rows, cols, comps, count_x, count_y = sizes
    vmem = pl.BlockSpec(memory_space=pltpu.VMEM)
    scalar = pl.BlockSpec(memory_space=pltpu.SMEM)
    anywhere = pl.BlockSpec(memory_space=pl.ANY)
    surface = jax.ShapeDtypeStruct((3, rows, cols), F32)
    return pl.pallas_call(
        functools.partial(upper_body, sizes, end),
        in_specs=[anywhere] + [vmem] * 4 + [scalar] * 3 + [vmem] * 2,
        out_specs=[anywhere, vmem, vmem],
        out_shape=[jax.ShapeDtypeStruct(begun.shape, F32), surface, surface],
        scratch_shapes=place_scratch(cols)
        + [pltpu.VMEM((4, end, rows, cols), F32), pltpu.SemaphoreType.DMA((end, 4))],
        input_output_aliases={0: 0},
        compiler_params=pltpu.CompilerParams(vmem_limit_bytes=VMEM_BYTES),
    )(begun, model_state, sea_mask, edge_rows, edge_columns, wave_speed, diffusivity, gains, *matrices)


def add_slots(rows, cols, groups, slab_ref, total_ref, chunks, plan, length, runs=1):
    row_ids = packed_ids(rows)
    col_ids = packed_ids(cols)
    lane = iota((1, LANES), 1)
    one = jnp.ones((), BF16)
    zero = jnp.zeros((), BF16)
    block = 4 if runs == 1 else DEPTH

    def one_chunk(total_ref, chunk):
        n, first, low_slot, high_slot = plan(chunk)
        start = n * (CHANNELS * groups) + first
        for begin in range(0, DEPTH, block):
            columns, spreads = [], []
            for g in range(begin, begin + block):
                cells = slab_ref[pl.ds(start + 4 * groups + g, 1), :].astype(I32)
                slot = lane + (first + g) * LANES
                mine = jnp.logical_and(slot >= low_slot, slot < high_slot)
                row = spread_row(jnp.where(mine, cells // cols, -1)).astype(F32).astype(BF16)
                col = spread_row(cells % cols).astype(F32).astype(BF16)
                columns.append(jnp.where(col_ids == col[None], one, zero).reshape(cols, LANES))
                in_row = row_ids == row[None]
                highs, lows = [], []
                for v in range(4):
                    value = spread_row(slab_ref[pl.ds(start + v * groups + g, 1), :])
                    high, low = split_two(value)
                    highs.append(jnp.where(in_row, high[None], zero).reshape(rows, LANES))
                    lows.append(jnp.where(in_row, low[None], zero).reshape(rows, LANES))
                spreads.append(jnp.concatenate(highs + lows, axis=0))
            total_ref[...] += lax.dot_general(
                jnp.concatenate(spreads, axis=1), jnp.concatenate(columns, axis=1), (((1,), (1,)), ((), ())),
                preferred_element_type=F32,
            )

    def turn(c, carry):
        for i in range(length):
            one_chunk(total_ref if runs == 1 else total_ref.at[c], c * length + i)
        return carry

    def single(c, carry):
        one_chunk(total_ref, c)
        return carry

    total_ref[...] = jnp.zeros_like(total_ref)
    turns = chunks // length
    lax.fori_loop(0, turns, turn, 0)
    if runs == 1:
        lax.fori_loop(turns * length, chunks, single, 0)


def halves_added(total_ref, rows):
    return total_ref[: 4 * rows] + total_ref[4 * rows :]


def add_own(rows, cols, comps, groups, slab_ref, total_ref, skipped):
    here = lax.axis_index("comp")
    pieces = groups // DEPTH
    near = slab_ref.shape[0] // (CHANNELS * groups) - skipped
    bounds = share_bounds(groups * LANES, comps - 1)
    is_ocean = here == comps - 1
    beside = here == comps - 2

    def plan(chunk):
        n = skipped + jnp.where(is_ocean, chunk, chunk // pieces)
        first = jnp.where(is_ocean, groups - DEPTH, chunk % pieces * DEPTH)
        return n, first, jnp.where(is_ocean, bounds[comps - 2], 0), groups * LANES

    chunks = jnp.where(is_ocean, near, jnp.where(beside, near * pieces, 0))
    add_slots(rows, cols, groups, slab_ref, total_ref, chunks, plan, 3 if near == 3 else 2)


def own_body(rows, cols, comps, groups, slab_ref, before_ref, sent_ref, total_ref):
    add_own(rows, cols, comps, groups, slab_ref, total_ref, 0)
    sent_ref[...] = before_ref[...] + halves_added(total_ref, rows)


def other_body(
    rows, cols, comps, groups, slab_ref, before_ref, deep_ref, kept_ref, sent_ref, state_ref,
    totals_ref, copies,
):
    here = lax.axis_index("comp")
    pieces = groups // DEPTH
    near = slab_ref.shape[0] // (CHANNELS * groups)
    bounds = share_bounds(groups * LANES, comps - 1)
    is_ocean = here == comps - 1
    beside = here == comps - 2
    for_two = here == comps - 3
    middle = bounds[1] // LANES // 4 * 4
    count = deep_ref.shape[1]
    stores = [
        pltpu.make_async_copy(
            deep_ref.at[v], state_ref.at[0, v, pl.ds(state_ref.shape[2] - count, count)], copies.at[v]
        )
        for v in range(4)
    ]
    for store in stores:
        store.start()

    def plan(chunk):
        mine = chunk >= near
        n = jnp.where(for_two, chunk % near, chunk // pieces)
        first = jnp.where(for_two, jnp.where(mine, middle, 0), chunk % pieces * DEPTH)
        low_slot = jnp.where(jnp.logical_and(for_two, mine), bounds[1], 0)
        high_slot = jnp.where(for_two, jnp.where(mine, bounds[2], bounds[1]), groups * LANES)
        return n, first, low_slot, high_slot

    chunks = jnp.where(here == 0, 0, near * pieces)
    add_slots(rows, cols, groups, slab_ref, totals_ref, chunks, plan, near * pieces // 2, 2)
    first_ref, second_ref = totals_ref.at[0], totals_ref.at[1]
    for start in range(0, 4 * rows, rows):
        first = first_ref[start : start + rows] + first_ref[start + 4 * rows : start + 5 * rows]
        second = second_ref[start : start + rows] + second_ref[start + 4 * rows : start + 5 * rows]
        kept_ref[start : start + rows] = jnp.where(beside, 0.0, second) + jnp.where(is_ocean, first, 0.0)
        sent = jnp.where(is_ocean, 0.0, first) + jnp.where(beside, second, 0.0)
        sent_ref[start : start + rows] = sent + before_ref[start : start + rows]
    for store in stores:
        store.wait()


def scatter_own(arrived, before, rows, cols, comps, slots):
    vmem = pl.BlockSpec(memory_space=pltpu.VMEM)
    return pl.pallas_call(
        functools.partial(own_body, rows, cols, comps, slots // LANES),
        in_specs=[vmem] * 2,
        out_specs=vmem,
        out_shape=jax.ShapeDtypeStruct((4 * rows, cols), F32),
        scratch_shapes=[pltpu.VMEM((8 * rows, cols), F32)],
        compiler_params=pltpu.CompilerParams(vmem_limit_bytes=VMEM_BYTES),
    )(arrived, before)


def scatter_other(other, before, deep, state_shape, rows, cols, comps, slots):
    vmem = pl.BlockSpec(memory_space=pltpu.VMEM)
    sums = jax.ShapeDtypeStruct((4 * rows, cols), F32)
    return pl.pallas_call(
        functools.partial(other_body, rows, cols, comps, slots // LANES),
        in_specs=[vmem] * 3,
        out_specs=[vmem, vmem, pl.BlockSpec(memory_space=pl.ANY)],
        out_shape=[sums, sums, jax.ShapeDtypeStruct(state_shape, F32)],
        scratch_shapes=[pltpu.VMEM((2, 8 * rows, cols), F32), pltpu.SemaphoreType.DMA((4,))],
        compiler_params=pltpu.CompilerParams(vmem_limit_bytes=VMEM_BYTES),
    )(other, before, deep)


def finish_body(rows, comps, state_ref, new_ref, old_ref, kept_ref, came_ref, mask_ref, gains_ref, out_ref, news_ref, copies):
    is_ocean = lax.axis_index("comp") == comps - 1
    tendency = jnp.where(is_ocean, mask_ref[0].astype(F32), 1.0)
    sums = [kept_ref[v * rows : (v + 1) * rows, :] + came_ref[v * rows : (v + 1) * rows, :] for v in range(4)]
    saves = []
    for v, total, gain in ((0, sums[1], 1), (1, sums[2], 1), (2, sums[0], 0)):
        news_ref[v] = new_ref[v] + tendency * gains_ref[0, gain] * (total - sums[3] * old_ref[v])
        saves.append(pltpu.make_async_copy(news_ref.at[v], out_ref.at[0, v + 1, 0], copies.at[v]))
        saves[-1].start()
    for save in saves:
        save.wait()


def finish(state, new_surface, old_surface, kept, came, sea_mask, gains, comps):
    rows, cols = state.shape[3:]
    vmem = pl.BlockSpec(memory_space=pltpu.VMEM)
    anywhere = pl.BlockSpec(memory_space=pl.ANY)
    return pl.pallas_call(
        functools.partial(finish_body, rows, comps),
        in_specs=[anywhere] + [vmem] * 5 + [pl.BlockSpec(memory_space=pltpu.SMEM)],
        out_specs=anywhere,
        out_shape=jax.ShapeDtypeStruct(state.shape, F32),
        scratch_shapes=[pltpu.VMEM((3, rows, cols), F32), pltpu.SemaphoreType.DMA((3,))],
        input_output_aliases={0: 0},
        compiler_params=pltpu.CompilerParams(vmem_limit_bytes=VMEM_BYTES),
    )(state, new_surface, old_surface, kept, came, sea_mask, gains)


def shards(
    model_state, sea_mask, wave_speed, diffusivity, surface_gains, area_table,
    own_cells, target_cells, weight_ids, pair_counts, fold_map,
):
    comps, count_x, count_y = (lax.axis_size(a) for a in ("comp", "tx", "ty"))
    positions = count_x * count_y
    rows, cols = model_state.shape[3:]
    slots = own_cells.shape[3]
    slot_arrays = (own_cells, target_cells, weight_ids, area_table.reshape(-1, LANES), pair_counts)

    def along(block, shift):
        return lax.ppermute(block, ("tx", "ty"), [(s, (s + shift) % positions) for s in range(positions)])

    y_pair = count_y == 2
    slab_rows = CHANNELS * slots // LANES
    slab1, up, slab3, fold = first_side(model_state, slot_arrays, sea_mask, comps)
    slab3 = along(slab3, 1 + count_y)
    slab1 = along(slab1, 1)
    up = along(up, count_y)
    slab0, down, high, low, pair, before = second_side(model_state, slot_arrays, fold, sea_mask, comps, y_pair)
    others = jnp.concatenate([slab1, up[:slab_rows], slab3[:slab_rows]])
    arrived = jnp.concatenate([slab0, others])
    other = lax.ppermute(arrived, "comp", [(g, g ^ 2) for g in range(comps)])

    down = along(down, -count_y)
    fars = []
    if y_pair and count_x == 4:
        south = north = lax.ppermute(jnp.concatenate([pair, slab3[slab_rows:]]), "ty", [(0, 1), (1, 0)])
    else:
        south = lax.ppermute(high, "ty", [(j, j + 1) for j in range(count_y - 1)])
        north = lax.ppermute(low, "ty", [(j + 1, j) for j in range(count_y - 1)])
        for shift in range(2, count_x - 1):
            pairs = []
            for i in range(count_x):
                ends = [((comps - 1) * count_x + k) * count_y + count_y - 1 for k in ((i + shift) % count_x, i)]
                pairs.append(tuple(ends))
            fars.append(lax.ppermute(fold, ("comp", "tx", "ty"), pairs))

    sizes = (*model_state.shape[2:], comps, count_x, count_y)
    cut = sizes[0] // 2
    matrices = stencil_matrices(rows, cols)
    before = scatter_own(others, before, rows, cols, comps, slots)
    deep, edge_rows, edge_columns = deep_levels(
        model_state, sea_mask, (up, down, south, north, fold), fars, fold_map,
        wave_speed, diffusivity, surface_gains, matrices, sizes, cut,
    )
    kept, sent, begun = scatter_other(other, before, deep, model_state.shape, rows, cols, comps, slots)
    came = lax.ppermute(sent, "comp", [(g, g ^ 1) for g in range(comps)])
    new_state, new_surface, old_surface = upper_levels(
        begun, model_state, sea_mask, edge_rows, edge_columns, wave_speed, diffusivity, surface_gains,
        matrices, sizes, cut,
    )
    return finish(new_state, new_surface, old_surface, kept, came, sea_mask, surface_gains, comps)


def solution(mesh):
    in_specs = (
        P("comp", None, None, "tx", "ty"),
        P("comp", "tx", "ty"),
        P("comp", None),
        P("comp", None),
        P("comp", None),
        P(),
        P("comp", ("tx", "ty"), None, None),
        P("comp", ("tx", "ty"), None, None),
        P("comp", ("tx", "ty"), None, None),
        P("comp", ("tx", "ty"), None),
        P(),
    )
    out_specs = P("comp", None, None, "tx", "ty")
    return jax.shard_map(shards, mesh=mesh, in_specs=in_specs, out_specs=out_specs, check_vma=False)
```

```python
import functools

import jax
import jax.numpy as jnp
import numpy
from jax import lax
from jax.experimental import pallas as pl
from jax.experimental.pallas import tpu as pltpu
from jax.sharding import PartitionSpec as P

LANES = 128
DEPTH = 8
PACKED = 16
VMEM_BYTES = 28 * 1024 * 1024
F32 = jnp.float32
BF16 = jnp.bfloat16
I32 = jnp.int32
CHANNELS = 5

EDGE_P, SECOND_P, EDGE_VELOCITY, EDGE_T, MASK = range(5)


def iota(shape, dim):
    return lax.broadcasted_iota(I32, shape, dim)


def halo_rows(levels):
    return (4 * levels + 1 + 7) // 8 * 8


def split_two(values):
    high = values.astype(BF16)
    low = (values - high.astype(F32)).astype(BF16)
    return high, low


def packed_ids(count):
    ids = iota((count, LANES), 0).astype(F32).astype(BF16)
    return ids.reshape(count // PACKED, PACKED, LANES)


def spread_row(row):
    return jnp.broadcast_to(row, (PACKED, LANES))


def share_bounds(slots, shares):
    bounds = [0]
    for m in range(shares):
        bounds.append(bounds[-1] + (slots - m + shares - 1) // shares)
    return bounds


def slot_order(slots, shares, sort, half):
    place = iota((8, LANES), 0) * LANES + iota((8, LANES), 1) + half * 8 * LANES
    source = jnp.zeros((8, LANES), I32)
    bounds = share_bounds(slots, shares)
    for m in range(shares):
        inside = jnp.logical_and(place >= bounds[m], place < bounds[m + 1])
        source = jnp.where(inside, (place - bounds[m]) * shares + m, source)
    return jnp.where(sort, source, place)


def pick_rows(ref, n, source):
    total = jnp.zeros((8, LANES), I32)
    for t in range(ref.shape[3] // LANES):
        row = jnp.broadcast_to(ref[0, 0, n : n + 1, t * LANES : (t + 1) * LANES], (8, LANES))
        picked = jnp.take_along_axis(row, source % LANES, axis=1)
        total = jnp.where(source // LANES == t, picked, total)
    return total


def prepare_partner(n, comps, refs, cells_ref, out):
    own_ref, target_ref, ids_ref, table_ref, counts_ref, picked_ref = refs
    slots = own_ref.shape[3]
    groups = slots // LANES
    is_ocean = lax.axis_index("comp") == comps - 1

    @pl.when(is_ocean)
    def _():
        for half in range(groups // 8):
            source = slot_order(slots, comps - 1, True, half)
            at = slice(half * 8, (half + 1) * 8)
            cells_ref[at, :] = pick_rows(own_ref, n, source)
            picked_ref[at, :] = pick_rows(ids_ref, n, source)
            out[4 * groups + half * 8 : 4 * groups + (half + 1) * 8, :] = pick_rows(target_ref, n, source).astype(F32)

    @pl.when(jnp.logical_not(is_ocean))
    def _():
        for g in range(groups):
            cut = slice(g * LANES, (g + 1) * LANES)
            cells_ref[g : g + 1, :] = own_ref[0, 0, n : n + 1, cut]
            picked_ref[g : g + 1, :] = ids_ref[0, 0, n : n + 1, cut]
            out[4 * groups + g : 4 * groups + g + 1, :] = target_ref[0, 0, n : n + 1, cut].astype(F32)

    count = jnp.broadcast_to(counts_ref[0, :, n : n + 1], (8, LANES))
    for half in range(groups // 8):
        source = slot_order(slots, comps - 1, is_ocean, half)
        ids = picked_ref[half * 8 : (half + 1) * 8, :]
        weight = jnp.zeros((8, LANES), F32)
        for t in range(table_ref.shape[0]):
            table = jnp.broadcast_to(table_ref[t : t + 1, :], (8, LANES))
            looked = jnp.take_along_axis(table, ids % LANES, axis=1)
            weight = jnp.where(ids // LANES == t, looked, weight)
        out[3 * groups + half * 8 : 3 * groups + (half + 1) * 8, :] = jnp.where(source < count, weight, 0.0)


def gather_partner(rows, cols, halves_ref, cells_ref, parts_ref, out):
    groups = cells_ref.shape[0]
    col_ids = packed_ids(cols)
    row_ids = iota((rows, LANES), 0)
    one = jnp.ones((), BF16)
    zero = jnp.zeros((), BF16)
    wide = 2
    subs = groups // wide

    def some(c, carry):
        for sub in range(subs):
            first = (c * subs + sub) * wide
            cells = [cells_ref[pl.ds(first + g, 1), :] for g in range(wide)]
            picks = []
            for cell in cells:
                col = spread_row(cell % cols).astype(F32).astype(BF16)
                picks.append(jnp.where(col_ids == col[None], one, zero).reshape(cols, LANES))
            picks = jnp.concatenate(picks, axis=1)
            if halves_ref.shape[1] > cols:
                picks = jnp.concatenate([picks, picks], axis=0)
                found = jnp.dot(halves_ref[...], picks, preferred_element_type=F32)
            else:
                found = jnp.dot(halves_ref[...], picks, preferred_element_type=F32)
                found = found[: 3 * rows] + found[3 * rows :]
            for g in range(wide):
                in_row = row_ids == cells[g] // cols
                for place, v in enumerate((2, 0, 1)):
                    block = found[v * rows : (v + 1) * rows, g * LANES : (g + 1) * LANES]
                    block = jnp.where(in_row, block, 0.0).reshape(rows // 8, 8, LANES)
                    start = pl.multiple_of((place * groups + first + g) * 8, 8)
                    parts_ref[pl.ds(start, 8), :] = jnp.sum(block, axis=0)
        return carry

    lax.fori_loop(0, groups // (subs * wide), some, 0)
    weight = out[3 * groups : 4 * groups, :]
    for place in range(3):
        total = jnp.zeros((groups, LANES), F32)
        for i in range(8):
            total += parts_ref[pl.ds(place * groups * 8 + i, groups, stride=8), :]
        out[place * groups : (place + 1) * groups, :] = total * weight


def split_surface(surface_ref, halves_ref, rows, cols):
    for v in range(3):
        high, low = split_two(surface_ref[v])
        if halves_ref.shape[1] > cols:
            halves_ref[v * rows : (v + 1) * rows, :cols] = high
            halves_ref[v * rows : (v + 1) * rows, cols:] = low
        else:
            halves_ref[v * rows : (v + 1) * rows, :] = high
            halves_ref[(v + 3) * rows : (v + 4) * rows, :] = low


def put_rows(ref, start, levels, cols, fields, sea, edge, second):
    height = halo_rows(levels)
    for p in range(cols // LANES):
        cut = slice(p * LANES, (p + 1) * LANES)
        base = start + p * height
        ref[base + 4 * levels : base + height, :] = jnp.zeros((height - 4 * levels, LANES), F32)
        ref[base + 4 * levels : base + 4 * levels + 1, :] = sea[edge : edge + 1, cut].astype(F32)
        for q, v, at in ((EDGE_P, 0, edge), (SECOND_P, 0, second), (EDGE_VELOCITY, 1, edge), (EDGE_T, 3, edge)):
            for l in range(levels):
                row = base + q * levels + l
                ref[row : row + 1, :] = fields(v, l)[at : at + 1, cut]


def turned_columns(levels, rows, fields, sea, begin):
    edge = 1 if begin else 0
    lanes = iota((rows, LANES), 1)
    total = pltpu.roll(sea.astype(F32), (4 * levels - begin - edge) % LANES, 1)
    for l in range(levels):
        total = jnp.where(lanes // 2 == l, pltpu.roll(fields(0, l), (2 * l - begin) % LANES, 1), total)
        for q, v in ((EDGE_VELOCITY, 2), (EDGE_T, 3)):
            at = q * levels + l
            moved = pltpu.roll(fields(v, l), (at - begin - edge) % LANES, 1)
            total = jnp.where(lanes == at, moved, total)
    return total.T[: halo_rows(levels)]


def first_body(
    levels, rows, cols, comps,
    state_hbm, own_hbm, target_hbm, ids_hbm, table_hbm, counts_hbm, mask_hbm,
    slab1_ref, up_ref, slab3_ref, fold_ref,
    surface_ref, own_ref, target_ref, ids_ref, table_ref, counts_ref, edge_ref, sea_edge_ref, mask_ref, columns_ref,
    halves_ref, cells_ref, picked_ref, parts_ref, copies, column_copies,
):
    sources = (
        own_hbm, target_hbm, ids_hbm, table_hbm, counts_hbm, state_hbm.at[0, pl.ds(1, 3), 0],
        state_hbm.at[0, :, :, pl.ds(rows - 8, 8), :], mask_hbm.at[0, pl.ds(rows - 8, 8), :],
    )
    places = (own_ref, target_ref, ids_ref, table_ref, counts_ref, surface_ref, edge_ref, sea_edge_ref)
    fetches = [
        pltpu.make_async_copy(source, place, copies.at[i])
        for i, (source, place) in enumerate(zip(sources, places))
    ]
    outer = pl.ds(cols - LANES, LANES)
    for_fold = [
        pltpu.make_async_copy(state_hbm.at[0, v, :, :, outer], columns_ref.at[i], column_copies.at[i])
        for i, v in enumerate((0, 2, 3))
    ] + [pltpu.make_async_copy(mask_hbm.at[0, :, outer], mask_ref, column_copies.at[3])]
    northern = lax.axis_index("ty") == lax.axis_size("ty") - 1
    folds = jnp.logical_and(lax.axis_index("comp") == comps - 1, northern)
    for fetch in fetches:
        fetch.start()

    @pl.when(folds)
    def _():
        for fetch in for_fold:
            fetch.start()

    for fetch in fetches[:5]:
        fetch.wait()
    refs = (own_ref, target_ref, ids_ref, table_ref, counts_ref, picked_ref)
    slabs = ((3, slab3_ref), (1, slab1_ref), (2, up_ref))
    for i, (n, out) in enumerate(slabs):
        prepare_partner(n, comps, refs, cells_ref.at[i], out)
    fetches[5].wait()
    split_surface(surface_ref, halves_ref, rows, cols)
    for i, (n, out) in enumerate(slabs):
        gather_partner(rows, cols, halves_ref, cells_ref.at[i], parts_ref, out)
    for fetch in fetches[6:]:
        fetch.wait()
    slab_rows = slab1_ref.shape[0]
    tall = halo_rows(levels) * (cols // LANES)
    put_rows(up_ref, slab_rows, levels, cols, lambda v, l: edge_ref.at[v, l], sea_edge_ref, 7, 6)

    @pl.when(folds)
    def _():
        for fetch in for_fold:
            fetch.wait()
        places = {0: 0, 2: 1, 3: 2}
        fold_ref[...] = turned_columns(
            levels, rows, lambda v, l: columns_ref[places[v], l], mask_ref[...], LANES - 2
        )

    @pl.when(jnp.logical_not(folds))
    def _():
        fold_ref[...] = jnp.zeros_like(fold_ref)

    up_ref[slab_rows + tall :, :] = fold_ref[...]
    slab3_ref[slab_rows:, :] = fold_ref[...]


def gather_scratch(rows, cols, slots, stacked):
    return [
        pltpu.VMEM((6 * rows, cols) if stacked else (3 * rows, 2 * cols), BF16),
        pltpu.VMEM((3, slots // LANES, LANES), I32),
        pltpu.VMEM((slots // LANES, LANES), I32),
        pltpu.VMEM((3 * slots // LANES * 8 + 8, LANES), F32),
    ]


def first_side(model_state, slot_arrays, sea_mask, comps):
    levels, rows, cols = model_state.shape[2:]
    near, slots = slot_arrays[0].shape[2:]
    table_shape = slot_arrays[3].shape
    slab = CHANNELS * slots // LANES
    height = halo_rows(levels)
    heights = (slab, slab + height * (cols // LANES) + height, slab + height, height)
    vmem = pl.BlockSpec(memory_space=pltpu.VMEM)
    arrays = (model_state, *slot_arrays, sea_mask)
    return pl.pallas_call(
        functools.partial(first_body, levels, rows, cols, comps),
        in_specs=[pl.BlockSpec(memory_space=pltpu.HBM)] * len(arrays),
        out_specs=[vmem] * len(heights),
        out_shape=[jax.ShapeDtypeStruct((h, LANES), F32) for h in heights],
        scratch_shapes=[pltpu.VMEM((3, rows, cols), F32)]
        + [pltpu.VMEM((1, 1, near, slots), I32)] * 3
        + [pltpu.VMEM(table_shape, F32), pltpu.VMEM((1, 1, near), I32)]
        + [
            pltpu.VMEM((4, levels, 8, cols), F32),
            pltpu.VMEM((8, cols), I32),
            pltpu.VMEM((rows, LANES), I32),
            pltpu.VMEM((3, levels, rows, LANES), F32),
        ]
        + gather_scratch(rows, cols, slots, True)
        + [pltpu.SemaphoreType.DMA((8,)), pltpu.SemaphoreType.DMA((4,))],
        compiler_params=pltpu.CompilerParams(vmem_limit_bytes=VMEM_BYTES),
    )(*(pltpu.with_memory_space_constraint(array, pltpu.HBM) for array in arrays))


def second_body(
    levels, rows, cols, comps, y_pair,
    state_ref, own_ref, target_ref, ids_ref, table_ref, counts_ref, fold_ref, mask_hbm,
    slab0_ref, down_ref, high_ref, low_ref, pair_ref, sent_ref,
    halves_ref, cells_ref, picked_ref, parts_ref, mask_ref, total_ref, copied,
):
    fetch = pltpu.make_async_copy(mask_hbm, mask_ref, copied)
    fetch.start()
    split_surface(state_ref.at[0, pl.ds(1, 3), 0], halves_ref, rows, cols)
    refs = (own_ref, target_ref, ids_ref, table_ref, counts_ref, picked_ref)
    prepare_partner(0, comps, refs, cells_ref.at[0], slab0_ref)
    gather_partner(rows, cols, halves_ref, cells_ref.at[0], parts_ref, slab0_ref)
    fetch.wait()
    put_rows(down_ref, 0, levels, cols, lambda v, l: state_ref.at[0, v, l], mask_ref.at[0], 0, 1)
    down_ref[halo_rows(levels) * (cols // LANES) :, :] = fold_ref[...]
    index_y = lax.axis_index("ty")
    high_used = index_y == 0 if y_pair else index_y >= 0
    low_used = index_y > 0 if y_pair else index_y >= 0

    def columns(start, begin):
        cut = slice(start, start + LANES)
        return turned_columns(levels, rows, lambda v, l: state_ref[0, v, l, :, cut], mask_ref[0, :, cut], begin)

    @pl.when(high_used)
    def _():
        highest = columns(cols - LANES, LANES - 2)
        high_ref[...] = highest
        pair_ref[...] = highest

    @pl.when(jnp.logical_not(high_used))
    def _():
        high_ref[...] = jnp.zeros_like(high_ref)

    @pl.when(low_used)
    def _():
        lowest = columns(0, 0)
        low_ref[...] = lowest
        pair_ref[...] = lowest

    @pl.when(jnp.logical_not(low_used))
    def _():
        low_ref[...] = jnp.zeros_like(low_ref)

    add_own(rows, cols, comps, own_ref.shape[3] // LANES, slab0_ref, total_ref, 0)
    sent_ref[...] = halves_added(total_ref, rows)


def second_side(model_state, slot_arrays, fold, sea_mask, comps, y_pair):
    levels, rows, cols = model_state.shape[2:]
    slots = slot_arrays[0].shape[3]
    height = halo_rows(levels)
    heights = (CHANNELS * slots // LANES, height * (cols // LANES) + height, height, height, height)
    vmem = pl.BlockSpec(memory_space=pltpu.VMEM)
    return pl.pallas_call(
        functools.partial(second_body, levels, rows, cols, comps, y_pair),
        in_specs=[vmem] * 7 + [pl.BlockSpec(memory_space=pltpu.HBM)],
        out_specs=[vmem] * (len(heights) + 1),
        out_shape=[jax.ShapeDtypeStruct((h, LANES), F32) for h in heights]
        + [jax.ShapeDtypeStruct((4 * rows, cols), F32)],
        scratch_shapes=gather_scratch(rows, cols, slots, False)
        + [pltpu.VMEM((1, rows, cols), I32), pltpu.VMEM((8 * rows, cols), F32), pltpu.SemaphoreType.DMA],
        compiler_params=pltpu.CompilerParams(vmem_limit_bytes=VMEM_BYTES),
    )(model_state, *slot_arrays, fold, pltpu.with_memory_space_constraint(sea_mask, pltpu.HBM))


def stencil_halos(
    levels, rows, cols, comps, count_x, count_y,
    state_ref, up_ref, down_ref, south_ref, north_ref, own_ref, fold_ref, far_refs, wave_ref, gains_ref,
    folded_ref, rows_ref, turned_ref,
):
    height = halo_rows(levels)
    parts = cols // LANES
    index_x = lax.axis_index("tx")
    index_y = lax.axis_index("ty")
    is_ocean = lax.axis_index("comp") == comps - 1
    last_y = index_y == count_y - 1
    has_west = jnp.where(jnp.logical_or(is_ocean, index_x > 0), 1.0, 0.0)
    has_east = jnp.where(jnp.logical_or(is_ocean, index_x < count_x - 1), 1.0, 0.0)
    has_south = jnp.where(index_y > 0, 1.0, 0.0)
    has_north = jnp.where(jnp.logical_or(is_ocean, jnp.logical_not(last_y)), 1.0, 0.0)
    drag = gains_ref[0, 2]
    mask_at = 4 * levels

    fold = fold_ref[pl.ds(index_x, 1), :]
    total = jnp.zeros((height, LANES), F32)
    up_start = up_ref.shape[0] - height * (parts + 1)
    sources = [(0, own_ref, 0), (-1, up_ref, up_start + height * parts), (1, down_ref, height * parts)]
    if north_ref.shape[0] > height:
        sources.append((2, north_ref, height))
    else:
        sources += [(shift, ref, 0) for shift, ref in zip(range(2, count_x - 1), far_refs)]
    for shift, ref, start in sources:
        at = lax.rem(index_x + shift + count_x, count_x)
        chosen = (iota((rows, rows), 0) + at * rows == fold).astype(F32)
        total += jnp.dot(
            ref[start : start + height, :], chosen,
            precision=lax.Precision.HIGHEST, preferred_element_type=F32,
        )
    folded_ref[...] = total

    line = iota((levels, LANES), 0)
    halves = jnp.zeros((levels, LANES), F32)
    for l in range(levels):
        halves = jnp.where(line == l, 0.5 * wave_ref[0, l], halves)

    def keeping(sea_values, drags):
        return jnp.where(is_ocean, sea_values, 1.0 - drags * (1.0 - sea_values))

    drags = jnp.where(line == 0, drag, 0.0)

    def by_level(ref, start, q):
        return ref[start + q * levels : start + (q + 1) * levels, :]

    for side, (ref, begin, sign, has) in enumerate(
        ((up_ref, up_start, 1.0, has_west), (down_ref, 0, -1.0, has_east))
    ):
        for p in range(parts):
            start = begin + p * height
            kept = keeping(ref[start + mask_at : start + mask_at + 1, :], drags)
            fixed = kept * (by_level(ref, start, EDGE_VELOCITY) + sign * halves * by_level(ref, start, SECOND_P))
            inner = rows - 1 if side else 0
            own = jnp.concatenate(
                [state_ref[0, 0, l, inner : inner + 1, p * LANES : (p + 1) * LANES] for l in range(levels)], axis=0
            )
            rows_ref[side, p, 0] = has * by_level(ref, start, EDGE_P)
            rows_ref[side, p, 1] = has * by_level(ref, start, EDGE_T)
            rows_ref[side, p, 2] = has * (fixed - sign * kept * halves * own)

    even = lambda ref: ref[pl.ds(0, levels, stride=2), :]
    odd = lambda ref: ref[pl.ds(1, levels, stride=2), :]
    north = [
        jnp.where(last_y, jnp.where(is_ocean, folded, 0.0), low)
        for folded, low in (
            (odd(folded_ref), even(north_ref)),
            (even(folded_ref), odd(north_ref)),
            (-by_level(folded_ref, 0, EDGE_VELOCITY), by_level(north_ref, 0, EDGE_VELOCITY)),
            (by_level(folded_ref, 0, EDGE_T), by_level(north_ref, 0, EDGE_T)),
            (folded_ref[mask_at : mask_at + 1, :], north_ref[mask_at : mask_at + 1, :]),
        )
    ]
    south = [
        odd(south_ref), even(south_ref), by_level(south_ref, 0, EDGE_VELOCITY), by_level(south_ref, 0, EDGE_T),
        south_ref[mask_at : mask_at + 1, :],
    ]
    fill = jnp.zeros((LANES // 2 - 4 * levels, LANES), F32)
    lines = []
    for (edge, second, velocity, tracer, sea), sign, has in (
        (south, 1.0, has_south), (north, -1.0, has_north)
    ):
        kept = keeping(sea, drags)
        fixed = has * kept * (velocity + sign * halves * second)
        lines += [has * edge, has * tracer, fixed, has * kept * halves, fill]
    high, low = split_two(jnp.concatenate(lines, axis=0).T)
    turned_ref[:, :LANES] = high
    turned_ref[:, LANES:] = low


def stencil_matrices(rows, cols):
    steps = [[numpy.eye(n, k=k, dtype=numpy.float32) for k in (1, -1, 0)] for n in (rows, cols)]
    after, before, _ = steps[0]
    along = [numpy.concatenate([m, m], axis=1) for m in (after - before, after + before)]
    before, after, centre = steps[1]
    across = [numpy.concatenate([m, m], axis=0) for m in (after - before, after + before - 4 * centre)]
    return jnp.asarray(numpy.stack(along), BF16), jnp.asarray(numpy.stack(across), BF16)


def stencil_levels(
    rows, cols, comps, begin, end, state_ref, mask_ref, rows_ref, turned_ref, wave_ref, spread_ref, gains_ref,
    along_ref, across_ref, place_refs, news_ref, after,
):
    levels = state_ref.shape[2]
    parts = cols // LANES
    is_ocean = lax.axis_index("comp") == comps - 1
    drag = gains_ref[0, 2]
    for ref in place_refs:
        ref[...] = jnp.zeros_like(ref)
    sea = mask_ref[0].astype(F32)
    tendency = jnp.where(is_ocean, sea, 1.0)
    first = iota((8, cols), 0) == 0
    last = iota((8, cols), 0) == 7
    places, lanes = iota((4 * levels, LANES), 0), iota((4 * levels, LANES), 1)

    def product(left, right):
        return jnp.dot(left, right, preferred_element_type=F32)

    def one_level(level, place_ref):
        half = 0.5 * wave_ref[0, level]
        spread = spread_ref[0, level]
        level_drag = jnp.where(level == 0, drag, 0.0)
        for q, sign in enumerate((-1.0, 1.0, -1.0, 1.0)):
            found = places == q * levels + level
            south = jnp.where(jnp.logical_and(found, lanes == 0), sign, 0.0).astype(BF16)
            north = jnp.where(jnp.logical_and(found, lanes == LANES - 1), 1.0, 0.0).astype(BF16)
            for term in range(2):
                at = term * LANES
                place_ref[q, at : at + 4 * levels, :LANES] = south
                at += LANES // 2
                place_ref[q, at : at + 4 * levels, cols - LANES :] = north

        def across(which, q, field):
            inner = product(jnp.concatenate(split_two(field), axis=1), across_ref[which])
            return inner + product(turned_ref[...], place_ref[q])

        def along(which, q, field):
            found = product(along_ref[which], jnp.concatenate(split_two(field), axis=0))
            west, east = (
                jnp.concatenate([rows_ref[side, p, q, pl.ds(level, 1), :] for p in range(parts)], axis=1)
                for side in range(2)
            )
            if which == 0:
                west = -west
            upper = found[:8] + jnp.where(first, west, 0.0)
            lower = found[rows - 8 :] + jnp.where(last, east, 0.0)
            return jnp.concatenate([upper, found[8 : rows - 8], lower], axis=0)

        pressure, zonal, meridional, tracer = (state_ref[0, v, level] for v in range(4))
        keep = jnp.where(is_ocean, sea, 1.0 - level_drag * (1.0 - sea))
        new_zonal = keep * (zonal - half * along(0, 0, pressure))
        new_meridional = keep * (meridional - half * across(0, 0, pressure))
        new_tracer = tracer + spread * tendency * (along(1, 1, tracer) + across(1, 1, tracer))
        beyond = product(turned_ref[...], place_ref[3]) * pressure
        divergence = along(0, 2, new_zonal) + across(0, 2, new_meridional) + beyond
        now = level - begin
        news_ref[0, now] = pressure - half * divergence
        news_ref[1, now] = new_zonal
        news_ref[2, now] = new_meridional
        news_ref[3, now] = new_tracer
        after(level)

    def some(c, carry):
        for i in range(length):
            one_level(begin + c * length + i, place_refs[i % len(place_refs)])
        return carry

    length = 2 if (end - begin) % 2 == 0 else 1
    lax.fori_loop(0, (end - begin) // length, some, 0)


def place_scratch(cols):
    return [pltpu.VMEM((4, 2 * LANES, cols), BF16)] * 2


def deep_body(
    sizes, begin,
    state_ref, mask_ref, up_ref, down_ref, south_ref, north_ref, own_ref, fold_ref,
    wave_ref, spread_ref, gains_ref, along_ref, across_ref, *rest,
):
    levels, rows, cols, comps, count_x, count_y = sizes
    far_refs, (news_ref, rows_ref, turned_ref, folded_ref, *place_refs) = rest[:-6], rest[-6:]
    stencil_halos(
        *sizes, state_ref, up_ref, down_ref, south_ref, north_ref, own_ref, fold_ref, far_refs, wave_ref, gains_ref,
        folded_ref, rows_ref, turned_ref,
    )
    stencil_levels(
        rows, cols, comps, begin, levels, state_ref, mask_ref, rows_ref, turned_ref, wave_ref, spread_ref, gains_ref,
        along_ref, across_ref, place_refs, news_ref, lambda level: None,
    )


def upper_body(
    sizes, end, begun_ref, state_ref, mask_ref, rows_ref, turned_ref, wave_ref, spread_ref, gains_ref,
    along_ref, across_ref, out_ref, new_surface_ref, old_surface_ref, place0, place1, news_ref, stores,
):
    levels, rows, cols, comps, count_x, count_y = sizes

    def store(l, v):
        return pltpu.make_async_copy(news_ref.at[v, l], out_ref.at[0, v, l], stores.at[l, v])

    def after(level):
        for v in range(4):
            store(level, v).start()

    stencil_levels(
        rows, cols, comps, 0, end, state_ref, mask_ref, rows_ref, turned_ref, wave_ref, spread_ref, gains_ref,
        along_ref, across_ref, (place0, place1), news_ref, after,
    )
    for v in range(3):
        new_surface_ref[v] = news_ref[v + 1, 0]
        old_surface_ref[v] = state_ref[0, v + 1, 0]
    for l in range(end):
        for v in range(4):
            store(l, v).wait()


def deep_levels(model_state, sea_mask, halos, fars, fold_map, wave_speed, diffusivity, gains, matrices, sizes, begin):
    levels, rows, cols, comps, count_x, count_y = sizes
    parts = cols // LANES
    fold = fold_map.reshape(count_x, rows)
    vmem = pl.BlockSpec(memory_space=pltpu.VMEM)
    scalar = pl.BlockSpec(memory_space=pltpu.SMEM)
    shapes = ((4, levels - begin, rows, cols), (2, parts, 3, levels, LANES), (rows, 2 * LANES))
    return pl.pallas_call(
        functools.partial(deep_body, sizes, begin),
        in_specs=[vmem] * 8 + [scalar] * 3 + [vmem] * (2 + len(fars)),
        out_specs=[vmem] * 3,
        out_shape=[jax.ShapeDtypeStruct(shape, kind) for shape, kind in zip(shapes, (F32, F32, BF16))],
        scratch_shapes=[
            pltpu.VMEM((halo_rows(levels), LANES), F32),
        ]
        + place_scratch(cols),
        compiler_params=pltpu.CompilerParams(vmem_limit_bytes=VMEM_BYTES),
    )(model_state, sea_mask, *halos, fold, wave_speed, diffusivity, gains, *matrices, *fars)


def upper_levels(
    begun, model_state, sea_mask, edge_rows, edge_columns, wave_speed, diffusivity, gains, matrices, sizes, end
):
    levels, rows, cols, comps, count_x, count_y = sizes
    vmem = pl.BlockSpec(memory_space=pltpu.VMEM)
    scalar = pl.BlockSpec(memory_space=pltpu.SMEM)
    anywhere = pl.BlockSpec(memory_space=pl.ANY)
    surface = jax.ShapeDtypeStruct((3, rows, cols), F32)
    return pl.pallas_call(
        functools.partial(upper_body, sizes, end),
        in_specs=[anywhere] + [vmem] * 4 + [scalar] * 3 + [vmem] * 2,
        out_specs=[anywhere, vmem, vmem],
        out_shape=[jax.ShapeDtypeStruct(begun.shape, F32), surface, surface],
        scratch_shapes=place_scratch(cols)
        + [pltpu.VMEM((4, end, rows, cols), F32), pltpu.SemaphoreType.DMA((end, 4))],
        input_output_aliases={0: 0},
        compiler_params=pltpu.CompilerParams(vmem_limit_bytes=VMEM_BYTES),
    )(begun, model_state, sea_mask, edge_rows, edge_columns, wave_speed, diffusivity, gains, *matrices)


def add_slots(rows, cols, groups, slab_ref, total_ref, chunks, plan, length, runs=1):
    row_ids = packed_ids(rows)
    col_ids = packed_ids(cols)
    lane = iota((1, LANES), 1)
    one = jnp.ones((), BF16)
    zero = jnp.zeros((), BF16)
    block = 4

    def one_chunk(total_ref, chunk):
        n, first, low_slot, high_slot = plan(chunk)
        start = n * (CHANNELS * groups) + first
        for begin in range(0, DEPTH, block):
            columns, spreads = [], []
            for g in range(begin, begin + block):
                cells = slab_ref[pl.ds(start + 4 * groups + g, 1), :].astype(I32)
                slot = lane + (first + g) * LANES
                mine = jnp.logical_and(slot >= low_slot, slot < high_slot)
                row = spread_row(jnp.where(mine, cells // cols, -1)).astype(F32).astype(BF16)
                col = spread_row(cells % cols).astype(F32).astype(BF16)
                columns.append(jnp.where(col_ids == col[None], one, zero).reshape(cols, LANES))
                in_row = row_ids == row[None]
                highs, lows = [], []
                for v in range(4):
                    value = spread_row(slab_ref[pl.ds(start + v * groups + g, 1), :])
                    high, low = split_two(value)
                    highs.append(jnp.where(in_row, high[None], zero).reshape(rows, LANES))
                    lows.append(jnp.where(in_row, low[None], zero).reshape(rows, LANES))
                spreads.append(jnp.concatenate(highs + lows, axis=0))
            total_ref[...] += lax.dot_general(
                jnp.concatenate(spreads, axis=1), jnp.concatenate(columns, axis=1), (((1,), (1,)), ((), ())),
                preferred_element_type=F32,
            )

    def turn(c, carry):
        for i in range(length):
            one_chunk(total_ref if runs == 1 else total_ref.at[c], c * length + i)
        return carry

    def single(c, carry):
        one_chunk(total_ref, c)
        return carry

    total_ref[...] = jnp.zeros_like(total_ref)
    turns = chunks // length
    lax.fori_loop(0, turns, turn, 0)
    if runs == 1:
        lax.fori_loop(turns * length, chunks, single, 0)


def halves_added(total_ref, rows):
    return total_ref[: 4 * rows] + total_ref[4 * rows :]


def add_own(rows, cols, comps, groups, slab_ref, total_ref, skipped):
    here = lax.axis_index("comp")
    pieces = groups // DEPTH
    near = slab_ref.shape[0] // (CHANNELS * groups) - skipped
    bounds = share_bounds(groups * LANES, comps - 1)
    is_ocean = here == comps - 1
    beside = here == comps - 2

    def plan(chunk):
        n = skipped + jnp.where(is_ocean, chunk, chunk // pieces)
        first = jnp.where(is_ocean, groups - DEPTH, chunk % pieces * DEPTH)
        return n, first, jnp.where(is_ocean, bounds[comps - 2], 0), groups * LANES

    chunks = jnp.where(is_ocean, near, jnp.where(beside, near * pieces, 0))
    add_slots(rows, cols, groups, slab_ref, total_ref, chunks, plan, 3 if near == 3 else 2)


def own_body(rows, cols, comps, groups, slab_ref, before_ref, sent_ref, total_ref):
    add_own(rows, cols, comps, groups, slab_ref, total_ref, 0)
    sent_ref[...] = before_ref[...] + halves_added(total_ref, rows)


def other_body(
    rows, cols, comps, groups, slab_ref, before_ref, deep_ref, kept_ref, sent_ref, state_ref,
    totals_ref, copies,
):
    here = lax.axis_index("comp")
    pieces = groups // DEPTH
    near = slab_ref.shape[0] // (CHANNELS * groups)
    bounds = share_bounds(groups * LANES, comps - 1)
    is_ocean = here == comps - 1
    beside = here == comps - 2
    for_two = here == comps - 3
    middle = bounds[1] // LANES // 4 * 4
    count = deep_ref.shape[1]
    stores = [
        pltpu.make_async_copy(
            deep_ref.at[v], state_ref.at[0, v, pl.ds(state_ref.shape[2] - count, count)], copies.at[v]
        )
        for v in range(4)
    ]
    for store in stores:
        store.start()

    def plan(chunk):
        mine = chunk >= near
        n = jnp.where(for_two, chunk % near, chunk // pieces)
        first = jnp.where(for_two, jnp.where(mine, middle, 0), chunk % pieces * DEPTH)
        low_slot = jnp.where(jnp.logical_and(for_two, mine), bounds[1], 0)
        high_slot = jnp.where(for_two, jnp.where(mine, bounds[2], bounds[1]), groups * LANES)
        return n, first, low_slot, high_slot

    chunks = jnp.where(here == 0, 0, near * pieces)
    add_slots(rows, cols, groups, slab_ref, totals_ref, chunks, plan, near * pieces // 2, 2)
    first_ref, second_ref = totals_ref.at[0], totals_ref.at[1]
    for start in range(0, 4 * rows, rows):
        first = first_ref[start : start + rows] + first_ref[start + 4 * rows : start + 5 * rows]
        second = second_ref[start : start + rows] + second_ref[start + 4 * rows : start + 5 * rows]
        kept_ref[start : start + rows] = jnp.where(beside, 0.0, second) + jnp.where(is_ocean, first, 0.0)
        sent = jnp.where(is_ocean, 0.0, first) + jnp.where(beside, second, 0.0)
        sent_ref[start : start + rows] = sent + before_ref[start : start + rows]
    for store in stores:
        store.wait()


def scatter_own(arrived, before, rows, cols, comps, slots):
    vmem = pl.BlockSpec(memory_space=pltpu.VMEM)
    return pl.pallas_call(
        functools.partial(own_body, rows, cols, comps, slots // LANES),
        in_specs=[vmem] * 2,
        out_specs=vmem,
        out_shape=jax.ShapeDtypeStruct((4 * rows, cols), F32),
        scratch_shapes=[pltpu.VMEM((8 * rows, cols), F32)],
        compiler_params=pltpu.CompilerParams(vmem_limit_bytes=VMEM_BYTES),
    )(arrived, before)


def scatter_other(other, before, deep, state_shape, rows, cols, comps, slots):
    vmem = pl.BlockSpec(memory_space=pltpu.VMEM)
    sums = jax.ShapeDtypeStruct((4 * rows, cols), F32)
    return pl.pallas_call(
        functools.partial(other_body, rows, cols, comps, slots // LANES),
        in_specs=[vmem] * 3,
        out_specs=[vmem, vmem, pl.BlockSpec(memory_space=pl.ANY)],
        out_shape=[sums, sums, jax.ShapeDtypeStruct(state_shape, F32)],
        scratch_shapes=[pltpu.VMEM((2, 8 * rows, cols), F32), pltpu.SemaphoreType.DMA((4,))],
        compiler_params=pltpu.CompilerParams(vmem_limit_bytes=VMEM_BYTES),
    )(other, before, deep)


def finish_body(rows, comps, state_ref, new_ref, old_ref, kept_ref, came_ref, mask_ref, gains_ref, out_ref, news_ref, copies):
    is_ocean = lax.axis_index("comp") == comps - 1
    tendency = jnp.where(is_ocean, mask_ref[0].astype(F32), 1.0)
    sums = [kept_ref[v * rows : (v + 1) * rows, :] + came_ref[v * rows : (v + 1) * rows, :] for v in range(4)]
    saves = []
    for v, total, gain in ((0, sums[1], 1), (1, sums[2], 1), (2, sums[0], 0)):
        news_ref[v] = new_ref[v] + tendency * gains_ref[0, gain] * (total - sums[3] * old_ref[v])
        saves.append(pltpu.make_async_copy(news_ref.at[v], out_ref.at[0, v + 1, 0], copies.at[v]))
        saves[-1].start()
    for save in saves:
        save.wait()


def finish(state, new_surface, old_surface, kept, came, sea_mask, gains, comps):
    rows, cols = state.shape[3:]
    vmem = pl.BlockSpec(memory_space=pltpu.VMEM)
    anywhere = pl.BlockSpec(memory_space=pl.ANY)
    return pl.pallas_call(
        functools.partial(finish_body, rows, comps),
        in_specs=[anywhere] + [vmem] * 5 + [pl.BlockSpec(memory_space=pltpu.SMEM)],
        out_specs=anywhere,
        out_shape=jax.ShapeDtypeStruct(state.shape, F32),
        scratch_shapes=[pltpu.VMEM((3, rows, cols), F32), pltpu.SemaphoreType.DMA((3,))],
        input_output_aliases={0: 0},
        compiler_params=pltpu.CompilerParams(vmem_limit_bytes=VMEM_BYTES),
    )(state, new_surface, old_surface, kept, came, sea_mask, gains)


def shards(
    model_state, sea_mask, wave_speed, diffusivity, surface_gains, area_table,
    own_cells, target_cells, weight_ids, pair_counts, fold_map,
):
    comps, count_x, count_y = (lax.axis_size(a) for a in ("comp", "tx", "ty"))
    positions = count_x * count_y
    rows, cols = model_state.shape[3:]
    slots = own_cells.shape[3]
    slot_arrays = (own_cells, target_cells, weight_ids, area_table.reshape(-1, LANES), pair_counts)

    def along(block, shift):
        return lax.ppermute(block, ("tx", "ty"), [(s, (s + shift) % positions) for s in range(positions)])

    y_pair = count_y == 2
    slab_rows = CHANNELS * slots // LANES
    slab1, up, slab3, fold = first_side(model_state, slot_arrays, sea_mask, comps)
    slab3 = along(slab3, 1 + count_y)
    slab1 = along(slab1, 1)
    up = along(up, count_y)
    slab0, down, high, low, pair, before = second_side(model_state, slot_arrays, fold, sea_mask, comps, y_pair)
    others = jnp.concatenate([slab1, up[:slab_rows], slab3[:slab_rows]])
    arrived = jnp.concatenate([slab0, others])
    other = lax.ppermute(arrived, "comp", [(g, g ^ 2) for g in range(comps)])

    down = along(down, -count_y)
    fars = []
    if y_pair and count_x == 4:
        south = north = lax.ppermute(jnp.concatenate([pair, slab3[slab_rows:]]), "ty", [(0, 1), (1, 0)])
    else:
        south = lax.ppermute(high, "ty", [(j, j + 1) for j in range(count_y - 1)])
        north = lax.ppermute(low, "ty", [(j + 1, j) for j in range(count_y - 1)])
        for shift in range(2, count_x - 1):
            pairs = []
            for i in range(count_x):
                ends = [((comps - 1) * count_x + k) * count_y + count_y - 1 for k in ((i + shift) % count_x, i)]
                pairs.append(tuple(ends))
            fars.append(lax.ppermute(fold, ("comp", "tx", "ty"), pairs))

    sizes = (*model_state.shape[2:], comps, count_x, count_y)
    cut = sizes[0] // 2
    matrices = stencil_matrices(rows, cols)
    before = scatter_own(others, before, rows, cols, comps, slots)
    deep, edge_rows, edge_columns = deep_levels(
        model_state, sea_mask, (up, down, south, north, fold), fars, fold_map,
        wave_speed, diffusivity, surface_gains, matrices, sizes, cut,
    )
    kept, sent, begun = scatter_other(other, before, deep, model_state.shape, rows, cols, comps, slots)
    came = lax.ppermute(sent, "comp", [(g, g ^ 1) for g in range(comps)])
    new_state, new_surface, old_surface = upper_levels(
        begun, model_state, sea_mask, edge_rows, edge_columns, wave_speed, diffusivity, surface_gains,
        matrices, sizes, cut,
    )
    return finish(new_state, new_surface, old_surface, kept, came, sea_mask, surface_gains, comps)


def solution(mesh):
    in_specs = (
        P("comp", None, None, "tx", "ty"),
        P("comp", "tx", "ty"),
        P("comp", None),
        P("comp", None),
        P("comp", None),
        P(),
        P("comp", ("tx", "ty"), None, None),
        P("comp", ("tx", "ty"), None, None),
        P("comp", ("tx", "ty"), None, None),
        P("comp", ("tx", "ty"), None),
        P(),
    )
    out_specs = P("comp", None, None, "tx", "ty")
    return jax.shard_map(shards, mesh=mesh, in_specs=in_specs, out_specs=out_specs, check_vma=False)
```
